32 devices in a mesh: grp: 2 (over x), sfc: 16 (over z, y, core).
Axes of the slice: x: 2, y: 2, z: 4, core: 2. Of those that a mesh axis runs over, the one named last changes fastest.
Arguments:
- charges: bfloat16 [512, 8, 256], P(('grp', 'sfc')), parts along dimension 0, may hold values from -6 to 6
- self_blocks: bfloat16 [512, 256, 256], P(('grp', 'sfc')), parts along dimension 0, may hold values from -0.375 to 0.375
- near_blocks: bfloat16 [1024, 256, 256], P(('grp', 'sfc')), parts along dimension 0, may hold values from -0.375 to 0.375
- near_pairs: int32 [1024, 2], P(('grp', 'sfc')), parts along dimension 0, may hold values from 0 to 255, as said below
- bases: bfloat16 [512, 64, 256], P(('grp', 'sfc')), parts along dimension 0, may hold values from -0.375 to 0.375
- transfers: bfloat16 [512, 64, 64], P(('grp', 'sfc')), parts along dimension 0, may hold values from -0.75 to 0.75
- parent_of: int32 [512], P(('grp', 'sfc')), parts along dimension 0, may hold values from 0 to 127, as said below
- far_pairs: int32 [4096, 2], P(('grp', 'sfc')), parts along dimension 0, may hold values from -1 to 255, as said below
- far_coupling: bfloat16 [4096, 64, 64], P(('grp', 'sfc')), parts along dimension 0, may hold values from -0.75 to 0.75
- par_pairs: int32 [1024, 2], P(('grp', 'sfc')), parts along dimension 0, may hold values from 0 to 127, as said below
- par_coupling: bfloat16 [1024, 64, 64], P(('grp', 'sfc')), parts along dimension 0, may hold values from -0.75 to 0.75
Outputs:
- potentials: float32 [512, 8, 256], P(('grp', 'sfc')), parts along dimension 0
The draws below stay inside these ranges and needn't reach their ends.
There are 2 independent parts, one for each index of `grp`. The reference program is written for one: setup_inputs(seed, part) draws one part's arguments, and reference() takes and returns one part's arrays. A program takes and returns all parts, laid end to end along the dimension named above; each array names one. Nothing has to cross between parts.
Inputs may be any that keep to these rules, and one draw needn't show every extreme that they name: `near_pairs`: slot s lies on device d = s // 32; column 0 is a leaf of device d (leaves d * 16 to (d + 1) * 16 - 1), column 1 a different leaf of device d or of device d + 1; on the last device only of device d. `parent_of`: leaves of device d have parents of device d (parents d * 8 to (d + 1) * 8 - 1), non-decreasing along the leaves; every parent has at least one child. `far_pairs`: the 128 slots of device d form 16 buckets of 8 slots; column 0 is always a leaf of device d; in bucket k a live slot has column 1 a leaf of device k (different from column 0 when k = d), an empty slot has -1; live slots come first in a bucket. At most 8 live slots a bucket, and every device has a full bucket. `par_pairs`: pair s lies on device d = s // 32; column 0 is a parent of device d, column 1 any other parent.
All inputs are finite; a program needn't handle non-finite values.
Results may differ from the reference program's by a relative error of at most 0.004.
Values may be sent and summed in bfloat16 or wider, within the bound.
No kernel may reach another device: no remote copies, remote signals or barrier semaphores. Data moves between devices by JAX's collectives and lax.ppermute only.
A program may use at most 128 MiB of HBM per device.

```python
import jax
import jax.numpy as jnp
from jax import lax

R = 8
P_SIZE = 256
K = 64
L_DEV = 16
F_PEER = 8
PF_DEV = 32
PAR_DEV = 8
NP_DEV = 32
LEAVES = 256
PARENTS = 128
NEAR = 512
FAR = 2048
PFAR = 512


def draw_near_pairs(key, part):
    key = jax.random.fold_in(key, 11)
    device_count = LEAVES // L_DEV
    key_owner, key_other = jax.random.split(key)
    device = jnp.arange(NEAR) // NP_DEV
    owner = jax.random.randint(key_owner, (NEAR,), 0, L_DEV)
    other = jax.random.randint(key_other, (NEAR,), 0, 2 * L_DEV - 1)
    reach = jnp.where(device == device_count - 1, L_DEV, 2 * L_DEV)
    partner = (owner + 1 + other % (reach - 1)) % reach
    return jnp.stack([device * L_DEV + owner, device * L_DEV + partner], axis=1).astype(jnp.int32)


def draw_parent_of(key, part):
    key = jax.random.fold_in(key, 17)
    device_count = LEAVES // L_DEV
    keys = jax.random.split(key, device_count)
    orders = jax.vmap(lambda one_key: jax.random.permutation(one_key, L_DEV - 1))(keys)
    breaks = (orders < PAR_DEV - 1).astype(jnp.int32)
    local_parent = jnp.concatenate([jnp.zeros((device_count, 1), jnp.int32), jnp.cumsum(breaks, axis=1)], axis=1)
    device = jnp.arange(device_count, dtype=jnp.int32)[:, None]
    return (device * PAR_DEV + local_parent).reshape(-1).astype(jnp.int32)


def draw_far_pairs(key, part):
    key = jax.random.fold_in(key, 23)
    device_count = LEAVES // L_DEV
    key_count, key_owner, key_other = jax.random.split(key, 3)
    slot = jnp.arange(FAR)
    device = slot // (device_count * F_PEER)
    peer = slot // F_PEER % device_count
    position = slot % F_PEER
    counts = jax.random.randint(key_count, (device_count, device_count), 0, F_PEER + 1)
    column = jnp.arange(device_count)
    full_bucket = column[None, :] == (column[:, None] + 1) % device_count
    counts = jnp.where(full_bucket, F_PEER, counts)
    is_live = position < counts[device, peer]
    owner = jax.random.randint(key_owner, (FAR,), 0, L_DEV)
    other = jax.random.randint(key_other, (FAR,), 0, L_DEV)
    same_device = (owner + 1 + other % (L_DEV - 1)) % L_DEV
    partner = jnp.where(peer == device, same_device, other)
    first_col = device * L_DEV + owner
    second_col = jnp.where(is_live, peer * L_DEV + partner, -1)
    return jnp.stack([first_col, second_col], axis=1).astype(jnp.int32)


def draw_par_pairs(key, part):
    key = jax.random.fold_in(key, 29)
    key_owner, key_other = jax.random.split(key)
    device = jnp.arange(PFAR) // PF_DEV
    owner = device * PAR_DEV + jax.random.randint(key_owner, (PFAR,), 0, PAR_DEV)
    other = jax.random.randint(key_other, (PFAR,), 0, PARENTS - 1)
    partner = jnp.where(other >= owner, other + 1, other)
    return jnp.stack([owner, partner], axis=1).astype(jnp.int32)


def block_levels(own_key, shape, shards, low, high):
    loudness = 1.0
    for axis_at, parts in shards:
        draws = jax.random.uniform(jax.random.fold_in(jax.random.fold_in(own_key, 6), axis_at), (parts,), jnp.float32, low / len(shards), high / len(shards))
        loudness = loudness * jnp.repeat(jnp.exp(draws), shape[axis_at] // parts).reshape((-1,) + (1,) * (len(shape) - 1 - axis_at))
    return loudness


def bell_draw(own_key, shape, scale, most, shards=(), held_as=jnp.bfloat16):
    loudness = block_levels(own_key, shape, shards, -0.22, 0.18) if shards else 1.0
    values = jax.random.normal(own_key, shape, jnp.float32) * scale * loudness
    return jnp.minimum(jnp.maximum(values, -most), most).astype(held_as)


def setup_inputs(seed: int = 0, part: int = 0) -> dict:
    key_list = jax.random.split(jax.random.key(seed), 12)
    own_keys = jax.random.split(jax.random.fold_in(key_list[11], part), 12)
    charges = bell_draw(own_keys[0], (LEAVES, R, P_SIZE), 1.0, 6.0, ((0, 16),))
    self_blocks = bell_draw(own_keys[1], (LEAVES, P_SIZE, P_SIZE), P_SIZE ** -0.5, 0.375, ((0, 16),))
    near_blocks = bell_draw(own_keys[2], (NEAR, P_SIZE, P_SIZE), P_SIZE ** -0.5, 0.375, ((0, 16),))
    near_pairs = draw_near_pairs(jax.random.fold_in(jax.random.fold_in(key_list[11], part), 71), part)
    bases = bell_draw(own_keys[4], (LEAVES, K, P_SIZE), P_SIZE ** -0.5, 0.375, ((0, 16),))
    transfers = bell_draw(own_keys[5], (LEAVES, K, K), K ** -0.5, 0.75, ((0, 16),))
    parent_of = draw_parent_of(jax.random.fold_in(jax.random.fold_in(key_list[11], part), 71), part)
    far_pairs = draw_far_pairs(jax.random.fold_in(jax.random.fold_in(key_list[11], part), 71), part)
    far_coupling = bell_draw(own_keys[8], (FAR, K, K), K ** -0.5, 0.75, ((0, 16),))
    par_pairs = draw_par_pairs(jax.random.fold_in(jax.random.fold_in(key_list[11], part), 71), part)
    par_coupling = bell_draw(own_keys[10], (PFAR, K, K), K ** -0.5, 0.75, ((0, 16),))
    return dict(charges=charges, self_blocks=self_blocks, near_blocks=near_blocks, near_pairs=near_pairs, bases=bases, transfers=transfers, parent_of=parent_of, far_pairs=far_pairs, far_coupling=far_coupling, par_pairs=par_pairs, par_coupling=par_coupling)


def rounded(values):
    return lax.optimization_barrier(values.astype(jnp.bfloat16)).astype(jnp.float32)


def reference(charges, self_blocks, near_blocks, near_pairs, bases, transfers, parent_of, far_pairs, far_coupling, par_pairs, par_coupling):
    wide = jnp.float32
    charge_f = charges.astype(wide)
    base_f = bases.astype(wide)
    transfer_f = transfers.astype(wide)
    moments = rounded(jnp.einsum("lkp,lrp->lrk", base_f, charge_f))
    child_terms = jnp.einsum("lkj,lrj->lrk", transfer_f, moments)
    parent_moments = rounded(jax.ops.segment_sum(child_terms, parent_of, num_segments=PARENTS))

    owner = far_pairs[:, 0]
    partner = far_pairs[:, 1]
    is_live = (partner >= 0).astype(wide)[:, None, None]
    partner_safe = jnp.where(partner >= 0, partner, 0)
    coupling_f = far_coupling.astype(wide)
    forward_far = jnp.einsum("skj,srj->srk", coupling_f, moments[partner_safe]) * is_live
    backward_far = jnp.einsum("sjk,srj->srk", coupling_f, moments[owner]) * is_live
    leaf_locals = jax.ops.segment_sum(forward_far, owner, num_segments=LEAVES) + jax.ops.segment_sum(backward_far, partner_safe, num_segments=LEAVES)

    par_owner = par_pairs[:, 0]
    par_partner = par_pairs[:, 1]
    par_f = par_coupling.astype(wide)
    forward_par = jnp.einsum("skj,srj->srk", par_f, parent_moments[par_partner])
    backward_par = jnp.einsum("sjk,srj->srk", par_f, parent_moments[par_owner])
    parent_locals = rounded(jax.ops.segment_sum(forward_par, par_owner, num_segments=PARENTS) + jax.ops.segment_sum(backward_par, par_partner, num_segments=PARENTS))

    downward = jnp.einsum("ljk,lrj->lrk", transfer_f, parent_locals[parent_of])
    locals_all = rounded(leaf_locals + downward)
    potentials = jnp.einsum("lkp,lrk->lrp", base_f, locals_all)
    potentials = potentials + jnp.einsum("lpq,lrq->lrp", self_blocks.astype(wide), charge_f)

    near_owner = near_pairs[:, 0]
    near_partner = near_pairs[:, 1]
    near_f = near_blocks.astype(wide)
    forward_near = jnp.einsum("spq,srq->srp", near_f, charge_f[near_partner])
    backward_near = jnp.einsum("spq,srp->srq", near_f, charge_f[near_owner])
    potentials = potentials + jax.ops.segment_sum(forward_near, near_owner, num_segments=LEAVES)
    potentials = potentials + jax.ops.segment_sum(backward_near, near_partner, num_segments=LEAVES)
    return potentials
```

```python
import functools

import jax
import jax.numpy as jnp
from jax import lax
from jax.experimental import pallas as pl
from jax.experimental.pallas import tpu as pltpu
from jax.sharding import PartitionSpec as P

F32 = jnp.float32
BF16 = jnp.bfloat16
LANES = 128


def dot_nn(a, b):
    return lax.dot_general(a, b, (((1,), (0,)), ((), ())), preferred_element_type=F32)


def dot_nt(a, b):
    return lax.dot_general(a, b, (((1,), (1,)), ((), ())), preferred_element_type=F32)


def dot_tn(a, b):
    return lax.dot_general(a, b, (((0,), (0,)), ((), ())), preferred_element_type=F32)


def split2(x):
    high = x.astype(BF16)
    return high, (x - high.astype(F32)).astype(BF16)


def iota(shape, axis):
    return lax.broadcasted_iota(jnp.int32, shape, axis)


def one_hot(condition):
    return jnp.where(condition, 1.0, 0.0).astype(BF16)


def rows_to_lanes(ref, count, rhs):
    return jnp.concatenate([ref[pl.ds(r, count, stride=rhs), :] for r in range(rhs)], axis=1)


def lanes_to_rows(ref, value, rhs):
    count, width = value.shape
    rank = width // rhs
    for r in range(rhs):
        ref[pl.ds(r, count, stride=rhs), :] = value[:, r * rank : (r + 1) * rank]


def pre_kernel(
    par_smem,
    charges,
    bases,
    transfers,
    parent_of,
    far_pairs,
    far_c,
    par_pairs,
    par_c,
    send,
    mo,
    ch,
    pm3,
    pb,
    a_ref,
    ob,
):
    leaves, rhs, _ = charges.shape
    rank = bases.shape[1]
    width = rhs * rank
    slots = far_c.shape[2]
    pairs = par_c.shape[0]
    parents = leaves // 2
    rows = send.shape[0]

    for l in range(leaves):
        m = dot_nt(charges[l], bases[l]).astype(BF16)
        mo[l * rhs : (l + 1) * rhs, :] = m.astype(F32)
        ch[l * rhs : (l + 1) * rhs, :] = dot_nt(m, transfers[l])
    m2 = rows_to_lanes(mo, leaves, rhs)
    high, low = split2(rows_to_lanes(ch, leaves, rhs))
    par_hot = one_hot(parent_of[...] % parents == iota((parents, leaves), 0))
    pm = (dot_nn(par_hot, high) + dot_nn(par_hot, low)).astype(BF16).astype(F32)
    lanes_to_rows(pm3, pm, rhs)
    shared = jnp.concatenate([m2[:parents], m2[parents:], pm], axis=1)
    shared = jnp.concatenate([shared, shared], axis=0).astype(BF16)
    at = 2 * width + LANES
    for p in range(rows // (2 * parents)):
        send[p * 2 * parents : (p + 1) * 2 * parents, at : at + 3 * width] = shared

    owner_hot = one_hot(far_pairs[0:1, :] % leaves == iota((leaves, slots), 0))
    a_ref[...] = dot_tn(m2.astype(BF16), owner_hot)
    half = rank // 2
    for sb in range(slots // LANES):
        lanes = slice(sb * LANES, (sb + 1) * LANES)
        for jh in range(2):

            def body(k8, acc):
                rows_a = [
                    a_ref[pl.ds(pl.multiple_of(r * rank + k8 * 8, 8), 8), lanes]
                    for r in range(rhs)
                ]
                for i in range(8):
                    c = far_c[k8 * 8 + i, jh * half : (jh + 1) * half, lanes].astype(F32)
                    acc = tuple(acc[r] + c * rows_a[r][i : i + 1, :] for r in range(rhs))
                return acc

            acc = lax.fori_loop(
                0, rank // 8, body, tuple(jnp.zeros((half, LANES), F32) for _ in range(rhs))
            )
            for r in range(rhs):
                first = r * rank + jh * half
                ob[first : first + half, lanes] = acc[r].astype(BF16)
    partner = far_pairs[1:2, :]
    local = jnp.where(partner >= 0, partner % leaves, -1).astype(F32)
    ob[width : width + LANES, :] = jnp.broadcast_to(local, (LANES, slots)).astype(BF16)
    unit = one_hot(iota((LANES, LANES), 0) == iota((LANES, LANES), 1))
    for sb in range(slots // LANES):
        lanes = slice(sb * LANES, (sb + 1) * LANES)
        send[lanes, 0 : width + LANES] = dot_nt(unit, ob[:, lanes]).astype(BF16)

    for s in range(pairs):
        q = par_smem[0, s] % parents
        x = pm3[pl.ds(pl.multiple_of(q * rhs, rhs), rhs), :].astype(BF16)
        pb[s * rhs : (s + 1) * rhs, :] = dot_nn(x, par_c[s])
    high, low = split2(rows_to_lanes(pb, pairs, rhs))
    hot = one_hot(par_pairs[1:2, :] == iota((rows, pairs), 0))
    at = width + LANES
    send[:, at : at + width] = (dot_nn(hot, high) + dot_nn(hot, low)).astype(BF16)


def near_kernel(pairs, charges, following, self_blocks, near_blocks, own, away, ext, out):
    leaves = charges.shape[0]
    step = pl.program_id(0)
    selves, nears = self_blocks.shape[0], near_blocks.shape[0]

    @pl.when(step == 0)
    def _():
        ext[0:leaves] = charges[...]
        ext[leaves:] = following[...]
        out[...] = jnp.zeros_like(out)

    for i in range(selves):
        l = step * selves + i
        out[l] += dot_nt(ext[l], self_blocks[i])
    for i in range(nears):
        s = step * nears + i
        a, b = pairs[0, s], pairs[1, s]
        first = (a // leaves) * leaves
        a, b = a - first, b - first
        out[a] += dot_nt(ext[b], near_blocks[i])
        out[b] += dot_nn(ext[a], near_blocks[i])

    @pl.when(step == pl.num_programs(0) - 1)
    def _():
        own[...] = out[0:leaves]
        away[...] = out[leaves:].astype(BF16)


def post_kernel(
    got,
    bases,
    transfers,
    parent_of,
    far_pairs,
    far_c,
    par_pairs,
    par_c,
    near_own,
    near_back,
    out,
    b_ref,
    fw,
    g_ref,
    pf,
    lf,
    pg,
):
    leaves, rank, _ = bases.shape
    slots = far_c.shape[2]
    pairs = par_c.shape[0]
    parents = leaves // 2
    rows = got.shape[0]
    rhs = b_ref.shape[0] // rank
    width = rhs * rank
    at_par = width + LANES
    at_mom = at_par + width

    row_id = iota((rows, slots), 0)
    base_leaf = row_id // parents * leaves + row_id % parents
    partner = far_pairs[1:2, :]
    total = None
    for h in range(2):
        hot = one_hot(partner == base_leaf + h * parents)
        part = dot_tn(got[:, at_mom + h * width : at_mom + (h + 1) * width], hot)
        total = part if total is None else total + part
    b_ref[...] = total

    hot = one_hot(par_pairs[1:2, :] == iota((rows, pairs), 0))
    picked = dot_tn(hot, got[:, at_mom + 2 * width : at_mom + 3 * width])
    lanes_to_rows(g_ref, picked, rhs)
    for s in range(pairs):
        x = g_ref[s * rhs : (s + 1) * rhs, :].astype(BF16)
        pf[s * rhs : (s + 1) * rhs, :] = dot_nt(x, par_c[s])
    high, low = split2(rows_to_lanes(pf, pairs, rhs))
    hot = one_hot(par_pairs[0:1, :] % parents == iota((parents, pairs), 0))
    fold = one_hot(iota((parents, rows), 1) % parents == iota((parents, rows), 0))
    locals_p = dot_nn(hot, high) + dot_nn(hot, low) + dot_nn(fold, got[:, at_par : at_par + width])
    hot = one_hot(parent_of[...] % parents == iota((parents, leaves), 0))
    lanes_to_rows(pg, dot_tn(hot, locals_p.astype(BF16)), rhs)

    for sb in range(slots // LANES):
        lanes = slice(sb * LANES, (sb + 1) * LANES)

        def body(k8, carry):
            for r in range(rhs):
                b = b_ref[r * rank : (r + 1) * rank, lanes]
                sums = [
                    jnp.sum(far_c[k8 * 8 + i, :, lanes].astype(F32) * b, axis=0, keepdims=True)
                    for i in range(8)
                ]
                fw[pl.ds(pl.multiple_of(r * rank + k8 * 8, 8), 8), lanes] = jnp.concatenate(
                    sums, axis=0
                )
            return carry

        lax.fori_loop(0, rank // 8, body, 0)

    hot = one_hot(far_pairs[0:1, :] % leaves == iota((leaves, slots), 0))
    high, low = split2(fw[...])
    leaf = dot_nt(hot, high) + dot_nt(hot, low)
    index = got[:, width : width + LANES].astype(F32)[:, :leaves].astype(jnp.int32)
    hot = one_hot(index == iota((rows, leaves), 1))
    leaf = leaf + dot_tn(hot, got[:, 0:width])
    lanes_to_rows(lf, leaf, rhs)

    for l in range(leaves):
        at = slice(l * rhs, (l + 1) * rhs)
        down = dot_nn(pg[at, :].astype(BF16), transfers[l])
        mine = (lf[at, :] + down).astype(BF16)
        out[l] = dot_nn(mine, bases[l]) + near_own[l] + near_back[l].astype(F32)


def passed_along(value, axis, steps):
    count = lax.axis_size(axis)
    leading, last = (max(0, -steps), min(count, count - steps))
    return lax.ppermute(value, axis, [(source, source + steps) for source in range(leading, last)])


def on_device(
    charges,
    self_blocks,
    near_blocks,
    near_pairs,
    bases,
    transfers,
    parent_of,
    far_pairs,
    far_coupling,
    par_pairs,
    par_coupling,
):
    leaves, rhs, panels = charges.shape
    rank = bases.shape[1]
    width = rhs * rank
    slots = far_coupling.shape[0]
    pairs = par_coupling.shape[0]
    parents = leaves // 2
    devices = lax.axis_size("sfc")
    rows = devices * parents
    columns = 5 * width + LANES
    vmem = pl.BlockSpec(memory_space=pltpu.VMEM)
    smem = pl.BlockSpec(memory_space=pltpu.SMEM)
    params = pltpu.CompilerParams(vmem_limit_bytes=48 * 1024 * 1024)

    following = passed_along(charges, "sfc", -1)
    far_pairs = far_pairs.T
    par_pairs = par_pairs.T
    near_pairs = near_pairs.T
    far_c = jnp.transpose(far_coupling, (1, 2, 0))
    parent_of = parent_of.reshape(1, leaves)

    send = pl.pallas_call(
        pre_kernel,
        out_shape=jax.ShapeDtypeStruct((rows, columns), BF16),
        in_specs=[smem] + [vmem] * 8,
        out_specs=vmem,
        scratch_shapes=[
            pltpu.VMEM((leaves * rhs, rank), F32),
            pltpu.VMEM((leaves * rhs, rank), F32),
            pltpu.VMEM((parents * rhs, rank), F32),
            pltpu.VMEM((pairs * rhs, rank), F32),
            pltpu.VMEM((width, slots), F32),
            pltpu.VMEM((width + LANES, slots), BF16),
        ],
        compiler_params=params,
        name="upward",
    )(par_pairs, charges, bases, transfers, parent_of, far_pairs, far_c, par_pairs, par_coupling)
    got = lax.all_to_all(send, "sfc", split_axis=0, concat_axis=0, tiled=True)

    steps = 8
    selves, nears = leaves // steps, near_blocks.shape[0] // steps
    whole = lambda *shape: pl.BlockSpec(shape, lambda i: (0,) * len(shape))
    near_own, near_away = pl.pallas_call(
        near_kernel,
        grid=(steps,),
        out_shape=[
            jax.ShapeDtypeStruct((leaves, rhs, panels), F32),
            jax.ShapeDtypeStruct((leaves, rhs, panels), BF16),
        ],
        in_specs=[
            smem,
            whole(leaves, rhs, panels),
            whole(leaves, rhs, panels),
            pl.BlockSpec((selves, panels, panels), lambda i: (i, 0, 0)),
            pl.BlockSpec((nears, panels, panels), lambda i: (i, 0, 0)),
        ],
        out_specs=[whole(leaves, rhs, panels)] * 2,
        scratch_shapes=[
            pltpu.VMEM((2 * leaves, rhs, panels), BF16),
            pltpu.VMEM((2 * leaves, rhs, panels), F32),
        ],
        compiler_params=params,
        name="near",
    )(near_pairs, charges, following, self_blocks, near_blocks)
    near_back = passed_along(near_away, "sfc", 1)

    return pl.pallas_call(
        post_kernel,
        out_shape=jax.ShapeDtypeStruct((leaves, rhs, panels), F32),
        in_specs=[vmem] * 10,
        out_specs=vmem,
        scratch_shapes=[
            pltpu.VMEM((width, slots), F32),
            pltpu.VMEM((width, slots), F32),
            pltpu.VMEM((pairs * rhs, rank), F32),
            pltpu.VMEM((pairs * rhs, rank), F32),
            pltpu.VMEM((leaves * rhs, rank), F32),
            pltpu.VMEM((leaves * rhs, rank), F32),
        ],
        compiler_params=params,
        name="downward",
    )(
        got,
        bases,
        transfers,
        parent_of,
        far_pairs,
        far_c,
        par_pairs,
        par_coupling,
        near_own,
        near_back,
    )


def solution(mesh):
    split = ("grp", "sfc")
    cube, flat = P(split, None, None), P(split, None)
    placed = (cube, cube, cube, flat, cube, cube, P(split), flat, cube, flat, cube)
    return jax.shard_map(
        on_device, mesh=mesh, in_specs=placed, out_specs=cube, check_vma=False
    )
```

```python
import functools

import jax
import jax.numpy as jnp
from jax import lax
from jax.experimental import pallas as pl
from jax.experimental.pallas import tpu as pltpu
from jax.sharding import PartitionSpec as P

F32 = jnp.float32
BF16 = jnp.bfloat16
LANES = 128


def dot_nn(a, b):
    return lax.dot_general(a, b, (((1,), (0,)), ((), ())), preferred_element_type=F32)


def dot_nt(a, b):
    return lax.dot_general(a, b, (((1,), (1,)), ((), ())), preferred_element_type=F32)


def dot_tn(a, b):
    return lax.dot_general(a, b, (((0,), (0,)), ((), ())), preferred_element_type=F32)


def split2(x):
    high = x.astype(BF16)
    return high, (x - high.astype(F32)).astype(BF16)


def iota(shape, axis):
    return lax.broadcasted_iota(jnp.int32, shape, axis)


def one_hot(condition):
    return jnp.where(condition, 1.0, 0.0).astype(BF16)


def rows_to_lanes(ref, count, rhs):
    return jnp.concatenate([ref[pl.ds(r, count, stride=rhs), :] for r in range(rhs)], axis=1)


def lanes_to_rows(ref, value, rhs):
    count, width = value.shape
    rank = width // rhs
    for r in range(rhs):
        ref[pl.ds(r, count, stride=rhs), :] = value[:, r * rank : (r + 1) * rank]


def fetch(pairs, sems):
    copies = [pltpu.make_async_copy(src, dst, sems.at[i]) for i, (src, dst) in enumerate(pairs)]
    for copy in copies:
        copy.start()
    return copies


def pre_kernel(
    charges_h,
    bases_h,
    transfers_h,
    parent_of_h,
    far_pairs_h,
    far_c_h,
    par_pairs_h,
    par_c_h,
    send,
    charges,
    bases,
    transfers,
    parent_of,
    far_pairs,
    far_c,
    par_pairs,
    par_c,
    par_smem,
    sems,
    mo,
    ch,
    pm3,
    pb,
    a_ref,
    ob,
):
    leaves, rhs, _ = charges.shape
    rank = bases.shape[1]
    width = rhs * rank
    slots = far_c.shape[2]
    pairs = par_c.shape[0]
    parents = leaves // 2
    rows = send.shape[0]
    copies = fetch(
        [
            (charges_h, charges),
            (bases_h, bases),
            (transfers_h, transfers),
            (parent_of_h, parent_of),
            (far_pairs_h, far_pairs),
            (par_pairs_h, par_pairs),
            (par_pairs_h, par_smem),
            (far_c_h, far_c),
            (par_c_h, par_c),
        ],
        sems,
    )
    for copy in copies[:3]:
        copy.wait()

    for l in range(leaves):
        m = dot_nt(charges[l], bases[l]).astype(BF16)
        mo[l * rhs : (l + 1) * rhs, :] = m.astype(F32)
        ch[l * rhs : (l + 1) * rhs, :] = dot_nt(m, transfers[l])
    for copy in copies[3:]:
        copy.wait()
    m2 = rows_to_lanes(mo, leaves, rhs)
    high, low = split2(rows_to_lanes(ch, leaves, rhs))
    par_hot = one_hot(parent_of[...] % parents == iota((parents, leaves), 0))
    pm = (dot_nn(par_hot, high) + dot_nn(par_hot, low)).astype(BF16).astype(F32)
    lanes_to_rows(pm3, pm, rhs)
    shared = jnp.concatenate([m2[:parents], m2[parents:], pm], axis=1)
    shared = jnp.concatenate([shared, shared], axis=0).astype(BF16)
    at = 2 * width + LANES
    for p in range(rows // (2 * parents)):
        send[p * 2 * parents : (p + 1) * 2 * parents, at : at + 3 * width] = shared

    owner_hot = one_hot(far_pairs[0:1, :] % leaves == iota((leaves, slots), 0))
    a_ref[...] = dot_tn(m2.astype(BF16), owner_hot)
    half = rank // 2
    for sb in range(slots // LANES):
        lanes = slice(sb * LANES, (sb + 1) * LANES)
        for jh in range(2):

            def body(k8, acc):
                rows_a = [
                    a_ref[pl.ds(pl.multiple_of(r * rank + k8 * 8, 8), 8), lanes]
                    for r in range(rhs)
                ]
                for i in range(8):
                    c = far_c[k8 * 8 + i, jh * half : (jh + 1) * half, lanes].astype(F32)
                    acc = tuple(acc[r] + c * rows_a[r][i : i + 1, :] for r in range(rhs))
                return acc

            acc = lax.fori_loop(
                0, rank // 8, body, tuple(jnp.zeros((half, LANES), F32) for _ in range(rhs))
            )
            for r in range(rhs):
                first = r * rank + jh * half
                ob[first : first + half, lanes] = acc[r].astype(BF16)
    partner = far_pairs[1:2, :]
    local = jnp.where(partner >= 0, partner % leaves, -1).astype(F32)
    ob[width : width + LANES, :] = jnp.broadcast_to(local, (LANES, slots)).astype(BF16)
    unit = one_hot(iota((LANES, LANES), 0) == iota((LANES, LANES), 1))
    for sb in range(slots // LANES):
        lanes = slice(sb * LANES, (sb + 1) * LANES)
        send[lanes, 0 : width + LANES] = dot_nt(unit, ob[:, lanes]).astype(BF16)

    for s in range(pairs):
        q = par_smem[0, s] % parents
        x = pm3[pl.ds(pl.multiple_of(q * rhs, rhs), rhs), :].astype(BF16)
        pb[s * rhs : (s + 1) * rhs, :] = dot_nn(x, par_c[s])
    high, low = split2(rows_to_lanes(pb, pairs, rhs))
    hot = one_hot(par_pairs[1:2, :] == iota((rows, pairs), 0))
    at = width + LANES
    send[:, at : at + width] = (dot_nn(hot, high) + dot_nn(hot, low)).astype(BF16)


def near_kernel(pairs, charges, following, self_blocks, near_blocks, own, away, ext, out):
    leaves = charges.shape[0]
    step = pl.program_id(0)
    selves, nears = self_blocks.shape[0], near_blocks.shape[0]

    @pl.when(step == 0)
    def _():
        ext[0:leaves] = charges[...]
        ext[leaves:] = following[...]
        out[...] = jnp.zeros_like(out)

    terms = [(step * selves + i, dot_nt(ext[step * selves + i], self_blocks[i])) for i in range(selves)]
    for i in range(nears):
        a, b = pairs[0, step * nears + i], pairs[1, step * nears + i]
        first = (a // leaves) * leaves
        a, b = a - first, b - first
        terms.append((a, dot_nt(ext[b], near_blocks[i])))
        terms.append((b, dot_nn(ext[a], near_blocks[i])))
    for at, term in terms:
        out[at] += term

    @pl.when(step == pl.num_programs(0) - 1)
    def _():
        own[...] = out[0:leaves]
        away[...] = out[leaves:].astype(BF16)


def post_kernel(
    bases_h,
    transfers_h,
    parent_of_h,
    far_pairs_h,
    far_c_h,
    par_pairs_h,
    par_c_h,
    got,
    near_own,
    near_back,
    out,
    bases,
    transfers,
    parent_of,
    far_pairs,
    far_c,
    par_pairs,
    par_c,
    sems,
    b_ref,
    fw,
    g_ref,
    pf,
    lf,
    pg,
):
    leaves, rank, _ = bases.shape
    slots = far_c.shape[2]
    pairs = par_c.shape[0]
    parents = leaves // 2
    rows = got.shape[0]
    rhs = b_ref.shape[0] // rank
    width = rhs * rank
    at_par = width + LANES
    at_mom = at_par + width
    copies = fetch(
        [
            (far_pairs_h, far_pairs),
            (par_pairs_h, par_pairs),
            (parent_of_h, parent_of),
            (par_c_h, par_c),
            (far_c_h, far_c),
            (transfers_h, transfers),
            (bases_h, bases),
        ],
        sems,
    )
    for copy in copies:
        copy.wait()

    row_id = iota((rows, slots), 0)
    base_leaf = row_id // parents * leaves + row_id % parents
    partner = far_pairs[1:2, :]
    total = None
    for h in range(2):
        hot = one_hot(partner == base_leaf + h * parents)
        part = dot_tn(got[:, at_mom + h * width : at_mom + (h + 1) * width], hot)
        total = part if total is None else total + part
    b_ref[...] = total

    hot = one_hot(par_pairs[1:2, :] == iota((rows, pairs), 0))
    picked = dot_tn(hot, got[:, at_mom + 2 * width : at_mom + 3 * width])
    lanes_to_rows(g_ref, picked, rhs)
    for s in range(pairs):
        x = g_ref[s * rhs : (s + 1) * rhs, :].astype(BF16)
        pf[s * rhs : (s + 1) * rhs, :] = dot_nt(x, par_c[s])
    high, low = split2(rows_to_lanes(pf, pairs, rhs))
    hot = one_hot(par_pairs[0:1, :] % parents == iota((parents, pairs), 0))
    fold = one_hot(iota((parents, rows), 1) % parents == iota((parents, rows), 0))
    locals_p = dot_nn(hot, high) + dot_nn(hot, low) + dot_nn(fold, got[:, at_par : at_par + width])
    hot = one_hot(parent_of[...] % parents == iota((parents, leaves), 0))
    lanes_to_rows(pg, dot_tn(hot, locals_p.astype(BF16)), rhs)

    for sb in range(slots // LANES):
        lanes = slice(sb * LANES, (sb + 1) * LANES)

        def body(k8, carry):
            for r in range(rhs):
                b = b_ref[r * rank : (r + 1) * rank, lanes]
                sums = [
                    jnp.sum(far_c[k8 * 8 + i, :, lanes].astype(F32) * b, axis=0, keepdims=True)
                    for i in range(8)
                ]
                fw[pl.ds(pl.multiple_of(r * rank + k8 * 8, 8), 8), lanes] = jnp.concatenate(
                    sums, axis=0
                )
            return carry

        lax.fori_loop(0, rank // 8, body, 0)

    hot = one_hot(far_pairs[0:1, :] % leaves == iota((leaves, slots), 0))
    high, low = split2(fw[...])
    leaf = dot_nt(hot, high) + dot_nt(hot, low)
    index = got[:, width : width + LANES].astype(F32)[:, :leaves].astype(jnp.int32)
    hot = one_hot(index == iota((rows, leaves), 1))
    leaf = leaf + dot_tn(hot, got[:, 0:width])
    lanes_to_rows(lf, leaf, rhs)

    for l in range(leaves):
        at = slice(l * rhs, (l + 1) * rhs)
        down = dot_nn(pg[at, :].astype(BF16), transfers[l])
        mine = (lf[at, :] + down).astype(BF16)
        out[l] = dot_nn(mine, bases[l]) + near_own[l] + near_back[l].astype(F32)


def passed_along(value, axis, steps):
    count = lax.axis_size(axis)
    leading, last = (max(0, -steps), min(count, count - steps))
    return lax.ppermute(value, axis, [(source, source + steps) for source in range(leading, last)])


def on_device(
    charges,
    self_blocks,
    near_blocks,
    near_pairs,
    bases,
    transfers,
    parent_of,
    far_pairs,
    far_coupling,
    par_pairs,
    par_coupling,
):
    leaves, rhs, panels = charges.shape
    rank = bases.shape[1]
    width = rhs * rank
    slots = far_coupling.shape[0]
    pairs = par_coupling.shape[0]
    parents = leaves // 2
    devices = lax.axis_size("sfc")
    rows = devices * parents
    columns = 5 * width + LANES
    vmem = pl.BlockSpec(memory_space=pltpu.VMEM)
    smem = pl.BlockSpec(memory_space=pltpu.SMEM)
    hbm = pl.BlockSpec(memory_space=pltpu.HBM)
    params = pltpu.CompilerParams(vmem_limit_bytes=60 * 1024 * 1024)

    following = passed_along(charges, "sfc", -1)
    far_pairs = far_pairs.T
    par_pairs = par_pairs.T
    near_pairs = near_pairs.T
    far_c = jnp.transpose(far_coupling, (1, 2, 0))
    parent_of = parent_of.reshape(1, leaves)

    def like(value, memory=pltpu.VMEM):
        return memory(value.shape, value.dtype)

    send = pl.pallas_call(
        pre_kernel,
        out_shape=jax.ShapeDtypeStruct((rows, columns), BF16),
        in_specs=[hbm] * 8,
        out_specs=vmem,
        scratch_shapes=[
            like(charges),
            like(bases),
            like(transfers),
            like(parent_of),
            like(far_pairs),
            like(far_c),
            like(par_pairs),
            like(par_coupling),
            like(par_pairs, pltpu.SMEM),
            pltpu.SemaphoreType.DMA((9,)),
            pltpu.VMEM((leaves * rhs, rank), F32),
            pltpu.VMEM((leaves * rhs, rank), F32),
            pltpu.VMEM((parents * rhs, rank), F32),
            pltpu.VMEM((pairs * rhs, rank), F32),
            pltpu.VMEM((width, slots), F32),
            pltpu.VMEM((width + LANES, slots), BF16),
        ],
        compiler_params=params,
        name="upward",
    )(charges, bases, transfers, parent_of, far_pairs, far_c, par_pairs, par_coupling)
    got = lax.all_to_all(send, "sfc", split_axis=0, concat_axis=0, tiled=True)

    steps = 8
    selves, nears = leaves // steps, near_blocks.shape[0] // steps
    whole = lambda *shape: pl.BlockSpec(shape, lambda i: (0,) * len(shape))
    near_own, near_away = pl.pallas_call(
        near_kernel,
        grid=(steps,),
        out_shape=[
            jax.ShapeDtypeStruct((leaves, rhs, panels), F32),
            jax.ShapeDtypeStruct((leaves, rhs, panels), BF16),
        ],
        in_specs=[
            smem,
            whole(leaves, rhs, panels),
            whole(leaves, rhs, panels),
            pl.BlockSpec((selves, panels, panels), lambda i: (i, 0, 0)),
            pl.BlockSpec((nears, panels, panels), lambda i: (i, 0, 0)),
        ],
        out_specs=[whole(leaves, rhs, panels)] * 2,
        scratch_shapes=[
            pltpu.VMEM((2 * leaves, rhs, panels), BF16),
            pltpu.VMEM((2 * leaves, rhs, panels), F32),
        ],
        compiler_params=params,
        name="near",
    )(near_pairs, charges, following, self_blocks, near_blocks)
    near_back = passed_along(near_away, "sfc", 1)

    return pl.pallas_call(
        post_kernel,
        out_shape=jax.ShapeDtypeStruct((leaves, rhs, panels), F32),
        in_specs=[hbm] * 7 + [vmem] * 3,
        out_specs=vmem,
        scratch_shapes=[
            like(bases),
            like(transfers),
            like(parent_of),
            like(far_pairs),
            like(far_c),
            like(par_pairs),
            like(par_coupling),
            pltpu.SemaphoreType.DMA((7,)),
            pltpu.VMEM((width, slots), F32),
            pltpu.VMEM((width, slots), F32),
            pltpu.VMEM((pairs * rhs, rank), F32),
            pltpu.VMEM((pairs * rhs, rank), F32),
            pltpu.VMEM((leaves * rhs, rank), F32),
            pltpu.VMEM((leaves * rhs, rank), F32),
        ],
        compiler_params=params,
        name="downward",
    )(
        bases,
        transfers,
        parent_of,
        far_pairs,
        far_c,
        par_pairs,
        par_coupling,
        got,
        near_own,
        near_back,
    )


def solution(mesh):
    split = ("grp", "sfc")
    cube, flat = P(split, None, None), P(split, None)
    placed = (cube, cube, cube, flat, cube, cube, P(split), flat, cube, flat, cube)
    return jax.shard_map(
        on_device, mesh=mesh, in_specs=placed, out_specs=cube, check_vma=False
    )
```

```python
import functools

import jax
import jax.numpy as jnp
from jax import lax
from jax.experimental import pallas as pl
from jax.experimental.pallas import tpu as pltpu
from jax.sharding import PartitionSpec as P

F32 = jnp.float32
BF16 = jnp.bfloat16
LANES = 128


def dot_nn(a, b):
    return lax.dot_general(a, b, (((1,), (0,)), ((), ())), preferred_element_type=F32)


def dot_nt(a, b):
    return lax.dot_general(a, b, (((1,), (1,)), ((), ())), preferred_element_type=F32)


def dot_tn(a, b):
    return lax.dot_general(a, b, (((0,), (0,)), ((), ())), preferred_element_type=F32)


def split2(x):
    high = x.astype(BF16)
    return high, (x - high.astype(F32)).astype(BF16)


def iota(shape, axis):
    return lax.broadcasted_iota(jnp.int32, shape, axis)


def one_hot(condition):
    return jnp.where(condition, 1.0, 0.0).astype(BF16)


def rows_to_lanes(ref, count, rhs):
    return jnp.concatenate([ref[pl.ds(r, count, stride=rhs), :] for r in range(rhs)], axis=1)


def lanes_to_rows(ref, value, rhs):
    count, width = value.shape
    rank = width // rhs
    for r in range(rhs):
        ref[pl.ds(r, count, stride=rhs), :] = value[:, r * rank : (r + 1) * rank]


def fetch(pairs, sems):
    copies = [pltpu.make_async_copy(src, dst, sems.at[i]) for i, (src, dst) in enumerate(pairs)]
    for copy in copies:
        copy.start()
    return copies


def pre_kernel(
    charges_h,
    bases_h,
    transfers_h,
    parent_of_h,
    far_pairs_h,
    far_c_h,
    par_pairs_h,
    par_c_h,
    near_pairs_h,
    near_h,
    following_h,
    send,
    back_own,
    back_away,
    charges,
    bases,
    transfers,
    parent_of,
    far_pairs,
    far_c,
    par_pairs,
    par_c,
    par_smem,
    near_smem,
    near_v,
    back,
    sems,
    mo,
    ch,
    pm3,
    pb,
    a_ref,
    ob,
):
    leaves, rhs, _ = charges.shape
    rank = bases.shape[1]
    width = rhs * rank
    slots = far_c.shape[2]
    pairs = par_c.shape[0]
    parents = leaves // 2
    rows = send.shape[0]
    copies = fetch(
        [
            (charges_h, charges),
            (bases_h, bases),
            (transfers_h, transfers),
            (parent_of_h, parent_of),
            (far_pairs_h, far_pairs),
            (par_pairs_h, par_pairs),
            (par_pairs_h, par_smem),
            (far_c_h, far_c),
            (par_c_h, par_c),
            (near_pairs_h, near_smem),
            (near_h, near_v),
        ],
        sems,
    )
    for copy in copies[:3]:
        copy.wait()

    for l in range(leaves):
        m = dot_nt(charges[l], bases[l]).astype(BF16)
        mo[l * rhs : (l + 1) * rhs, :] = m.astype(F32)
        ch[l * rhs : (l + 1) * rhs, :] = dot_nt(m, transfers[l])
    for copy in copies[3:-1]:
        copy.wait()
    m2 = rows_to_lanes(mo, leaves, rhs)
    high, low = split2(rows_to_lanes(ch, leaves, rhs))
    par_hot = one_hot(parent_of[...] % parents == iota((parents, leaves), 0))
    pm = (dot_nn(par_hot, high) + dot_nn(par_hot, low)).astype(BF16).astype(F32)
    lanes_to_rows(pm3, pm, rhs)
    shared = jnp.concatenate([m2[:parents], m2[parents:], pm], axis=1)
    shared = jnp.concatenate([shared, shared], axis=0).astype(BF16)
    at = 2 * width + LANES
    for p in range(rows // (2 * parents)):
        send[p * 2 * parents : (p + 1) * 2 * parents, at : at + 3 * width] = shared

    owner_hot = one_hot(far_pairs[0:1, :] % leaves == iota((leaves, slots), 0))
    a_ref[...] = dot_tn(m2.astype(BF16), owner_hot)
    copies[-1].wait()
    back[...] = jnp.zeros_like(back)
    half = rank // 2
    trips = (slots // LANES) * 2 * (rank // 8)
    nears = near_v.shape[0] // trips
    for sb in range(slots // LANES):
        lanes = slice(sb * LANES, (sb + 1) * LANES)
        for jh in range(2):
            first_pair = (sb * 2 + jh) * (rank // 8) * nears

            def body(k8, acc):
                terms = []
                for i in range(nears):
                    s = first_pair + k8 * nears + i
                    a, b = near_smem[0, s], near_smem[1, s]
                    first = (a // leaves) * leaves
                    terms.append((b - first, dot_nn(charges[a - first], near_v[s])))
                rows_a = [
                    a_ref[pl.ds(pl.multiple_of(r * rank + k8 * 8, 8), 8), lanes]
                    for r in range(rhs)
                ]
                for i in range(8):
                    c = far_c[k8 * 8 + i, jh * half : (jh + 1) * half, lanes].astype(F32)
                    acc = tuple(acc[r] + c * rows_a[r][i : i + 1, :] for r in range(rhs))
                for at, term in terms:
                    back[at] += term
                return acc

            acc = lax.fori_loop(
                0, rank // 8, body, tuple(jnp.zeros((half, LANES), F32) for _ in range(rhs))
            )
            for r in range(rhs):
                first = r * rank + jh * half
                ob[first : first + half, lanes] = acc[r].astype(BF16)
    for s in range(nears * trips, near_v.shape[0]):
        a, b = near_smem[0, s], near_smem[1, s]
        first = (a // leaves) * leaves
        back[b - first] += dot_nn(charges[a - first], near_v[s])
    back_own[...] = back[0:leaves]
    back_away[...] = back[leaves:].astype(BF16)
    partner = far_pairs[1:2, :]
    local = jnp.where(partner >= 0, partner % leaves, -1).astype(F32)
    ob[width : width + LANES, :] = jnp.broadcast_to(local, (LANES, slots)).astype(BF16)
    unit = one_hot(iota((LANES, LANES), 0) == iota((LANES, LANES), 1))
    for sb in range(slots // LANES):
        lanes = slice(sb * LANES, (sb + 1) * LANES)
        send[lanes, 0 : width + LANES] = dot_nt(unit, ob[:, lanes]).astype(BF16)

    for s in range(pairs):
        q = par_smem[0, s] % parents
        x = pm3[pl.ds(pl.multiple_of(q * rhs, rhs), rhs), :].astype(BF16)
        pb[s * rhs : (s + 1) * rhs, :] = dot_nn(x, par_c[s])
    high, low = split2(rows_to_lanes(pb, pairs, rhs))
    hot = one_hot(par_pairs[1:2, :] == iota((rows, pairs), 0))
    at = width + LANES
    send[:, at : at + width] = (dot_nn(hot, high) + dot_nn(hot, low)).astype(BF16)


def near_kernel(pairs, charges, following, self_blocks, near_blocks, own, ext):
    leaves = charges.shape[0]
    step = pl.program_id(0)
    selves, nears = self_blocks.shape[0], near_blocks.shape[0]

    @pl.when(step == 0)
    def _():
        ext[0:leaves] = charges[...]
        ext[leaves:] = following[...]
        own[...] = jnp.zeros_like(own)

    terms = []
    for i in range(selves):
        l = step * selves + i
        terms.append((l, dot_nt(ext[l], self_blocks[i])))
    for i in range(nears):
        a, b = pairs[0, step * nears + i], pairs[1, step * nears + i]
        first = (a // leaves) * leaves
        terms.append((a - first, dot_nt(ext[b - first], near_blocks[i])))
    for at, term in terms:
        own[at] += term


def post_kernel(
    bases_h,
    transfers_h,
    parent_of_h,
    far_pairs_h,
    far_c_h,
    par_pairs_h,
    par_c_h,
    got_h,
    near_own_h,
    back_own_h,
    near_back_h,
    out,
    bases,
    transfers,
    parent_of,
    far_pairs,
    far_c,
    par_pairs,
    par_c,
    got,
    near_own,
    back_own,
    near_back,
    sems,
    b_ref,
    fw,
    g_ref,
    pf,
    lf,
    pg,
):
    leaves, rank, _ = bases.shape
    slots = far_c.shape[2]
    pairs = par_c.shape[0]
    parents = leaves // 2
    rows = got.shape[0]
    rhs = b_ref.shape[0] // rank
    width = rhs * rank
    at_par = width + LANES
    at_mom = at_par + width
    copies = fetch(
        [
            (far_pairs_h, far_pairs),
            (par_pairs_h, par_pairs),
            (got_h, got),
            (parent_of_h, parent_of),
            (par_c_h, par_c),
            (far_c_h, far_c),
            (transfers_h, transfers),
            (bases_h, bases),
            (near_own_h, near_own),
            (back_own_h, back_own),
            (near_back_h, near_back),
        ],
        sems,
    )
    for copy in copies[:6]:
        copy.wait()

    row_id = iota((rows, slots), 0)
    base_leaf = row_id // parents * leaves + row_id % parents
    partner = far_pairs[1:2, :]
    total = None
    for h in range(2):
        hot = one_hot(partner == base_leaf + h * parents)
        part = dot_tn(got[:, at_mom + h * width : at_mom + (h + 1) * width], hot)
        total = part if total is None else total + part
    b_ref[...] = total

    hot = one_hot(par_pairs[1:2, :] == iota((rows, pairs), 0))
    picked = dot_tn(hot, got[:, at_mom + 2 * width : at_mom + 3 * width])
    lanes_to_rows(g_ref, picked, rhs)
    for s in range(pairs):
        x = g_ref[s * rhs : (s + 1) * rhs, :].astype(BF16)
        pf[s * rhs : (s + 1) * rhs, :] = dot_nt(x, par_c[s])
    high, low = split2(rows_to_lanes(pf, pairs, rhs))
    hot = one_hot(par_pairs[0:1, :] % parents == iota((parents, pairs), 0))
    fold = one_hot(iota((parents, rows), 1) % parents == iota((parents, rows), 0))
    locals_p = dot_nn(hot, high) + dot_nn(hot, low) + dot_nn(fold, got[:, at_par : at_par + width])
    hot = one_hot(parent_of[...] % parents == iota((parents, leaves), 0))
    lanes_to_rows(pg, dot_tn(hot, locals_p.astype(BF16)), rhs)

    for sb in range(slots // LANES):
        lanes = slice(sb * LANES, (sb + 1) * LANES)

        def body(k8, carry):
            for r in range(rhs):
                b = b_ref[r * rank : (r + 1) * rank, lanes]
                sums = [
                    jnp.sum(far_c[k8 * 8 + i, :, lanes].astype(F32) * b, axis=0, keepdims=True)
                    for i in range(8)
                ]
                fw[pl.ds(pl.multiple_of(r * rank + k8 * 8, 8), 8), lanes] = jnp.concatenate(
                    sums, axis=0
                )
            return carry

        lax.fori_loop(0, rank // 8, body, 0)

    hot = one_hot(far_pairs[0:1, :] % leaves == iota((leaves, slots), 0))
    high, low = split2(fw[...])
    leaf = dot_nt(hot, high) + dot_nt(hot, low)
    index = got[:, width : width + LANES].astype(F32)[:, :leaves].astype(jnp.int32)
    hot = one_hot(index == iota((rows, leaves), 1))
    leaf = leaf + dot_tn(hot, got[:, 0:width])
    lanes_to_rows(lf, leaf, rhs)

    for copy in copies[6:]:
        copy.wait()
    for l in range(leaves):
        at = slice(l * rhs, (l + 1) * rhs)
        down = dot_nn(pg[at, :].astype(BF16), transfers[l])
        mine = (lf[at, :] + down).astype(BF16)
        near = near_own[l] + back_own[l] + near_back[l].astype(F32)
        out[l] = dot_nn(mine, bases[l]) + near


def passed_along(value, axis, steps):
    count = lax.axis_size(axis)
    leading, last = (max(0, -steps), min(count, count - steps))
    return lax.ppermute(value, axis, [(source, source + steps) for source in range(leading, last)])


def on_device(
    charges,
    self_blocks,
    near_blocks,
    near_pairs,
    bases,
    transfers,
    parent_of,
    far_pairs,
    far_coupling,
    par_pairs,
    par_coupling,
):
    leaves, rhs, panels = charges.shape
    rank = bases.shape[1]
    width = rhs * rank
    slots = far_coupling.shape[0]
    pairs = par_coupling.shape[0]
    parents = leaves // 2
    devices = lax.axis_size("sfc")
    rows = devices * parents
    columns = 5 * width + LANES
    vmem = pl.BlockSpec(memory_space=pltpu.VMEM)
    smem = pl.BlockSpec(memory_space=pltpu.SMEM)
    hbm = pl.BlockSpec(memory_space=pltpu.HBM)
    params = pltpu.CompilerParams(vmem_limit_bytes=60 * 1024 * 1024)

    following = passed_along(charges, "sfc", -1)
    far_pairs = far_pairs.T
    par_pairs = par_pairs.T
    near_pairs = near_pairs.T
    far_c = jnp.transpose(far_coupling, (1, 2, 0))
    parent_of = parent_of.reshape(1, leaves)

    def like(value, memory=pltpu.VMEM):
        return memory(value.shape, value.dtype)

    send, back_own, back_away = pl.pallas_call(
        pre_kernel,
        out_shape=[
            jax.ShapeDtypeStruct((rows, columns), BF16),
            jax.ShapeDtypeStruct((leaves, rhs, panels), F32),
            jax.ShapeDtypeStruct((leaves, rhs, panels), BF16),
        ],
        in_specs=[hbm] * 11,
        out_specs=[vmem] * 3,
        scratch_shapes=[
            like(charges),
            like(bases),
            like(transfers),
            like(parent_of),
            like(far_pairs),
            like(far_c),
            like(par_pairs),
            like(par_coupling),
            like(par_pairs, pltpu.SMEM),
            like(near_pairs, pltpu.SMEM),
            like(near_blocks),
            pltpu.VMEM((2 * leaves, rhs, panels), F32),
            pltpu.SemaphoreType.DMA((11,)),
            pltpu.VMEM((leaves * rhs, rank), F32),
            pltpu.VMEM((leaves * rhs, rank), F32),
            pltpu.VMEM((parents * rhs, rank), F32),
            pltpu.VMEM((pairs * rhs, rank), F32),
            pltpu.VMEM((width, slots), F32),
            pltpu.VMEM((width + LANES, slots), BF16),
        ],
        compiler_params=params,
        name="upward",
    )(
        charges,
        bases,
        transfers,
        parent_of,
        far_pairs,
        far_c,
        par_pairs,
        par_coupling,
        near_pairs,
        near_blocks,
        following,
    )
    near_back = passed_along(back_away, "sfc", 1)
    got = lax.all_to_all(send, "sfc", split_axis=0, concat_axis=0, tiled=True)

    steps = 8
    selves, nears = leaves // steps, near_blocks.shape[0] // steps
    whole = lambda *shape: pl.BlockSpec(shape, lambda i: (0,) * len(shape))
    near_own = pl.pallas_call(
        near_kernel,
        grid=(steps,),
        out_shape=jax.ShapeDtypeStruct((leaves, rhs, panels), F32),
        in_specs=[
            smem,
            whole(leaves, rhs, panels),
            whole(leaves, rhs, panels),
            pl.BlockSpec((selves, panels, panels), lambda i: (i, 0, 0)),
            pl.BlockSpec((nears, panels, panels), lambda i: (i, 0, 0)),
        ],
        out_specs=whole(leaves, rhs, panels),
        scratch_shapes=[pltpu.VMEM((2 * leaves, rhs, panels), BF16)],
        compiler_params=params,
        name="near",
    )(near_pairs, charges, following, self_blocks, near_blocks)

    return pl.pallas_call(
        post_kernel,
        out_shape=jax.ShapeDtypeStruct((leaves, rhs, panels), F32),
        in_specs=[hbm] * 11,
        out_specs=vmem,
        scratch_shapes=[
            like(bases),
            like(transfers),
            like(parent_of),
            like(far_pairs),
            like(far_c),
            like(par_pairs),
            like(par_coupling),
            like(got),
            like(near_own),
            like(back_own),
            like(near_back),
            pltpu.SemaphoreType.DMA((11,)),
            pltpu.VMEM((width, slots), F32),
            pltpu.VMEM((width, slots), F32),
            pltpu.VMEM((pairs * rhs, rank), F32),
            pltpu.VMEM((pairs * rhs, rank), F32),
            pltpu.VMEM((leaves * rhs, rank), F32),
            pltpu.VMEM((leaves * rhs, rank), F32),
        ],
        compiler_params=params,
        name="downward",
    )(
        bases,
        transfers,
        parent_of,
        far_pairs,
        far_c,
        par_pairs,
        par_coupling,
        got,
        near_own,
        back_own,
        near_back,
    )


def solution(mesh):
    split = ("grp", "sfc")
    cube, flat = P(split, None, None), P(split, None)
    placed = (cube, cube, cube, flat, cube, cube, P(split), flat, cube, flat, cube)
    return jax.shard_map(
        on_device, mesh=mesh, in_specs=placed, out_specs=cube, check_vma=False
    )
```

```python
import functools

import jax
import jax.numpy as jnp
from jax import lax
from jax.experimental import pallas as pl
from jax.experimental.pallas import tpu as pltpu
from jax.sharding import PartitionSpec as P

F32 = jnp.float32
BF16 = jnp.bfloat16
LANES = 128


def dot_nn(a, b):
    return lax.dot_general(a, b, (((1,), (0,)), ((), ())), preferred_element_type=F32)


def dot_nt(a, b):
    return lax.dot_general(a, b, (((1,), (1,)), ((), ())), preferred_element_type=F32)


def dot_tn(a, b):
    return lax.dot_general(a, b, (((0,), (0,)), ((), ())), preferred_element_type=F32)


def split2(x):
    high = x.astype(BF16)
    return high, (x - high.astype(F32)).astype(BF16)


def iota(shape, axis):
    return lax.broadcasted_iota(jnp.int32, shape, axis)


def one_hot(condition):
    return jnp.where(condition, 1.0, 0.0).astype(BF16)


def rows_to_lanes(ref, count, rhs):
    return jnp.concatenate([ref[pl.ds(r, count, stride=rhs), :] for r in range(rhs)], axis=1)


def lanes_to_rows(ref, value, rhs):
    count, width = value.shape
    rank = width // rhs
    for r in range(rhs):
        ref[pl.ds(r, count, stride=rhs), :] = value[:, r * rank : (r + 1) * rank]


def fetch(pairs, sems):
    copies = [pltpu.make_async_copy(src, dst, sems.at[i]) for i, (src, dst) in enumerate(pairs)]
    for copy in copies:
        copy.start()
    return copies


def moment_kernel(
    charges_h,
    bases_h,
    transfers_h,
    parent_of_h,
    shared,
    charges,
    bases,
    transfers,
    parent_of,
    sems,
    mo,
    ch,
):
    leaves, rhs, _ = charges.shape
    parents = leaves // 2
    copies = fetch(
        [
            (charges_h, charges),
            (bases_h, bases),
            (transfers_h, transfers),
            (parent_of_h, parent_of),
        ],
        sems,
    )
    for copy in copies:
        copy.wait()
    for l in range(leaves):
        m = dot_nt(charges[l], bases[l]).astype(BF16)
        mo[l * rhs : (l + 1) * rhs, :] = m.astype(F32)
        ch[l * rhs : (l + 1) * rhs, :] = dot_nt(m, transfers[l])
    m2 = rows_to_lanes(mo, leaves, rhs)
    high, low = split2(rows_to_lanes(ch, leaves, rhs))
    par_hot = one_hot(parent_of[...] % parents == iota((parents, leaves), 0))
    pm = dot_nn(par_hot, high) + dot_nn(par_hot, low)
    block = jnp.concatenate([m2[:parents], m2[parents:], pm], axis=1)
    block = jnp.concatenate([block, block], axis=0).astype(BF16)
    for p in range(shared.shape[0] // (2 * parents)):
        shared[p * 2 * parents : (p + 1) * 2 * parents, :] = block


def back_kernel(
    charges_h,
    shared_h,
    far_pairs_h,
    far_c_h,
    par_pairs_h,
    par_c_h,
    near_pairs_h,
    near_h,
    following_h,
    send,
    back_own,
    back_away,
    charges,
    mine,
    far_pairs,
    far_c,
    par_pairs,
    par_c,
    par_smem,
    near_smem,
    near_v,
    back,
    sems,
    pm3,
    pb,
    a_ref,
    ob,
):
    leaves, rhs, _ = charges.shape
    rank = far_c.shape[0]
    width = rhs * rank
    slots = far_c.shape[2]
    pairs = par_c.shape[0]
    parents = leaves // 2
    rows = send.shape[0]
    copies = fetch(
        [
            (shared_h.at[0 : 2 * parents], mine),
            (far_pairs_h, far_pairs),
            (par_pairs_h, par_pairs),
            (par_pairs_h, par_smem),
            (near_pairs_h, near_smem),
            (charges_h, charges),
            (far_c_h, far_c),
            (par_c_h, par_c),
            (near_h, near_v),
        ],
        sems,
    )
    for copy in copies[:-1]:
        copy.wait()
    m2 = jnp.concatenate([mine[:parents, 0:width], mine[:parents, width : 2 * width]], axis=0)
    lanes_to_rows(pm3, mine[:parents, 2 * width :].astype(F32), rhs)

    owner_hot = one_hot(far_pairs[0:1, :] % leaves == iota((leaves, slots), 0))
    a_ref[...] = dot_tn(m2, owner_hot)
    for s in range(pairs):
        q = par_smem[0, s] % parents
        x = pm3[pl.ds(pl.multiple_of(q * rhs, rhs), rhs), :].astype(BF16)
        pb[s * rhs : (s + 1) * rhs, :] = dot_nn(x, par_c[s])
    high, low = split2(rows_to_lanes(pb, pairs, rhs))
    hot = one_hot(par_pairs[1:2, :] == iota((rows, pairs), 0))
    at = width + LANES
    send[:, at : at + width] = (dot_nn(hot, high) + dot_nn(hot, low)).astype(BF16)

    copies[-1].wait()
    back[...] = jnp.zeros_like(back)
    half = rank // 2
    trips = (slots // LANES) * 2 * (rank // 8)
    nears = near_v.shape[0] // trips
    for sb in range(slots // LANES):
        lanes = slice(sb * LANES, (sb + 1) * LANES)
        for jh in range(2):
            first_pair = (sb * 2 + jh) * (rank // 8) * nears

            def body(k8, acc):
                terms = []
                for i in range(nears):
                    s = first_pair + k8 * nears + i
                    a, b = near_smem[0, s], near_smem[1, s]
                    first = (a // leaves) * leaves
                    terms.append((b - first, dot_nn(charges[a - first], near_v[s])))
                rows_a = [
                    a_ref[pl.ds(pl.multiple_of(r * rank + k8 * 8, 8), 8), lanes]
                    for r in range(rhs)
                ]
                for i in range(8):
                    c = far_c[k8 * 8 + i, jh * half : (jh + 1) * half, lanes].astype(F32)
                    acc = tuple(acc[r] + c * rows_a[r][i : i + 1, :] for r in range(rhs))
                for at, term in terms:
                    back[at] += term
                return acc

            acc = lax.fori_loop(
                0, rank // 8, body, tuple(jnp.zeros((half, LANES), F32) for _ in range(rhs))
            )
            for r in range(rhs):
                first = r * rank + jh * half
                ob[first : first + half, lanes] = acc[r].astype(BF16)
    for s in range(nears * trips, near_v.shape[0]):
        a, b = near_smem[0, s], near_smem[1, s]
        first = (a // leaves) * leaves
        back[b - first] += dot_nn(charges[a - first], near_v[s])
    back_own[...] = back[0:leaves]
    back_away[...] = back[leaves:].astype(BF16)
    partner = far_pairs[1:2, :]
    local = jnp.where(partner >= 0, partner % leaves, -1).astype(F32)
    ob[width : width + LANES, :] = jnp.broadcast_to(local, (LANES, slots)).astype(BF16)
    unit = one_hot(iota((LANES, LANES), 0) == iota((LANES, LANES), 1))
    for sb in range(slots // LANES):
        lanes = slice(sb * LANES, (sb + 1) * LANES)
        send[lanes, 0 : width + LANES] = dot_nt(unit, ob[:, lanes]).astype(BF16)


def near_kernel(pairs, charges, following, self_blocks, near_blocks, own, ext):
    leaves = charges.shape[0]
    step = pl.program_id(0)
    selves, nears = self_blocks.shape[0], near_blocks.shape[0]

    @pl.when(step == 0)
    def _():
        ext[0:leaves] = charges[...]
        ext[leaves:] = following[...]
        own[...] = jnp.zeros_like(own)

    terms = []
    for i in range(selves):
        l = step * selves + i
        terms.append((l, dot_nt(ext[l], self_blocks[i])))
    for i in range(nears):
        a, b = pairs[0, step * nears + i], pairs[1, step * nears + i]
        first = (a // leaves) * leaves
        terms.append((a - first, dot_nt(ext[b - first], near_blocks[i])))
    for at, term in terms:
        own[at] += term


def post_kernel(
    bases_h,
    transfers_h,
    parent_of_h,
    far_pairs_h,
    far_c_h,
    par_pairs_h,
    par_c_h,
    mom_h,
    mom2_h,
    got_h,
    near_own_h,
    back_own_h,
    near_back_h,
    out,
    bases,
    transfers,
    parent_of,
    far_pairs,
    far_c,
    par_pairs,
    par_c,
    mom,
    got,
    near_own,
    back_own,
    near_back,
    sems,
    b_ref,
    fw,
    g_ref,
    pf,
    lf,
    pg,
):
    leaves, rank, _ = bases.shape
    slots = far_c.shape[2]
    pairs = par_c.shape[0]
    parents = leaves // 2
    rows = got.shape[0]
    rhs = b_ref.shape[0] // rank
    width = rhs * rank
    at_par = width + LANES
    copies = fetch(
        [
            (far_pairs_h, far_pairs),
            (par_pairs_h, par_pairs),
            (mom_h, mom.at[0 : rows // 2]),
            (mom2_h, mom.at[rows // 2 :]),
            (got_h, got),
            (parent_of_h, parent_of),
            (par_c_h, par_c),
            (far_c_h, far_c),
            (transfers_h, transfers),
            (bases_h, bases),
            (near_own_h, near_own),
            (back_own_h, back_own),
            (near_back_h, near_back),
        ],
        sems,
    )
    for copy in copies[:8]:
        copy.wait()

    parity = far_pairs[0:1, 0:1] // leaves % 2

    def source(row):
        chip = row // parents
        own = chip < rows // parents // 2
        return jnp.where(own, 2 * chip + parity, 2 * chip - rows // parents + 1 - parity)

    row_id = iota((rows, slots), 0)
    base_leaf = source(row_id) * leaves + row_id % parents
    partner = far_pairs[1:2, :]
    total = None
    for h in range(2):
        hot = one_hot(partner == base_leaf + h * parents)
        part = dot_tn(mom[:, h * width : (h + 1) * width], hot)
        total = part if total is None else total + part
    b_ref[...] = total

    row_id = iota((rows, pairs), 0)
    hot = one_hot(par_pairs[1:2, :] == source(row_id) * parents + row_id % parents)
    picked = dot_tn(hot, mom[:, 2 * width :])
    lanes_to_rows(g_ref, picked, rhs)
    for s in range(pairs):
        x = g_ref[s * rhs : (s + 1) * rhs, :].astype(BF16)
        pf[s * rhs : (s + 1) * rhs, :] = dot_nt(x, par_c[s])
    high, low = split2(rows_to_lanes(pf, pairs, rhs))
    hot = one_hot(par_pairs[0:1, :] % parents == iota((parents, pairs), 0))
    fold = one_hot(iota((parents, rows), 1) % parents == iota((parents, rows), 0))
    locals_p = dot_nn(hot, high) + dot_nn(hot, low) + dot_nn(fold, got[:, at_par : at_par + width])
    hot = one_hot(parent_of[...] % parents == iota((parents, leaves), 0))
    lanes_to_rows(pg, dot_tn(hot, locals_p.astype(BF16)), rhs)

    for sb in range(slots // LANES):
        lanes = slice(sb * LANES, (sb + 1) * LANES)

        def body(k8, carry):
            for r in range(rhs):
                b = b_ref[r * rank : (r + 1) * rank, lanes]
                sums = [
                    jnp.sum(far_c[k8 * 8 + i, :, lanes].astype(F32) * b, axis=0, keepdims=True)
                    for i in range(8)
                ]
                fw[pl.ds(pl.multiple_of(r * rank + k8 * 8, 8), 8), lanes] = jnp.concatenate(
                    sums, axis=0
                )
            return carry

        lax.fori_loop(0, rank // 8, body, 0)

    hot = one_hot(far_pairs[0:1, :] % leaves == iota((leaves, slots), 0))
    high, low = split2(fw[...])
    leaf = dot_nt(hot, high) + dot_nt(hot, low)
    index = got[:, width : width + LANES].astype(F32)[:, :leaves].astype(jnp.int32)
    hot = one_hot(index == iota((rows, leaves), 1))
    leaf = leaf + dot_tn(hot, got[:, 0:width])
    lanes_to_rows(lf, leaf, rhs)

    for copy in copies[8:]:
        copy.wait()
    for l in range(leaves):
        at = slice(l * rhs, (l + 1) * rhs)
        down = dot_nn(pg[at, :].astype(BF16), transfers[l])
        mine = (lf[at, :] + down).astype(BF16)
        near = near_own[l] + back_own[l] + near_back[l].astype(F32)
        out[l] = dot_nn(mine, bases[l]) + near


def passed_along(value, axis, steps):
    count = lax.axis_size(axis)
    leading, last = (max(0, -steps), min(count, count - steps))
    return lax.ppermute(value, axis, [(source, source + steps) for source in range(leading, last)])


def on_device(
    charges,
    self_blocks,
    near_blocks,
    near_pairs,
    bases,
    transfers,
    parent_of,
    far_pairs,
    far_coupling,
    par_pairs,
    par_coupling,
):
    leaves, rhs, panels = charges.shape
    rank = bases.shape[1]
    width = rhs * rank
    slots = far_coupling.shape[0]
    pairs = par_coupling.shape[0]
    parents = leaves // 2
    devices = lax.axis_size("sfc")
    rows = devices * parents
    columns = 2 * width + LANES
    vmem = pl.BlockSpec(memory_space=pltpu.VMEM)
    smem = pl.BlockSpec(memory_space=pltpu.SMEM)
    hbm = pl.BlockSpec(memory_space=pltpu.HBM)
    params = pltpu.CompilerParams(vmem_limit_bytes=60 * 1024 * 1024)

    def cost(moved):
        return pl.CostEstimate(flops=4 * moved, bytes_accessed=moved, transcendentals=0)

    following = passed_along(charges, "sfc", -1)
    far_pairs = far_pairs.T
    par_pairs = par_pairs.T
    near_pairs = near_pairs.T
    far_c = jnp.transpose(far_coupling, (1, 2, 0))
    parent_of = parent_of.reshape(1, leaves)

    def like(value, memory=pltpu.VMEM):
        return memory(value.shape, value.dtype)

    shared = pl.pallas_call(
        moment_kernel,
        out_shape=jax.ShapeDtypeStruct((rows // 2, 3 * width), BF16),
        in_specs=[hbm] * 4,
        out_specs=vmem,
        scratch_shapes=[
            like(charges),
            like(bases),
            like(transfers),
            like(parent_of),
            pltpu.SemaphoreType.DMA((4,)),
            pltpu.VMEM((leaves * rhs, rank), F32),
            pltpu.VMEM((leaves * rhs, rank), F32),
        ],
        compiler_params=params,
        cost_estimate=cost(4_000_000),
        name="moments",
    )(charges, bases, transfers, parent_of)
    same_core = [list(range(core, devices, 2)) for core in range(2)]
    mom = lax.all_to_all(
        shared, "sfc", split_axis=0, concat_axis=0, tiled=True, axis_index_groups=same_core
    )
    mom2 = lax.ppermute(mom, "sfc", [(i, i ^ 1) for i in range(devices)])

    send, back_own, back_away = pl.pallas_call(
        back_kernel,
        out_shape=[
            jax.ShapeDtypeStruct((rows, columns), BF16),
            jax.ShapeDtypeStruct((leaves, rhs, panels), F32),
            jax.ShapeDtypeStruct((leaves, rhs, panels), BF16),
        ],
        in_specs=[hbm] * 9,
        out_specs=[vmem] * 3,
        scratch_shapes=[
            like(charges),
            pltpu.VMEM((2 * parents, 3 * width), BF16),
            like(far_pairs),
            like(far_c),
            like(par_pairs),
            like(par_coupling),
            like(par_pairs, pltpu.SMEM),
            like(near_pairs, pltpu.SMEM),
            like(near_blocks),
            pltpu.VMEM((2 * leaves, rhs, panels), F32),
            pltpu.SemaphoreType.DMA((9,)),
            pltpu.VMEM((parents * rhs, rank), F32),
            pltpu.VMEM((pairs * rhs, rank), F32),
            pltpu.VMEM((width, slots), F32),
            pltpu.VMEM((width + LANES, slots), BF16),
        ],
        compiler_params=params,
        cost_estimate=cost(12_000_000),
        name="transposed",
    )(
        charges,
        shared,
        far_pairs,
        far_c,
        par_pairs,
        par_coupling,
        near_pairs,
        near_blocks,
        following,
    )
    near_back = passed_along(back_away, "sfc", 1)
    got = lax.all_to_all(send, "sfc", split_axis=0, concat_axis=0, tiled=True)

    steps = 8
    selves, nears = leaves // steps, near_blocks.shape[0] // steps
    whole = lambda *shape: pl.BlockSpec(shape, lambda i: (0,) * len(shape))
    near_own = pl.pallas_call(
        near_kernel,
        grid=(steps,),
        out_shape=jax.ShapeDtypeStruct((leaves, rhs, panels), F32),
        in_specs=[
            smem,
            whole(leaves, rhs, panels),
            whole(leaves, rhs, panels),
            pl.BlockSpec((selves, panels, panels), lambda i: (i, 0, 0)),
            pl.BlockSpec((nears, panels, panels), lambda i: (i, 0, 0)),
        ],
        out_specs=whole(leaves, rhs, panels),
        scratch_shapes=[pltpu.VMEM((2 * leaves, rhs, panels), BF16)],
        compiler_params=params,
        cost_estimate=cost(20_000_000),
        name="near",
    )(near_pairs, charges, following, self_blocks, near_blocks)

    return pl.pallas_call(
        post_kernel,
        out_shape=jax.ShapeDtypeStruct((leaves, rhs, panels), F32),
        in_specs=[hbm] * 13,
        out_specs=vmem,
        scratch_shapes=[
            like(bases),
            like(transfers),
            like(parent_of),
            like(far_pairs),
            like(far_c),
            like(par_pairs),
            like(par_coupling),
            pltpu.VMEM((rows, 3 * width), BF16),
            like(got),
            like(near_own),
            like(back_own),
            like(near_back),
            pltpu.SemaphoreType.DMA((13,)),
            pltpu.VMEM((width, slots), F32),
            pltpu.VMEM((width, slots), F32),
            pltpu.VMEM((pairs * rhs, rank), F32),
            pltpu.VMEM((pairs * rhs, rank), F32),
            pltpu.VMEM((leaves * rhs, rank), F32),
            pltpu.VMEM((leaves * rhs, rank), F32),
        ],
        compiler_params=params,
        name="downward",
    )(
        bases,
        transfers,
        parent_of,
        far_pairs,
        far_c,
        par_pairs,
        par_coupling,
        mom,
        mom2,
        got,
        near_own,
        back_own,
        near_back,
    )


def solution(mesh):
    split = ("grp", "sfc")
    cube, flat = P(split, None, None), P(split, None)
    placed = (cube, cube, cube, flat, cube, cube, P(split), flat, cube, flat, cube)
    return jax.shard_map(
        on_device, mesh=mesh, in_specs=placed, out_specs=cube, check_vma=False
    )
```

```python
import functools

import jax
import jax.numpy as jnp
from jax import lax
from jax.experimental import pallas as pl
from jax.experimental.pallas import tpu as pltpu
from jax.sharding import PartitionSpec as P

F32 = jnp.float32
BF16 = jnp.bfloat16
LANES = 128


def dot_nn(a, b):
    return lax.dot_general(a, b, (((1,), (0,)), ((), ())), preferred_element_type=F32)


def dot_nt(a, b):
    return lax.dot_general(a, b, (((1,), (1,)), ((), ())), preferred_element_type=F32)


def dot_tn(a, b):
    return lax.dot_general(a, b, (((0,), (0,)), ((), ())), preferred_element_type=F32)


def split2(x):
    high = x.astype(BF16)
    return high, (x - high.astype(F32)).astype(BF16)


def iota(shape, axis):
    return lax.broadcasted_iota(jnp.int32, shape, axis)


def one_hot(condition):
    return jnp.where(condition, 1.0, 0.0).astype(BF16)


def rows_to_lanes(ref, count, rhs):
    return jnp.concatenate([ref[pl.ds(r, count, stride=rhs), :] for r in range(rhs)], axis=1)


def lanes_to_rows(ref, value, rhs):
    count, width = value.shape
    rank = width // rhs
    for r in range(rhs):
        ref[pl.ds(r, count, stride=rhs), :] = value[:, r * rank : (r + 1) * rank]


def fetch(pairs, sems):
    copies = [pltpu.make_async_copy(src, dst, sems.at[i]) for i, (src, dst) in enumerate(pairs)]
    for copy in copies:
        copy.start()
    return copies


def pre_kernel(
    charges_h,
    bases_h,
    transfers_h,
    parent_of_h,
    far_pairs_h,
    far_c_h,
    par_pairs_h,
    par_c_h,
    send,
    charges,
    bases,
    transfers,
    parent_of,
    far_pairs,
    far_c,
    par_pairs,
    par_c,
    par_smem,
    sems,
    mo,
    ch,
    pm3,
    pb,
    a_ref,
    ob,
):
    leaves, rhs, _ = charges.shape
    rank = bases.shape[1]
    width = rhs * rank
    slots = far_c.shape[2]
    pairs = par_c.shape[0]
    parents = leaves // 2
    rows = send.shape[0]
    copies = fetch(
        [
            (charges_h, charges),
            (bases_h, bases),
            (transfers_h, transfers),
            (parent_of_h, parent_of),
            (far_pairs_h, far_pairs),
            (par_pairs_h, par_pairs),
            (par_pairs_h, par_smem),
            (far_c_h, far_c),
            (par_c_h, par_c),
        ],
        sems,
    )
    for copy in copies[:3]:
        copy.wait()

    for l in range(leaves):
        m = dot_nt(charges[l], bases[l]).astype(BF16)
        mo[l * rhs : (l + 1) * rhs, :] = m.astype(F32)
        ch[l * rhs : (l + 1) * rhs, :] = dot_nt(m, transfers[l])
    for copy in copies[3:]:
        copy.wait()
    m2 = rows_to_lanes(mo, leaves, rhs)
    high, low = split2(rows_to_lanes(ch, leaves, rhs))
    par_hot = one_hot(parent_of[...] % parents == iota((parents, leaves), 0))
    pm = (dot_nn(par_hot, high) + dot_nn(par_hot, low)).astype(BF16).astype(F32)
    lanes_to_rows(pm3, pm, rhs)
    shared = jnp.concatenate([m2[:parents], m2[parents:], pm], axis=1)
    half = 3 * width // 2
    shared = jnp.concatenate([shared[:, :half], shared[:, half:]], axis=0).astype(BF16)
    at = 2 * width + LANES
    for p in range(rows // (2 * parents)):
        send[p * 2 * parents : (p + 1) * 2 * parents, at : at + half] = shared

    owner_hot = one_hot(far_pairs[0:1, :] % leaves == iota((leaves, slots), 0))
    a_ref[...] = dot_tn(m2.astype(BF16), owner_hot)
    half = rank // 2
    for sb in range(slots // LANES):
        lanes = slice(sb * LANES, (sb + 1) * LANES)
        for jh in range(2):

            def body(k8, acc):
                rows_a = [
                    a_ref[pl.ds(pl.multiple_of(r * rank + k8 * 8, 8), 8), lanes]
                    for r in range(rhs)
                ]
                for i in range(8):
                    c = far_c[k8 * 8 + i, jh * half : (jh + 1) * half, lanes].astype(F32)
                    acc = tuple(acc[r] + c * rows_a[r][i : i + 1, :] for r in range(rhs))
                return acc

            acc = lax.fori_loop(
                0, rank // 8, body, tuple(jnp.zeros((half, LANES), F32) for _ in range(rhs))
            )
            for r in range(rhs):
                first = r * rank + jh * half
                ob[first : first + half, lanes] = acc[r].astype(BF16)
    partner = far_pairs[1:2, :]
    local = jnp.where(partner >= 0, partner % leaves, -1).astype(F32)
    ob[width : width + LANES, :] = jnp.broadcast_to(local, (LANES, slots)).astype(BF16)
    unit = one_hot(iota((LANES, LANES), 0) == iota((LANES, LANES), 1))
    for sb in range(slots // LANES):
        lanes = slice(sb * LANES, (sb + 1) * LANES)
        send[lanes, 0 : width + LANES] = dot_nt(unit, ob[:, lanes]).astype(BF16)

    for s in range(pairs):
        q = par_smem[0, s] % parents
        x = pm3[pl.ds(pl.multiple_of(q * rhs, rhs), rhs), :].astype(BF16)
        pb[s * rhs : (s + 1) * rhs, :] = dot_nn(x, par_c[s])
    high, low = split2(rows_to_lanes(pb, pairs, rhs))
    hot = one_hot(par_pairs[1:2, :] == iota((rows, pairs), 0))
    at = width + LANES
    send[:, at : at + width] = (dot_nn(hot, high) + dot_nn(hot, low)).astype(BF16)


def near_kernel(pairs, charges, following, self_blocks, near_blocks, own, away, ext, out):
    leaves = charges.shape[0]
    step = pl.program_id(0)
    selves, nears = self_blocks.shape[0], near_blocks.shape[0]

    @pl.when(step == 0)
    def _():
        ext[0:leaves] = charges[...]
        ext[leaves:] = following[...]
        out[...] = jnp.zeros_like(out)

    terms = [(step * selves + i, dot_nt(ext[step * selves + i], self_blocks[i])) for i in range(selves)]
    for i in range(nears):
        a, b = pairs[0, step * nears + i], pairs[1, step * nears + i]
        first = (a // leaves) * leaves
        a, b = a - first, b - first
        terms.append((a, dot_nt(ext[b], near_blocks[i])))
        terms.append((b, dot_nn(ext[a], near_blocks[i])))
    for at, term in terms:
        out[at] += term

    @pl.when(step == pl.num_programs(0) - 1)
    def _():
        own[...] = out[0:leaves]
        away[...] = out[leaves:].astype(BF16)


def post_kernel(
    core_smem,
    mom2,
    got,
    bases,
    transfers,
    parent_of,
    far_pairs,
    far_c,
    par_pairs,
    par_c,
    near_own,
    near_back,
    out,
    b_ref,
    fw,
    g_ref,
    pf,
    lf,
    pg,
):
    leaves, rank, _ = bases.shape
    slots = far_c.shape[2]
    pairs = par_c.shape[0]
    parents = leaves // 2
    rows = got.shape[0]
    rhs = b_ref.shape[0] // rank
    width = rhs * rank
    at_par = width + LANES
    at_mom = at_par + width
    core = core_smem[0, 0] // leaves % 2
    mom = got[:, at_mom:]
    shared = jnp.concatenate(
        [jnp.where(core == 0, mom, mom2[...]), jnp.where(core == 0, mom2[...], mom)], axis=1
    )
    row_id = iota((rows, slots), 0)
    base_leaf = row_id // parents * leaves + row_id % parents
    partner = far_pairs[1:2, :]
    total = None
    for h in range(2):
        hot = one_hot(partner == base_leaf + h * parents)
        part = dot_tn(shared[:, h * width : (h + 1) * width], hot)
        total = part if total is None else total + part
    b_ref[...] = total

    hot = one_hot(par_pairs[1:2, :] == iota((rows, pairs), 0))
    picked = dot_tn(hot, shared[:, 2 * width :])
    lanes_to_rows(g_ref, picked, rhs)
    for s in range(pairs):
        x = g_ref[s * rhs : (s + 1) * rhs, :].astype(BF16)
        pf[s * rhs : (s + 1) * rhs, :] = dot_nt(x, par_c[s])
    high, low = split2(rows_to_lanes(pf, pairs, rhs))
    hot = one_hot(par_pairs[0:1, :] % parents == iota((parents, pairs), 0))
    fold = one_hot(iota((parents, rows), 1) % parents == iota((parents, rows), 0))
    locals_p = dot_nn(hot, high) + dot_nn(hot, low) + dot_nn(fold, got[:, at_par : at_par + width])
    hot = one_hot(parent_of[...] % parents == iota((parents, leaves), 0))
    lanes_to_rows(pg, dot_tn(hot, locals_p.astype(BF16)), rhs)

    for sb in range(slots // LANES):
        lanes = slice(sb * LANES, (sb + 1) * LANES)

        def body(k8, carry):
            for r in range(rhs):
                b = b_ref[r * rank : (r + 1) * rank, lanes]
                sums = [
                    jnp.sum(far_c[k8 * 8 + i, :, lanes].astype(F32) * b, axis=0, keepdims=True)
                    for i in range(8)
                ]
                fw[pl.ds(pl.multiple_of(r * rank + k8 * 8, 8), 8), lanes] = jnp.concatenate(
                    sums, axis=0
                )
            return carry

        lax.fori_loop(0, rank // 8, body, 0)

    hot = one_hot(far_pairs[0:1, :] % leaves == iota((leaves, slots), 0))
    high, low = split2(fw[...])
    leaf = dot_nt(hot, high) + dot_nt(hot, low)
    index = got[:, width : width + LANES].astype(F32)[:, :leaves].astype(jnp.int32)
    hot = one_hot(index == iota((rows, leaves), 1))
    leaf = leaf + dot_tn(hot, got[:, 0:width])
    lanes_to_rows(lf, leaf, rhs)

    for l in range(leaves):
        at = slice(l * rhs, (l + 1) * rhs)
        down = dot_nn(pg[at, :].astype(BF16), transfers[l])
        mine = (lf[at, :] + down).astype(BF16)
        near = near_own[l] + near_back[l].astype(F32)
        out[l] = dot_nn(mine, bases[l]) + near


def after(value, earlier):
    anywhere = pl.BlockSpec(memory_space=pl.ANY)
    return pl.pallas_call(
        lambda value, earlier, same: None,
        out_shape=jax.ShapeDtypeStruct(value.shape, value.dtype),
        in_specs=[anywhere] * 2,
        out_specs=anywhere,
        input_output_aliases={0: 0},
        name="after",
    )(value, earlier)


def passed_along(value, axis, steps):
    count = lax.axis_size(axis)
    leading, last = (max(0, -steps), min(count, count - steps))
    return lax.ppermute(value, axis, [(source, source + steps) for source in range(leading, last)])


def on_device(
    charges,
    self_blocks,
    near_blocks,
    near_pairs,
    bases,
    transfers,
    parent_of,
    far_pairs,
    far_coupling,
    par_pairs,
    par_coupling,
):
    leaves, rhs, panels = charges.shape
    rank = bases.shape[1]
    width = rhs * rank
    slots = far_coupling.shape[0]
    pairs = par_coupling.shape[0]
    parents = leaves // 2
    devices = lax.axis_size("sfc")
    rows = devices * parents
    columns = 2 * width + LANES + 3 * width // 2
    vmem = pl.BlockSpec(memory_space=pltpu.VMEM)
    smem = pl.BlockSpec(memory_space=pltpu.SMEM)
    hbm = pl.BlockSpec(memory_space=pltpu.HBM)
    params = pltpu.CompilerParams(vmem_limit_bytes=60 * 1024 * 1024)
    late = pltpu.CompilerParams(vmem_limit_bytes=48 * 1024 * 1024)

    def cost(moved):
        return pl.CostEstimate(flops=4 * moved, bytes_accessed=moved, transcendentals=0)

    following = passed_along(charges, "sfc", -1)
    far_pairs = far_pairs.T
    par_pairs = par_pairs.T
    near_pairs = near_pairs.T
    far_c = jnp.transpose(far_coupling, (1, 2, 0))
    parent_of = parent_of.reshape(1, leaves)

    def like(value, memory=pltpu.VMEM):
        return memory(value.shape, value.dtype)

    send = pl.pallas_call(
        pre_kernel,
        out_shape=jax.ShapeDtypeStruct((rows, columns), BF16),
        in_specs=[hbm] * 8,
        out_specs=vmem,
        scratch_shapes=[
            like(charges),
            like(bases),
            like(transfers),
            like(parent_of),
            like(far_pairs),
            like(far_c),
            like(par_pairs),
            like(par_coupling),
            like(par_pairs, pltpu.SMEM),
            pltpu.SemaphoreType.DMA((9,)),
            pltpu.VMEM((leaves * rhs, rank), F32),
            pltpu.VMEM((leaves * rhs, rank), F32),
            pltpu.VMEM((parents * rhs, rank), F32),
            pltpu.VMEM((pairs * rhs, rank), F32),
            pltpu.VMEM((width, slots), F32),
            pltpu.VMEM((width + LANES, slots), BF16),
        ],
        compiler_params=params,
        cost_estimate=cost(10_000_000),
        name="upward",
    )(charges, bases, transfers, parent_of, far_pairs, far_c, par_pairs, par_coupling)
    send = after(send, following)
    got = lax.all_to_all(send, "sfc", split_axis=0, concat_axis=0, tiled=True)
    steps = 8
    selves, nears = leaves // steps, near_blocks.shape[0] // steps
    whole = lambda *shape: pl.BlockSpec(shape, lambda i: (0,) * len(shape))
    near_own, near_away = pl.pallas_call(
        near_kernel,
        grid=(steps,),
        out_shape=[
            jax.ShapeDtypeStruct((leaves, rhs, panels), F32),
            jax.ShapeDtypeStruct((leaves, rhs, panels), BF16),
        ],
        in_specs=[
            smem,
            whole(leaves, rhs, panels),
            whole(leaves, rhs, panels),
            pl.BlockSpec((selves, panels, panels), lambda i: (i, 0, 0)),
            pl.BlockSpec((nears, panels, panels), lambda i: (i, 0, 0)),
        ],
        out_specs=[whole(leaves, rhs, panels)] * 2,
        scratch_shapes=[
            pltpu.VMEM((2 * leaves, rhs, panels), BF16),
            pltpu.VMEM((2 * leaves, rhs, panels), F32),
        ],
        compiler_params=late,
        cost_estimate=cost(20_000_000),
        name="near",
    )(near_pairs, charges, following, self_blocks, near_blocks)
    near_back = passed_along(near_away, "sfc", 1)

    got = after(got, near_back)
    mom2 = lax.ppermute(
        got[:, 2 * width + LANES :], "sfc", [(i, i ^ 1) for i in range(devices)]
    )

    return pl.pallas_call(
        post_kernel,
        out_shape=jax.ShapeDtypeStruct((leaves, rhs, panels), F32),
        in_specs=[smem] + [vmem] * 11,
        out_specs=vmem,
        scratch_shapes=[
            pltpu.VMEM((width, slots), F32),
            pltpu.VMEM((width, slots), F32),
            pltpu.VMEM((pairs * rhs, rank), F32),
            pltpu.VMEM((pairs * rhs, rank), F32),
            pltpu.VMEM((leaves * rhs, rank), F32),
            pltpu.VMEM((leaves * rhs, rank), F32),
        ],
        compiler_params=late,
        name="downward",
    )(
        far_pairs,
        mom2,
        got,
        bases,
        transfers,
        parent_of,
        far_pairs,
        far_c,
        par_pairs,
        par_coupling,
        near_own,
        near_back,
    )


def solution(mesh):
    split = ("grp", "sfc")
    cube, flat = P(split, None, None), P(split, None)
    placed = (cube, cube, cube, flat, cube, cube, P(split), flat, cube, flat, cube)
    return jax.shard_map(
        on_device, mesh=mesh, in_specs=placed, out_specs=cube, check_vma=False
    )
```

```python
import functools

import jax
import jax.numpy as jnp
from jax import lax
from jax.experimental import pallas as pl
from jax.experimental.pallas import tpu as pltpu
from jax.sharding import PartitionSpec as P

F32 = jnp.float32
BF16 = jnp.bfloat16
LANES = 128


def dot_nn(a, b):
    return lax.dot_general(a, b, (((1,), (0,)), ((), ())), preferred_element_type=F32)


def dot_nt(a, b):
    return lax.dot_general(a, b, (((1,), (1,)), ((), ())), preferred_element_type=F32)


def dot_tn(a, b):
    return lax.dot_general(a, b, (((0,), (0,)), ((), ())), preferred_element_type=F32)


def split2(x):
    high = x.astype(BF16)
    return high, (x - high.astype(F32)).astype(BF16)


def iota(shape, axis):
    return lax.broadcasted_iota(jnp.int32, shape, axis)


def one_hot(condition):
    return jnp.where(condition, 1.0, 0.0).astype(BF16)


def rows_to_lanes(ref, count, rhs):
    return jnp.concatenate([ref[pl.ds(r, count, stride=rhs), :] for r in range(rhs)], axis=1)


def lanes_to_rows(ref, value, rhs):
    count, width = value.shape
    rank = width // rhs
    for r in range(rhs):
        ref[pl.ds(r, count, stride=rhs), :] = value[:, r * rank : (r + 1) * rank]


def fetch(pairs, sems):
    copies = [pltpu.make_async_copy(src, dst, sems.at[i]) for i, (src, dst) in enumerate(pairs)]
    for copy in copies:
        copy.start()
    return copies


def pre_kernel(
    charges_h,
    bases_h,
    transfers_h,
    parent_of_h,
    far_pairs_h,
    far_c_h,
    par_pairs_h,
    par_c_h,
    send,
    charges,
    bases,
    transfers,
    parent_of,
    far_pairs,
    far_c,
    par_pairs,
    par_c,
    par_smem,
    sems,
    mo,
    ch,
    pm3,
    pb,
    a_ref,
    ob,
):
    leaves, rhs, _ = charges.shape
    rank = bases.shape[1]
    width = rhs * rank
    slots = far_c.shape[2]
    pairs = par_c.shape[0]
    parents = leaves // 2
    rows = send.shape[0]
    copies = fetch(
        [
            (charges_h, charges),
            (bases_h, bases),
            (transfers_h, transfers),
            (parent_of_h, parent_of),
            (far_pairs_h, far_pairs),
            (par_pairs_h, par_pairs),
            (par_pairs_h, par_smem),
            (far_c_h, far_c),
            (par_c_h, par_c),
        ],
        sems,
    )
    for copy in copies[:3]:
        copy.wait()

    for l in range(leaves):
        m = dot_nt(charges[l], bases[l]).astype(BF16)
        mo[l * rhs : (l + 1) * rhs, :] = m.astype(F32)
        ch[l * rhs : (l + 1) * rhs, :] = dot_nt(m, transfers[l])
    for copy in copies[3:]:
        copy.wait()
    m2 = rows_to_lanes(mo, leaves, rhs)
    high, low = split2(rows_to_lanes(ch, leaves, rhs))
    par_hot = one_hot(parent_of[...] % parents == iota((parents, leaves), 0))
    pm = (dot_nn(par_hot, high) + dot_nn(par_hot, low)).astype(BF16).astype(F32)
    lanes_to_rows(pm3, pm, rhs)
    shared = jnp.concatenate([m2[:parents], m2[parents:], pm], axis=1)
    half = 3 * width // 2
    shared = jnp.concatenate([shared[:, :half], shared[:, half:]], axis=0).astype(BF16)
    at = 2 * width + LANES
    for p in range(rows // (2 * parents)):
        send[p * 2 * parents : (p + 1) * 2 * parents, at : at + half] = shared

    owner_hot = one_hot(far_pairs[0:1, :] % leaves == iota((leaves, slots), 0))
    a_ref[...] = dot_tn(m2.astype(BF16), owner_hot)
    half = rank // 2
    for sb in range(slots // LANES):
        lanes = slice(sb * LANES, (sb + 1) * LANES)
        for jh in range(2):

            def body(k8, acc):
                rows_a = [
                    a_ref[pl.ds(pl.multiple_of(r * rank + k8 * 8, 8), 8), lanes]
                    for r in range(rhs)
                ]
                for i in range(8):
                    c = far_c[k8 * 8 + i, jh * half : (jh + 1) * half, lanes].astype(F32)
                    acc = tuple(acc[r] + c * rows_a[r][i : i + 1, :] for r in range(rhs))
                return acc

            acc = lax.fori_loop(
                0, rank // 8, body, tuple(jnp.zeros((half, LANES), F32) for _ in range(rhs))
            )
            for r in range(rhs):
                first = r * rank + jh * half
                ob[first : first + half, lanes] = acc[r].astype(BF16)
    partner = far_pairs[1:2, :]
    local = jnp.where(partner >= 0, partner % leaves, -1).astype(F32)
    ob[width : width + LANES, :] = jnp.broadcast_to(local, (LANES, slots)).astype(BF16)
    unit = one_hot(iota((LANES, LANES), 0) == iota((LANES, LANES), 1))
    for sb in range(slots // LANES):
        lanes = slice(sb * LANES, (sb + 1) * LANES)
        send[lanes, 0 : width + LANES] = dot_nt(unit, ob[:, lanes]).astype(BF16)

    for s in range(pairs):
        q = par_smem[0, s] % parents
        x = pm3[pl.ds(pl.multiple_of(q * rhs, rhs), rhs), :].astype(BF16)
        pb[s * rhs : (s + 1) * rhs, :] = dot_nn(x, par_c[s])
    high, low = split2(rows_to_lanes(pb, pairs, rhs))
    hot = one_hot(par_pairs[1:2, :] == iota((rows, pairs), 0))
    at = width + LANES
    send[:, at : at + width] = (dot_nn(hot, high) + dot_nn(hot, low)).astype(BF16)


def near_kernel(pairs, charges, following, self_blocks, near_blocks, own, away, ext, out):
    leaves = charges.shape[0]
    step = pl.program_id(0)
    selves, nears = self_blocks.shape[0], near_blocks.shape[0]

    @pl.when(step == 0)
    def _():
        ext[0:leaves] = charges[...]
        ext[leaves:] = following[...]
        out[...] = jnp.zeros_like(out)

    terms = [(step * selves + i, dot_nt(ext[step * selves + i], self_blocks[i])) for i in range(selves)]
    for i in range(nears):
        a, b = pairs[0, step * nears + i], pairs[1, step * nears + i]
        first = (a // leaves) * leaves
        a, b = a - first, b - first
        terms.append((a, dot_nt(ext[b], near_blocks[i])))
        terms.append((b, dot_nn(ext[a], near_blocks[i])))
    for at, term in terms:
        out[at] += term

    @pl.when(step == pl.num_programs(0) - 1)
    def _():
        own[...] = out[0:leaves]
        away[...] = out[leaves:].astype(BF16)


def post_kernel(
    core_smem,
    mom2,
    got,
    bases,
    transfers,
    parent_of,
    far_pairs,
    far_c,
    par_pairs,
    par_c,
    near_own,
    near_back,
    out,
    b_ref,
    fw,
    g_ref,
    pf,
    lf,
    pg,
):
    leaves, rank, _ = bases.shape
    slots = far_c.shape[2]
    pairs = par_c.shape[0]
    parents = leaves // 2
    rows = got.shape[0]
    rhs = b_ref.shape[0] // rank
    width = rhs * rank
    at_par = width + LANES
    at_mom = at_par + width
    core = core_smem[0, 0] // leaves % 2
    mom = got[:, at_mom:]
    shared = jnp.concatenate(
        [jnp.where(core == 0, mom, mom2[...]), jnp.where(core == 0, mom2[...], mom)], axis=1
    )
    row_id = iota((rows, slots), 0)
    base_leaf = row_id // parents * leaves + row_id % parents
    partner = far_pairs[1:2, :]
    total = None
    for h in range(2):
        hot = one_hot(partner == base_leaf + h * parents)
        part = dot_tn(shared[:, h * width : (h + 1) * width], hot)
        total = part if total is None else total + part
    b_ref[...] = total

    hot = one_hot(par_pairs[1:2, :] == iota((rows, pairs), 0))
    picked = dot_tn(hot, shared[:, 2 * width :])
    lanes_to_rows(g_ref, picked, rhs)
    for s in range(pairs):
        x = g_ref[s * rhs : (s + 1) * rhs, :].astype(BF16)
        pf[s * rhs : (s + 1) * rhs, :] = dot_nt(x, par_c[s])
    high, low = split2(rows_to_lanes(pf, pairs, rhs))
    hot = one_hot(par_pairs[0:1, :] % parents == iota((parents, pairs), 0))
    fold = one_hot(iota((parents, rows), 1) % parents == iota((parents, rows), 0))
    locals_p = dot_nn(hot, high) + dot_nn(hot, low) + dot_nn(fold, got[:, at_par : at_par + width])
    hot = one_hot(parent_of[...] % parents == iota((parents, leaves), 0))
    lanes_to_rows(pg, dot_tn(hot, locals_p.astype(BF16)), rhs)

    for sb in range(slots // LANES):
        lanes = slice(sb * LANES, (sb + 1) * LANES)

        def body(k8, carry):
            for r in range(rhs):
                b = b_ref[r * rank : (r + 1) * rank, lanes]
                sums = [
                    jnp.sum(far_c[k8 * 8 + i, :, lanes].astype(F32) * b, axis=0, keepdims=True)
                    for i in range(8)
                ]
                fw[pl.ds(pl.multiple_of(r * rank + k8 * 8, 8), 8), lanes] = jnp.concatenate(
                    sums, axis=0
                )
            return carry

        lax.fori_loop(0, rank // 8, body, 0)

    hot = one_hot(far_pairs[0:1, :] % leaves == iota((leaves, slots), 0))
    high, low = split2(fw[...])
    leaf = dot_nt(hot, high) + dot_nt(hot, low)
    index = got[:, width : width + LANES].astype(F32)[:, :leaves].astype(jnp.int32)
    hot = one_hot(index == iota((rows, leaves), 1))
    leaf = leaf + dot_tn(hot, got[:, 0:width])
    lanes_to_rows(lf, leaf, rhs)

    for l in range(leaves):
        at = slice(l * rhs, (l + 1) * rhs)
        down = dot_nn(pg[at, :].astype(BF16), transfers[l])
        mine = (lf[at, :] + down).astype(BF16)
        near = near_own[l] + near_back[l].astype(F32)
        out[l] = dot_nn(mine, bases[l]) + near


def after(value, earlier):
    anywhere = pl.BlockSpec(memory_space=pl.ANY)
    return pl.pallas_call(
        lambda value, earlier, same: None,
        out_shape=jax.ShapeDtypeStruct(value.shape, value.dtype),
        in_specs=[anywhere] * 2,
        out_specs=anywhere,
        input_output_aliases={0: 0},
        compiler_params=pltpu.CompilerParams(vmem_limit_bytes=1024 * 1024),
        name="after",
    )(value, earlier)


def passed_along(value, axis, steps):
    count = lax.axis_size(axis)
    leading, last = (max(0, -steps), min(count, count - steps))
    return lax.ppermute(value, axis, [(source, source + steps) for source in range(leading, last)])


def on_device(
    charges,
    self_blocks,
    near_blocks,
    near_pairs,
    bases,
    transfers,
    parent_of,
    far_pairs,
    far_coupling,
    par_pairs,
    par_coupling,
):
    leaves, rhs, panels = charges.shape
    rank = bases.shape[1]
    width = rhs * rank
    slots = far_coupling.shape[0]
    pairs = par_coupling.shape[0]
    parents = leaves // 2
    devices = lax.axis_size("sfc")
    rows = devices * parents
    columns = 2 * width + LANES + 3 * width // 2
    vmem = pl.BlockSpec(memory_space=pltpu.VMEM)
    smem = pl.BlockSpec(memory_space=pltpu.SMEM)
    hbm = pl.BlockSpec(memory_space=pltpu.HBM)
    params = pltpu.CompilerParams(vmem_limit_bytes=60 * 1024 * 1024)
    late = pltpu.CompilerParams(vmem_limit_bytes=48 * 1024 * 1024)

    def cost(moved):
        return pl.CostEstimate(flops=4 * moved, bytes_accessed=moved, transcendentals=0)

    following = passed_along(charges, "sfc", -1)
    far_pairs = far_pairs.T
    par_pairs = par_pairs.T
    near_pairs = near_pairs.T
    far_c = jnp.transpose(far_coupling, (1, 2, 0))
    parent_of = parent_of.reshape(1, leaves)

    def like(value, memory=pltpu.VMEM):
        return memory(value.shape, value.dtype)

    send = pl.pallas_call(
        pre_kernel,
        out_shape=jax.ShapeDtypeStruct((rows, columns), BF16),
        in_specs=[hbm] * 8,
        out_specs=vmem,
        scratch_shapes=[
            like(charges),
            like(bases),
            like(transfers),
            like(parent_of),
            like(far_pairs),
            like(far_c),
            like(par_pairs),
            like(par_coupling),
            like(par_pairs, pltpu.SMEM),
            pltpu.SemaphoreType.DMA((9,)),
            pltpu.VMEM((leaves * rhs, rank), F32),
            pltpu.VMEM((leaves * rhs, rank), F32),
            pltpu.VMEM((parents * rhs, rank), F32),
            pltpu.VMEM((pairs * rhs, rank), F32),
            pltpu.VMEM((width, slots), F32),
            pltpu.VMEM((width + LANES, slots), BF16),
        ],
        compiler_params=params,
        cost_estimate=cost(10_000_000),
        name="upward",
    )(charges, bases, transfers, parent_of, far_pairs, far_c, par_pairs, par_coupling)
    send = after(send, following)
    got = lax.all_to_all(send, "sfc", split_axis=0, concat_axis=0, tiled=True)
    steps = 8
    selves, nears = leaves // steps, near_blocks.shape[0] // steps
    whole = lambda *shape: pl.BlockSpec(shape, lambda i: (0,) * len(shape))
    near_own, near_away = pl.pallas_call(
        near_kernel,
        grid=(steps,),
        out_shape=[
            jax.ShapeDtypeStruct((leaves, rhs, panels), F32),
            jax.ShapeDtypeStruct((leaves, rhs, panels), BF16),
        ],
        in_specs=[
            smem,
            whole(leaves, rhs, panels),
            whole(leaves, rhs, panels),
            pl.BlockSpec((selves, panels, panels), lambda i: (i, 0, 0)),
            pl.BlockSpec((nears, panels, panels), lambda i: (i, 0, 0)),
        ],
        out_specs=[whole(leaves, rhs, panels)] * 2,
        scratch_shapes=[
            pltpu.VMEM((2 * leaves, rhs, panels), BF16),
            pltpu.VMEM((2 * leaves, rhs, panels), F32),
        ],
        compiler_params=pltpu.CompilerParams(vmem_limit_bytes=52 * 1024 * 1024),
        cost_estimate=cost(20_000_000),
        name="near",
    )(near_pairs, charges, following, self_blocks, near_blocks)
    near_back = passed_along(near_away, "sfc", 1)

    got = after(got, near_back)
    mom2 = lax.ppermute(
        got[:, 2 * width + LANES :], "sfc", [(i, i ^ 1) for i in range(devices)]
    )

    return pl.pallas_call(
        post_kernel,
        out_shape=jax.ShapeDtypeStruct((leaves, rhs, panels), F32),
        in_specs=[smem] + [vmem] * 11,
        out_specs=vmem,
        scratch_shapes=[
            pltpu.VMEM((width, slots), F32),
            pltpu.VMEM((width, slots), F32),
            pltpu.VMEM((pairs * rhs, rank), F32),
            pltpu.VMEM((pairs * rhs, rank), F32),
            pltpu.VMEM((leaves * rhs, rank), F32),
            pltpu.VMEM((leaves * rhs, rank), F32),
        ],
        compiler_params=late,
        name="downward",
    )(
        far_pairs,
        mom2,
        got,
        bases,
        transfers,
        parent_of,
        far_pairs,
        far_c,
        par_pairs,
        par_coupling,
        near_own,
        near_back,
    )


def solution(mesh):
    split = ("grp", "sfc")
    cube, flat = P(split, None, None), P(split, None)
    placed = (cube, cube, cube, flat, cube, cube, P(split), flat, cube, flat, cube)
    return jax.shard_map(
        on_device, mesh=mesh, in_specs=placed, out_specs=cube, check_vma=False
    )
```

```python
import functools

import jax
import jax.numpy as jnp
from jax import lax
from jax.experimental import pallas as pl
from jax.experimental.pallas import tpu as pltpu
from jax.sharding import PartitionSpec as P

F32 = jnp.float32
BF16 = jnp.bfloat16
LANES = 128


def dot_nn(a, b):
    return lax.dot_general(a, b, (((1,), (0,)), ((), ())), preferred_element_type=F32)


def dot_nt(a, b):
    return lax.dot_general(a, b, (((1,), (1,)), ((), ())), preferred_element_type=F32)


def dot_tn(a, b):
    return lax.dot_general(a, b, (((0,), (0,)), ((), ())), preferred_element_type=F32)


def split2(x):
    high = x.astype(BF16)
    return high, (x - high.astype(F32)).astype(BF16)


def iota(shape, axis):
    return lax.broadcasted_iota(jnp.int32, shape, axis)


def one_hot(condition):
    return jnp.where(condition, 1.0, 0.0).astype(BF16)


def rows_to_lanes(ref, count, rhs):
    return jnp.concatenate([ref[pl.ds(r, count, stride=rhs), :] for r in range(rhs)], axis=1)


def lanes_to_rows(ref, value, rhs):
    count, width = value.shape
    rank = width // rhs
    for r in range(rhs):
        ref[pl.ds(r, count, stride=rhs), :] = value[:, r * rank : (r + 1) * rank]


def row_sums(parts):
    row = iota(parts[0].shape, 0)
    for step in (4, 2, 1):
        upper = row % (2 * step) >= step
        merged = []
        for a, b in zip(parts[:step], parts[step:]):
            swapped = jnp.where(upper, a, b)
            if step == 4:
                moved = pltpu.roll(swapped, 4, axis=0)
            else:
                moved = jnp.where(
                    upper,
                    pltpu.roll(swapped, step, axis=0),
                    pltpu.roll(swapped, 8 - step, axis=0),
                )
            merged.append(jnp.where(upper, b, a) + moved)
        parts = merged
    return parts[0]


def fetch(pairs, sems):
    copies = [pltpu.make_async_copy(src, dst, sems.at[i]) for i, (src, dst) in enumerate(pairs)]
    for copy in copies:
        copy.start()
    return copies


def pre_kernel(
    charges_h,
    bases_h,
    transfers_h,
    parent_of_h,
    far_pairs_h,
    far_c_h,
    par_pairs_h,
    par_c_h,
    send,
    charges,
    bases,
    transfers,
    parent_of,
    far_pairs,
    far_c,
    par_pairs,
    par_c,
    par_smem,
    sems,
    mo,
    ch,
    pm3,
    pb,
    a_ref,
    ob,
):
    leaves, rhs, _ = charges.shape
    rank = bases.shape[1]
    width = rhs * rank
    slots = far_c.shape[2]
    pairs = par_c.shape[0]
    parents = leaves // 2
    rows = send.shape[0]
    copies = fetch(
        [
            (charges_h, charges),
            (bases_h, bases),
            (transfers_h, transfers),
            (parent_of_h, parent_of),
            (far_pairs_h, far_pairs),
            (par_pairs_h, par_pairs),
            (par_pairs_h, par_smem),
            (far_c_h, far_c),
            (par_c_h, par_c),
        ],
        sems,
    )
    for copy in copies[:3]:
        copy.wait()

    for l in range(leaves):
        m = dot_nt(charges[l], bases[l]).astype(BF16)
        mo[l * rhs : (l + 1) * rhs, :] = m.astype(F32)
        ch[l * rhs : (l + 1) * rhs, :] = dot_nt(m, transfers[l])
    for copy in copies[3:]:
        copy.wait()
    m2 = rows_to_lanes(mo, leaves, rhs)
    high, low = split2(rows_to_lanes(ch, leaves, rhs))
    par_hot = one_hot(parent_of[...] % parents == iota((parents, leaves), 0))
    pm = (dot_nn(par_hot, high) + dot_nn(par_hot, low)).astype(BF16).astype(F32)
    lanes_to_rows(pm3, pm, rhs)
    shared = jnp.concatenate([m2[:parents], m2[parents:], pm], axis=1)
    half = 3 * width // 2
    shared = jnp.concatenate([shared[:, :half], shared[:, half:]], axis=0).astype(BF16)
    at = 2 * width + LANES
    for p in range(rows // (2 * parents)):
        send[p * 2 * parents : (p + 1) * 2 * parents, at : at + half] = shared

    owner_hot = one_hot(far_pairs[0:1, :] % leaves == iota((leaves, slots), 0))
    a_ref[...] = dot_tn(m2.astype(BF16), owner_hot)
    half = rank // 2
    each = max(1, pairs // (slots // LANES * 2 * (rank // 8)))
    for sb in range(slots // LANES):
        lanes = slice(sb * LANES, (sb + 1) * LANES)
        for jh in range(2):
            first_pair = (sb * 2 + jh) * (rank // 8) * each

            def body(k8, acc):
                for i in range(each if first_pair < pairs else 0):
                    s = first_pair + k8 * each + i
                    q = par_smem[0, s] % parents
                    x = pm3[pl.ds(pl.multiple_of(q * rhs, rhs), rhs), :].astype(BF16)
                    pb[pl.ds(pl.multiple_of(s * rhs, rhs), rhs), :] = dot_nn(x, par_c[s])
                rows_a = [
                    a_ref[pl.ds(pl.multiple_of(r * rank + k8 * 8, 8), 8), lanes]
                    for r in range(rhs)
                ]
                for i in range(8):
                    c = far_c[k8 * 8 + i, jh * half : (jh + 1) * half, lanes].astype(F32)
                    acc = tuple(acc[r] + c * rows_a[r][i : i + 1, :] for r in range(rhs))
                return acc

            acc = lax.fori_loop(
                0, rank // 8, body, tuple(jnp.zeros((half, LANES), F32) for _ in range(rhs))
            )
            for r in range(rhs):
                first = r * rank + jh * half
                ob[first : first + half, lanes] = acc[r].astype(BF16)
    partner = far_pairs[1:2, :]
    local = jnp.where(partner >= 0, partner % leaves, -1).astype(F32)
    ob[width : width + LANES, :] = jnp.broadcast_to(local, (LANES, slots)).astype(BF16)
    unit = one_hot(iota((LANES, LANES), 0) == iota((LANES, LANES), 1))
    for sb in range(slots // LANES):
        lanes = slice(sb * LANES, (sb + 1) * LANES)
        send[lanes, 0 : width + LANES] = dot_nt(unit, ob[:, lanes]).astype(BF16)

    high, low = split2(rows_to_lanes(pb, pairs, rhs))
    hot = one_hot(par_pairs[1:2, :] == iota((rows, pairs), 0))
    at = width + LANES
    send[:, at : at + width] = (dot_nn(hot, high) + dot_nn(hot, low)).astype(BF16)


def near_kernel(pairs, charges, following, self_blocks, near_blocks, own, away, ext, out):
    leaves = charges.shape[0]
    step = pl.program_id(0)
    selves, nears = self_blocks.shape[0], near_blocks.shape[0]

    @pl.when(step == 0)
    def _():
        ext[0:leaves] = charges[...]
        ext[leaves:] = following[...]
        out[...] = jnp.zeros_like(out)

    terms = [(step * selves + i, dot_nt(ext[step * selves + i], self_blocks[i])) for i in range(selves)]
    for i in range(nears):
        a, b = pairs[0, step * nears + i], pairs[1, step * nears + i]
        first = (a // leaves) * leaves
        a, b = a - first, b - first
        terms.append((a, dot_nt(ext[b], near_blocks[i])))
        terms.append((b, dot_nn(ext[a], near_blocks[i])))
    for at, term in terms:
        out[at] += term

    @pl.when(step == pl.num_programs(0) - 1)
    def _():
        own[...] = out[0:leaves]
        away[...] = out[leaves:].astype(BF16)


def post_kernel(
    core_smem,
    mom2,
    got,
    bases,
    transfers,
    parent_of,
    far_pairs,
    far_c,
    par_pairs,
    par_c,
    near_own,
    near_back,
    out,
    b_ref,
    fw,
    g_ref,
    pf,
    lf,
    pg,
    dn,
):
    leaves, rank, _ = bases.shape
    slots = far_c.shape[2]
    pairs = par_c.shape[0]
    parents = leaves // 2
    rows = got.shape[0]
    rhs = b_ref.shape[0] // rank
    width = rhs * rank
    at_par = width + LANES
    at_mom = at_par + width
    core = core_smem[0, 0] // leaves % 2
    mom = got[:, at_mom:]
    shared = jnp.concatenate(
        [jnp.where(core == 0, mom, mom2[...]), jnp.where(core == 0, mom2[...], mom)], axis=1
    )
    row_id = iota((rows, slots), 0)
    base_leaf = row_id // parents * leaves + row_id % parents
    partner = far_pairs[1:2, :]
    total = None
    for h in range(2):
        hot = one_hot(partner == base_leaf + h * parents)
        part = dot_tn(shared[:, h * width : (h + 1) * width], hot)
        total = part if total is None else total + part
    b_ref[...] = total

    hot = one_hot(par_pairs[1:2, :] == iota((rows, pairs), 0))
    lanes_to_rows(g_ref, dot_tn(hot, shared[:, 2 * width :]), rhs)

    def couple(k8, sb):
        lanes = slice(sb * LANES, (sb + 1) * LANES)
        parts = [[] for _ in range(rhs)]
        for i in range(8):
            c = far_c[k8 * 8 + i, :, lanes].astype(F32)
            for r in range(rhs):
                prod = c * b_ref[r * rank : (r + 1) * rank, lanes]
                parts[r].append(sum(prod[j * 8 : (j + 1) * 8] for j in range(rank // 8)))
        for r in range(rhs):
            fw[pl.ds(pl.multiple_of(r * rank + k8 * 8, 8), 8), lanes] = row_sums(parts[r])

    blocks = slots // LANES
    trips = rank // 16
    each = max(1, pairs // (blocks * trips))
    for sb in range(blocks):
        first_pair = sb * trips * each

        def body(k8, carry):
            for i in range(each if first_pair < pairs else 0):
                s = first_pair + k8 * each + i
                at = pl.ds(pl.multiple_of(s * rhs, rhs), rhs)
                pf[at, :] = dot_nt(g_ref[at, :].astype(BF16), par_c[s])
            couple(k8, sb)
            return carry

        lax.fori_loop(0, trips, body, 0)

    high, low = split2(rows_to_lanes(pf, pairs, rhs))
    hot = one_hot(par_pairs[0:1, :] % parents == iota((parents, pairs), 0))
    fold = one_hot(iota((parents, rows), 1) % parents == iota((parents, rows), 0))
    locals_p = dot_nn(hot, high) + dot_nn(hot, low) + dot_nn(fold, got[:, at_par : at_par + width])
    hot = one_hot(parent_of[...] % parents == iota((parents, leaves), 0))
    lanes_to_rows(pg, dot_tn(hot, locals_p.astype(BF16)), rhs)

    each = max(1, leaves // (blocks * trips))
    for sb in range(blocks):
        first_leaf = sb * trips * each

        def body(k8, carry):
            for i in range(each if first_leaf < leaves else 0):
                l = first_leaf + k8 * each + i
                at = pl.ds(pl.multiple_of(l * rhs, rhs), rhs)
                dn[at, :] = dot_nn(pg[at, :].astype(BF16), transfers[l])
            couple(trips + k8, sb)
            return carry

        lax.fori_loop(0, trips, body, 0)

    hot = one_hot(far_pairs[0:1, :] % leaves == iota((leaves, slots), 0))
    high, low = split2(fw[...])
    leaf = dot_nt(hot, high) + dot_nt(hot, low)
    index = got[:, width : width + LANES].astype(F32)[:, :leaves].astype(jnp.int32)
    hot = one_hot(index == iota((rows, leaves), 1))
    leaf = leaf + dot_tn(hot, got[:, 0:width])
    lanes_to_rows(lf, leaf, rhs)

    for l in range(leaves):
        at = slice(l * rhs, (l + 1) * rhs)
        mine = (lf[at, :] + dn[at, :]).astype(BF16)
        near = near_own[l] + near_back[l].astype(F32)
        out[l] = dot_nn(mine, bases[l]) + near


def after(value, earlier, vmem_limit):
    anywhere = pl.BlockSpec(memory_space=pl.ANY)
    return pl.pallas_call(
        lambda value, earlier, same: None,
        out_shape=jax.ShapeDtypeStruct(value.shape, value.dtype),
        in_specs=[anywhere] * 2,
        out_specs=anywhere,
        input_output_aliases={0: 0},
        compiler_params=pltpu.CompilerParams(vmem_limit_bytes=vmem_limit),
        name="after",
    )(value, earlier)


def passed_along(value, axis, steps):
    count = lax.axis_size(axis)
    leading, last = (max(0, -steps), min(count, count - steps))
    return lax.ppermute(value, axis, [(source, source + steps) for source in range(leading, last)])


def on_device(
    charges,
    self_blocks,
    near_blocks,
    near_pairs,
    bases,
    transfers,
    parent_of,
    far_pairs,
    far_coupling,
    par_pairs,
    par_coupling,
):
    leaves, rhs, panels = charges.shape
    rank = bases.shape[1]
    width = rhs * rank
    slots = far_coupling.shape[0]
    pairs = par_coupling.shape[0]
    parents = leaves // 2
    devices = lax.axis_size("sfc")
    rows = devices * parents
    columns = 2 * width + LANES + 3 * width // 2
    vmem = pl.BlockSpec(memory_space=pltpu.VMEM)
    smem = pl.BlockSpec(memory_space=pltpu.SMEM)
    hbm = pl.BlockSpec(memory_space=pltpu.HBM)
    params = pltpu.CompilerParams(vmem_limit_bytes=60 * 1024 * 1024)
    late = pltpu.CompilerParams(vmem_limit_bytes=48 * 1024 * 1024)

    def cost(moved):
        return pl.CostEstimate(flops=4 * moved, bytes_accessed=moved, transcendentals=0)

    following = passed_along(charges, "sfc", -1)
    far_pairs = far_pairs.T
    par_pairs = par_pairs.T
    near_pairs = near_pairs.T
    far_c = jnp.transpose(far_coupling, (1, 2, 0))
    parent_of = parent_of.reshape(1, leaves)

    def like(value, memory=pltpu.VMEM):
        return memory(value.shape, value.dtype)

    send = pl.pallas_call(
        pre_kernel,
        out_shape=jax.ShapeDtypeStruct((rows, columns), BF16),
        in_specs=[hbm] * 8,
        out_specs=vmem,
        scratch_shapes=[
            like(charges),
            like(bases),
            like(transfers),
            like(parent_of),
            like(far_pairs),
            like(far_c),
            like(par_pairs),
            like(par_coupling),
            like(par_pairs, pltpu.SMEM),
            pltpu.SemaphoreType.DMA((9,)),
            pltpu.VMEM((leaves * rhs, rank), F32),
            pltpu.VMEM((leaves * rhs, rank), F32),
            pltpu.VMEM((parents * rhs, rank), F32),
            pltpu.VMEM((pairs * rhs, rank), F32),
            pltpu.VMEM((width, slots), F32),
            pltpu.VMEM((width + LANES, slots), BF16),
        ],
        compiler_params=params,
        cost_estimate=cost(10_000_000),
        name="upward",
    )(charges, bases, transfers, parent_of, far_pairs, far_c, par_pairs, par_coupling)
    send = after(send, following, 107 << 19)
    got = lax.all_to_all(send, "sfc", split_axis=0, concat_axis=0, tiled=True)
    steps = 8
    selves, nears = leaves // steps, near_blocks.shape[0] // steps
    whole = lambda *shape: pl.BlockSpec(shape, lambda i: (0,) * len(shape))
    near_own, near_away = pl.pallas_call(
        near_kernel,
        grid=(steps,),
        out_shape=[
            jax.ShapeDtypeStruct((leaves, rhs, panels), F32),
            jax.ShapeDtypeStruct((leaves, rhs, panels), BF16),
        ],
        in_specs=[
            smem,
            whole(leaves, rhs, panels),
            whole(leaves, rhs, panels),
            pl.BlockSpec((selves, panels, panels), lambda i: (i, 0, 0)),
            pl.BlockSpec((nears, panels, panels), lambda i: (i, 0, 0)),
        ],
        out_specs=[whole(leaves, rhs, panels)] * 2,
        scratch_shapes=[
            pltpu.VMEM((2 * leaves, rhs, panels), BF16),
            pltpu.VMEM((2 * leaves, rhs, panels), F32),
        ],
        compiler_params=pltpu.CompilerParams(vmem_limit_bytes=52 * 1024 * 1024),
        cost_estimate=cost(20_000_000),
        name="near",
    )(near_pairs, charges, following, self_blocks, near_blocks)
    near_back = passed_along(near_away, "sfc", 1)

    got = after(got, near_back, 1 << 20)
    mom2 = lax.ppermute(
        got[:, 2 * width + LANES :], "sfc", [(i, i ^ 1) for i in range(devices)]
    )

    return pl.pallas_call(
        post_kernel,
        out_shape=jax.ShapeDtypeStruct((leaves, rhs, panels), F32),
        in_specs=[smem] + [vmem] * 11,
        out_specs=vmem,
        scratch_shapes=[
            pltpu.VMEM((width, slots), F32),
            pltpu.VMEM((width, slots), F32),
            pltpu.VMEM((pairs * rhs, rank), F32),
            pltpu.VMEM((pairs * rhs, rank), F32),
            pltpu.VMEM((leaves * rhs, rank), F32),
            pltpu.VMEM((leaves * rhs, rank), F32),
            pltpu.VMEM((leaves * rhs, rank), F32),
        ],
        compiler_params=late,
        name="downward",
    )(
        far_pairs,
        mom2,
        got,
        bases,
        transfers,
        parent_of,
        far_pairs,
        far_c,
        par_pairs,
        par_coupling,
        near_own,
        near_back,
    )


def solution(mesh):
    split = ("grp", "sfc")
    cube, flat = P(split, None, None), P(split, None)
    placed = (cube, cube, cube, flat, cube, cube, P(split), flat, cube, flat, cube)
    return jax.shard_map(
        on_device, mesh=mesh, in_specs=placed, out_specs=cube, check_vma=False
    )
```

```python
import functools

import jax
import jax.numpy as jnp
from jax import lax
from jax.experimental import pallas as pl
from jax.experimental.pallas import tpu as pltpu
from jax.sharding import PartitionSpec as P

F32 = jnp.float32
BF16 = jnp.bfloat16
LANES = 128


def dot_nn(a, b):
    return lax.dot_general(a, b, (((1,), (0,)), ((), ())), preferred_element_type=F32)


def dot_nt(a, b):
    return lax.dot_general(a, b, (((1,), (1,)), ((), ())), preferred_element_type=F32)


def dot_tn(a, b):
    return lax.dot_general(a, b, (((0,), (0,)), ((), ())), preferred_element_type=F32)


def split2(x):
    high = x.astype(BF16)
    return high, (x - high.astype(F32)).astype(BF16)


def iota(shape, axis):
    return lax.broadcasted_iota(jnp.int32, shape, axis)


def one_hot(condition):
    return jnp.where(condition, 1.0, 0.0).astype(BF16)


def rows_to_lanes(ref, count, rhs):
    return jnp.concatenate([ref[pl.ds(r, count, stride=rhs), :] for r in range(rhs)], axis=1)


def lanes_to_rows(ref, value, rhs):
    count, width = value.shape
    rank = width // rhs
    for r in range(rhs):
        ref[pl.ds(r, count, stride=rhs), :] = value[:, r * rank : (r + 1) * rank]


def row_sums(parts):
    row = iota(parts[0].shape, 0)
    for step in (4, 2, 1):
        upper = row % (2 * step) >= step
        merged = []
        for a, b in zip(parts[:step], parts[step:]):
            swapped = jnp.where(upper, a, b)
            if step == 4:
                moved = pltpu.roll(swapped, 4, axis=0)
            else:
                moved = jnp.where(
                    upper,
                    pltpu.roll(swapped, step, axis=0),
                    pltpu.roll(swapped, 8 - step, axis=0),
                )
            merged.append(jnp.where(upper, b, a) + moved)
        parts = merged
    return parts[0]


def fetch(pairs, sems):
    copies = [pltpu.make_async_copy(src, dst, sems.at[i]) for i, (src, dst) in enumerate(pairs)]
    for copy in copies:
        copy.start()
    return copies


def pre_kernel(
    charges_h,
    bases_h,
    transfers_h,
    parent_of_h,
    far_pairs_h,
    far_c_h,
    par_pairs_h,
    par_c_h,
    send,
    charges,
    bases,
    transfers,
    parent_of,
    far_pairs,
    far_c,
    par_pairs,
    par_c,
    par_smem,
    sems,
    mo,
    ch,
    pm3,
    pb,
    a_ref,
    ob,
):
    leaves, rhs, _ = charges.shape
    rank = bases.shape[1]
    width = rhs * rank
    slots = far_c.shape[2]
    pairs = par_c.shape[0]
    parents = leaves // 2
    rows = send.shape[0]
    copies = fetch(
        [
            (charges_h, charges),
            (bases_h, bases),
            (transfers_h, transfers),
            (parent_of_h, parent_of),
            (far_pairs_h, far_pairs),
            (par_pairs_h, par_pairs),
            (par_pairs_h, par_smem),
            (far_c_h, far_c),
            (par_c_h, par_c),
        ],
        sems,
    )
    for copy in copies[:3]:
        copy.wait()

    for l in range(leaves):
        m = dot_nt(charges[l], bases[l]).astype(BF16)
        mo[l * rhs : (l + 1) * rhs, :] = m.astype(F32)
        ch[l * rhs : (l + 1) * rhs, :] = dot_nt(m, transfers[l])
    for copy in copies[3:]:
        copy.wait()
    m2 = rows_to_lanes(mo, leaves, rhs)
    high, low = split2(rows_to_lanes(ch, leaves, rhs))
    par_hot = one_hot(parent_of[...] % parents == iota((parents, leaves), 0))
    pm = (dot_nn(par_hot, high) + dot_nn(par_hot, low)).astype(BF16).astype(F32)
    lanes_to_rows(pm3, pm, rhs)
    shared = jnp.concatenate([m2[:parents], m2[parents:], pm], axis=1)
    half = 3 * width // 2
    shared = jnp.concatenate([shared[:, :half], shared[:, half:]], axis=0).astype(BF16)
    at = 2 * width + LANES
    for p in range(rows // (2 * parents)):
        send[p * 2 * parents : (p + 1) * 2 * parents, at : at + half] = shared

    owner_hot = one_hot(far_pairs[0:1, :] % leaves == iota((leaves, slots), 0))
    a_ref[...] = dot_tn(m2.astype(BF16), owner_hot)
    for s in range(pairs):
        q = par_smem[0, s] % parents
        x = pm3[pl.ds(pl.multiple_of(q * rhs, rhs), rhs), :].astype(BF16)
        pb[s * rhs : (s + 1) * rhs, :] = dot_nn(x, par_c[s])
    half = rank // 2
    for sb in range(slots // LANES):
        lanes = slice(sb * LANES, (sb + 1) * LANES)
        for jh in range(2):

            def body(k8, acc):
                rows_a = [
                    a_ref[pl.ds(pl.multiple_of(r * rank + k8 * 8, 8), 8), lanes]
                    for r in range(rhs)
                ]
                for i in range(8):
                    c = far_c[k8 * 8 + i, jh * half : (jh + 1) * half, lanes].astype(F32)
                    acc = tuple(acc[r] + c * rows_a[r][i : i + 1, :] for r in range(rhs))
                return acc

            acc = tuple(jnp.zeros((half, LANES), F32) for _ in range(rhs))
            acc = lax.fori_loop(0, rank // 8, body, acc, unroll=4)
            for r in range(rhs):
                first = r * rank + jh * half
                ob[first : first + half, lanes] = acc[r].astype(BF16)
    partner = far_pairs[1:2, :]
    local = jnp.where(partner >= 0, partner % leaves, -1).astype(F32)
    ob[width : width + LANES, :] = jnp.broadcast_to(local, (LANES, slots)).astype(BF16)
    unit = one_hot(iota((LANES, LANES), 0) == iota((LANES, LANES), 1))
    for sb in range(slots // LANES):
        lanes = slice(sb * LANES, (sb + 1) * LANES)
        send[lanes, 0 : width + LANES] = dot_nt(unit, ob[:, lanes]).astype(BF16)

    high, low = split2(rows_to_lanes(pb, pairs, rhs))
    hot = one_hot(par_pairs[1:2, :] == iota((rows, pairs), 0))
    at = width + LANES
    send[:, at : at + width] = (dot_nn(hot, high) + dot_nn(hot, low)).astype(BF16)


def near_kernel(pairs, charges, following, self_blocks, near_blocks, own, away, ext, out):
    leaves = charges.shape[0]
    step = pl.program_id(0)
    selves, nears = self_blocks.shape[0], near_blocks.shape[0]

    @pl.when(step == 0)
    def _():
        ext[0:leaves] = charges[...]
        ext[leaves:] = following[...]
        out[...] = jnp.zeros_like(out)

    terms = [(step * selves + i, dot_nt(ext[step * selves + i], self_blocks[i])) for i in range(selves)]
    for i in range(nears):
        a, b = pairs[0, step * nears + i], pairs[1, step * nears + i]
        first = (a // leaves) * leaves
        a, b = a - first, b - first
        terms.append((a, dot_nt(ext[b], near_blocks[i])))
        terms.append((b, dot_nn(ext[a], near_blocks[i])))
    for at, term in terms:
        out[at] += term

    @pl.when(step == pl.num_programs(0) - 1)
    def _():
        own[...] = out[0:leaves]
        away[...] = out[leaves:].astype(BF16)


def post_kernel(
    core_smem,
    mom2,
    got,
    bases,
    transfers,
    parent_of,
    far_pairs,
    far_c,
    par_pairs,
    par_c,
    near_own,
    near_back,
    out,
    b_ref,
    fw,
    g_ref,
    pf,
    lf,
    pg,
    dn,
):
    leaves, rank, _ = bases.shape
    slots = far_c.shape[2]
    pairs = par_c.shape[0]
    parents = leaves // 2
    rows = got.shape[0]
    rhs = b_ref.shape[0] // rank
    width = rhs * rank
    at_par = width + LANES
    at_mom = at_par + width
    core = core_smem[0, 0] // leaves % 2
    mom = got[:, at_mom:]
    shared = jnp.concatenate(
        [jnp.where(core == 0, mom, mom2[...]), jnp.where(core == 0, mom2[...], mom)], axis=1
    )
    row_id = iota((rows, slots), 0)
    base_leaf = row_id // parents * leaves + row_id % parents
    partner = far_pairs[1:2, :]
    total = None
    for h in range(2):
        hot = one_hot(partner == base_leaf + h * parents)
        part = dot_tn(shared[:, h * width : (h + 1) * width], hot)
        total = part if total is None else total + part
    b_ref[...] = total

    hot = one_hot(par_pairs[1:2, :] == iota((rows, pairs), 0))
    lanes_to_rows(g_ref, dot_tn(hot, shared[:, 2 * width :]), rhs)

    def couple(k8, sb):
        lanes = slice(sb * LANES, (sb + 1) * LANES)
        parts = [[] for _ in range(rhs)]
        for i in range(8):
            c = far_c[k8 * 8 + i, :, lanes].astype(F32)
            for r in range(rhs):
                prod = c * b_ref[r * rank : (r + 1) * rank, lanes]
                parts[r].append(sum(prod[j * 8 : (j + 1) * 8] for j in range(rank // 8)))
        for r in range(rhs):
            fw[pl.ds(pl.multiple_of(r * rank + k8 * 8, 8), 8), lanes] = row_sums(parts[r])

    for s in range(pairs):
        at = slice(s * rhs, (s + 1) * rhs)
        pf[at, :] = dot_nt(g_ref[at, :].astype(BF16), par_c[s])
    high, low = split2(rows_to_lanes(pf, pairs, rhs))
    hot = one_hot(par_pairs[0:1, :] % parents == iota((parents, pairs), 0))
    fold = one_hot(iota((parents, rows), 1) % parents == iota((parents, rows), 0))
    locals_p = dot_nn(hot, high) + dot_nn(hot, low) + dot_nn(fold, got[:, at_par : at_par + width])
    hot = one_hot(parent_of[...] % parents == iota((parents, leaves), 0))
    lanes_to_rows(pg, dot_tn(hot, locals_p.astype(BF16)), rhs)

    for l in range(leaves):
        at = slice(l * rhs, (l + 1) * rhs)
        dn[at, :] = dot_nn(pg[at, :].astype(BF16), transfers[l])

    for sb in range(slots // LANES):

        def body(k8, carry):
            couple(k8, sb)
            return carry

        lax.fori_loop(0, rank // 8, body, 0, unroll=4)

    hot = one_hot(far_pairs[0:1, :] % leaves == iota((leaves, slots), 0))
    high, low = split2(fw[...])
    leaf = dot_nt(hot, high) + dot_nt(hot, low)
    index = got[:, width : width + LANES].astype(F32)[:, :leaves].astype(jnp.int32)
    hot = one_hot(index == iota((rows, leaves), 1))
    leaf = leaf + dot_tn(hot, got[:, 0:width])
    lanes_to_rows(lf, leaf, rhs)

    for l in range(leaves):
        at = slice(l * rhs, (l + 1) * rhs)
        mine = (lf[at, :] + dn[at, :]).astype(BF16)
        near = near_own[l] + near_back[l].astype(F32)
        out[l] = dot_nn(mine, bases[l]) + near


def after(value, earlier, vmem_limit):
    anywhere = pl.BlockSpec(memory_space=pl.ANY)
    return pl.pallas_call(
        lambda value, earlier, same: None,
        out_shape=jax.ShapeDtypeStruct(value.shape, value.dtype),
        in_specs=[anywhere] * 2,
        out_specs=anywhere,
        input_output_aliases={0: 0},
        compiler_params=pltpu.CompilerParams(vmem_limit_bytes=vmem_limit),
        name="after",
    )(value, earlier)


def passed_along(value, axis, steps):
    count = lax.axis_size(axis)
    leading, last = (max(0, -steps), min(count, count - steps))
    return lax.ppermute(value, axis, [(source, source + steps) for source in range(leading, last)])


def on_device(
    charges,
    self_blocks,
    near_blocks,
    near_pairs,
    bases,
    transfers,
    parent_of,
    far_pairs,
    far_coupling,
    par_pairs,
    par_coupling,
):
    leaves, rhs, panels = charges.shape
    rank = bases.shape[1]
    width = rhs * rank
    slots = far_coupling.shape[0]
    pairs = par_coupling.shape[0]
    parents = leaves // 2
    devices = lax.axis_size("sfc")
    rows = devices * parents
    columns = 2 * width + LANES + 3 * width // 2
    vmem = pl.BlockSpec(memory_space=pltpu.VMEM)
    smem = pl.BlockSpec(memory_space=pltpu.SMEM)
    hbm = pl.BlockSpec(memory_space=pltpu.HBM)
    params = pltpu.CompilerParams(vmem_limit_bytes=60 * 1024 * 1024)
    late = pltpu.CompilerParams(vmem_limit_bytes=48 * 1024 * 1024)

    def cost(moved):
        return pl.CostEstimate(flops=4 * moved, bytes_accessed=moved, transcendentals=0)

    following = passed_along(charges, "sfc", -1)
    far_pairs = far_pairs.T
    par_pairs = par_pairs.T
    near_pairs = near_pairs.T
    far_c = jnp.transpose(far_coupling, (1, 2, 0))
    parent_of = parent_of.reshape(1, leaves)

    def like(value, memory=pltpu.VMEM):
        return memory(value.shape, value.dtype)

    send = pl.pallas_call(
        pre_kernel,
        out_shape=jax.ShapeDtypeStruct((rows, columns), BF16),
        in_specs=[hbm] * 8,
        out_specs=vmem,
        scratch_shapes=[
            like(charges),
            like(bases),
            like(transfers),
            like(parent_of),
            like(far_pairs),
            like(far_c),
            like(par_pairs),
            like(par_coupling),
            like(par_pairs, pltpu.SMEM),
            pltpu.SemaphoreType.DMA((9,)),
            pltpu.VMEM((leaves * rhs, rank), F32),
            pltpu.VMEM((leaves * rhs, rank), F32),
            pltpu.VMEM((parents * rhs, rank), F32),
            pltpu.VMEM((pairs * rhs, rank), F32),
            pltpu.VMEM((width, slots), F32),
            pltpu.VMEM((width + LANES, slots), BF16),
        ],
        compiler_params=params,
        cost_estimate=cost(10_000_000),
        name="upward",
    )(charges, bases, transfers, parent_of, far_pairs, far_c, par_pairs, par_coupling)
    send = after(send, following, 107 << 19)
    got = lax.all_to_all(send, "sfc", split_axis=0, concat_axis=0, tiled=True)
    steps = 8
    selves, nears = leaves // steps, near_blocks.shape[0] // steps
    whole = lambda *shape: pl.BlockSpec(shape, lambda i: (0,) * len(shape))
    near_own, near_away = pl.pallas_call(
        near_kernel,
        grid=(steps,),
        out_shape=[
            jax.ShapeDtypeStruct((leaves, rhs, panels), F32),
            jax.ShapeDtypeStruct((leaves, rhs, panels), BF16),
        ],
        in_specs=[
            smem,
            whole(leaves, rhs, panels),
            whole(leaves, rhs, panels),
            pl.BlockSpec((selves, panels, panels), lambda i: (i, 0, 0)),
            pl.BlockSpec((nears, panels, panels), lambda i: (i, 0, 0)),
        ],
        out_specs=[whole(leaves, rhs, panels)] * 2,
        scratch_shapes=[
            pltpu.VMEM((2 * leaves, rhs, panels), BF16),
            pltpu.VMEM((2 * leaves, rhs, panels), F32),
        ],
        compiler_params=pltpu.CompilerParams(vmem_limit_bytes=52 * 1024 * 1024),
        cost_estimate=cost(20_000_000),
        name="near",
    )(near_pairs, charges, following, self_blocks, near_blocks)
    near_back = passed_along(near_away, "sfc", 1)

    got = after(got, near_back, 1 << 20)
    mom2 = lax.ppermute(
        got[:, 2 * width + LANES :], "sfc", [(i, i ^ 1) for i in range(devices)]
    )

    return pl.pallas_call(
        post_kernel,
        out_shape=jax.ShapeDtypeStruct((leaves, rhs, panels), F32),
        in_specs=[smem] + [vmem] * 11,
        out_specs=vmem,
        scratch_shapes=[
            pltpu.VMEM((width, slots), F32),
            pltpu.VMEM((width, slots), F32),
            pltpu.VMEM((pairs * rhs, rank), F32),
            pltpu.VMEM((pairs * rhs, rank), F32),
            pltpu.VMEM((leaves * rhs, rank), F32),
            pltpu.VMEM((leaves * rhs, rank), F32),
            pltpu.VMEM((leaves * rhs, rank), F32),
        ],
        compiler_params=late,
        name="downward",
    )(
        far_pairs,
        mom2,
        got,
        bases,
        transfers,
        parent_of,
        far_pairs,
        far_c,
        par_pairs,
        par_coupling,
        near_own,
        near_back,
    )


def solution(mesh):
    split = ("grp", "sfc")
    cube, flat = P(split, None, None), P(split, None)
    placed = (cube, cube, cube, flat, cube, cube, P(split), flat, cube, flat, cube)
    return jax.shard_map(
        on_device, mesh=mesh, in_specs=placed, out_specs=cube, check_vma=False
    )
```

```python
import functools

import jax
import jax.numpy as jnp
from jax import lax
from jax.experimental import pallas as pl
from jax.experimental.pallas import tpu as pltpu
from jax.sharding import PartitionSpec as P

F32 = jnp.float32
BF16 = jnp.bfloat16
LANES = 128


def dot_nn(a, b):
    return lax.dot_general(a, b, (((1,), (0,)), ((), ())), preferred_element_type=F32)


def dot_nt(a, b):
    return lax.dot_general(a, b, (((1,), (1,)), ((), ())), preferred_element_type=F32)


def dot_tn(a, b):
    return lax.dot_general(a, b, (((0,), (0,)), ((), ())), preferred_element_type=F32)


def split2(x):
    high = x.astype(BF16)
    return high, (x - high.astype(F32)).astype(BF16)


def iota(shape, axis):
    return lax.broadcasted_iota(jnp.int32, shape, axis)


def one_hot(condition):
    return jnp.where(condition, 1.0, 0.0).astype(BF16)


def rows_to_lanes(ref, count, rhs):
    return jnp.concatenate([ref[pl.ds(r, count, stride=rhs), :] for r in range(rhs)], axis=1)


def lanes_to_rows(ref, value, rhs):
    count, width = value.shape
    rank = width // rhs
    for r in range(rhs):
        ref[pl.ds(r, count, stride=rhs), :] = value[:, r * rank : (r + 1) * rank]


def row_sums(parts):
    row = iota(parts[0].shape, 0)
    for step in (4, 2, 1):
        upper = row % (2 * step) >= step
        merged = []
        for a, b in zip(parts[:step], parts[step:]):
            swapped = jnp.where(upper, a, b)
            if step == 4:
                moved = pltpu.roll(swapped, 4, axis=0)
            else:
                moved = jnp.where(
                    upper,
                    pltpu.roll(swapped, step, axis=0),
                    pltpu.roll(swapped, 8 - step, axis=0),
                )
            merged.append(jnp.where(upper, b, a) + moved)
        parts = merged
    return parts[0]


def fetch(pairs, sems):
    copies = [pltpu.make_async_copy(src, dst, sems.at[i]) for i, (src, dst) in enumerate(pairs)]
    for copy in copies:
        copy.start()
    return copies


def pre_kernel(
    charges_h,
    bases_h,
    transfers_h,
    parent_of_h,
    far_pairs_h,
    far_c_h,
    par_pairs_h,
    par_c_h,
    send,
    charges,
    bases,
    transfers,
    parent_of,
    far_pairs,
    far_c,
    par_pairs,
    par_c,
    par_smem,
    sems,
    mo,
    ch,
    pm3,
    pb,
    a_ref,
    ob,
):
    leaves, rhs, _ = charges.shape
    rank = bases.shape[1]
    width = rhs * rank
    slots = far_c.shape[2]
    pairs = par_c.shape[0]
    parents = leaves // 2
    rows = send.shape[0]
    copies = fetch(
        [
            (charges_h, charges),
            (bases_h, bases),
            (transfers_h, transfers),
            (parent_of_h, parent_of),
            (far_pairs_h, far_pairs),
            (par_pairs_h, par_pairs),
            (par_pairs_h, par_smem),
            (far_c_h, far_c),
            (par_c_h, par_c),
        ],
        sems,
    )
    for copy in copies[:3]:
        copy.wait()

    for l in range(leaves):
        m = dot_nt(charges[l], bases[l]).astype(BF16)
        mo[l * rhs : (l + 1) * rhs, :] = m.astype(F32)
        ch[l * rhs : (l + 1) * rhs, :] = dot_nt(m, transfers[l])
    for copy in copies[3:]:
        copy.wait()
    m2 = rows_to_lanes(mo, leaves, rhs)
    high, low = split2(rows_to_lanes(ch, leaves, rhs))
    par_hot = one_hot(parent_of[...] % parents == iota((parents, leaves), 0))
    pm = (dot_nn(par_hot, high) + dot_nn(par_hot, low)).astype(BF16).astype(F32)
    lanes_to_rows(pm3, pm, rhs)
    shared = jnp.concatenate([m2[:parents], m2[parents:], pm], axis=1)
    half = 3 * width // 2
    shared = jnp.concatenate([shared[:, :half], shared[:, half:]], axis=0).astype(BF16)
    at = 2 * width + LANES
    for p in range(rows // (2 * parents)):
        send[p * 2 * parents : (p + 1) * 2 * parents, at : at + half] = shared

    owner_hot = one_hot(far_pairs[0:1, :] % leaves == iota((leaves, slots), 0))
    a_ref[...] = dot_tn(m2.astype(BF16), owner_hot)
    for s in range(pairs):
        q = par_smem[0, s] % parents
        x = pm3[pl.ds(pl.multiple_of(q * rhs, rhs), rhs), :].astype(BF16)
        pb[s * rhs : (s + 1) * rhs, :] = dot_nn(x, par_c[s])
    half = rank // 2
    for sb in range(slots // LANES):
        lanes = slice(sb * LANES, (sb + 1) * LANES)
        for jh in range(2):

            def body(k8, acc):
                rows_a = [
                    a_ref[pl.ds(pl.multiple_of(r * rank + k8 * 8, 8), 8), lanes]
                    for r in range(rhs)
                ]
                for i in range(8):
                    c = far_c[k8 * 8 + i, jh * half : (jh + 1) * half, lanes].astype(F32)
                    acc = tuple(acc[r] + c * rows_a[r][i : i + 1, :] for r in range(rhs))
                return acc

            acc = tuple(jnp.zeros((half, LANES), F32) for _ in range(rhs))
            acc = lax.fori_loop(0, rank // 8, body, acc, unroll=4)
            for r in range(rhs):
                first = r * rank + jh * half
                ob[first : first + half, lanes] = acc[r].astype(BF16)
    partner = far_pairs[1:2, :]
    local = jnp.where(partner >= 0, partner % leaves, -1).astype(F32)
    ob[width : width + LANES, :] = jnp.broadcast_to(local, (LANES, slots)).astype(BF16)
    unit = one_hot(iota((LANES, LANES), 0) == iota((LANES, LANES), 1))
    for sb in range(slots // LANES):
        lanes = slice(sb * LANES, (sb + 1) * LANES)
        send[lanes, 0 : width + LANES] = dot_nt(unit, ob[:, lanes]).astype(BF16)

    high, low = split2(rows_to_lanes(pb, pairs, rhs))
    hot = one_hot(par_pairs[1:2, :] == iota((rows, pairs), 0))
    at = width + LANES
    send[:, at : at + width] = (dot_nn(hot, high) + dot_nn(hot, low)).astype(BF16)


def near_kernel(pairs, charges, following, self_blocks, near_blocks, own, away, ct, acc, back):
    leaves, rhs, panels = charges.shape
    step = pl.program_id(0)
    selves, nears = self_blocks.shape[0], near_blocks.shape[0]

    @pl.when(step == 0)
    def _():
        ct[0] = charges[...].astype(F32).reshape(leaves * rhs, panels).T
        ct[1] = following[...].astype(F32).reshape(leaves * rhs, panels).T
        acc[...] = jnp.zeros_like(acc)
        back[...] = jnp.zeros_like(back)

    column_leaf = iota((panels, leaves * rhs), 1) // rhs
    total = None
    for i in range(selves):
        placed = jnp.where(column_leaf == step * selves + i, ct[0], 0.0).astype(BF16)
        term = dot_nn(self_blocks[i], placed)
        total = term if total is None else total + term
    terms = []
    for i in range(nears):
        a, b = pairs[0, step * nears + i], pairs[1, step * nears + i]
        first = (a // leaves) * leaves
        a, b = a - first, b - first
        shift = (a - b + 2 * leaves) % leaves * rhs
        turned = pltpu.roll(ct[b // leaves], shift, axis=1)
        placed = jnp.where(column_leaf == a, turned, 0.0).astype(BF16)
        total = total + dot_nn(near_blocks[i], placed)
        terms.append((b, dot_nn(charges[a], near_blocks[i])))
    acc[...] += total
    for at, term in terms:
        back[at] += term

    @pl.when(step == pl.num_programs(0) - 1)
    def _():
        own[...] = acc[...].T.reshape(leaves, rhs, panels) + back[0:leaves]
        away[...] = back[leaves:].astype(BF16)


def post_kernel(
    core_smem,
    mom2,
    got,
    bases,
    transfers,
    parent_of,
    far_pairs,
    far_c,
    par_pairs,
    par_c,
    near_own,
    near_back,
    out,
    b_ref,
    fw,
    g_ref,
    pf,
    lf,
    pg,
    dn,
):
    leaves, rank, _ = bases.shape
    slots = far_c.shape[2]
    pairs = par_c.shape[0]
    parents = leaves // 2
    rows = got.shape[0]
    rhs = b_ref.shape[0] // rank
    width = rhs * rank
    at_par = width + LANES
    at_mom = at_par + width
    core = core_smem[0, 0] // leaves % 2
    mom = got[:, at_mom:]
    shared = jnp.concatenate(
        [jnp.where(core == 0, mom, mom2[...]), jnp.where(core == 0, mom2[...], mom)], axis=1
    )
    row_id = iota((rows, slots), 0)
    base_leaf = row_id // parents * leaves + row_id % parents
    partner = far_pairs[1:2, :]
    total = None
    for h in range(2):
        hot = one_hot(partner == base_leaf + h * parents)
        part = dot_tn(shared[:, h * width : (h + 1) * width], hot)
        total = part if total is None else total + part
    b_ref[...] = total

    hot = one_hot(par_pairs[1:2, :] == iota((rows, pairs), 0))
    lanes_to_rows(g_ref, dot_tn(hot, shared[:, 2 * width :]), rhs)

    def couple(k8, sb):
        lanes = slice(sb * LANES, (sb + 1) * LANES)
        parts = [[] for _ in range(rhs)]
        for i in range(8):
            c = far_c[k8 * 8 + i, :, lanes].astype(F32)
            for r in range(rhs):
                prod = c * b_ref[r * rank : (r + 1) * rank, lanes]
                parts[r].append(sum(prod[j * 8 : (j + 1) * 8] for j in range(rank // 8)))
        for r in range(rhs):
            fw[pl.ds(pl.multiple_of(r * rank + k8 * 8, 8), 8), lanes] = row_sums(parts[r])

    for s in range(pairs):
        at = slice(s * rhs, (s + 1) * rhs)
        pf[at, :] = dot_nt(g_ref[at, :].astype(BF16), par_c[s])
    high, low = split2(rows_to_lanes(pf, pairs, rhs))
    hot = one_hot(par_pairs[0:1, :] % parents == iota((parents, pairs), 0))
    fold = one_hot(iota((parents, rows), 1) % parents == iota((parents, rows), 0))
    locals_p = dot_nn(hot, high) + dot_nn(hot, low) + dot_nn(fold, got[:, at_par : at_par + width])
    hot = one_hot(parent_of[...] % parents == iota((parents, leaves), 0))
    lanes_to_rows(pg, dot_tn(hot, locals_p.astype(BF16)), rhs)

    for l in range(leaves):
        at = slice(l * rhs, (l + 1) * rhs)
        dn[at, :] = dot_nn(pg[at, :].astype(BF16), transfers[l])

    for sb in range(slots // LANES):

        def body(k8, carry):
            couple(k8, sb)
            return carry

        lax.fori_loop(0, rank // 8, body, 0, unroll=4)

    hot = one_hot(far_pairs[0:1, :] % leaves == iota((leaves, slots), 0))
    high, low = split2(fw[...])
    leaf = dot_nt(hot, high) + dot_nt(hot, low)
    index = got[:, width : width + LANES].astype(F32)[:, :leaves].astype(jnp.int32)
    hot = one_hot(index == iota((rows, leaves), 1))
    leaf = leaf + dot_tn(hot, got[:, 0:width])
    lanes_to_rows(lf, leaf, rhs)

    for l in range(leaves):
        at = slice(l * rhs, (l + 1) * rhs)
        mine = (lf[at, :] + dn[at, :]).astype(BF16)
        near = near_own[l] + near_back[l].astype(F32)
        out[l] = dot_nn(mine, bases[l]) + near


def after(value, earlier, vmem_limit):
    anywhere = pl.BlockSpec(memory_space=pl.ANY)
    return pl.pallas_call(
        lambda value, earlier, same: None,
        out_shape=jax.ShapeDtypeStruct(value.shape, value.dtype),
        in_specs=[anywhere] * 2,
        out_specs=anywhere,
        input_output_aliases={0: 0},
        compiler_params=pltpu.CompilerParams(vmem_limit_bytes=vmem_limit),
        name="after",
    )(value, earlier)


def passed_along(value, axis, steps):
    count = lax.axis_size(axis)
    leading, last = (max(0, -steps), min(count, count - steps))
    return lax.ppermute(value, axis, [(source, source + steps) for source in range(leading, last)])


def on_device(
    charges,
    self_blocks,
    near_blocks,
    near_pairs,
    bases,
    transfers,
    parent_of,
    far_pairs,
    far_coupling,
    par_pairs,
    par_coupling,
):
    leaves, rhs, panels = charges.shape
    rank = bases.shape[1]
    width = rhs * rank
    slots = far_coupling.shape[0]
    pairs = par_coupling.shape[0]
    parents = leaves // 2
    devices = lax.axis_size("sfc")
    rows = devices * parents
    columns = 2 * width + LANES + 3 * width // 2
    vmem = pl.BlockSpec(memory_space=pltpu.VMEM)
    smem = pl.BlockSpec(memory_space=pltpu.SMEM)
    hbm = pl.BlockSpec(memory_space=pltpu.HBM)
    params = pltpu.CompilerParams(vmem_limit_bytes=60 * 1024 * 1024)
    late = pltpu.CompilerParams(vmem_limit_bytes=48 * 1024 * 1024)

    def cost(moved):
        return pl.CostEstimate(flops=4 * moved, bytes_accessed=moved, transcendentals=0)

    following = passed_along(charges, "sfc", -1)
    far_pairs = far_pairs.T
    par_pairs = par_pairs.T
    near_pairs = near_pairs.T
    far_c = jnp.transpose(far_coupling, (1, 2, 0))
    parent_of = parent_of.reshape(1, leaves)

    def like(value, memory=pltpu.VMEM):
        return memory(value.shape, value.dtype)

    send = pl.pallas_call(
        pre_kernel,
        out_shape=jax.ShapeDtypeStruct((rows, columns), BF16),
        in_specs=[hbm] * 8,
        out_specs=vmem,
        scratch_shapes=[
            like(charges),
            like(bases),
            like(transfers),
            like(parent_of),
            like(far_pairs),
            like(far_c),
            like(par_pairs),
            like(par_coupling),
            like(par_pairs, pltpu.SMEM),
            pltpu.SemaphoreType.DMA((9,)),
            pltpu.VMEM((leaves * rhs, rank), F32),
            pltpu.VMEM((leaves * rhs, rank), F32),
            pltpu.VMEM((parents * rhs, rank), F32),
            pltpu.VMEM((pairs * rhs, rank), F32),
            pltpu.VMEM((width, slots), F32),
            pltpu.VMEM((width + LANES, slots), BF16),
        ],
        compiler_params=params,
        cost_estimate=cost(10_000_000),
        name="upward",
    )(charges, bases, transfers, parent_of, far_pairs, far_c, par_pairs, par_coupling)
    send = after(send, following, 107 << 19)
    got = lax.all_to_all(send, "sfc", split_axis=0, concat_axis=0, tiled=True)
    steps = 8
    selves, nears = leaves // steps, near_blocks.shape[0] // steps
    whole = lambda *shape: pl.BlockSpec(shape, lambda i: (0,) * len(shape))
    near_own, near_away = pl.pallas_call(
        near_kernel,
        grid=(steps,),
        out_shape=[
            jax.ShapeDtypeStruct((leaves, rhs, panels), F32),
            jax.ShapeDtypeStruct((leaves, rhs, panels), BF16),
        ],
        in_specs=[
            smem,
            whole(leaves, rhs, panels),
            whole(leaves, rhs, panels),
            pl.BlockSpec((selves, panels, panels), lambda i: (i, 0, 0)),
            pl.BlockSpec((nears, panels, panels), lambda i: (i, 0, 0)),
        ],
        out_specs=[whole(leaves, rhs, panels)] * 2,
        scratch_shapes=[
            pltpu.VMEM((2, panels, leaves * rhs), F32),
            pltpu.VMEM((panels, leaves * rhs), F32),
            pltpu.VMEM((2 * leaves, rhs, panels), F32),
        ],
        compiler_params=pltpu.CompilerParams(vmem_limit_bytes=52 * 1024 * 1024),
        cost_estimate=cost(20_000_000),
        name="near",
    )(near_pairs, charges, following, self_blocks, near_blocks)
    near_back = passed_along(near_away, "sfc", 1)

    got = after(got, near_back, 1 << 20)
    mom2 = lax.ppermute(
        got[:, 2 * width + LANES :], "sfc", [(i, i ^ 1) for i in range(devices)]
    )

    return pl.pallas_call(
        post_kernel,
        out_shape=jax.ShapeDtypeStruct((leaves, rhs, panels), F32),
        in_specs=[smem] + [vmem] * 11,
        out_specs=vmem,
        scratch_shapes=[
            pltpu.VMEM((width, slots), F32),
            pltpu.VMEM((width, slots), F32),
            pltpu.VMEM((pairs * rhs, rank), F32),
            pltpu.VMEM((pairs * rhs, rank), F32),
            pltpu.VMEM((leaves * rhs, rank), F32),
            pltpu.VMEM((leaves * rhs, rank), F32),
            pltpu.VMEM((leaves * rhs, rank), F32),
        ],
        compiler_params=late,
        name="downward",
    )(
        far_pairs,
        mom2,
        got,
        bases,
        transfers,
        parent_of,
        far_pairs,
        far_c,
        par_pairs,
        par_coupling,
        near_own,
        near_back,
    )


def solution(mesh):
    split = ("grp", "sfc")
    cube, flat = P(split, None, None), P(split, None)
    placed = (cube, cube, cube, flat, cube, cube, P(split), flat, cube, flat, cube)
    return jax.shard_map(
        on_device, mesh=mesh, in_specs=placed, out_specs=cube, check_vma=False
    )
```

```python
import functools

import jax
import jax.numpy as jnp
from jax import lax
from jax.experimental import pallas as pl
from jax.experimental.pallas import tpu as pltpu
from jax.sharding import PartitionSpec as P

F32 = jnp.float32
BF16 = jnp.bfloat16
LANES = 128


def dot_nn(a, b):
    return lax.dot_general(a, b, (((1,), (0,)), ((), ())), preferred_element_type=F32)


def dot_nt(a, b):
    return lax.dot_general(a, b, (((1,), (1,)), ((), ())), preferred_element_type=F32)


def dot_tn(a, b):
    return lax.dot_general(a, b, (((0,), (0,)), ((), ())), preferred_element_type=F32)


def split2(x):
    high = x.astype(BF16)
    return high, (x - high.astype(F32)).astype(BF16)


def iota(shape, axis):
    return lax.broadcasted_iota(jnp.int32, shape, axis)


def one_hot(condition):
    return jnp.where(condition, 1.0, 0.0).astype(BF16)


def rows_to_lanes(ref, count, rhs):
    return jnp.concatenate([ref[pl.ds(r, count, stride=rhs), :] for r in range(rhs)], axis=1)


def lanes_to_rows(ref, value, rhs):
    count, width = value.shape
    rank = width // rhs
    for r in range(rhs):
        ref[pl.ds(r, count, stride=rhs), :] = value[:, r * rank : (r + 1) * rank]


def row_sums(parts):
    row = iota(parts[0].shape, 0)
    for step in (4, 2, 1):
        upper = row % (2 * step) >= step
        merged = []
        for a, b in zip(parts[:step], parts[step:]):
            swapped = jnp.where(upper, a, b)
            if step == 4:
                moved = pltpu.roll(swapped, 4, axis=0)
            else:
                moved = jnp.where(
                    upper,
                    pltpu.roll(swapped, step, axis=0),
                    pltpu.roll(swapped, 8 - step, axis=0),
                )
            merged.append(jnp.where(upper, b, a) + moved)
        parts = merged
    return parts[0]


def fetch(pairs, sems):
    copies = [pltpu.make_async_copy(src, dst, sems.at[i]) for i, (src, dst) in enumerate(pairs)]
    for copy in copies:
        copy.start()
    return copies


def pre_kernel(
    charges_h,
    bases_h,
    transfers_h,
    parent_of_h,
    far_pairs_h,
    far_c_h,
    par_pairs_h,
    par_c_h,
    send,
    charges,
    bases,
    transfers,
    parent_of,
    far_pairs,
    far_c,
    par_pairs,
    par_c,
    par_smem,
    sems,
    mo,
    ch,
    pm3,
    pb,
    a_ref,
    ob,
):
    leaves, rhs, _ = charges.shape
    rank = bases.shape[1]
    width = rhs * rank
    slots = far_c.shape[2]
    pairs = par_c.shape[0]
    parents = leaves // 2
    rows = send.shape[0]
    copies = fetch(
        [
            (charges_h, charges),
            (bases_h, bases),
            (transfers_h, transfers),
            (parent_of_h, parent_of),
            (far_pairs_h, far_pairs),
            (par_pairs_h, par_pairs),
            (par_pairs_h, par_smem),
            (far_c_h, far_c),
            (par_c_h, par_c),
        ],
        sems,
    )
    for copy in copies[:3]:
        copy.wait()

    for l in range(leaves):
        m = dot_nt(charges[l], bases[l]).astype(BF16)
        mo[l * rhs : (l + 1) * rhs, :] = m.astype(F32)
        ch[l * rhs : (l + 1) * rhs, :] = dot_nt(m, transfers[l])
    for copy in copies[3:]:
        copy.wait()
    m2 = rows_to_lanes(mo, leaves, rhs)
    high, low = split2(rows_to_lanes(ch, leaves, rhs))
    par_hot = one_hot(parent_of[...] % parents == iota((parents, leaves), 0))
    pm = (dot_nn(par_hot, high) + dot_nn(par_hot, low)).astype(BF16).astype(F32)
    lanes_to_rows(pm3, pm, rhs)
    shared = jnp.concatenate([m2[:parents], m2[parents:], pm], axis=1)
    half = 3 * width // 2
    shared = jnp.concatenate([shared[:, :half], shared[:, half:]], axis=0).astype(BF16)
    at = 2 * width + LANES
    for p in range(rows // (2 * parents)):
        send[p * 2 * parents : (p + 1) * 2 * parents, at : at + half] = shared

    owner_hot = one_hot(far_pairs[0:1, :] % leaves == iota((leaves, slots), 0))
    a_ref[...] = dot_tn(m2.astype(BF16), owner_hot)
    for s in range(pairs):
        q = par_smem[0, s] % parents
        x = pm3[pl.ds(pl.multiple_of(q * rhs, rhs), rhs), :].astype(BF16)
        pb[s * rhs : (s + 1) * rhs, :] = dot_nn(x, par_c[s])
    half = rank // 2
    for sb in range(slots // LANES):
        lanes = slice(sb * LANES, (sb + 1) * LANES)
        for jh in range(2):

            def body(k8, acc):
                rows_a = [
                    a_ref[pl.ds(pl.multiple_of(r * rank + k8 * 8, 8), 8), lanes]
                    for r in range(rhs)
                ]
                for i in range(8):
                    c = far_c[k8 * 8 + i, jh * half : (jh + 1) * half, lanes].astype(F32)
                    acc = tuple(acc[r] + c * rows_a[r][i : i + 1, :] for r in range(rhs))
                return acc

            acc = tuple(jnp.zeros((half, LANES), F32) for _ in range(rhs))
            acc = lax.fori_loop(0, rank // 8, body, acc, unroll=4)
            for r in range(rhs):
                first = r * rank + jh * half
                ob[first : first + half, lanes] = acc[r].astype(BF16)
    partner = far_pairs[1:2, :]
    local = jnp.where(partner >= 0, partner % leaves, -1).astype(F32)
    ob[width : width + LANES, :] = jnp.broadcast_to(local, (LANES, slots)).astype(BF16)
    unit = one_hot(iota((LANES, LANES), 0) == iota((LANES, LANES), 1))
    for sb in range(slots // LANES):
        lanes = slice(sb * LANES, (sb + 1) * LANES)
        send[lanes, 0 : width + LANES] = dot_nt(unit, ob[:, lanes]).astype(BF16)

    high, low = split2(rows_to_lanes(pb, pairs, rhs))
    hot = one_hot(par_pairs[1:2, :] == iota((rows, pairs), 0))
    at = width + LANES
    send[:, at : at + width] = (dot_nn(hot, high) + dot_nn(hot, low)).astype(BF16)


def near_kernel(pairs, charges, following, self_blocks, near_blocks, own, away, ext, out):
    leaves = charges.shape[0]
    step = pl.program_id(0)
    selves, nears = self_blocks.shape[0], near_blocks.shape[0]

    @pl.when(step == 0)
    def _():
        ext[0:leaves] = charges[...]
        ext[leaves:] = following[...]
        out[...] = jnp.zeros_like(out)

    terms = [(step * selves + i, dot_nt(ext[step * selves + i], self_blocks[i])) for i in range(selves)]
    for i in range(nears):
        a, b = pairs[0, step * nears + i], pairs[1, step * nears + i]
        first = (a // leaves) * leaves
        a, b = a - first, b - first
        terms.append((a, dot_nt(ext[b], near_blocks[i])))
        terms.append((b, dot_nn(ext[a], near_blocks[i])))
    for at, term in terms:
        out[at] += term

    @pl.when(step == pl.num_programs(0) - 1)
    def _():
        own[...] = out[0:leaves]
        away[...] = out[leaves:].astype(BF16)


def post_kernel(
    core_smem,
    mom2,
    got,
    bases,
    transfers,
    parent_of,
    far_pairs,
    far_c,
    par_pairs,
    par_c,
    near_own,
    near_back,
    out,
    b_ref,
    fw,
    g_ref,
    pf,
    lf,
    pg,
    dn,
):
    leaves, rank, _ = bases.shape
    slots = far_c.shape[2]
    pairs = par_c.shape[0]
    parents = leaves // 2
    rows = got.shape[0]
    rhs = b_ref.shape[0] // rank
    width = rhs * rank
    at_par = width + LANES
    at_mom = at_par + width
    core = core_smem[0, 0] // leaves % 2
    mom = got[:, at_mom:]
    shared = jnp.concatenate(
        [jnp.where(core == 0, mom, mom2[...]), jnp.where(core == 0, mom2[...], mom)], axis=1
    )
    row_id = iota((rows, slots), 0)
    base_leaf = row_id // parents * leaves + row_id % parents
    partner = far_pairs[1:2, :]
    total = None
    for h in range(2):
        hot = one_hot(partner == base_leaf + h * parents)
        part = dot_tn(shared[:, h * width : (h + 1) * width], hot)
        total = part if total is None else total + part
    b_ref[...] = total

    hot = one_hot(par_pairs[1:2, :] == iota((rows, pairs), 0))
    lanes_to_rows(g_ref, dot_tn(hot, shared[:, 2 * width :]), rhs)

    def couple(k8, sb):
        lanes = slice(sb * LANES, (sb + 1) * LANES)
        parts = [[] for _ in range(rhs)]
        for i in range(8):
            c = far_c[k8 * 8 + i, :, lanes].astype(F32)
            for r in range(rhs):
                prod = c * b_ref[r * rank : (r + 1) * rank, lanes]
                parts[r].append(sum(prod[j * 8 : (j + 1) * 8] for j in range(rank // 8)))
        for r in range(rhs):
            fw[pl.ds(pl.multiple_of(r * rank + k8 * 8, 8), 8), lanes] = row_sums(parts[r])

    for s in range(pairs):
        at = slice(s * rhs, (s + 1) * rhs)
        pf[at, :] = dot_nt(g_ref[at, :].astype(BF16), par_c[s])
    high, low = split2(rows_to_lanes(pf, pairs, rhs))
    hot = one_hot(par_pairs[0:1, :] % parents == iota((parents, pairs), 0))
    fold = one_hot(iota((parents, rows), 1) % parents == iota((parents, rows), 0))
    locals_p = dot_nn(hot, high) + dot_nn(hot, low) + dot_nn(fold, got[:, at_par : at_par + width])
    hot = one_hot(parent_of[...] % parents == iota((parents, leaves), 0))
    lanes_to_rows(pg, dot_tn(hot, locals_p.astype(BF16)), rhs)

    for l in range(leaves):
        at = slice(l * rhs, (l + 1) * rhs)
        dn[at, :] = dot_nn(pg[at, :].astype(BF16), transfers[l])

    for sb in range(slots // LANES):

        def body(k8, carry):
            couple(k8, sb)
            return carry

        lax.fori_loop(0, rank // 8, body, 0, unroll=4)

    hot = one_hot(far_pairs[0:1, :] % leaves == iota((leaves, slots), 0))
    high, low = split2(fw[...])
    leaf = dot_nt(hot, high) + dot_nt(hot, low)
    index = got[:, width : width + LANES].astype(F32)[:, :leaves].astype(jnp.int32)
    hot = one_hot(index == iota((rows, leaves), 1))
    leaf = leaf + dot_tn(hot, got[:, 0:width])
    lanes_to_rows(lf, leaf, rhs)

    for l in range(leaves):
        at = slice(l * rhs, (l + 1) * rhs)
        mine = (lf[at, :] + dn[at, :]).astype(BF16)
        near = near_own[l] + near_back[l].astype(F32)
        out[l] = dot_nn(mine, bases[l]) + near


def after(value, earlier, vmem_limit):
    anywhere = pl.BlockSpec(memory_space=pl.ANY)
    return pl.pallas_call(
        lambda value, earlier, same: None,
        out_shape=jax.ShapeDtypeStruct(value.shape, value.dtype),
        in_specs=[anywhere] * 2,
        out_specs=anywhere,
        input_output_aliases={0: 0},
        compiler_params=pltpu.CompilerParams(vmem_limit_bytes=vmem_limit),
        name="after",
    )(value, earlier)


def passed_along(value, axis, steps):
    count = lax.axis_size(axis)
    leading, last = (max(0, -steps), min(count, count - steps))
    return lax.ppermute(value, axis, [(source, source + steps) for source in range(leading, last)])


def on_device(
    charges,
    self_blocks,
    near_blocks,
    near_pairs,
    bases,
    transfers,
    parent_of,
    far_pairs,
    far_coupling,
    par_pairs,
    par_coupling,
):
    leaves, rhs, panels = charges.shape
    rank = bases.shape[1]
    width = rhs * rank
    slots = far_coupling.shape[0]
    pairs = par_coupling.shape[0]
    parents = leaves // 2
    devices = lax.axis_size("sfc")
    rows = devices * parents
    columns = 2 * width + LANES + 3 * width // 2
    vmem = pl.BlockSpec(memory_space=pltpu.VMEM)
    smem = pl.BlockSpec(memory_space=pltpu.SMEM)
    hbm = pl.BlockSpec(memory_space=pltpu.HBM)
    params = pltpu.CompilerParams(vmem_limit_bytes=60 * 1024 * 1024)
    late = pltpu.CompilerParams(vmem_limit_bytes=48 * 1024 * 1024)

    def cost(moved):
        return pl.CostEstimate(flops=4 * moved, bytes_accessed=moved, transcendentals=0)

    following = passed_along(charges, "sfc", -1)
    far_pairs = far_pairs.T
    par_pairs = par_pairs.T
    near_pairs = near_pairs.T
    far_c = jnp.transpose(far_coupling, (1, 2, 0))
    parent_of = parent_of.reshape(1, leaves)

    def like(value, memory=pltpu.VMEM):
        return memory(value.shape, value.dtype)

    send = pl.pallas_call(
        pre_kernel,
        out_shape=jax.ShapeDtypeStruct((rows, columns), BF16),
        in_specs=[hbm] * 8,
        out_specs=vmem,
        scratch_shapes=[
            like(charges),
            like(bases),
            like(transfers),
            like(parent_of),
            like(far_pairs),
            like(far_c),
            like(par_pairs),
            like(par_coupling),
            like(par_pairs, pltpu.SMEM),
            pltpu.SemaphoreType.DMA((9,)),
            pltpu.VMEM((leaves * rhs, rank), F32),
            pltpu.VMEM((leaves * rhs, rank), F32),
            pltpu.VMEM((parents * rhs, rank), F32),
            pltpu.VMEM((pairs * rhs, rank), F32),
            pltpu.VMEM((width, slots), F32),
            pltpu.VMEM((width + LANES, slots), BF16),
        ],
        compiler_params=params,
        cost_estimate=cost(10_000_000),
        name="upward",
    )(charges, bases, transfers, parent_of, far_pairs, far_c, par_pairs, par_coupling)
    send = after(send, following, 107 << 19)
    got = lax.all_to_all(send, "sfc", split_axis=0, concat_axis=0, tiled=True)
    steps = 4
    selves, nears = leaves // steps, near_blocks.shape[0] // steps
    whole = lambda *shape: pl.BlockSpec(shape, lambda i: (0,) * len(shape))
    near_own, near_away = pl.pallas_call(
        near_kernel,
        grid=(steps,),
        out_shape=[
            jax.ShapeDtypeStruct((leaves, rhs, panels), F32),
            jax.ShapeDtypeStruct((leaves, rhs, panels), BF16),
        ],
        in_specs=[
            smem,
            whole(leaves, rhs, panels),
            whole(leaves, rhs, panels),
            pl.BlockSpec((selves, panels, panels), lambda i: (i, 0, 0)),
            pl.BlockSpec((nears, panels, panels), lambda i: (i, 0, 0)),
        ],
        out_specs=[whole(leaves, rhs, panels)] * 2,
        scratch_shapes=[
            pltpu.VMEM((2 * leaves, rhs, panels), BF16),
            pltpu.VMEM((2 * leaves, rhs, panels), F32),
        ],
        compiler_params=pltpu.CompilerParams(vmem_limit_bytes=52 * 1024 * 1024),
        cost_estimate=cost(20_000_000),
        name="near",
    )(near_pairs, charges, following, self_blocks, near_blocks)
    near_back = passed_along(near_away, "sfc", 1)

    got = after(got, near_back, 1 << 20)
    mom2 = lax.ppermute(
        got[:, 2 * width + LANES :], "sfc", [(i, i ^ 1) for i in range(devices)]
    )

    return pl.pallas_call(
        post_kernel,
        out_shape=jax.ShapeDtypeStruct((leaves, rhs, panels), F32),
        in_specs=[smem] + [vmem] * 11,
        out_specs=vmem,
        scratch_shapes=[
            pltpu.VMEM((width, slots), F32),
            pltpu.VMEM((width, slots), F32),
            pltpu.VMEM((pairs * rhs, rank), F32),
            pltpu.VMEM((pairs * rhs, rank), F32),
            pltpu.VMEM((leaves * rhs, rank), F32),
            pltpu.VMEM((leaves * rhs, rank), F32),
            pltpu.VMEM((leaves * rhs, rank), F32),
        ],
        compiler_params=late,
        name="downward",
    )(
        far_pairs,
        mom2,
        got,
        bases,
        transfers,
        parent_of,
        far_pairs,
        far_c,
        par_pairs,
        par_coupling,
        near_own,
        near_back,
    )


def solution(mesh):
    split = ("grp", "sfc")
    cube, flat = P(split, None, None), P(split, None)
    placed = (cube, cube, cube, flat, cube, cube, P(split), flat, cube, flat, cube)
    return jax.shard_map(
        on_device, mesh=mesh, in_specs=placed, out_specs=cube, check_vma=False
    )
```

```python
import functools

import jax
import jax.numpy as jnp
from jax import lax
from jax.experimental import pallas as pl
from jax.experimental.pallas import tpu as pltpu
from jax.sharding import PartitionSpec as P

F32 = jnp.float32
BF16 = jnp.bfloat16
LANES = 128


def dot_nn(a, b):
    return lax.dot_general(a, b, (((1,), (0,)), ((), ())), preferred_element_type=F32)


def dot_nt(a, b):
    return lax.dot_general(a, b, (((1,), (1,)), ((), ())), preferred_element_type=F32)


def dot_tn(a, b):
    return lax.dot_general(a, b, (((0,), (0,)), ((), ())), preferred_element_type=F32)


def split2(x):
    high = x.astype(BF16)
    return high, (x - high.astype(F32)).astype(BF16)


def iota(shape, axis):
    return lax.broadcasted_iota(jnp.int32, shape, axis)


def one_hot(condition):
    return jnp.where(condition, 1.0, 0.0).astype(BF16)


def rows_to_lanes(ref, count, rhs):
    return jnp.concatenate([ref[pl.ds(r, count, stride=rhs), :] for r in range(rhs)], axis=1)


def lanes_to_rows(ref, value, rhs):
    count, width = value.shape
    rank = width // rhs
    for r in range(rhs):
        ref[pl.ds(r, count, stride=rhs), :] = value[:, r * rank : (r + 1) * rank]


def row_sums(parts):
    row = iota(parts[0].shape, 0)
    for step in (4, 2, 1):
        upper = row % (2 * step) >= step
        merged = []
        for a, b in zip(parts[:step], parts[step:]):
            swapped = jnp.where(upper, a, b)
            if step == 4:
                moved = pltpu.roll(swapped, 4, axis=0)
            else:
                moved = jnp.where(
                    upper,
                    pltpu.roll(swapped, step, axis=0),
                    pltpu.roll(swapped, 8 - step, axis=0),
                )
            merged.append(jnp.where(upper, b, a) + moved)
        parts = merged
    return parts[0]


def fetch(pairs, sems):
    copies = [pltpu.make_async_copy(src, dst, sems.at[i]) for i, (src, dst) in enumerate(pairs)]
    for copy in copies:
        copy.start()
    return copies


def pre_kernel(
    charges_h,
    bases_h,
    transfers_h,
    parent_of_h,
    far_pairs_h,
    far_c_h,
    par_pairs_h,
    par_c_h,
    send,
    charges,
    bases,
    transfers,
    parent_of,
    far_pairs,
    far_c,
    par_pairs,
    par_c,
    par_smem,
    sems,
    mo,
    ch,
    pm3,
    pb,
    a_ref,
    ob,
):
    leaves, rhs, _ = charges.shape
    rank = bases.shape[1]
    width = rhs * rank
    slots = far_c.shape[2]
    pairs = par_c.shape[0]
    parents = leaves // 2
    rows = send.shape[0]
    copies = fetch(
        [
            (charges_h, charges),
            (bases_h, bases),
            (transfers_h, transfers),
            (parent_of_h, parent_of),
            (far_pairs_h, far_pairs),
            (par_pairs_h, par_pairs),
            (par_pairs_h, par_smem),
            (far_c_h, far_c),
            (par_c_h, par_c),
        ],
        sems,
    )
    for copy in copies[:3]:
        copy.wait()

    for l in range(leaves):
        m = dot_nt(charges[l], bases[l]).astype(BF16)
        mo[l * rhs : (l + 1) * rhs, :] = m.astype(F32)
        ch[l * rhs : (l + 1) * rhs, :] = dot_nt(m, transfers[l])
    for copy in copies[3:]:
        copy.wait()
    m2 = rows_to_lanes(mo, leaves, rhs)
    high, low = split2(rows_to_lanes(ch, leaves, rhs))
    par_hot = one_hot(parent_of[...] % parents == iota((parents, leaves), 0))
    pm = (dot_nn(par_hot, high) + dot_nn(par_hot, low)).astype(BF16).astype(F32)
    lanes_to_rows(pm3, pm, rhs)
    shared = jnp.concatenate([m2[:parents], m2[parents:], pm], axis=1)
    half = 3 * width // 2
    shared = jnp.concatenate([shared[:, :half], shared[:, half:]], axis=0).astype(BF16)
    at = 2 * width + LANES
    for p in range(rows // (2 * parents)):
        send[p * 2 * parents : (p + 1) * 2 * parents, at : at + half] = shared

    owner_hot = one_hot(far_pairs[0:1, :] % leaves == iota((leaves, slots), 0))
    a_ref[...] = dot_tn(m2.astype(BF16), owner_hot)
    for s in range(pairs):
        q = par_smem[0, s] % parents
        x = pm3[pl.ds(pl.multiple_of(q * rhs, rhs), rhs), :].astype(BF16)
        pb[s * rhs : (s + 1) * rhs, :] = dot_nn(x, par_c[s])
    half = rank // 2
    for sb in range(slots // LANES):
        lanes = slice(sb * LANES, (sb + 1) * LANES)
        for jh in range(2):

            def body(k8, acc):
                rows_a = [
                    a_ref[pl.ds(pl.multiple_of(r * rank + k8 * 8, 8), 8), lanes]
                    for r in range(rhs)
                ]
                for i in range(8):
                    c = far_c[k8 * 8 + i, jh * half : (jh + 1) * half, lanes].astype(F32)
                    acc = tuple(acc[r] + c * rows_a[r][i : i + 1, :] for r in range(rhs))
                return acc

            acc = tuple(jnp.zeros((half, LANES), F32) for _ in range(rhs))
            acc = lax.fori_loop(0, rank // 8, body, acc, unroll=8)
            for r in range(rhs):
                first = r * rank + jh * half
                ob[first : first + half, lanes] = acc[r].astype(BF16)
    partner = far_pairs[1:2, :]
    local = jnp.where(partner >= 0, partner % leaves, -1).astype(F32)
    ob[width : width + LANES, :] = jnp.broadcast_to(local, (LANES, slots)).astype(BF16)
    unit = one_hot(iota((LANES, LANES), 0) == iota((LANES, LANES), 1))
    for sb in range(slots // LANES):
        lanes = slice(sb * LANES, (sb + 1) * LANES)
        send[lanes, 0 : width + LANES] = dot_nt(unit, ob[:, lanes]).astype(BF16)

    high, low = split2(rows_to_lanes(pb, pairs, rhs))
    hot = one_hot(par_pairs[1:2, :] == iota((rows, pairs), 0))
    at = width + LANES
    send[:, at : at + width] = (dot_nn(hot, high) + dot_nn(hot, low)).astype(BF16)


def near_kernel(pairs, charges, following, self_blocks, near_blocks, own, away, ext, out):
    leaves = charges.shape[0]
    step = pl.program_id(0)
    selves, nears = self_blocks.shape[0], near_blocks.shape[0]

    @pl.when(step == 0)
    def _():
        ext[0:leaves] = charges[...]
        ext[leaves:] = following[...]
        out[...] = jnp.zeros_like(out)

    terms = [(step * selves + i, dot_nt(ext[step * selves + i], self_blocks[i])) for i in range(selves)]
    for i in range(nears):
        a, b = pairs[0, step * nears + i], pairs[1, step * nears + i]
        first = (a // leaves) * leaves
        a, b = a - first, b - first
        terms.append((a, dot_nt(ext[b], near_blocks[i])))
        terms.append((b, dot_nn(ext[a], near_blocks[i])))
    for at, term in terms:
        out[at] += term

    @pl.when(step == pl.num_programs(0) - 1)
    def _():
        own[...] = out[0:leaves]
        away[...] = out[leaves:].astype(BF16)


def post_kernel(
    core_smem,
    mom2,
    got,
    bases,
    transfers,
    parent_of,
    far_pairs,
    far_c,
    par_pairs,
    par_c,
    near_own,
    near_back,
    out,
    b_ref,
    fw,
    g_ref,
    pf,
    lf,
    pg,
    dn,
):
    leaves, rank, _ = bases.shape
    slots = far_c.shape[2]
    pairs = par_c.shape[0]
    parents = leaves // 2
    rows = got.shape[0]
    rhs = b_ref.shape[0] // rank
    width = rhs * rank
    at_par = width + LANES
    at_mom = at_par + width
    core = core_smem[0, 0] // leaves % 2
    mom = got[:, at_mom:]
    shared = jnp.concatenate(
        [jnp.where(core == 0, mom, mom2[...]), jnp.where(core == 0, mom2[...], mom)], axis=1
    )
    row_id = iota((rows, slots), 0)
    base_leaf = row_id // parents * leaves + row_id % parents
    partner = far_pairs[1:2, :]
    total = None
    for h in range(2):
        hot = one_hot(partner == base_leaf + h * parents)
        part = dot_tn(shared[:, h * width : (h + 1) * width], hot)
        total = part if total is None else total + part
    b_ref[...] = total

    hot = one_hot(par_pairs[1:2, :] == iota((rows, pairs), 0))
    lanes_to_rows(g_ref, dot_tn(hot, shared[:, 2 * width :]), rhs)

    def couple(k8, sb):
        lanes = slice(sb * LANES, (sb + 1) * LANES)
        parts = [[] for _ in range(rhs)]
        for i in range(8):
            c = far_c[k8 * 8 + i, :, lanes].astype(F32)
            for r in range(rhs):
                prod = c * b_ref[r * rank : (r + 1) * rank, lanes]
                parts[r].append(sum(prod[j * 8 : (j + 1) * 8] for j in range(rank // 8)))
        for r in range(rhs):
            fw[pl.ds(pl.multiple_of(r * rank + k8 * 8, 8), 8), lanes] = row_sums(parts[r])

    for s in range(pairs):
        at = slice(s * rhs, (s + 1) * rhs)
        pf[at, :] = dot_nt(g_ref[at, :].astype(BF16), par_c[s])
    high, low = split2(rows_to_lanes(pf, pairs, rhs))
    hot = one_hot(par_pairs[0:1, :] % parents == iota((parents, pairs), 0))
    fold = one_hot(iota((parents, rows), 1) % parents == iota((parents, rows), 0))
    locals_p = dot_nn(hot, high) + dot_nn(hot, low) + dot_nn(fold, got[:, at_par : at_par + width])
    hot = one_hot(parent_of[...] % parents == iota((parents, leaves), 0))
    lanes_to_rows(pg, dot_tn(hot, locals_p.astype(BF16)), rhs)

    for l in range(leaves):
        at = slice(l * rhs, (l + 1) * rhs)
        dn[at, :] = dot_nn(pg[at, :].astype(BF16), transfers[l])

    for sb in range(slots // LANES):

        def body(k8, carry):
            couple(k8, sb)
            return carry

        lax.fori_loop(0, rank // 8, body, 0, unroll=8)

    hot = one_hot(far_pairs[0:1, :] % leaves == iota((leaves, slots), 0))
    high, low = split2(fw[...])
    leaf = dot_nt(hot, high) + dot_nt(hot, low)
    index = got[:, width : width + LANES].astype(F32)[:, :leaves].astype(jnp.int32)
    hot = one_hot(index == iota((rows, leaves), 1))
    leaf = leaf + dot_tn(hot, got[:, 0:width])
    lanes_to_rows(lf, leaf, rhs)

    for l in range(leaves):
        at = slice(l * rhs, (l + 1) * rhs)
        mine = (lf[at, :] + dn[at, :]).astype(BF16)
        near = near_own[l] + near_back[l].astype(F32)
        out[l] = dot_nn(mine, bases[l]) + near


def after(value, earlier, vmem_limit):
    anywhere = pl.BlockSpec(memory_space=pl.ANY)
    return pl.pallas_call(
        lambda value, earlier, same: None,
        out_shape=jax.ShapeDtypeStruct(value.shape, value.dtype),
        in_specs=[anywhere] * 2,
        out_specs=anywhere,
        input_output_aliases={0: 0},
        compiler_params=pltpu.CompilerParams(vmem_limit_bytes=vmem_limit),
        name="after",
    )(value, earlier)


def passed_along(value, axis, steps):
    count = lax.axis_size(axis)
    leading, last = (max(0, -steps), min(count, count - steps))
    return lax.ppermute(value, axis, [(source, source + steps) for source in range(leading, last)])


def on_device(
    charges,
    self_blocks,
    near_blocks,
    near_pairs,
    bases,
    transfers,
    parent_of,
    far_pairs,
    far_coupling,
    par_pairs,
    par_coupling,
):
    leaves, rhs, panels = charges.shape
    rank = bases.shape[1]
    width = rhs * rank
    slots = far_coupling.shape[0]
    pairs = par_coupling.shape[0]
    parents = leaves // 2
    devices = lax.axis_size("sfc")
    rows = devices * parents
    columns = 2 * width + LANES + 3 * width // 2
    vmem = pl.BlockSpec(memory_space=pltpu.VMEM)
    smem = pl.BlockSpec(memory_space=pltpu.SMEM)
    hbm = pl.BlockSpec(memory_space=pltpu.HBM)
    params = pltpu.CompilerParams(vmem_limit_bytes=60 * 1024 * 1024)
    late = pltpu.CompilerParams(vmem_limit_bytes=48 * 1024 * 1024)

    def cost(moved):
        return pl.CostEstimate(flops=4 * moved, bytes_accessed=moved, transcendentals=0)

    following = passed_along(charges, "sfc", -1)
    far_pairs = far_pairs.T
    par_pairs = par_pairs.T
    near_pairs = near_pairs.T
    far_c = jnp.transpose(far_coupling, (1, 2, 0))
    parent_of = parent_of.reshape(1, leaves)

    def like(value, memory=pltpu.VMEM):
        return memory(value.shape, value.dtype)

    send = pl.pallas_call(
        pre_kernel,
        out_shape=jax.ShapeDtypeStruct((rows, columns), BF16),
        in_specs=[hbm] * 8,
        out_specs=vmem,
        scratch_shapes=[
            like(charges),
            like(bases),
            like(transfers),
            like(parent_of),
            like(far_pairs),
            like(far_c),
            like(par_pairs),
            like(par_coupling),
            like(par_pairs, pltpu.SMEM),
            pltpu.SemaphoreType.DMA((9,)),
            pltpu.VMEM((leaves * rhs, rank), F32),
            pltpu.VMEM((leaves * rhs, rank), F32),
            pltpu.VMEM((parents * rhs, rank), F32),
            pltpu.VMEM((pairs * rhs, rank), F32),
            pltpu.VMEM((width, slots), F32),
            pltpu.VMEM((width + LANES, slots), BF16),
        ],
        compiler_params=params,
        cost_estimate=cost(10_000_000),
        name="upward",
    )(charges, bases, transfers, parent_of, far_pairs, far_c, par_pairs, par_coupling)
    send = after(send, following, 107 << 19)
    got = lax.all_to_all(send, "sfc", split_axis=0, concat_axis=0, tiled=True)
    steps = 4
    selves, nears = leaves // steps, near_blocks.shape[0] // steps
    whole = lambda *shape: pl.BlockSpec(shape, lambda i: (0,) * len(shape))
    near_own, near_away = pl.pallas_call(
        near_kernel,
        grid=(steps,),
        out_shape=[
            jax.ShapeDtypeStruct((leaves, rhs, panels), F32),
            jax.ShapeDtypeStruct((leaves, rhs, panels), BF16),
        ],
        in_specs=[
            smem,
            whole(leaves, rhs, panels),
            whole(leaves, rhs, panels),
            pl.BlockSpec((selves, panels, panels), lambda i: (i, 0, 0)),
            pl.BlockSpec((nears, panels, panels), lambda i: (i, 0, 0)),
        ],
        out_specs=[whole(leaves, rhs, panels)] * 2,
        scratch_shapes=[
            pltpu.VMEM((2 * leaves, rhs, panels), BF16),
            pltpu.VMEM((2 * leaves, rhs, panels), F32),
        ],
        compiler_params=pltpu.CompilerParams(vmem_limit_bytes=52 * 1024 * 1024),
        cost_estimate=cost(20_000_000),
        name="near",
    )(near_pairs, charges, following, self_blocks, near_blocks)
    near_back = passed_along(near_away, "sfc", 1)

    got = after(got, near_back, 1 << 20)
    mom2 = lax.ppermute(
        got[:, 2 * width + LANES :], "sfc", [(i, i ^ 1) for i in range(devices)]
    )

    return pl.pallas_call(
        post_kernel,
        out_shape=jax.ShapeDtypeStruct((leaves, rhs, panels), F32),
        in_specs=[smem] + [vmem] * 11,
        out_specs=vmem,
        scratch_shapes=[
            pltpu.VMEM((width, slots), F32),
            pltpu.VMEM((width, slots), F32),
            pltpu.VMEM((pairs * rhs, rank), F32),
            pltpu.VMEM((pairs * rhs, rank), F32),
            pltpu.VMEM((leaves * rhs, rank), F32),
            pltpu.VMEM((leaves * rhs, rank), F32),
            pltpu.VMEM((leaves * rhs, rank), F32),
        ],
        compiler_params=late,
        name="downward",
    )(
        far_pairs,
        mom2,
        got,
        bases,
        transfers,
        parent_of,
        far_pairs,
        far_c,
        par_pairs,
        par_coupling,
        near_own,
        near_back,
    )


def solution(mesh):
    split = ("grp", "sfc")
    cube, flat = P(split, None, None), P(split, None)
    placed = (cube, cube, cube, flat, cube, cube, P(split), flat, cube, flat, cube)
    return jax.shard_map(
        on_device, mesh=mesh, in_specs=placed, out_specs=cube, check_vma=False
    )
```

```python
import functools

import jax
import jax.numpy as jnp
from jax import lax
from jax.experimental import pallas as pl
from jax.experimental.pallas import tpu as pltpu
from jax.sharding import PartitionSpec as P

F32 = jnp.float32
BF16 = jnp.bfloat16
LANES = 128


def dot_nn(a, b):
    return lax.dot_general(a, b, (((1,), (0,)), ((), ())), preferred_element_type=F32)


def dot_nt(a, b):
    return lax.dot_general(a, b, (((1,), (1,)), ((), ())), preferred_element_type=F32)


def dot_tn(a, b):
    return lax.dot_general(a, b, (((0,), (0,)), ((), ())), preferred_element_type=F32)


def split2(x):
    high = x.astype(BF16)
    return high, (x - high.astype(F32)).astype(BF16)


def iota(shape, axis):
    return lax.broadcasted_iota(jnp.int32, shape, axis)


def one_hot(condition):
    return jnp.where(condition, 1.0, 0.0).astype(BF16)


def rows_to_lanes(ref, count, rhs):
    return jnp.concatenate([ref[pl.ds(r, count, stride=rhs), :] for r in range(rhs)], axis=1)


def lanes_to_rows(ref, value, rhs):
    count, width = value.shape
    rank = width // rhs
    for r in range(rhs):
        ref[pl.ds(r, count, stride=rhs), :] = value[:, r * rank : (r + 1) * rank]


def row_sums(parts):
    row = iota(parts[0].shape, 0)
    for step in (4, 2, 1):
        upper = row % (2 * step) >= step
        merged = []
        for a, b in zip(parts[:step], parts[step:]):
            swapped = jnp.where(upper, a, b)
            if step == 4:
                moved = pltpu.roll(swapped, 4, axis=0)
            else:
                moved = jnp.where(
                    upper,
                    pltpu.roll(swapped, step, axis=0),
                    pltpu.roll(swapped, 8 - step, axis=0),
                )
            merged.append(jnp.where(upper, b, a) + moved)
        parts = merged
    return parts[0]


def fetch(pairs, sems):
    copies = [pltpu.make_async_copy(src, dst, sems.at[i]) for i, (src, dst) in enumerate(pairs)]
    for copy in copies:
        copy.start()
    return copies


def pre_kernel(
    charges_h,
    bases_h,
    transfers_h,
    parent_of_h,
    far_pairs_h,
    far_c_h,
    par_pairs_h,
    par_c_h,
    send,
    charges,
    bases,
    transfers,
    parent_of,
    far_pairs,
    far_c,
    par_pairs,
    par_c,
    par_smem,
    sems,
    mo,
    ch,
    pm3,
    pb,
    a_ref,
):
    leaves, rhs, _ = charges.shape
    rank = bases.shape[1]
    width = rhs * rank
    slots = far_c.shape[2]
    pairs = par_c.shape[0]
    parents = leaves // 2
    rows = send.shape[0]
    copies = fetch(
        [
            (charges_h, charges),
            (bases_h, bases),
            (transfers_h, transfers),
            (parent_of_h, parent_of),
            (far_pairs_h, far_pairs),
            (par_pairs_h, par_pairs),
            (par_pairs_h, par_smem),
            (far_c_h, far_c),
            (par_c_h, par_c),
        ],
        sems,
    )
    def own_blocks(big):
        lane_leaf = iota((rank, leaves * rhs), 1) // rhs
        kept = big[0:rank]
        for l in range(1, leaves):
            kept = jnp.where(lane_leaf == l, big[l * rank : (l + 1) * rank], kept)
        return kept

    for copy in copies[:2]:
        copy.wait()
    panels = charges.shape[2]
    flat = charges[...].astype(F32).reshape(leaves * rhs, panels).astype(BF16)
    mt = own_blocks(dot_nt(bases[...].reshape(leaves * rank, panels), flat)).astype(BF16)
    mo[...] = mt.astype(F32).T
    copies[2].wait()
    ch[...] = own_blocks(dot_nn(transfers[...].reshape(leaves * rank, rank), mt)).T
    for copy in copies[3:]:
        copy.wait()
    m2 = rows_to_lanes(mo, leaves, rhs)
    high, low = split2(rows_to_lanes(ch, leaves, rhs))
    par_hot = one_hot(parent_of[...] % parents == iota((parents, leaves), 0))
    pm = (dot_nn(par_hot, high) + dot_nn(par_hot, low)).astype(BF16).astype(F32)
    lanes_to_rows(pm3, pm, rhs)
    shared = jnp.concatenate([m2[:parents], m2[parents:], pm], axis=1)
    half = 3 * width // 2
    shared = jnp.concatenate([shared[:, :half], shared[:, half:]], axis=0).astype(BF16)
    at = 2 * width + LANES
    for p in range(rows // (2 * parents)):
        send[p * 2 * parents : (p + 1) * 2 * parents, at : at + half] = shared

    owner_hot = one_hot(far_pairs[0:1, :] % leaves == iota((leaves, slots), 0))
    a_ref[...] = dot_tn(m2.astype(BF16), owner_hot)
    for s in range(pairs):
        q = par_smem[0, s] % parents
        x = pm3[pl.ds(pl.multiple_of(q * rhs, rhs), rhs), :].astype(BF16)
        pb[s * rhs : (s + 1) * rhs, :] = dot_nn(x, par_c[s])
    partner = far_pairs[1:2, :]
    local = jnp.where(partner >= 0, partner % leaves, -1).astype(F32)
    unit = one_hot(iota((LANES, LANES), 0) == iota((LANES, LANES), 1))
    some = rhs // 2
    for sb in range(slots // LANES):
        lanes = slice(sb * LANES, (sb + 1) * LANES)
        for rh in range(2):

            def body(k8, acc):
                rows_a = [
                    a_ref[pl.ds(pl.multiple_of((rh * some + r) * rank + k8 * 8, 8), 8), lanes]
                    for r in range(some)
                ]
                for i in range(8):
                    c = far_c[k8 * 8 + i, :, lanes].astype(F32)
                    acc = tuple(acc[r] + c * rows_a[r][i : i + 1, :] for r in range(some))
                return acc

            acc = tuple(jnp.zeros((rank, LANES), F32) for _ in range(some))
            acc = lax.fori_loop(0, rank // 8, body, acc, unroll=8)
            part = jnp.concatenate(acc, axis=0).astype(BF16)
            at = rh * some * rank
            send[lanes, at : at + some * rank] = dot_nt(unit, part).astype(BF16)
        index = jnp.broadcast_to(local[:, lanes], (LANES, LANES)).astype(BF16)
        send[lanes, width : width + LANES] = dot_nt(unit, index).astype(BF16)

    high, low = split2(rows_to_lanes(pb, pairs, rhs))
    hot = one_hot(par_pairs[1:2, :] == iota((rows, pairs), 0))
    at = width + LANES
    send[:, at : at + width] = (dot_nn(hot, high) + dot_nn(hot, low)).astype(BF16)


def near_kernel(pairs, charges, following, self_blocks, near_blocks, own, away, ext, out):
    leaves = charges.shape[0]
    step = pl.program_id(0)
    selves, nears = self_blocks.shape[0], near_blocks.shape[0]

    @pl.when(step == 0)
    def _():
        ext[0:leaves] = charges[...]
        ext[leaves:] = following[...]
        out[...] = jnp.zeros_like(out)

    terms = [(step * selves + i, dot_nt(ext[step * selves + i], self_blocks[i])) for i in range(selves)]
    for i in range(nears):
        a, b = pairs[0, step * nears + i], pairs[1, step * nears + i]
        first = (a // leaves) * leaves
        a, b = a - first, b - first
        terms.append((a, dot_nt(ext[b], near_blocks[i])))
        terms.append((b, dot_nn(ext[a], near_blocks[i])))
    for at, term in terms:
        out[at] += term

    @pl.when(step == pl.num_programs(0) - 1)
    def _():
        own[...] = out[0:leaves]
        away[...] = out[leaves:].astype(BF16)


def post_kernel(
    core_smem,
    mom2,
    got,
    bases,
    transfers,
    parent_of,
    far_pairs,
    far_c,
    par_pairs,
    par_c,
    near_own,
    near_back,
    out,
    b_ref,
    fw,
    g_ref,
    pf,
    lf,
    pg,
    dn,
):
    leaves, rank, _ = bases.shape
    slots = far_c.shape[2]
    pairs = par_c.shape[0]
    parents = leaves // 2
    rows = got.shape[0]
    rhs = b_ref.shape[0] // rank
    width = rhs * rank
    at_par = width + LANES
    at_mom = at_par + width
    core = core_smem[0, 0] // leaves % 2
    mom = got[:, at_mom:]
    shared = jnp.concatenate(
        [jnp.where(core == 0, mom, mom2[...]), jnp.where(core == 0, mom2[...], mom)], axis=1
    )
    row_id = iota((rows, slots), 0)
    base_leaf = row_id // parents * leaves + row_id % parents
    partner = far_pairs[1:2, :]
    total = None
    for h in range(2):
        hot = one_hot(partner == base_leaf + h * parents)
        part = dot_tn(shared[:, h * width : (h + 1) * width], hot)
        total = part if total is None else total + part
    b_ref[...] = total

    hot = one_hot(par_pairs[1:2, :] == iota((rows, pairs), 0))
    lanes_to_rows(g_ref, dot_tn(hot, shared[:, 2 * width :]), rhs)

    def couple(k8, sb):
        lanes = slice(sb * LANES, (sb + 1) * LANES)
        parts = [[] for _ in range(rhs)]
        for i in range(8):
            c = far_c[k8 * 8 + i, :, lanes].astype(F32)
            for r in range(rhs):
                prod = c * b_ref[r * rank : (r + 1) * rank, lanes]
                parts[r].append(sum(prod[j * 8 : (j + 1) * 8] for j in range(rank // 8)))
        for r in range(rhs):
            fw[pl.ds(pl.multiple_of(r * rank + k8 * 8, 8), 8), lanes] = row_sums(parts[r])

    for s in range(pairs):
        at = slice(s * rhs, (s + 1) * rhs)
        pf[at, :] = dot_nt(g_ref[at, :].astype(BF16), par_c[s])
    high, low = split2(rows_to_lanes(pf, pairs, rhs))
    hot = one_hot(par_pairs[0:1, :] % parents == iota((parents, pairs), 0))
    fold = one_hot(iota((parents, rows), 1) % parents == iota((parents, rows), 0))
    locals_p = dot_nn(hot, high) + dot_nn(hot, low) + dot_nn(fold, got[:, at_par : at_par + width])
    hot = one_hot(parent_of[...] % parents == iota((parents, leaves), 0))
    lanes_to_rows(pg, dot_tn(hot, locals_p.astype(BF16)), rhs)

    for l in range(leaves):
        at = slice(l * rhs, (l + 1) * rhs)
        dn[at, :] = dot_nn(pg[at, :].astype(BF16), transfers[l])

    for sb in range(slots // LANES):

        def body(k8, carry):
            couple(k8, sb)
            return carry

        lax.fori_loop(0, rank // 8, body, 0, unroll=8)

    hot = one_hot(far_pairs[0:1, :] % leaves == iota((leaves, slots), 0))
    high, low = split2(fw[...])
    leaf = dot_nt(hot, high) + dot_nt(hot, low)
    index = got[:, width : width + LANES].astype(F32)[:, :leaves].astype(jnp.int32)
    hot = one_hot(index == iota((rows, leaves), 1))
    leaf = leaf + dot_tn(hot, got[:, 0:width])
    lanes_to_rows(lf, leaf, rhs)

    for l in range(leaves):
        at = slice(l * rhs, (l + 1) * rhs)
        mine = (lf[at, :] + dn[at, :]).astype(BF16)
        near = near_own[l] + near_back[l].astype(F32)
        out[l] = dot_nn(mine, bases[l]) + near


def after(value, earlier, vmem_limit):
    anywhere = pl.BlockSpec(memory_space=pl.ANY)
    return pl.pallas_call(
        lambda value, earlier, same: None,
        out_shape=jax.ShapeDtypeStruct(value.shape, value.dtype),
        in_specs=[anywhere] * 2,
        out_specs=anywhere,
        input_output_aliases={0: 0},
        compiler_params=pltpu.CompilerParams(vmem_limit_bytes=vmem_limit),
        name="after",
    )(value, earlier)


def passed_along(value, axis, steps):
    count = lax.axis_size(axis)
    leading, last = (max(0, -steps), min(count, count - steps))
    return lax.ppermute(value, axis, [(source, source + steps) for source in range(leading, last)])


def on_device(
    charges,
    self_blocks,
    near_blocks,
    near_pairs,
    bases,
    transfers,
    parent_of,
    far_pairs,
    far_coupling,
    par_pairs,
    par_coupling,
):
    leaves, rhs, panels = charges.shape
    rank = bases.shape[1]
    width = rhs * rank
    slots = far_coupling.shape[0]
    pairs = par_coupling.shape[0]
    parents = leaves // 2
    devices = lax.axis_size("sfc")
    rows = devices * parents
    columns = 2 * width + LANES + 3 * width // 2
    vmem = pl.BlockSpec(memory_space=pltpu.VMEM)
    smem = pl.BlockSpec(memory_space=pltpu.SMEM)
    hbm = pl.BlockSpec(memory_space=pltpu.HBM)
    params = pltpu.CompilerParams(vmem_limit_bytes=60 * 1024 * 1024)
    late = pltpu.CompilerParams(vmem_limit_bytes=48 * 1024 * 1024)

    def cost(moved):
        return pl.CostEstimate(flops=4 * moved, bytes_accessed=moved, transcendentals=0)

    following = passed_along(charges, "sfc", -1)
    far_pairs = far_pairs.T
    par_pairs = par_pairs.T
    near_pairs = near_pairs.T
    far_c = jnp.transpose(far_coupling, (1, 2, 0))
    parent_of = parent_of.reshape(1, leaves)

    def like(value, memory=pltpu.VMEM):
        return memory(value.shape, value.dtype)

    send = pl.pallas_call(
        pre_kernel,
        out_shape=jax.ShapeDtypeStruct((rows, columns), BF16),
        in_specs=[hbm] * 8,
        out_specs=vmem,
        scratch_shapes=[
            like(charges),
            like(bases),
            like(transfers),
            like(parent_of),
            like(far_pairs),
            like(far_c),
            like(par_pairs),
            like(par_coupling),
            like(par_pairs, pltpu.SMEM),
            pltpu.SemaphoreType.DMA((9,)),
            pltpu.VMEM((leaves * rhs, rank), F32),
            pltpu.VMEM((leaves * rhs, rank), F32),
            pltpu.VMEM((parents * rhs, rank), F32),
            pltpu.VMEM((pairs * rhs, rank), F32),
            pltpu.VMEM((width, slots), F32),
        ],
        compiler_params=params,
        cost_estimate=cost(10_000_000),
        name="upward",
    )(charges, bases, transfers, parent_of, far_pairs, far_c, par_pairs, par_coupling)
    send = after(send, following, 107 << 19)
    got = lax.all_to_all(send, "sfc", split_axis=0, concat_axis=0, tiled=True)
    steps = 4
    selves, nears = leaves // steps, near_blocks.shape[0] // steps
    whole = lambda *shape: pl.BlockSpec(shape, lambda i: (0,) * len(shape))
    near_own, near_away = pl.pallas_call(
        near_kernel,
        grid=(steps,),
        out_shape=[
            jax.ShapeDtypeStruct((leaves, rhs, panels), F32),
            jax.ShapeDtypeStruct((leaves, rhs, panels), BF16),
        ],
        in_specs=[
            smem,
            whole(leaves, rhs, panels),
            whole(leaves, rhs, panels),
            pl.BlockSpec((selves, panels, panels), lambda i: (i, 0, 0)),
            pl.BlockSpec((nears, panels, panels), lambda i: (i, 0, 0)),
        ],
        out_specs=[whole(leaves, rhs, panels)] * 2,
        scratch_shapes=[
            pltpu.VMEM((2 * leaves, rhs, panels), BF16),
            pltpu.VMEM((2 * leaves, rhs, panels), F32),
        ],
        compiler_params=pltpu.CompilerParams(vmem_limit_bytes=52 * 1024 * 1024),
        cost_estimate=cost(20_000_000),
        name="near",
    )(near_pairs, charges, following, self_blocks, near_blocks)
    near_back = passed_along(near_away, "sfc", 1)

    got = after(got, near_back, 1 << 20)
    mom2 = lax.ppermute(
        got[:, 2 * width + LANES :], "sfc", [(i, i ^ 1) for i in range(devices)]
    )

    return pl.pallas_call(
        post_kernel,
        out_shape=jax.ShapeDtypeStruct((leaves, rhs, panels), F32),
        in_specs=[smem] + [vmem] * 11,
        out_specs=vmem,
        scratch_shapes=[
            pltpu.VMEM((width, slots), F32),
            pltpu.VMEM((width, slots), F32),
            pltpu.VMEM((pairs * rhs, rank), F32),
            pltpu.VMEM((pairs * rhs, rank), F32),
            pltpu.VMEM((leaves * rhs, rank), F32),
            pltpu.VMEM((leaves * rhs, rank), F32),
            pltpu.VMEM((leaves * rhs, rank), F32),
        ],
        compiler_params=late,
        name="downward",
    )(
        far_pairs,
        mom2,
        got,
        bases,
        transfers,
        parent_of,
        far_pairs,
        far_c,
        par_pairs,
        par_coupling,
        near_own,
        near_back,
    )


def solution(mesh):
    split = ("grp", "sfc")
    cube, flat = P(split, None, None), P(split, None)
    placed = (cube, cube, cube, flat, cube, cube, P(split), flat, cube, flat, cube)
    return jax.shard_map(
        on_device, mesh=mesh, in_specs=placed, out_specs=cube, check_vma=False
    )
```

```python
import functools

import jax
import jax.numpy as jnp
from jax import lax
from jax.experimental import pallas as pl
from jax.experimental.pallas import tpu as pltpu
from jax.sharding import PartitionSpec as P

F32 = jnp.float32
BF16 = jnp.bfloat16
LANES = 128


def dot_nn(a, b):
    return lax.dot_general(a, b, (((1,), (0,)), ((), ())), preferred_element_type=F32)


def dot_nt(a, b):
    return lax.dot_general(a, b, (((1,), (1,)), ((), ())), preferred_element_type=F32)


def dot_tn(a, b):
    return lax.dot_general(a, b, (((0,), (0,)), ((), ())), preferred_element_type=F32)


def split2(x):
    high = x.astype(BF16)
    return high, (x - high.astype(F32)).astype(BF16)


def iota(shape, axis):
    return lax.broadcasted_iota(jnp.int32, shape, axis)


def one_hot(condition):
    return jnp.where(condition, 1.0, 0.0).astype(BF16)


def rows_to_lanes(ref, count, rhs):
    return jnp.concatenate([ref[pl.ds(r, count, stride=rhs), :] for r in range(rhs)], axis=1)


def lanes_to_rows(ref, value, rhs):
    count, width = value.shape
    rank = width // rhs
    for r in range(rhs):
        ref[pl.ds(r, count, stride=rhs), :] = value[:, r * rank : (r + 1) * rank]


def row_sums(parts):
    row = iota(parts[0].shape, 0)
    for step in (4, 2, 1):
        upper = row % (2 * step) >= step
        merged = []
        for a, b in zip(parts[:step], parts[step:]):
            swapped = jnp.where(upper, a, b)
            if step == 4:
                moved = pltpu.roll(swapped, 4, axis=0)
            else:
                moved = jnp.where(
                    upper,
                    pltpu.roll(swapped, step, axis=0),
                    pltpu.roll(swapped, 8 - step, axis=0),
                )
            merged.append(jnp.where(upper, b, a) + moved)
        parts = merged
    return parts[0]


def fetch(pairs, sems):
    copies = [pltpu.make_async_copy(src, dst, sems.at[i]) for i, (src, dst) in enumerate(pairs)]
    for copy in copies:
        copy.start()
    return copies


def pre_kernel(
    charges_h,
    bases_h,
    transfers_h,
    parent_of_h,
    far_pairs_h,
    far_c_h,
    par_pairs_h,
    par_c_h,
    send,
    charges,
    bases,
    transfers,
    parent_of,
    far_pairs,
    far_c,
    par_pairs,
    par_c,
    par_smem,
    sems,
    mo,
    ch,
    pm3,
    pb,
    a_ref,
    e_ref,
):
    leaves, rhs, _ = charges.shape
    rank = bases.shape[1]
    width = rhs * rank
    slots = far_c.shape[2]
    pairs = par_c.shape[0]
    parents = leaves // 2
    rows = send.shape[0]
    copies = fetch(
        [
            (far_pairs_h, far_pairs),
            (charges_h, charges),
            (bases_h, bases),
            (far_c_h, far_c),
            (transfers_h, transfers),
            (parent_of_h, parent_of),
            (par_pairs_h, par_pairs),
            (par_pairs_h, par_smem),
            (par_c_h, par_c),
        ],
        sems,
    )

    def own_blocks(big):
        lane_leaf = iota((rank, leaves * rhs), 1) // rhs
        kept = big[0:rank]
        for l in range(1, leaves):
            kept = jnp.where(lane_leaf == l, big[l * rank : (l + 1) * rank], kept)
        return kept

    copies[0].wait()
    owner_row = far_pairs[0:1, :] % leaves * rhs
    row = iota((leaves * rhs, slots), 0)
    for r in range(rhs):
        e_ref[:, r * slots : (r + 1) * slots] = one_hot(row == owner_row + r)
    partner = far_pairs[1:2, :]
    local = jnp.where(partner >= 0, partner % leaves, -1).astype(F32)
    unit = one_hot(iota((LANES, LANES), 0) == iota((LANES, LANES), 1))
    for sb in range(slots // LANES):
        lanes = slice(sb * LANES, (sb + 1) * LANES)
        index = jnp.broadcast_to(local[:, lanes], (LANES, LANES)).astype(BF16)
        send[lanes, width : width + LANES] = dot_nt(unit, index).astype(BF16)

    for copy in copies[1:3]:
        copy.wait()
    panels = charges.shape[2]
    flat = charges[...].astype(F32).reshape(leaves * rhs, panels).astype(BF16)
    mt = own_blocks(dot_nt(bases[...].reshape(leaves * rank, panels), flat)).astype(BF16)
    for r in range(rhs):
        a_ref[r * rank : (r + 1) * rank, :] = dot_nn(mt, e_ref[:, r * slots : (r + 1) * slots])
    for copy in copies[3:]:
        copy.wait()
    mo[...] = mt.astype(F32).T
    ch[...] = own_blocks(dot_nn(transfers[...].reshape(leaves * rank, rank), mt)).T
    m2 = rows_to_lanes(mo, leaves, rhs)
    high, low = split2(rows_to_lanes(ch, leaves, rhs))
    par_hot = one_hot(parent_of[...] % parents == iota((parents, leaves), 0))
    pm = (dot_nn(par_hot, high) + dot_nn(par_hot, low)).astype(BF16).astype(F32)
    lanes_to_rows(pm3, pm, rhs)
    shared = jnp.concatenate([m2[:parents], m2[parents:], pm], axis=1)
    half = 3 * width // 2
    shared = jnp.concatenate([shared[:, :half], shared[:, half:]], axis=0).astype(BF16)
    at = 2 * width + LANES
    for p in range(rows // (2 * parents)):
        send[p * 2 * parents : (p + 1) * 2 * parents, at : at + half] = shared

    for s in range(pairs):
        q = par_smem[0, s] % parents
        x = pm3[pl.ds(pl.multiple_of(q * rhs, rhs), rhs), :].astype(BF16)
        pb[s * rhs : (s + 1) * rhs, :] = dot_nn(x, par_c[s])
    some = rhs // 2
    for sb in range(slots // LANES):
        lanes = slice(sb * LANES, (sb + 1) * LANES)
        for rh in range(2):

            def body(k8, acc):
                rows_a = [
                    a_ref[pl.ds(pl.multiple_of((rh * some + r) * rank + k8 * 8, 8), 8), lanes]
                    for r in range(some)
                ]
                for i in range(8):
                    c = far_c[k8 * 8 + i, :, lanes].astype(F32)
                    acc = tuple(acc[r] + c * rows_a[r][i : i + 1, :] for r in range(some))
                return acc

            acc = tuple(jnp.zeros((rank, LANES), F32) for _ in range(some))
            acc = lax.fori_loop(0, rank // 8, body, acc, unroll=8)
            part = jnp.concatenate(acc, axis=0).astype(BF16)
            at = rh * some * rank
            send[lanes, at : at + some * rank] = dot_nt(unit, part).astype(BF16)

    high, low = split2(rows_to_lanes(pb, pairs, rhs))
    hot = one_hot(par_pairs[1:2, :] == iota((rows, pairs), 0))
    at = width + LANES
    send[:, at : at + width] = (dot_nn(hot, high) + dot_nn(hot, low)).astype(BF16)


def near_kernel(pairs, charges, following, self_blocks, near_blocks, own, away, ext, out):
    leaves = charges.shape[0]
    step = pl.program_id(0)
    selves, nears = self_blocks.shape[0], near_blocks.shape[0]

    @pl.when(step == 0)
    def _():
        ext[0:leaves] = charges[...]
        ext[leaves:] = following[...]
        out[...] = jnp.zeros_like(out)

    terms = [(step * selves + i, dot_nt(ext[step * selves + i], self_blocks[i])) for i in range(selves)]
    for i in range(nears):
        a, b = pairs[0, step * nears + i], pairs[1, step * nears + i]
        first = (a // leaves) * leaves
        a, b = a - first, b - first
        terms.append((a, dot_nt(ext[b], near_blocks[i])))
        terms.append((b, dot_nn(ext[a], near_blocks[i])))
    for at, term in terms:
        out[at] += term

    @pl.when(step == pl.num_programs(0) - 1)
    def _():
        own[...] = out[0:leaves]
        away[...] = out[leaves:].astype(BF16)


def post_kernel(
    core_smem,
    mom2,
    got,
    bases,
    transfers,
    parent_of,
    far_pairs,
    far_c,
    par_pairs,
    par_c,
    near_own,
    near_back,
    out,
    b_ref,
    fw,
    g_ref,
    pf,
    lf,
    pg,
    dn,
):
    leaves, rank, _ = bases.shape
    slots = far_c.shape[2]
    pairs = par_c.shape[0]
    parents = leaves // 2
    rows = got.shape[0]
    rhs = b_ref.shape[0] // rank
    width = rhs * rank
    at_par = width + LANES
    at_mom = at_par + width
    core = core_smem[0, 0] // leaves % 2
    mom = got[:, at_mom:]
    shared = jnp.concatenate(
        [jnp.where(core == 0, mom, mom2[...]), jnp.where(core == 0, mom2[...], mom)], axis=1
    )
    row_id = iota((rows, slots), 0)
    base_leaf = row_id // parents * leaves + row_id % parents
    partner = far_pairs[1:2, :]
    total = None
    for h in range(2):
        hot = one_hot(partner == base_leaf + h * parents)
        part = dot_tn(shared[:, h * width : (h + 1) * width], hot)
        total = part if total is None else total + part
    b_ref[...] = total

    hot = one_hot(par_pairs[1:2, :] == iota((rows, pairs), 0))
    lanes_to_rows(g_ref, dot_tn(hot, shared[:, 2 * width :]), rhs)

    def couple(k8, sb):
        lanes = slice(sb * LANES, (sb + 1) * LANES)
        parts = [[] for _ in range(rhs)]
        for i in range(8):
            c = far_c[k8 * 8 + i, :, lanes].astype(F32)
            for r in range(rhs):
                prod = c * b_ref[r * rank : (r + 1) * rank, lanes]
                parts[r].append(sum(prod[j * 8 : (j + 1) * 8] for j in range(rank // 8)))
        for r in range(rhs):
            fw[pl.ds(pl.multiple_of(r * rank + k8 * 8, 8), 8), lanes] = row_sums(parts[r])

    for s in range(pairs):
        at = slice(s * rhs, (s + 1) * rhs)
        pf[at, :] = dot_nt(g_ref[at, :].astype(BF16), par_c[s])
    high, low = split2(rows_to_lanes(pf, pairs, rhs))
    hot = one_hot(par_pairs[0:1, :] % parents == iota((parents, pairs), 0))
    fold = one_hot(iota((parents, rows), 1) % parents == iota((parents, rows), 0))
    locals_p = dot_nn(hot, high) + dot_nn(hot, low) + dot_nn(fold, got[:, at_par : at_par + width])
    hot = one_hot(parent_of[...] % parents == iota((parents, leaves), 0))
    lanes_to_rows(pg, dot_tn(hot, locals_p.astype(BF16)), rhs)

    for l in range(leaves):
        at = slice(l * rhs, (l + 1) * rhs)
        dn[at, :] = dot_nn(pg[at, :].astype(BF16), transfers[l])

    for sb in range(slots // LANES):

        def body(k8, carry):
            couple(k8, sb)
            return carry

        lax.fori_loop(0, rank // 8, body, 0, unroll=8)

    hot = one_hot(far_pairs[0:1, :] % leaves == iota((leaves, slots), 0))
    high, low = split2(fw[...])
    leaf = dot_nt(hot, high) + dot_nt(hot, low)
    index = got[:, width : width + LANES].astype(F32)[:, :leaves].astype(jnp.int32)
    hot = one_hot(index == iota((rows, leaves), 1))
    leaf = leaf + dot_tn(hot, got[:, 0:width])
    lanes_to_rows(lf, leaf, rhs)

    for l in range(leaves):
        at = slice(l * rhs, (l + 1) * rhs)
        mine = (lf[at, :] + dn[at, :]).astype(BF16)
        near = near_own[l] + near_back[l].astype(F32)
        out[l] = dot_nn(mine, bases[l]) + near


def after(value, earlier, vmem_limit):
    anywhere = pl.BlockSpec(memory_space=pl.ANY)
    return pl.pallas_call(
        lambda value, earlier, same: None,
        out_shape=jax.ShapeDtypeStruct(value.shape, value.dtype),
        in_specs=[anywhere] * 2,
        out_specs=anywhere,
        input_output_aliases={0: 0},
        compiler_params=pltpu.CompilerParams(vmem_limit_bytes=vmem_limit),
        name="after",
    )(value, earlier)


def passed_along(value, axis, steps):
    count = lax.axis_size(axis)
    leading, last = (max(0, -steps), min(count, count - steps))
    return lax.ppermute(value, axis, [(source, source + steps) for source in range(leading, last)])


def on_device(
    charges,
    self_blocks,
    near_blocks,
    near_pairs,
    bases,
    transfers,
    parent_of,
    far_pairs,
    far_coupling,
    par_pairs,
    par_coupling,
):
    leaves, rhs, panels = charges.shape
    rank = bases.shape[1]
    width = rhs * rank
    slots = far_coupling.shape[0]
    pairs = par_coupling.shape[0]
    parents = leaves // 2
    devices = lax.axis_size("sfc")
    rows = devices * parents
    columns = 2 * width + LANES + 3 * width // 2
    vmem = pl.BlockSpec(memory_space=pltpu.VMEM)
    smem = pl.BlockSpec(memory_space=pltpu.SMEM)
    hbm = pl.BlockSpec(memory_space=pltpu.HBM)
    params = pltpu.CompilerParams(vmem_limit_bytes=60 * 1024 * 1024)
    late = pltpu.CompilerParams(vmem_limit_bytes=48 * 1024 * 1024)

    def cost(moved):
        return pl.CostEstimate(flops=4 * moved, bytes_accessed=moved, transcendentals=0)

    following = passed_along(charges, "sfc", -1)
    far_pairs = far_pairs.T
    par_pairs = par_pairs.T
    near_pairs = near_pairs.T
    far_c = jnp.transpose(far_coupling, (1, 2, 0))
    parent_of = parent_of.reshape(1, leaves)

    def like(value, memory=pltpu.VMEM):
        return memory(value.shape, value.dtype)

    send = pl.pallas_call(
        pre_kernel,
        out_shape=jax.ShapeDtypeStruct((rows, columns), BF16),
        in_specs=[hbm] * 8,
        out_specs=vmem,
        scratch_shapes=[
            like(charges),
            like(bases),
            like(transfers),
            like(parent_of),
            like(far_pairs),
            like(far_c),
            like(par_pairs),
            like(par_coupling),
            like(par_pairs, pltpu.SMEM),
            pltpu.SemaphoreType.DMA((9,)),
            pltpu.VMEM((leaves * rhs, rank), F32),
            pltpu.VMEM((leaves * rhs, rank), F32),
            pltpu.VMEM((parents * rhs, rank), F32),
            pltpu.VMEM((pairs * rhs, rank), F32),
            pltpu.VMEM((width, slots), F32),
            pltpu.VMEM((leaves * rhs, rhs * slots), BF16),
        ],
        compiler_params=params,
        cost_estimate=cost(10_000_000),
        name="upward",
    )(charges, bases, transfers, parent_of, far_pairs, far_c, par_pairs, par_coupling)
    send = after(send, following, 107 << 19)
    got = lax.all_to_all(send, "sfc", split_axis=0, concat_axis=0, tiled=True)
    steps = 4
    selves, nears = leaves // steps, near_blocks.shape[0] // steps
    whole = lambda *shape: pl.BlockSpec(shape, lambda i: (0,) * len(shape))
    near_own, near_away = pl.pallas_call(
        near_kernel,
        grid=(steps,),
        out_shape=[
            jax.ShapeDtypeStruct((leaves, rhs, panels), F32),
            jax.ShapeDtypeStruct((leaves, rhs, panels), BF16),
        ],
        in_specs=[
            smem,
            whole(leaves, rhs, panels),
            whole(leaves, rhs, panels),
            pl.BlockSpec((selves, panels, panels), lambda i: (i, 0, 0)),
            pl.BlockSpec((nears, panels, panels), lambda i: (i, 0, 0)),
        ],
        out_specs=[whole(leaves, rhs, panels)] * 2,
        scratch_shapes=[
            pltpu.VMEM((2 * leaves, rhs, panels), BF16),
            pltpu.VMEM((2 * leaves, rhs, panels), F32),
        ],
        compiler_params=pltpu.CompilerParams(vmem_limit_bytes=52 * 1024 * 1024),
        cost_estimate=cost(20_000_000),
        name="near",
    )(near_pairs, charges, following, self_blocks, near_blocks)
    near_back = passed_along(near_away, "sfc", 1)

    got = after(got, near_back, 1 << 20)
    mom2 = lax.ppermute(
        got[:, 2 * width + LANES :], "sfc", [(i, i ^ 1) for i in range(devices)]
    )

    return pl.pallas_call(
        post_kernel,
        out_shape=jax.ShapeDtypeStruct((leaves, rhs, panels), F32),
        in_specs=[smem] + [vmem] * 11,
        out_specs=vmem,
        scratch_shapes=[
            pltpu.VMEM((width, slots), F32),
            pltpu.VMEM((width, slots), F32),
            pltpu.VMEM((pairs * rhs, rank), F32),
            pltpu.VMEM((pairs * rhs, rank), F32),
            pltpu.VMEM((leaves * rhs, rank), F32),
            pltpu.VMEM((leaves * rhs, rank), F32),
            pltpu.VMEM((leaves * rhs, rank), F32),
        ],
        compiler_params=late,
        name="downward",
    )(
        far_pairs,
        mom2,
        got,
        bases,
        transfers,
        parent_of,
        far_pairs,
        far_c,
        par_pairs,
        par_coupling,
        near_own,
        near_back,
    )


def solution(mesh):
    split = ("grp", "sfc")
    cube, flat = P(split, None, None), P(split, None)
    placed = (cube, cube, cube, flat, cube, cube, P(split), flat, cube, flat, cube)
    return jax.shard_map(
        on_device, mesh=mesh, in_specs=placed, out_specs=cube, check_vma=False
    )
```

```python
import functools

import jax
import jax.numpy as jnp
from jax import lax
from jax.experimental import pallas as pl
from jax.experimental.pallas import tpu as pltpu
from jax.sharding import PartitionSpec as P

F32 = jnp.float32
BF16 = jnp.bfloat16
LANES = 128


def dot_nn(a, b):
    return lax.dot_general(a, b, (((1,), (0,)), ((), ())), preferred_element_type=F32)


def dot_nt(a, b):
    return lax.dot_general(a, b, (((1,), (1,)), ((), ())), preferred_element_type=F32)


def dot_tn(a, b):
    return lax.dot_general(a, b, (((0,), (0,)), ((), ())), preferred_element_type=F32)


def split2(x):
    high = x.astype(BF16)
    return high, (x - high.astype(F32)).astype(BF16)


def iota(shape, axis):
    return lax.broadcasted_iota(jnp.int32, shape, axis)


def one_hot(condition):
    return jnp.where(condition, 1.0, 0.0).astype(BF16)


def rows_to_lanes(ref, count, rhs):
    return jnp.concatenate([ref[pl.ds(r, count, stride=rhs), :] for r in range(rhs)], axis=1)


def lanes_to_rows(ref, value, rhs):
    count, width = value.shape
    rank = width // rhs
    for r in range(rhs):
        ref[pl.ds(r, count, stride=rhs), :] = value[:, r * rank : (r + 1) * rank]


def row_sums(parts):
    row = iota(parts[0].shape, 0)
    for step in (4, 2, 1):
        upper = row % (2 * step) >= step
        merged = []
        for a, b in zip(parts[:step], parts[step:]):
            swapped = jnp.where(upper, a, b)
            if step == 4:
                moved = pltpu.roll(swapped, 4, axis=0)
            else:
                moved = jnp.where(
                    upper,
                    pltpu.roll(swapped, step, axis=0),
                    pltpu.roll(swapped, 8 - step, axis=0),
                )
            merged.append(jnp.where(upper, b, a) + moved)
        parts = merged
    return parts[0]


def fetch(pairs, sems):
    copies = [pltpu.make_async_copy(src, dst, sems.at[i]) for i, (src, dst) in enumerate(pairs)]
    for copy in copies:
        copy.start()
    return copies


def pre_kernel(
    charges_h,
    bases_h,
    transfers_h,
    parent_of_h,
    far_pairs_h,
    far_c_h,
    par_pairs_h,
    par_c_h,
    send,
    charges,
    bases,
    transfers,
    parent_of,
    far_pairs,
    far_c,
    par_pairs,
    par_c,
    par_smem,
    sems,
    mo,
    ch,
    pm3,
    pb,
    a_ref,
    ob,
):
    leaves, rhs, _ = charges.shape
    rank = bases.shape[1]
    width = rhs * rank
    slots = far_c.shape[2]
    pairs = par_c.shape[0]
    parents = leaves // 2
    rows = send.shape[0]
    copies = fetch(
        [
            (charges_h, charges),
            (bases_h, bases),
            (transfers_h, transfers),
            (parent_of_h, parent_of),
            (far_pairs_h, far_pairs),
            (par_pairs_h, par_pairs),
            (par_pairs_h, par_smem),
            (far_c_h, far_c),
            (par_c_h, par_c),
        ],
        sems,
    )
    for copy in copies[:3]:
        copy.wait()

    for l in range(leaves):
        m = dot_nt(charges[l], bases[l]).astype(BF16)
        mo[l * rhs : (l + 1) * rhs, :] = m.astype(F32)
        ch[l * rhs : (l + 1) * rhs, :] = dot_nt(m, transfers[l])
    for copy in copies[3:]:
        copy.wait()
    m2 = rows_to_lanes(mo, leaves, rhs)
    high, low = split2(rows_to_lanes(ch, leaves, rhs))
    par_hot = one_hot(parent_of[...] % parents == iota((parents, leaves), 0))
    pm = (dot_nn(par_hot, high) + dot_nn(par_hot, low)).astype(BF16).astype(F32)
    lanes_to_rows(pm3, pm, rhs)
    half = 3 * width // 2
    shared = [
        jnp.concatenate([x[:, c * width // 2 : (c + 1) * width // 2] for x in (m2[:parents], m2[parents:], pm)], axis=1)
        for c in range(2)
    ]
    shared = jnp.concatenate(shared, axis=0).astype(BF16)
    at = 2 * width + LANES
    for p in range(rows // (2 * parents)):
        send[p * 2 * parents : (p + 1) * 2 * parents, at : at + half] = shared

    owner_hot = one_hot(far_pairs[0:1, :] % leaves == iota((leaves, slots), 0))
    a_ref[...] = dot_tn(m2.astype(BF16), owner_hot)
    for s in range(pairs):
        q = par_smem[0, s] % parents
        x = pm3[pl.ds(pl.multiple_of(q * rhs, rhs), rhs), :].astype(BF16)
        pb[s * rhs : (s + 1) * rhs, :] = dot_nn(x, par_c[s])
    half = rank // 2
    for sb in range(slots // LANES):
        lanes = slice(sb * LANES, (sb + 1) * LANES)
        for jh in range(2):

            def body(k8, acc):
                rows_a = [
                    a_ref[pl.ds(pl.multiple_of(r * rank + k8 * 8, 8), 8), lanes]
                    for r in range(rhs)
                ]
                for i in range(8):
                    c = far_c[k8 * 8 + i, jh * half : (jh + 1) * half, lanes].astype(F32)
                    acc = tuple(acc[r] + c * rows_a[r][i : i + 1, :] for r in range(rhs))
                return acc

            acc = tuple(jnp.zeros((half, LANES), F32) for _ in range(rhs))
            acc = lax.fori_loop(0, rank // 8, body, acc, unroll=4)
            for r in range(rhs):
                first = r * rank + jh * half
                ob[first : first + half, lanes] = acc[r].astype(BF16)
    partner = far_pairs[1:2, :]
    local = jnp.where(partner >= 0, partner % leaves, -1).astype(F32)
    ob[width : width + LANES, :] = jnp.broadcast_to(local, (LANES, slots)).astype(BF16)
    unit = one_hot(iota((LANES, LANES), 0) == iota((LANES, LANES), 1))
    for sb in range(slots // LANES):
        lanes = slice(sb * LANES, (sb + 1) * LANES)
        send[lanes, 0 : width + LANES] = dot_nt(unit, ob[:, lanes]).astype(BF16)

    high, low = split2(rows_to_lanes(pb, pairs, rhs))
    hot = one_hot(par_pairs[1:2, :] == iota((rows, pairs), 0))
    at = width + LANES
    send[:, at : at + width] = (dot_nn(hot, high) + dot_nn(hot, low)).astype(BF16)


def near_kernel(pairs, charges, following, self_blocks, near_blocks, own, away, ext, out):
    leaves = charges.shape[0]
    step = pl.program_id(0)
    selves, nears = self_blocks.shape[0], near_blocks.shape[0]

    @pl.when(step == 0)
    def _():
        ext[0:leaves] = charges[...]
        ext[leaves:] = following[...]
        out[...] = jnp.zeros_like(out)

    terms = [(step * selves + i, dot_nt(ext[step * selves + i], self_blocks[i])) for i in range(selves)]
    for i in range(nears):
        a, b = pairs[0, step * nears + i], pairs[1, step * nears + i]
        first = (a // leaves) * leaves
        a, b = a - first, b - first
        terms.append((a, dot_nt(ext[b], near_blocks[i])))
        terms.append((b, dot_nn(ext[a], near_blocks[i])))
    for at, term in terms:
        out[at] += term

    @pl.when(step == pl.num_programs(0) - 1)
    def _():
        own[...] = out[0:leaves]
        away[...] = out[leaves:].astype(BF16)


def far_half(mom, far_pairs, far_c, b_ref, fw, leaves, parents):
    rows, slots = mom.shape[0], far_c.shape[2]
    rank = far_c.shape[0]
    wide = mom.shape[1] // 3
    some = wide // rank
    row_id = iota((rows, slots), 0)
    base_leaf = row_id // parents * leaves + row_id % parents
    partner = far_pairs[1:2, :]
    total = None
    for h in range(2):
        hot = one_hot(partner == base_leaf + h * parents)
        part = dot_tn(mom[:, h * wide : (h + 1) * wide], hot)
        total = part if total is None else total + part
    b_ref[...] = total

    for sb in range(slots // LANES):
        lanes = slice(sb * LANES, (sb + 1) * LANES)

        def body(k8, carry):
            parts = [[] for _ in range(some)]
            for i in range(8):
                c = far_c[k8 * 8 + i, :, lanes].astype(F32)
                for r in range(some):
                    prod = c * b_ref[r * rank : (r + 1) * rank, lanes]
                    parts[r].append(sum(prod[j * 8 : (j + 1) * 8] for j in range(rank // 8)))
            for r in range(some):
                fw[pl.ds(pl.multiple_of(r * rank + k8 * 8, 8), 8), lanes] = row_sums(parts[r])
            return carry

        lax.fori_loop(0, rank // 8, body, 0, unroll=8)

    hot = one_hot(far_pairs[0:1, :] % leaves == iota((leaves, slots), 0))
    high, low = split2(fw[...])
    return dot_nt(hot, high) + dot_nt(hot, low)


def far_kernel(got, far_pairs, far_c, half, back, b_ref, fw):
    leaves, width = back.shape
    parents = leaves // 2
    rows = got.shape[0]
    index = got[:, width : width + LANES].astype(F32)[:, :leaves].astype(jnp.int32)
    hot = one_hot(index == iota((rows, leaves), 1))
    back[...] = dot_tn(hot, got[:, 0:width])
    mom = got[:, 2 * width + LANES :]
    half[...] = far_half(mom, far_pairs, far_c, b_ref, fw, leaves, parents)


def post_kernel(
    core_smem,
    half,
    back,
    mom2,
    got,
    bases,
    transfers,
    parent_of,
    far_pairs,
    far_c,
    par_pairs,
    par_c,
    near_own,
    near_back,
    out,
    b_ref,
    fw,
    g_ref,
    pf,
    lf,
    pg,
    dn,
):
    leaves, rank, _ = bases.shape
    width = back.shape[1]
    rhs = width // rank
    pairs = par_c.shape[0]
    parents = leaves // 2
    rows = got.shape[0]
    core = core_smem[0, 0] // leaves % 2

    def in_order(mine, other):
        return jnp.concatenate(
            [jnp.where(core == 0, mine, other), jnp.where(core == 0, other, mine)], axis=1
        )

    wide = mom2.shape[1] // 3
    shared = in_order(got[:, got.shape[1] - wide :], mom2[:, 2 * wide :])
    hot = one_hot(par_pairs[1:2, :] == iota((rows, pairs), 0))
    lanes_to_rows(g_ref, dot_tn(hot, shared), rhs)
    for s in range(pairs):
        at = slice(s * rhs, (s + 1) * rhs)
        pf[at, :] = dot_nt(g_ref[at, :].astype(BF16), par_c[s])
    high, low = split2(rows_to_lanes(pf, pairs, rhs))
    hot = one_hot(par_pairs[0:1, :] % parents == iota((parents, pairs), 0))
    fold = one_hot(iota((parents, rows), 1) % parents == iota((parents, rows), 0))
    at = width + LANES
    locals_p = dot_nn(hot, high) + dot_nn(hot, low) + dot_nn(fold, got[:, at : at + width])
    hot = one_hot(parent_of[...] % parents == iota((parents, leaves), 0))
    lanes_to_rows(pg, dot_tn(hot, locals_p.astype(BF16)), rhs)
    for l in range(leaves):
        at = slice(l * rhs, (l + 1) * rhs)
        dn[at, :] = dot_nn(pg[at, :].astype(BF16), transfers[l])

    other = far_half(mom2[...], far_pairs, far_c, b_ref, fw, leaves, parents)
    lanes_to_rows(lf, back[...] + in_order(half[...], other), rhs)
    for l in range(leaves):
        at = slice(l * rhs, (l + 1) * rhs)
        mine = (lf[at, :] + dn[at, :]).astype(BF16)
        near = near_own[l] + near_back[l].astype(F32)
        out[l] = dot_nn(mine, bases[l]) + near


def after(value, earlier, vmem_limit):
    anywhere = pl.BlockSpec(memory_space=pl.ANY)
    return pl.pallas_call(
        lambda value, earlier, same: None,
        out_shape=jax.ShapeDtypeStruct(value.shape, value.dtype),
        in_specs=[anywhere] * 2,
        out_specs=anywhere,
        input_output_aliases={0: 0},
        compiler_params=pltpu.CompilerParams(vmem_limit_bytes=vmem_limit),
        name="after",
    )(value, earlier)


def passed_along(value, axis, steps):
    count = lax.axis_size(axis)
    leading, last = (max(0, -steps), min(count, count - steps))
    return lax.ppermute(value, axis, [(source, source + steps) for source in range(leading, last)])


def on_device(
    charges,
    self_blocks,
    near_blocks,
    near_pairs,
    bases,
    transfers,
    parent_of,
    far_pairs,
    far_coupling,
    par_pairs,
    par_coupling,
):
    leaves, rhs, panels = charges.shape
    rank = bases.shape[1]
    width = rhs * rank
    slots = far_coupling.shape[0]
    pairs = par_coupling.shape[0]
    parents = leaves // 2
    devices = lax.axis_size("sfc")
    rows = devices * parents
    columns = 2 * width + LANES + 3 * width // 2
    vmem = pl.BlockSpec(memory_space=pltpu.VMEM)
    smem = pl.BlockSpec(memory_space=pltpu.SMEM)
    hbm = pl.BlockSpec(memory_space=pltpu.HBM)
    params = pltpu.CompilerParams(vmem_limit_bytes=60 * 1024 * 1024)
    late = pltpu.CompilerParams(vmem_limit_bytes=48 * 1024 * 1024)

    def cost(moved):
        return pl.CostEstimate(flops=4 * moved, bytes_accessed=moved, transcendentals=0)

    following = passed_along(charges, "sfc", -1)
    far_pairs = far_pairs.T
    par_pairs = par_pairs.T
    near_pairs = near_pairs.T
    far_c = jnp.transpose(far_coupling, (1, 2, 0))
    parent_of = parent_of.reshape(1, leaves)

    def like(value, memory=pltpu.VMEM):
        return memory(value.shape, value.dtype)

    send = pl.pallas_call(
        pre_kernel,
        out_shape=jax.ShapeDtypeStruct((rows, columns), BF16),
        in_specs=[hbm] * 8,
        out_specs=vmem,
        scratch_shapes=[
            like(charges),
            like(bases),
            like(transfers),
            like(parent_of),
            like(far_pairs),
            like(far_c),
            like(par_pairs),
            like(par_coupling),
            like(par_pairs, pltpu.SMEM),
            pltpu.SemaphoreType.DMA((9,)),
            pltpu.VMEM((leaves * rhs, rank), F32),
            pltpu.VMEM((leaves * rhs, rank), F32),
            pltpu.VMEM((parents * rhs, rank), F32),
            pltpu.VMEM((pairs * rhs, rank), F32),
            pltpu.VMEM((width, slots), F32),
            pltpu.VMEM((width + LANES, slots), BF16),
        ],
        compiler_params=params,
        cost_estimate=cost(10_000_000),
        name="upward",
    )(charges, bases, transfers, parent_of, far_pairs, far_c, par_pairs, par_coupling)
    send = after(send, following, 107 << 19)
    got = lax.all_to_all(send, "sfc", split_axis=0, concat_axis=0, tiled=True)
    steps = 4
    selves, nears = leaves // steps, near_blocks.shape[0] // steps
    whole = lambda *shape: pl.BlockSpec(shape, lambda i: (0,) * len(shape))
    near_own, near_away = pl.pallas_call(
        near_kernel,
        grid=(steps,),
        out_shape=[
            jax.ShapeDtypeStruct((leaves, rhs, panels), F32),
            jax.ShapeDtypeStruct((leaves, rhs, panels), BF16),
        ],
        in_specs=[
            smem,
            whole(leaves, rhs, panels),
            whole(leaves, rhs, panels),
            pl.BlockSpec((selves, panels, panels), lambda i: (i, 0, 0)),
            pl.BlockSpec((nears, panels, panels), lambda i: (i, 0, 0)),
        ],
        out_specs=[whole(leaves, rhs, panels)] * 2,
        scratch_shapes=[
            pltpu.VMEM((2 * leaves, rhs, panels), BF16),
            pltpu.VMEM((2 * leaves, rhs, panels), F32),
        ],
        compiler_params=pltpu.CompilerParams(vmem_limit_bytes=52 * 1024 * 1024),
        cost_estimate=cost(20_000_000),
        name="near",
    )(near_pairs, charges, following, self_blocks, near_blocks)
    near_back = passed_along(near_away, "sfc", 1)

    got = after(got, near_back, 1 << 20)
    mom2 = lax.ppermute(
        got[:, 2 * width + LANES :], "sfc", [(i, i ^ 1) for i in range(devices)]
    )

    half, back = pl.pallas_call(
        far_kernel,
        out_shape=[
            jax.ShapeDtypeStruct((leaves, width // 2), F32),
            jax.ShapeDtypeStruct((leaves, width), F32),
        ],
        in_specs=[vmem] * 3,
        out_specs=[vmem] * 2,
        scratch_shapes=[pltpu.VMEM((width // 2, slots), F32)] * 2,
        compiler_params=late,
        cost_estimate=cost(8_000_000),
        name="far",
    )(got, far_pairs, far_c)

    return pl.pallas_call(
        post_kernel,
        out_shape=jax.ShapeDtypeStruct((leaves, rhs, panels), F32),
        in_specs=[smem] + [vmem] * 13,
        out_specs=vmem,
        scratch_shapes=[
            pltpu.VMEM((width // 2, slots), F32),
            pltpu.VMEM((width // 2, slots), F32),
            pltpu.VMEM((pairs * rhs, rank), F32),
            pltpu.VMEM((pairs * rhs, rank), F32),
            pltpu.VMEM((leaves * rhs, rank), F32),
            pltpu.VMEM((leaves * rhs, rank), F32),
            pltpu.VMEM((leaves * rhs, rank), F32),
        ],
        compiler_params=late,
        name="downward",
    )(
        far_pairs,
        half,
        back,
        mom2,
        got,
        bases,
        transfers,
        parent_of,
        far_pairs,
        far_c,
        par_pairs,
        par_coupling,
        near_own,
        near_back,
    )


def solution(mesh):
    split = ("grp", "sfc")
    cube, flat = P(split, None, None), P(split, None)
    placed = (cube, cube, cube, flat, cube, cube, P(split), flat, cube, flat, cube)
    return jax.shard_map(
        on_device, mesh=mesh, in_specs=placed, out_specs=cube, check_vma=False
    )
```

```python
import functools

import jax
import jax.numpy as jnp
from jax import lax
from jax.experimental import pallas as pl
from jax.experimental.pallas import tpu as pltpu
from jax.sharding import PartitionSpec as P

F32 = jnp.float32
BF16 = jnp.bfloat16
LANES = 128


def dot_nn(a, b):
    return lax.dot_general(a, b, (((1,), (0,)), ((), ())), preferred_element_type=F32)


def dot_nt(a, b):
    return lax.dot_general(a, b, (((1,), (1,)), ((), ())), preferred_element_type=F32)


def dot_tn(a, b):
    return lax.dot_general(a, b, (((0,), (0,)), ((), ())), preferred_element_type=F32)


def split2(x):
    high = x.astype(BF16)
    return high, (x - high.astype(F32)).astype(BF16)


def iota(shape, axis):
    return lax.broadcasted_iota(jnp.int32, shape, axis)


def one_hot(condition):
    return jnp.where(condition, 1.0, 0.0).astype(BF16)


def rows_to_lanes(ref, count, rhs):
    return jnp.concatenate([ref[pl.ds(r, count, stride=rhs), :] for r in range(rhs)], axis=1)


def lanes_to_rows(ref, value, rhs):
    count, width = value.shape
    rank = width // rhs
    for r in range(rhs):
        ref[pl.ds(r, count, stride=rhs), :] = value[:, r * rank : (r + 1) * rank]


def row_sums(parts):
    row = iota(parts[0].shape, 0)
    for step in (4, 2, 1):
        upper = row % (2 * step) >= step
        merged = []
        for a, b in zip(parts[:step], parts[step:]):
            swapped = jnp.where(upper, a, b)
            if step == 4:
                moved = pltpu.roll(swapped, 4, axis=0)
            else:
                moved = jnp.where(
                    upper,
                    pltpu.roll(swapped, step, axis=0),
                    pltpu.roll(swapped, 8 - step, axis=0),
                )
            merged.append(jnp.where(upper, b, a) + moved)
        parts = merged
    return parts[0]


def fetch(pairs, sems):
    copies = [pltpu.make_async_copy(src, dst, sems.at[i]) for i, (src, dst) in enumerate(pairs)]
    for copy in copies:
        copy.start()
    return copies


def pre_kernel(
    charges_h,
    bases_h,
    transfers_h,
    parent_of_h,
    far_pairs_h,
    far_c_h,
    par_pairs_h,
    par_c_h,
    send,
    charges,
    bases,
    transfers,
    parent_of,
    far_pairs,
    far_c,
    par_pairs,
    par_c,
    par_smem,
    sems,
    mo,
    ch,
    pm3,
    pb,
    a_ref,
    ob,
):
    leaves, rhs, _ = charges.shape
    rank = bases.shape[1]
    width = rhs * rank
    slots = far_c.shape[2]
    pairs = par_c.shape[0]
    parents = leaves // 2
    rows = send.shape[0]
    copies = fetch(
        [
            (charges_h, charges),
            (bases_h, bases),
            (transfers_h, transfers),
            (parent_of_h, parent_of),
            (far_pairs_h, far_pairs),
            (par_pairs_h, par_pairs),
            (par_pairs_h, par_smem),
            (far_c_h, far_c),
            (par_c_h, par_c),
        ],
        sems,
    )
    for copy in copies[:3]:
        copy.wait()

    for l in range(leaves):
        m = dot_nt(charges[l], bases[l]).astype(BF16)
        mo[l * rhs : (l + 1) * rhs, :] = m.astype(F32)
        ch[l * rhs : (l + 1) * rhs, :] = dot_nt(m, transfers[l])
    for copy in copies[3:]:
        copy.wait()
    m2 = rows_to_lanes(mo, leaves, rhs)
    high, low = split2(rows_to_lanes(ch, leaves, rhs))
    par_hot = one_hot(parent_of[...] % parents == iota((parents, leaves), 0))
    pm = (dot_nn(par_hot, high) + dot_nn(par_hot, low)).astype(BF16).astype(F32)
    lanes_to_rows(pm3, pm, rhs)
    half = 3 * width // 2
    shared = [
        jnp.concatenate([x[:, c * width // 2 : (c + 1) * width // 2] for x in (m2[:parents], m2[parents:], pm)], axis=1)
        for c in range(2)
    ]
    shared = jnp.concatenate(shared, axis=0).astype(BF16)
    at = 2 * width + LANES
    for p in range(rows // (2 * parents)):
        send[p * 2 * parents : (p + 1) * 2 * parents, at : at + half] = shared

    owner_hot = one_hot(far_pairs[0:1, :] % leaves == iota((leaves, slots), 0))
    a_ref[...] = dot_tn(m2.astype(BF16), owner_hot)
    for s in range(pairs):
        q = par_smem[0, s] % parents
        x = pm3[pl.ds(pl.multiple_of(q * rhs, rhs), rhs), :].astype(BF16)
        pb[s * rhs : (s + 1) * rhs, :] = dot_nn(x, par_c[s])
    half = rank // 2
    for sb in range(slots // LANES):
        lanes = slice(sb * LANES, (sb + 1) * LANES)
        for jh in range(2):

            def body(k8, acc):
                rows_a = [
                    a_ref[pl.ds(pl.multiple_of(r * rank + k8 * 8, 8), 8), lanes]
                    for r in range(rhs)
                ]
                for i in range(8):
                    c = far_c[k8 * 8 + i, jh * half : (jh + 1) * half, lanes].astype(F32)
                    acc = tuple(acc[r] + c * rows_a[r][i : i + 1, :] for r in range(rhs))
                return acc

            acc = tuple(jnp.zeros((half, LANES), F32) for _ in range(rhs))
            acc = lax.fori_loop(0, rank // 8, body, acc, unroll=4)
            for r in range(rhs):
                first = r * rank + jh * half
                ob[first : first + half, lanes] = acc[r].astype(BF16)
    partner = far_pairs[1:2, :]
    local = jnp.where(partner >= 0, partner % leaves, -1).astype(F32)
    ob[width : width + LANES, :] = jnp.broadcast_to(local, (LANES, slots)).astype(BF16)
    unit = one_hot(iota((LANES, LANES), 0) == iota((LANES, LANES), 1))
    for sb in range(slots // LANES):
        lanes = slice(sb * LANES, (sb + 1) * LANES)
        send[lanes, 0 : width + LANES] = dot_nt(unit, ob[:, lanes]).astype(BF16)

    high, low = split2(rows_to_lanes(pb, pairs, rhs))
    hot = one_hot(par_pairs[1:2, :] == iota((rows, pairs), 0))
    at = width + LANES
    send[:, at : at + width] = (dot_nn(hot, high) + dot_nn(hot, low)).astype(BF16)


def near_kernel(pairs, charges, following, self_blocks, near_blocks, own, away, ext, out):
    leaves = charges.shape[0]
    step = pl.program_id(0)
    selves, nears = self_blocks.shape[0], near_blocks.shape[0]

    @pl.when(step == 0)
    def _():
        ext[0:leaves] = charges[...]
        ext[leaves:] = following[...]
        out[...] = jnp.zeros_like(out)

    terms = [(step * selves + i, dot_nt(ext[step * selves + i], self_blocks[i])) for i in range(selves)]
    for i in range(nears):
        a, b = pairs[0, step * nears + i], pairs[1, step * nears + i]
        first = (a // leaves) * leaves
        a, b = a - first, b - first
        terms.append((a, dot_nt(ext[b], near_blocks[i])))
        terms.append((b, dot_nn(ext[a], near_blocks[i])))
    for at, term in terms:
        out[at] += term

    @pl.when(step == pl.num_programs(0) - 1)
    def _():
        own[...] = out[0:leaves]
        away[...] = out[leaves:].astype(BF16)


def far_half(mom, far_pairs, far_c, b_ref, fw, leaves, parents):
    rows, slots = mom.shape[0], far_c.shape[2]
    rank = far_c.shape[0]
    wide = mom.shape[1] // 3
    some = wide // rank
    row_id = iota((rows, slots), 0)
    base_leaf = row_id // parents * leaves + row_id % parents
    partner = far_pairs[1:2, :]
    total = None
    for h in range(2):
        hot = one_hot(partner == base_leaf + h * parents)
        part = dot_tn(mom[:, h * wide : (h + 1) * wide], hot)
        total = part if total is None else total + part
    b_ref[...] = total

    for sb in range(slots // LANES):
        lanes = slice(sb * LANES, (sb + 1) * LANES)

        def body(k8, carry):
            parts = [[] for _ in range(some)]
            for i in range(8):
                c = far_c[k8 * 8 + i, :, lanes].astype(F32)
                for r in range(some):
                    prod = c * b_ref[r * rank : (r + 1) * rank, lanes]
                    parts[r].append(sum(prod[j * 8 : (j + 1) * 8] for j in range(rank // 8)))
            for r in range(some):
                fw[pl.ds(pl.multiple_of(r * rank + k8 * 8, 8), 8), lanes] = row_sums(parts[r])
            return carry

        lax.fori_loop(0, rank // 8, body, 0, unroll=8)

    hot = one_hot(far_pairs[0:1, :] % leaves == iota((leaves, slots), 0))
    high, low = split2(fw[...])
    return dot_nt(hot, high) + dot_nt(hot, low)


def far_kernel(got, far_pairs, far_c, half, back, b_ref, fw):
    leaves, width = back.shape
    parents = leaves // 2
    rows = got.shape[0]
    index = got[:, width : width + LANES].astype(F32)[:, :leaves].astype(jnp.int32)
    hot = one_hot(index == iota((rows, leaves), 1))
    back[...] = dot_tn(hot, got[:, 0:width])
    mom = got[:, 2 * width + LANES :]
    half[...] = far_half(mom, far_pairs, far_c, b_ref, fw, leaves, parents)


def repeated(values, times):
    count = values.shape[1]
    spread = one_hot(iota((count, count * times), 1) // times == iota((count, count * times), 0))
    rows = jnp.broadcast_to(values.astype(F32), (8, count)).astype(BF16)
    return dot_nn(rows, spread)[0:1].astype(jnp.int32)


def prepare_kernel(earlier, par_pairs, parent_of, par_c, par_t, pick, to_owner, to_leaf):
    pairs = par_c.shape[0]
    rows = pick.shape[1]
    leaves = parent_of.shape[1]
    parents = leaves // 2
    rhs = to_owner.shape[0] // parents
    for s in range(pairs):
        par_t[s] = par_c[s].astype(F32).T.astype(BF16)
    hot = jnp.where(par_pairs[1:2, :] == iota((rows, pairs), 0), 1.0, 0.0)
    pick[...] = hot.T.astype(BF16)

    def by_rows(targets):
        shape = (parents * rhs, targets.shape[1] * rhs)
        row, column = iota(shape, 0), iota(shape, 1)
        same = (repeated(targets % parents, rhs) == row // rhs) & (row % rhs == column % rhs)
        return jnp.where(same, 1.0, 0.0)

    to_owner[...] = by_rows(par_pairs[0:1, :]).astype(BF16)
    to_leaf[...] = by_rows(parent_of[...]).T.astype(BF16)


def post_kernel(
    core_smem,
    half,
    back,
    mom2,
    got,
    bases,
    transfers,
    far_pairs,
    far_c,
    par_t,
    pick,
    to_owner,
    to_leaf,
    near_own,
    near_back,
    out,
    b_ref,
    fw,
    g_ref,
    pf,
    lf,
    pb,
    dn,
):
    leaves, rank, _ = bases.shape
    width = back.shape[1]
    rhs = width // rank
    pairs = par_t.shape[0]
    parents = leaves // 2
    rows = got.shape[0]
    core = core_smem[0, 0] // leaves % 2

    def in_order(mine, other):
        return jnp.concatenate(
            [jnp.where(core == 0, mine, other), jnp.where(core == 0, other, mine)], axis=1
        )

    wide = mom2.shape[1] // 3
    shared = in_order(got[:, got.shape[1] - wide :], mom2[:, 2 * wide :])
    fold = one_hot(iota((parents, rows), 1) % parents == iota((parents, rows), 0))
    at = width + LANES
    lanes_to_rows(pb, dot_nn(fold, got[:, at : at + width]), rhs)
    lanes_to_rows(g_ref, dot_nn(pick[...], shared), rhs)
    for s in range(pairs):
        at = slice(s * rhs, (s + 1) * rhs)
        pf[at, :] = dot_nn(g_ref[at, :].astype(BF16), par_t[s])
    high, low = split2(pf[...])
    locals_p = dot_nn(to_owner[...], high) + dot_nn(to_owner[...], low) + pb[...]
    picked = dot_nn(to_leaf[...], locals_p.astype(BF16)).astype(BF16)
    for l in range(leaves):
        at = slice(l * rhs, (l + 1) * rhs)
        dn[at, :] = dot_nn(picked[at, :], transfers[l])

    other = far_half(mom2[...], far_pairs, far_c, b_ref, fw, leaves, parents)
    lanes_to_rows(lf, back[...] + in_order(half[...], other), rhs)
    for l in range(leaves):
        at = slice(l * rhs, (l + 1) * rhs)
        mine = (lf[at, :] + dn[at, :]).astype(BF16)
        near = near_own[l] + near_back[l].astype(F32)
        out[l] = dot_nn(mine, bases[l]) + near


def after(value, earlier, vmem_limit):
    anywhere = pl.BlockSpec(memory_space=pl.ANY)
    return pl.pallas_call(
        lambda *refs: None,
        out_shape=jax.ShapeDtypeStruct(value.shape, value.dtype),
        in_specs=[anywhere] * (1 + len(earlier)),
        out_specs=anywhere,
        input_output_aliases={0: 0},
        compiler_params=pltpu.CompilerParams(vmem_limit_bytes=vmem_limit),
        name="after",
    )(value, *earlier)


def passed_along(value, axis, steps):
    count = lax.axis_size(axis)
    leading, last = (max(0, -steps), min(count, count - steps))
    return lax.ppermute(value, axis, [(source, source + steps) for source in range(leading, last)])


def on_device(
    charges,
    self_blocks,
    near_blocks,
    near_pairs,
    bases,
    transfers,
    parent_of,
    far_pairs,
    far_coupling,
    par_pairs,
    par_coupling,
):
    leaves, rhs, panels = charges.shape
    rank = bases.shape[1]
    width = rhs * rank
    slots = far_coupling.shape[0]
    pairs = par_coupling.shape[0]
    parents = leaves // 2
    devices = lax.axis_size("sfc")
    rows = devices * parents
    columns = 2 * width + LANES + 3 * width // 2
    vmem = pl.BlockSpec(memory_space=pltpu.VMEM)
    smem = pl.BlockSpec(memory_space=pltpu.SMEM)
    hbm = pl.BlockSpec(memory_space=pltpu.HBM)
    params = pltpu.CompilerParams(vmem_limit_bytes=60 * 1024 * 1024)
    late = pltpu.CompilerParams(vmem_limit_bytes=48 * 1024 * 1024)

    def cost(moved):
        return pl.CostEstimate(flops=4 * moved, bytes_accessed=moved, transcendentals=0)

    following = passed_along(charges, "sfc", -1)
    far_pairs = far_pairs.T
    par_pairs = par_pairs.T
    near_pairs = near_pairs.T
    far_c = jnp.transpose(far_coupling, (1, 2, 0))
    parent_of = parent_of.reshape(1, leaves)

    def like(value, memory=pltpu.VMEM):
        return memory(value.shape, value.dtype)

    send = pl.pallas_call(
        pre_kernel,
        out_shape=jax.ShapeDtypeStruct((rows, columns), BF16),
        in_specs=[hbm] * 8,
        out_specs=vmem,
        scratch_shapes=[
            like(charges),
            like(bases),
            like(transfers),
            like(parent_of),
            like(far_pairs),
            like(far_c),
            like(par_pairs),
            like(par_coupling),
            like(par_pairs, pltpu.SMEM),
            pltpu.SemaphoreType.DMA((9,)),
            pltpu.VMEM((leaves * rhs, rank), F32),
            pltpu.VMEM((leaves * rhs, rank), F32),
            pltpu.VMEM((parents * rhs, rank), F32),
            pltpu.VMEM((pairs * rhs, rank), F32),
            pltpu.VMEM((width, slots), F32),
            pltpu.VMEM((width + LANES, slots), BF16),
        ],
        compiler_params=params,
        cost_estimate=cost(10_000_000),
        name="upward",
    )(charges, bases, transfers, parent_of, far_pairs, far_c, par_pairs, par_coupling)
    send = after(send, [following], 107 << 19)
    got = lax.all_to_all(send, "sfc", split_axis=0, concat_axis=0, tiled=True)
    steps = 4
    selves, nears = leaves // steps, near_blocks.shape[0] // steps
    whole = lambda *shape: pl.BlockSpec(shape, lambda i: (0,) * len(shape))
    near_own, near_away = pl.pallas_call(
        near_kernel,
        grid=(steps,),
        out_shape=[
            jax.ShapeDtypeStruct((leaves, rhs, panels), F32),
            jax.ShapeDtypeStruct((leaves, rhs, panels), BF16),
        ],
        in_specs=[
            smem,
            whole(leaves, rhs, panels),
            whole(leaves, rhs, panels),
            pl.BlockSpec((selves, panels, panels), lambda i: (i, 0, 0)),
            pl.BlockSpec((nears, panels, panels), lambda i: (i, 0, 0)),
        ],
        out_specs=[whole(leaves, rhs, panels)] * 2,
        scratch_shapes=[
            pltpu.VMEM((2 * leaves, rhs, panels), BF16),
            pltpu.VMEM((2 * leaves, rhs, panels), F32),
        ],
        compiler_params=pltpu.CompilerParams(vmem_limit_bytes=52 * 1024 * 1024),
        cost_estimate=cost(20_000_000),
        name="near",
    )(near_pairs, charges, following, self_blocks, near_blocks)
    near_back = passed_along(near_away, "sfc", 1)

    prepared = pl.pallas_call(
        prepare_kernel,
        out_shape=[
            jax.ShapeDtypeStruct(shape, BF16)
            for shape in (
                par_coupling.shape,
                (pairs, rows),
                (parents * rhs, pairs * rhs),
                (leaves * rhs, parents * rhs),
            )
        ],
        in_specs=[pl.BlockSpec(memory_space=pl.ANY)] + [vmem] * 3,
        out_specs=[vmem] * 4,
        compiler_params=late,
        cost_estimate=cost(4_000_000),
        name="prepare",
    )(near_away, par_pairs, parent_of, par_coupling)

    got = after(got, [near_back, *prepared], 1 << 20)
    mom2 = lax.ppermute(
        got[:, 2 * width + LANES :], "sfc", [(i, i ^ 1) for i in range(devices)]
    )

    half, back = pl.pallas_call(
        far_kernel,
        out_shape=[
            jax.ShapeDtypeStruct((leaves, width // 2), F32),
            jax.ShapeDtypeStruct((leaves, width), F32),
        ],
        in_specs=[vmem] * 3,
        out_specs=[vmem] * 2,
        scratch_shapes=[pltpu.VMEM((width // 2, slots), F32)] * 2,
        compiler_params=late,
        cost_estimate=cost(8_000_000),
        name="far",
    )(got, far_pairs, far_c)

    return pl.pallas_call(
        post_kernel,
        out_shape=jax.ShapeDtypeStruct((leaves, rhs, panels), F32),
        in_specs=[smem] + [vmem] * 14,
        out_specs=vmem,
        scratch_shapes=[
            pltpu.VMEM((width // 2, slots), F32),
            pltpu.VMEM((width // 2, slots), F32),
            pltpu.VMEM((pairs * rhs, rank), F32),
            pltpu.VMEM((pairs * rhs, rank), F32),
            pltpu.VMEM((leaves * rhs, rank), F32),
            pltpu.VMEM((parents * rhs, rank), F32),
            pltpu.VMEM((leaves * rhs, rank), F32),
        ],
        compiler_params=late,
        name="downward",
    )(
        far_pairs,
        half,
        back,
        mom2,
        got,
        bases,
        transfers,
        far_pairs,
        far_c,
        *prepared,
        near_own,
        near_back,
    )


def solution(mesh):
    split = ("grp", "sfc")
    cube, flat = P(split, None, None), P(split, None)
    placed = (cube, cube, cube, flat, cube, cube, P(split), flat, cube, flat, cube)
    return jax.shard_map(
        on_device, mesh=mesh, in_specs=placed, out_specs=cube, check_vma=False
    )
```

```python
import functools

import jax
import jax.numpy as jnp
from jax import lax
from jax.experimental import pallas as pl
from jax.experimental.pallas import tpu as pltpu
from jax.sharding import PartitionSpec as P

F32 = jnp.float32
BF16 = jnp.bfloat16
LANES = 128


def dot_nn(a, b):
    return lax.dot_general(a, b, (((1,), (0,)), ((), ())), preferred_element_type=F32)


def dot_nt(a, b):
    return lax.dot_general(a, b, (((1,), (1,)), ((), ())), preferred_element_type=F32)


def dot_tn(a, b):
    return lax.dot_general(a, b, (((0,), (0,)), ((), ())), preferred_element_type=F32)


def split2(x):
    high = x.astype(BF16)
    return high, (x - high.astype(F32)).astype(BF16)


def iota(shape, axis):
    return lax.broadcasted_iota(jnp.int32, shape, axis)


def one_hot(condition):
    return jnp.where(condition, 1.0, 0.0).astype(BF16)


def rows_to_lanes(ref, count, rhs):
    return jnp.concatenate([ref[pl.ds(r, count, stride=rhs), :] for r in range(rhs)], axis=1)


def lanes_to_rows(ref, value, rhs):
    count, width = value.shape
    rank = width // rhs
    for r in range(rhs):
        ref[pl.ds(r, count, stride=rhs), :] = value[:, r * rank : (r + 1) * rank]


def row_sums(parts):
    row = iota(parts[0].shape, 0)
    for step in (4, 2, 1):
        upper = row % (2 * step) >= step
        merged = []
        for a, b in zip(parts[:step], parts[step:]):
            swapped = jnp.where(upper, a, b)
            if step == 4:
                moved = pltpu.roll(swapped, 4, axis=0)
            else:
                moved = jnp.where(
                    upper,
                    pltpu.roll(swapped, step, axis=0),
                    pltpu.roll(swapped, 8 - step, axis=0),
                )
            merged.append(jnp.where(upper, b, a) + moved)
        parts = merged
    return parts[0]


def fetch(pairs, sems):
    copies = [pltpu.make_async_copy(src, dst, sems.at[i]) for i, (src, dst) in enumerate(pairs)]
    for copy in copies:
        copy.start()
    return copies


def pre_kernel(
    charges_h,
    bases_h,
    transfers_h,
    parent_of_h,
    far_pairs_h,
    far_c_h,
    par_pairs_h,
    par_c_h,
    send,
    charges,
    bases,
    transfers,
    parent_of,
    far_pairs,
    far_c,
    par_pairs,
    par_c,
    par_smem,
    sems,
    mo,
    ch,
    pm3,
    pb,
    a_ref,
    ob,
):
    leaves, rhs, _ = charges.shape
    rank = bases.shape[1]
    width = rhs * rank
    slots = far_c.shape[2]
    pairs = par_c.shape[0]
    parents = leaves // 2
    rows = send.shape[0]
    copies = fetch(
        [
            (charges_h, charges),
            (bases_h, bases),
            (transfers_h, transfers),
            (parent_of_h, parent_of),
            (far_pairs_h, far_pairs),
            (par_pairs_h, par_pairs),
            (par_pairs_h, par_smem),
            (far_c_h, far_c),
            (par_c_h, par_c),
        ],
        sems,
    )
    for copy in copies[:3]:
        copy.wait()

    for l in range(leaves):
        m = dot_nt(charges[l], bases[l]).astype(BF16)
        mo[l * rhs : (l + 1) * rhs, :] = m.astype(F32)
        ch[l * rhs : (l + 1) * rhs, :] = dot_nt(m, transfers[l])
    for copy in copies[3:]:
        copy.wait()
    m2 = rows_to_lanes(mo, leaves, rhs)
    high, low = split2(rows_to_lanes(ch, leaves, rhs))
    par_hot = one_hot(parent_of[...] % parents == iota((parents, leaves), 0))
    pm = (dot_nn(par_hot, high) + dot_nn(par_hot, low)).astype(BF16).astype(F32)
    lanes_to_rows(pm3, pm, rhs)
    half = 3 * width // 2
    shared = [
        jnp.concatenate([x[:, c * width // 2 : (c + 1) * width // 2] for x in (m2[:parents], m2[parents:], pm)], axis=1)
        for c in range(2)
    ]
    shared = jnp.concatenate(shared, axis=0).astype(BF16)
    at = 2 * width + LANES
    for p in range(rows // (2 * parents)):
        send[p * 2 * parents : (p + 1) * 2 * parents, at : at + half] = shared

    owner_hot = one_hot(far_pairs[0:1, :] % leaves == iota((leaves, slots), 0))
    a_ref[...] = dot_tn(m2.astype(BF16), owner_hot)
    for s in range(pairs):
        q = par_smem[0, s] % parents
        x = pm3[pl.ds(pl.multiple_of(q * rhs, rhs), rhs), :].astype(BF16)
        pb[s * rhs : (s + 1) * rhs, :] = dot_nn(x, par_c[s])
    some = rank // 4
    for sb in range(slots // LANES):
        lanes = slice(sb * LANES, (sb + 1) * LANES)
        for first in range(0, rank, some):
            acc = [None] * rhs
            for k in range(rank):
                c = far_c[k, first : first + some, lanes].astype(F32)
                for r in range(rhs):
                    term = c * a_ref[r * rank + k : r * rank + k + 1, lanes]
                    acc[r] = term if k == 0 else acc[r] + term
            for r in range(rhs):
                at = r * rank + first
                ob[at : at + some, lanes] = acc[r].astype(BF16)
    partner = far_pairs[1:2, :]
    local = jnp.where(partner >= 0, partner % leaves, -1).astype(F32)
    ob[width : width + LANES, :] = jnp.broadcast_to(local, (LANES, slots)).astype(BF16)
    unit = one_hot(iota((LANES, LANES), 0) == iota((LANES, LANES), 1))
    for sb in range(slots // LANES):
        lanes = slice(sb * LANES, (sb + 1) * LANES)
        send[lanes, 0 : width + LANES] = dot_nt(unit, ob[:, lanes]).astype(BF16)

    high, low = split2(rows_to_lanes(pb, pairs, rhs))
    hot = one_hot(par_pairs[1:2, :] == iota((rows, pairs), 0))
    at = width + LANES
    send[:, at : at + width] = (dot_nn(hot, high) + dot_nn(hot, low)).astype(BF16)


def near_kernel(pairs, charges, following, self_blocks, near_blocks, own, away, ext, out):
    leaves = charges.shape[0]
    step = pl.program_id(0)
    selves, nears = self_blocks.shape[0], near_blocks.shape[0]

    @pl.when(step == 0)
    def _():
        ext[0:leaves] = charges[...]
        ext[leaves:] = following[...]
        out[...] = jnp.zeros_like(out)

    terms = [(step * selves + i, dot_nt(ext[step * selves + i], self_blocks[i])) for i in range(selves)]
    for i in range(nears):
        a, b = pairs[0, step * nears + i], pairs[1, step * nears + i]
        first = (a // leaves) * leaves
        a, b = a - first, b - first
        terms.append((a, dot_nt(ext[b], near_blocks[i])))
        terms.append((b, dot_nn(ext[a], near_blocks[i])))
    for at, term in terms:
        out[at] += term

    @pl.when(step == pl.num_programs(0) - 1)
    def _():
        own[...] = out[0:leaves]
        away[...] = out[leaves:].astype(BF16)


def far_half(mom, far_pairs, far_c, b_ref, fw, leaves, parents):
    rows, slots = mom.shape[0], far_c.shape[2]
    rank = far_c.shape[0]
    wide = mom.shape[1] // 3
    some = wide // rank
    row_id = iota((rows, slots), 0)
    base_leaf = row_id // parents * leaves + row_id % parents
    partner = far_pairs[1:2, :]
    total = None
    for h in range(2):
        hot = one_hot(partner == base_leaf + h * parents)
        part = dot_tn(mom[:, h * wide : (h + 1) * wide], hot)
        total = part if total is None else total + part
    b_ref[...] = total

    for sb in range(slots // LANES):
        lanes = slice(sb * LANES, (sb + 1) * LANES)

        def body(k8, carry):
            parts = [[] for _ in range(some)]
            for i in range(8):
                c = far_c[k8 * 8 + i, :, lanes].astype(F32)
                for r in range(some):
                    prod = c * b_ref[r * rank : (r + 1) * rank, lanes]
                    parts[r].append(sum(prod[j * 8 : (j + 1) * 8] for j in range(rank // 8)))
            for r in range(some):
                fw[pl.ds(pl.multiple_of(r * rank + k8 * 8, 8), 8), lanes] = row_sums(parts[r])
            return carry

        lax.fori_loop(0, rank // 8, body, 0, unroll=8)

    hot = one_hot(far_pairs[0:1, :] % leaves == iota((leaves, slots), 0))
    high, low = split2(fw[...])
    return dot_nt(hot, high) + dot_nt(hot, low)


def far_kernel(got, far_pairs, far_c, half, back, b_ref, fw):
    leaves, width = back.shape
    parents = leaves // 2
    rows = got.shape[0]
    index = got[:, width : width + LANES].astype(F32)[:, :leaves].astype(jnp.int32)
    hot = one_hot(index == iota((rows, leaves), 1))
    back[...] = dot_tn(hot, got[:, 0:width])
    mom = got[:, 2 * width + LANES :]
    half[...] = far_half(mom, far_pairs, far_c, b_ref, fw, leaves, parents)


def repeated(values, times):
    count = values.shape[1]
    spread = one_hot(iota((count, count * times), 1) // times == iota((count, count * times), 0))
    rows = jnp.broadcast_to(values.astype(F32), (8, count)).astype(BF16)
    return dot_nn(rows, spread)[0:1].astype(jnp.int32)


def prepare_kernel(earlier, par_pairs, parent_of, par_c, par_t, pick, to_owner, to_leaf):
    pairs = par_c.shape[0]
    rows = pick.shape[1]
    leaves = parent_of.shape[1]
    parents = leaves // 2
    rhs = to_owner.shape[0] // parents
    for s in range(pairs):
        par_t[s] = par_c[s].astype(F32).T.astype(BF16)
    hot = jnp.where(par_pairs[1:2, :] == iota((rows, pairs), 0), 1.0, 0.0)
    pick[...] = hot.T.astype(BF16)

    def by_rows(targets):
        shape = (parents * rhs, targets.shape[1] * rhs)
        row, column = iota(shape, 0), iota(shape, 1)
        same = (repeated(targets % parents, rhs) == row // rhs) & (row % rhs == column % rhs)
        return jnp.where(same, 1.0, 0.0)

    to_owner[...] = by_rows(par_pairs[0:1, :]).astype(BF16)
    to_leaf[...] = by_rows(parent_of[...]).T.astype(BF16)


def post_kernel(
    core_smem,
    half,
    back,
    mom2,
    got,
    bases,
    transfers,
    far_pairs,
    far_c,
    par_t,
    pick,
    to_owner,
    to_leaf,
    near_own,
    near_back,
    out,
    b_ref,
    fw,
    g_ref,
    pf,
    lf,
    pb,
    dn,
):
    leaves, rank, _ = bases.shape
    width = back.shape[1]
    rhs = width // rank
    pairs = par_t.shape[0]
    parents = leaves // 2
    rows = got.shape[0]
    core = core_smem[0, 0] // leaves % 2

    def in_order(mine, other):
        return jnp.concatenate(
            [jnp.where(core == 0, mine, other), jnp.where(core == 0, other, mine)], axis=1
        )

    wide = mom2.shape[1] // 3
    shared = in_order(got[:, got.shape[1] - wide :], mom2[:, 2 * wide :])
    fold = one_hot(iota((parents, rows), 1) % parents == iota((parents, rows), 0))
    at = width + LANES
    lanes_to_rows(pb, dot_nn(fold, got[:, at : at + width]), rhs)
    lanes_to_rows(g_ref, dot_nn(pick[...], shared), rhs)
    for s in range(pairs):
        at = slice(s * rhs, (s + 1) * rhs)
        pf[at, :] = dot_nn(g_ref[at, :].astype(BF16), par_t[s])
    high, low = split2(pf[...])
    locals_p = dot_nn(to_owner[...], high) + dot_nn(to_owner[...], low) + pb[...]
    picked = dot_nn(to_leaf[...], locals_p.astype(BF16)).astype(BF16)
    for l in range(leaves):
        at = slice(l * rhs, (l + 1) * rhs)
        dn[at, :] = dot_nn(picked[at, :], transfers[l])

    other = far_half(mom2[...], far_pairs, far_c, b_ref, fw, leaves, parents)
    lanes_to_rows(lf, back[...] + in_order(half[...], other), rhs)
    for l in range(leaves):
        at = slice(l * rhs, (l + 1) * rhs)
        mine = (lf[at, :] + dn[at, :]).astype(BF16)
        near = near_own[l] + near_back[l].astype(F32)
        out[l] = dot_nn(mine, bases[l]) + near


def after(value, earlier, vmem_limit):
    anywhere = pl.BlockSpec(memory_space=pl.ANY)
    return pl.pallas_call(
        lambda *refs: None,
        out_shape=jax.ShapeDtypeStruct(value.shape, value.dtype),
        in_specs=[anywhere] * (1 + len(earlier)),
        out_specs=anywhere,
        input_output_aliases={0: 0},
        compiler_params=pltpu.CompilerParams(vmem_limit_bytes=vmem_limit),
        name="after",
    )(value, *earlier)


def passed_along(value, axis, steps):
    count = lax.axis_size(axis)
    leading, last = (max(0, -steps), min(count, count - steps))
    return lax.ppermute(value, axis, [(source, source + steps) for source in range(leading, last)])


def on_device(
    charges,
    self_blocks,
    near_blocks,
    near_pairs,
    bases,
    transfers,
    parent_of,
    far_pairs,
    far_coupling,
    par_pairs,
    par_coupling,
):
    leaves, rhs, panels = charges.shape
    rank = bases.shape[1]
    width = rhs * rank
    slots = far_coupling.shape[0]
    pairs = par_coupling.shape[0]
    parents = leaves // 2
    devices = lax.axis_size("sfc")
    rows = devices * parents
    columns = 2 * width + LANES + 3 * width // 2
    vmem = pl.BlockSpec(memory_space=pltpu.VMEM)
    smem = pl.BlockSpec(memory_space=pltpu.SMEM)
    hbm = pl.BlockSpec(memory_space=pltpu.HBM)
    params = pltpu.CompilerParams(vmem_limit_bytes=60 * 1024 * 1024)
    late = pltpu.CompilerParams(vmem_limit_bytes=32 * 1024 * 1024)

    def cost(moved):
        return pl.CostEstimate(flops=4 * moved, bytes_accessed=moved, transcendentals=0)

    following = passed_along(charges, "sfc", -1)
    far_pairs = far_pairs.T
    par_pairs = par_pairs.T
    near_pairs = near_pairs.T
    far_c = jnp.transpose(far_coupling, (1, 2, 0))
    parent_of = parent_of.reshape(1, leaves)

    def like(value, memory=pltpu.VMEM):
        return memory(value.shape, value.dtype)

    send = pl.pallas_call(
        pre_kernel,
        out_shape=jax.ShapeDtypeStruct((rows, columns), BF16),
        in_specs=[hbm] * 8,
        out_specs=vmem,
        scratch_shapes=[
            like(charges),
            like(bases),
            like(transfers),
            like(parent_of),
            like(far_pairs),
            like(far_c),
            like(par_pairs),
            like(par_coupling),
            like(par_pairs, pltpu.SMEM),
            pltpu.SemaphoreType.DMA((9,)),
            pltpu.VMEM((leaves * rhs, rank), F32),
            pltpu.VMEM((leaves * rhs, rank), F32),
            pltpu.VMEM((parents * rhs, rank), F32),
            pltpu.VMEM((pairs * rhs, rank), F32),
            pltpu.VMEM((width, slots), F32),
            pltpu.VMEM((width + LANES, slots), BF16),
        ],
        compiler_params=params,
        cost_estimate=cost(10_000_000),
        name="upward",
    )(charges, bases, transfers, parent_of, far_pairs, far_c, par_pairs, par_coupling)
    send = after(send, [following], 107 << 19)
    got = lax.all_to_all(send, "sfc", split_axis=0, concat_axis=0, tiled=True)
    steps = 4
    selves, nears = leaves // steps, near_blocks.shape[0] // steps
    whole = lambda *shape: pl.BlockSpec(shape, lambda i: (0,) * len(shape))
    near_own, near_away = pl.pallas_call(
        near_kernel,
        grid=(steps,),
        out_shape=[
            jax.ShapeDtypeStruct((leaves, rhs, panels), F32),
            jax.ShapeDtypeStruct((leaves, rhs, panels), BF16),
        ],
        in_specs=[
            smem,
            whole(leaves, rhs, panels),
            whole(leaves, rhs, panels),
            pl.BlockSpec((selves, panels, panels), lambda i: (i, 0, 0)),
            pl.BlockSpec((nears, panels, panels), lambda i: (i, 0, 0)),
        ],
        out_specs=[whole(leaves, rhs, panels)] * 2,
        scratch_shapes=[
            pltpu.VMEM((2 * leaves, rhs, panels), BF16),
            pltpu.VMEM((2 * leaves, rhs, panels), F32),
        ],
        compiler_params=pltpu.CompilerParams(vmem_limit_bytes=52 * 1024 * 1024),
        cost_estimate=cost(20_000_000),
        name="near",
    )(near_pairs, charges, following, self_blocks, near_blocks)
    near_back = passed_along(near_away, "sfc", 1)

    prepared = pl.pallas_call(
        prepare_kernel,
        out_shape=[
            jax.ShapeDtypeStruct(shape, BF16)
            for shape in (
                par_coupling.shape,
                (pairs, rows),
                (parents * rhs, pairs * rhs),
                (leaves * rhs, parents * rhs),
            )
        ],
        in_specs=[pl.BlockSpec(memory_space=pl.ANY)] + [vmem] * 3,
        out_specs=[vmem] * 4,
        compiler_params=late,
        cost_estimate=cost(4_000_000),
        name="prepare",
    )(near_away, par_pairs, parent_of, par_coupling)

    got = after(got, [near_back, *prepared], 1 << 20)
    mom2 = lax.ppermute(
        got[:, 2 * width + LANES :], "sfc", [(i, i ^ 1) for i in range(devices)]
    )

    half, back = pl.pallas_call(
        far_kernel,
        out_shape=[
            jax.ShapeDtypeStruct((leaves, width // 2), F32),
            jax.ShapeDtypeStruct((leaves, width), F32),
        ],
        in_specs=[vmem] * 3,
        out_specs=[vmem] * 2,
        scratch_shapes=[pltpu.VMEM((width // 2, slots), F32)] * 2,
        compiler_params=late,
        cost_estimate=cost(8_000_000),
        name="far",
    )(got, far_pairs, far_c)

    return pl.pallas_call(
        post_kernel,
        out_shape=jax.ShapeDtypeStruct((leaves, rhs, panels), F32),
        in_specs=[smem] + [vmem] * 14,
        out_specs=vmem,
        scratch_shapes=[
            pltpu.VMEM((width // 2, slots), F32),
            pltpu.VMEM((width // 2, slots), F32),
            pltpu.VMEM((pairs * rhs, rank), F32),
            pltpu.VMEM((pairs * rhs, rank), F32),
            pltpu.VMEM((leaves * rhs, rank), F32),
            pltpu.VMEM((parents * rhs, rank), F32),
            pltpu.VMEM((leaves * rhs, rank), F32),
        ],
        compiler_params=late,
        name="downward",
    )(
        far_pairs,
        half,
        back,
        mom2,
        got,
        bases,
        transfers,
        far_pairs,
        far_c,
        *prepared,
        near_own,
        near_back,
    )


def solution(mesh):
    split = ("grp", "sfc")
    cube, flat = P(split, None, None), P(split, None)
    placed = (cube, cube, cube, flat, cube, cube, P(split), flat, cube, flat, cube)
    return jax.shard_map(
        on_device, mesh=mesh, in_specs=placed, out_specs=cube, check_vma=False
    )
```

```python
import functools

import jax
import jax.numpy as jnp
from jax import lax
from jax.experimental import pallas as pl
from jax.experimental.pallas import tpu as pltpu
from jax.sharding import PartitionSpec as P

F32 = jnp.float32
BF16 = jnp.bfloat16
LANES = 128


def dot_nn(a, b):
    return lax.dot_general(a, b, (((1,), (0,)), ((), ())), preferred_element_type=F32)


def dot_nt(a, b):
    return lax.dot_general(a, b, (((1,), (1,)), ((), ())), preferred_element_type=F32)


def dot_tn(a, b):
    return lax.dot_general(a, b, (((0,), (0,)), ((), ())), preferred_element_type=F32)


def split2(x):
    high = x.astype(BF16)
    return high, (x - high.astype(F32)).astype(BF16)


def iota(shape, axis):
    return lax.broadcasted_iota(jnp.int32, shape, axis)


def one_hot(condition):
    return jnp.where(condition, 1.0, 0.0).astype(BF16)


def rows_to_lanes(ref, count, rhs):
    return jnp.concatenate([ref[pl.ds(r, count, stride=rhs), :] for r in range(rhs)], axis=1)


def lanes_to_rows(ref, value, rhs):
    count, width = value.shape
    rank = width // rhs
    for r in range(rhs):
        ref[pl.ds(r, count, stride=rhs), :] = value[:, r * rank : (r + 1) * rank]


def repeated(values, times):
    count = values.shape[1]
    spread = one_hot(iota((count, count * times), 1) // times == iota((count, count * times), 0))
    rows = jnp.broadcast_to(values.astype(F32), (8, count)).astype(BF16)
    return dot_nn(rows, spread)[0:1].astype(jnp.int32)


def by_rows(targets, parents, rhs):
    shape = (parents * rhs, targets.shape[1] * rhs)
    row, column = iota(shape, 0), iota(shape, 1)
    same = (repeated(targets % parents, rhs) == row // rhs) & (row % rhs == column % rhs)
    return jnp.where(same, 1.0, 0.0)


def row_sums(parts):
    row = iota(parts[0].shape, 0)
    for step in (4, 2, 1):
        upper = row % (2 * step) >= step
        merged = []
        for a, b in zip(parts[:step], parts[step:]):
            swapped = jnp.where(upper, a, b)
            if step == 4:
                moved = pltpu.roll(swapped, 4, axis=0)
            else:
                moved = jnp.where(
                    upper,
                    pltpu.roll(swapped, step, axis=0),
                    pltpu.roll(swapped, 8 - step, axis=0),
                )
            merged.append(jnp.where(upper, b, a) + moved)
        parts = merged
    return parts[0]


def fetch(pairs, sems):
    copies = [pltpu.make_async_copy(src, dst, sems.at[i]) for i, (src, dst) in enumerate(pairs)]
    for copy in copies:
        copy.start()
    return copies


def pre_kernel(
    charges_h,
    bases_h,
    transfers_h,
    parent_of_h,
    far_pairs_h,
    far_c_h,
    par_pairs_h,
    par_c_h,
    send,
    charges,
    bases,
    transfers,
    parent_of,
    far_pairs,
    far_c,
    par_pairs,
    par_c,
    par_smem,
    sems,
    mo,
    ch,
    pm3,
    pb,
    a_ref,
    ob,
):
    leaves, rhs, _ = charges.shape
    rank = bases.shape[1]
    width = rhs * rank
    slots = far_c.shape[2]
    pairs = par_c.shape[0]
    parents = leaves // 2
    rows = send.shape[0]
    copies = fetch(
        [
            (parent_of_h, parent_of),
            (charges_h, charges),
            (bases_h, bases),
            (transfers_h, transfers),
            (far_pairs_h, far_pairs),
            (par_pairs_h, par_pairs),
            (par_pairs_h, par_smem),
            (far_c_h, far_c),
            (par_c_h, par_c),
        ],
        sems,
    )
    copies[0].wait()
    to_parent = by_rows(parent_of[...], parents, rhs).astype(BF16)
    for copy in copies[1:4]:
        copy.wait()

    for l in range(leaves):
        m = dot_nt(charges[l], bases[l]).astype(BF16)
        mo[l * rhs : (l + 1) * rhs, :] = m.astype(F32)
        ch[l * rhs : (l + 1) * rhs, :] = dot_nt(m, transfers[l])
    for copy in copies[4:]:
        copy.wait()
    high, low = split2(ch[...])
    pm3[...] = (dot_nn(to_parent, high) + dot_nn(to_parent, low)).astype(BF16).astype(F32)
    m2 = rows_to_lanes(mo, leaves, rhs)
    pm = rows_to_lanes(pm3, parents, rhs)
    half = 3 * width // 2
    shared = [
        jnp.concatenate([x[:, c * width // 2 : (c + 1) * width // 2] for x in (m2[:parents], m2[parents:], pm)], axis=1)
        for c in range(2)
    ]
    shared = jnp.concatenate(shared, axis=0).astype(BF16)
    at = 2 * width + LANES
    for p in range(rows // (2 * parents)):
        send[p * 2 * parents : (p + 1) * 2 * parents, at : at + half] = shared

    owner_hot = one_hot(far_pairs[0:1, :] % leaves == iota((leaves, slots), 0))
    a_ref[...] = dot_tn(m2.astype(BF16), owner_hot)
    for s in range(pairs):
        q = par_smem[0, s] % parents
        x = pm3[pl.ds(pl.multiple_of(q * rhs, rhs), rhs), :].astype(BF16)
        pb[s * rhs : (s + 1) * rhs, :] = dot_nn(x, par_c[s])
    some = rank // 4
    for sb in range(slots // LANES):
        lanes = slice(sb * LANES, (sb + 1) * LANES)
        for first in range(0, rank, some):
            acc = [None] * rhs
            for k in range(rank):
                c = far_c[k, first : first + some, lanes].astype(F32)
                for r in range(rhs):
                    term = c * a_ref[r * rank + k : r * rank + k + 1, lanes]
                    acc[r] = term if k == 0 else acc[r] + term
            for r in range(rhs):
                at = r * rank + first
                ob[at : at + some, lanes] = acc[r].astype(BF16)
    partner = far_pairs[1:2, :]
    local = jnp.where(partner >= 0, partner % leaves, -1).astype(F32)
    ob[width : width + LANES, :] = jnp.broadcast_to(local, (LANES, slots)).astype(BF16)
    unit = one_hot(iota((LANES, LANES), 0) == iota((LANES, LANES), 1))
    for sb in range(slots // LANES):
        lanes = slice(sb * LANES, (sb + 1) * LANES)
        send[lanes, 0 : width + LANES] = dot_nt(unit, ob[:, lanes]).astype(BF16)

    high, low = split2(rows_to_lanes(pb, pairs, rhs))
    hot = one_hot(par_pairs[1:2, :] == iota((rows, pairs), 0))
    at = width + LANES
    send[:, at : at + width] = (dot_nn(hot, high) + dot_nn(hot, low)).astype(BF16)


def near_kernel(pairs, charges, following, self_blocks, near_blocks, own, away, ext, out):
    leaves = charges.shape[0]
    step = pl.program_id(0)
    selves, nears = self_blocks.shape[0], near_blocks.shape[0]

    @pl.when(step == 0)
    def _():
        ext[0:leaves] = charges[...]
        ext[leaves:] = following[...]
        out[...] = jnp.zeros_like(out)

    terms = [(step * selves + i, dot_nt(ext[step * selves + i], self_blocks[i])) for i in range(selves)]
    for i in range(nears):
        a, b = pairs[0, step * nears + i], pairs[1, step * nears + i]
        first = (a // leaves) * leaves
        a, b = a - first, b - first
        terms.append((a, dot_nt(ext[b], near_blocks[i])))
        terms.append((b, dot_nn(ext[a], near_blocks[i])))
    for at, term in terms:
        out[at] += term

    @pl.when(step == pl.num_programs(0) - 1)
    def _():
        own[...] = out[0:leaves]
        away[...] = out[leaves:].astype(BF16)


def far_half(mom, far_pairs, far_c, b_ref, fw, leaves, parents):
    rows, slots = mom.shape[0], far_c.shape[2]
    rank = far_c.shape[0]
    wide = mom.shape[1] // 3
    some = wide // rank
    row_id = iota((rows, slots), 0)
    base_leaf = row_id // parents * leaves + row_id % parents
    partner = far_pairs[1:2, :]
    total = None
    for h in range(2):
        hot = one_hot(partner == base_leaf + h * parents)
        part = dot_tn(mom[:, h * wide : (h + 1) * wide], hot)
        total = part if total is None else total + part
    b_ref[...] = total

    for sb in range(slots // LANES):
        lanes = slice(sb * LANES, (sb + 1) * LANES)

        def body(k8, carry):
            parts = [[] for _ in range(some)]
            for i in range(8):
                c = far_c[k8 * 8 + i, :, lanes].astype(F32)
                for r in range(some):
                    prod = c * b_ref[r * rank : (r + 1) * rank, lanes]
                    parts[r].append(sum(prod[j * 8 : (j + 1) * 8] for j in range(rank // 8)))
            for r in range(some):
                fw[pl.ds(pl.multiple_of(r * rank + k8 * 8, 8), 8), lanes] = row_sums(parts[r])
            return carry

        lax.fori_loop(0, rank // 8, body, 0, unroll=8)

    hot = one_hot(far_pairs[0:1, :] % leaves == iota((leaves, slots), 0))
    high, low = split2(fw[...])
    return dot_nt(hot, high) + dot_nt(hot, low)


def far_kernel(got, far_pairs, far_c, half, back, b_ref, fw):
    leaves, width = back.shape
    parents = leaves // 2
    rows = got.shape[0]
    index = got[:, width : width + LANES].astype(F32)[:, :leaves].astype(jnp.int32)
    hot = one_hot(index == iota((rows, leaves), 1))
    back[...] = dot_tn(hot, got[:, 0:width])
    mom = got[:, 2 * width + LANES :]
    half[...] = far_half(mom, far_pairs, far_c, b_ref, fw, leaves, parents)


def prepare_kernel(
    near_own, near_back, par_pairs, parent_of, par_c, near, par_t, pick, to_owner, to_leaf
):
    pairs = par_c.shape[0]
    rows = pick.shape[1]
    leaves = parent_of.shape[1]
    parents = leaves // 2
    rhs = to_owner.shape[0] // parents
    near[...] = near_own[...] + near_back[...].astype(F32)
    for s in range(pairs):
        par_t[s] = par_c[s].astype(F32).T.astype(BF16)
    hot = jnp.where(par_pairs[1:2, :] == iota((rows, pairs), 0), 1.0, 0.0)
    pick[...] = hot.T.astype(BF16)

    to_owner[...] = by_rows(par_pairs[0:1, :], parents, rhs).astype(BF16)
    to_leaf[...] = by_rows(parent_of[...], parents, rhs).T.astype(BF16)


def post_kernel(
    core_smem,
    half,
    back,
    mom2,
    got,
    bases,
    transfers,
    far_pairs,
    far_c,
    par_t,
    pick,
    to_owner,
    to_leaf,
    near,
    out,
    b_ref,
    fw,
    g_ref,
    pf,
    lf,
    pb,
    dn,
):
    leaves, rank, _ = bases.shape
    width = back.shape[1]
    rhs = width // rank
    pairs = par_t.shape[0]
    parents = leaves // 2
    rows = got.shape[0]
    core = core_smem[0, 0] // leaves % 2

    def in_order(mine, other):
        return jnp.concatenate(
            [jnp.where(core == 0, mine, other), jnp.where(core == 0, other, mine)], axis=1
        )

    wide = mom2.shape[1] // 3
    shared = in_order(got[:, got.shape[1] - wide :], mom2[:, 2 * wide :])
    fold = one_hot(iota((parents, rows), 1) % parents == iota((parents, rows), 0))
    at = width + LANES
    lanes_to_rows(pb, dot_nn(fold, got[:, at : at + width]), rhs)
    lanes_to_rows(g_ref, dot_nn(pick[...], shared), rhs)
    for s in range(pairs):
        at = slice(s * rhs, (s + 1) * rhs)
        pf[at, :] = dot_nn(g_ref[at, :].astype(BF16), par_t[s])
    high, low = split2(pf[...])
    locals_p = dot_nn(to_owner[...], high) + dot_nn(to_owner[...], low) + pb[...]
    picked = dot_nn(to_leaf[...], locals_p.astype(BF16)).astype(BF16)
    for l in range(leaves):
        at = slice(l * rhs, (l + 1) * rhs)
        dn[at, :] = dot_nn(picked[at, :], transfers[l])

    other = far_half(mom2[...], far_pairs, far_c, b_ref, fw, leaves, parents)
    lanes_to_rows(lf, back[...] + in_order(half[...], other), rhs)
    for l in range(leaves):
        at = slice(l * rhs, (l + 1) * rhs)
        mine = (lf[at, :] + dn[at, :]).astype(BF16)
        out[l] = dot_nn(mine, bases[l]) + near[l]


def after(value, earlier, vmem_limit):
    anywhere = pl.BlockSpec(memory_space=pl.ANY)
    return pl.pallas_call(
        lambda *refs: None,
        out_shape=jax.ShapeDtypeStruct(value.shape, value.dtype),
        in_specs=[anywhere] * (1 + len(earlier)),
        out_specs=anywhere,
        input_output_aliases={0: 0},
        compiler_params=pltpu.CompilerParams(vmem_limit_bytes=vmem_limit),
        name="after",
    )(value, *earlier)


def passed_along(value, axis, steps):
    count = lax.axis_size(axis)
    leading, last = (max(0, -steps), min(count, count - steps))
    return lax.ppermute(value, axis, [(source, source + steps) for source in range(leading, last)])


def on_device(
    charges,
    self_blocks,
    near_blocks,
    near_pairs,
    bases,
    transfers,
    parent_of,
    far_pairs,
    far_coupling,
    par_pairs,
    par_coupling,
):
    leaves, rhs, panels = charges.shape
    rank = bases.shape[1]
    width = rhs * rank
    slots = far_coupling.shape[0]
    pairs = par_coupling.shape[0]
    parents = leaves // 2
    devices = lax.axis_size("sfc")
    rows = devices * parents
    columns = 2 * width + LANES + 3 * width // 2
    vmem = pl.BlockSpec(memory_space=pltpu.VMEM)
    smem = pl.BlockSpec(memory_space=pltpu.SMEM)
    hbm = pl.BlockSpec(memory_space=pltpu.HBM)
    params = pltpu.CompilerParams(vmem_limit_bytes=60 * 1024 * 1024)
    late = pltpu.CompilerParams(vmem_limit_bytes=32 * 1024 * 1024)

    def cost(moved):
        return pl.CostEstimate(flops=4 * moved, bytes_accessed=moved, transcendentals=0)

    following = passed_along(charges, "sfc", -1)
    far_pairs = far_pairs.T
    par_pairs = par_pairs.T
    near_pairs = near_pairs.T
    far_c = jnp.transpose(far_coupling, (1, 2, 0))
    parent_of = parent_of.reshape(1, leaves)

    def like(value, memory=pltpu.VMEM):
        return memory(value.shape, value.dtype)

    send = pl.pallas_call(
        pre_kernel,
        out_shape=jax.ShapeDtypeStruct((rows, columns), BF16),
        in_specs=[hbm] * 8,
        out_specs=vmem,
        scratch_shapes=[
            like(charges),
            like(bases),
            like(transfers),
            like(parent_of),
            like(far_pairs),
            like(far_c),
            like(par_pairs),
            like(par_coupling),
            like(par_pairs, pltpu.SMEM),
            pltpu.SemaphoreType.DMA((9,)),
            pltpu.VMEM((leaves * rhs, rank), F32),
            pltpu.VMEM((leaves * rhs, rank), F32),
            pltpu.VMEM((parents * rhs, rank), F32),
            pltpu.VMEM((pairs * rhs, rank), F32),
            pltpu.VMEM((width, slots), F32),
            pltpu.VMEM((width + LANES, slots), BF16),
        ],
        compiler_params=params,
        cost_estimate=cost(10_000_000),
        name="upward",
    )(charges, bases, transfers, parent_of, far_pairs, far_c, par_pairs, par_coupling)
    send = after(send, [following], 107 << 19)
    got = lax.all_to_all(send, "sfc", split_axis=0, concat_axis=0, tiled=True)
    steps = 4
    selves, nears = leaves // steps, near_blocks.shape[0] // steps
    whole = lambda *shape: pl.BlockSpec(shape, lambda i: (0,) * len(shape))
    near_own, near_away = pl.pallas_call(
        near_kernel,
        grid=(steps,),
        out_shape=[
            jax.ShapeDtypeStruct((leaves, rhs, panels), F32),
            jax.ShapeDtypeStruct((leaves, rhs, panels), BF16),
        ],
        in_specs=[
            smem,
            whole(leaves, rhs, panels),
            whole(leaves, rhs, panels),
            pl.BlockSpec((selves, panels, panels), lambda i: (i, 0, 0)),
            pl.BlockSpec((nears, panels, panels), lambda i: (i, 0, 0)),
        ],
        out_specs=[whole(leaves, rhs, panels)] * 2,
        scratch_shapes=[
            pltpu.VMEM((2 * leaves, rhs, panels), BF16),
            pltpu.VMEM((2 * leaves, rhs, panels), F32),
        ],
        compiler_params=pltpu.CompilerParams(vmem_limit_bytes=52 * 1024 * 1024),
        cost_estimate=cost(20_000_000),
        name="near",
    )(near_pairs, charges, following, self_blocks, near_blocks)
    near_back = passed_along(near_away, "sfc", 1)

    near, *prepared = pl.pallas_call(
        prepare_kernel,
        out_shape=[jax.ShapeDtypeStruct(near_own.shape, F32)]
        + [
            jax.ShapeDtypeStruct(shape, BF16)
            for shape in (
                par_coupling.shape,
                (pairs, rows),
                (parents * rhs, pairs * rhs),
                (leaves * rhs, parents * rhs),
            )
        ],
        in_specs=[vmem] * 5,
        out_specs=[vmem] * 5,
        compiler_params=late,
        cost_estimate=cost(4_000_000),
        name="prepare",
    )(near_own, near_back, par_pairs, parent_of, par_coupling)

    got = after(got, [near, *prepared], 1 << 20)
    mom2 = lax.ppermute(
        got[:, 2 * width + LANES :], "sfc", [(i, i ^ 1) for i in range(devices)]
    )

    half, back = pl.pallas_call(
        far_kernel,
        out_shape=[
            jax.ShapeDtypeStruct((leaves, width // 2), F32),
            jax.ShapeDtypeStruct((leaves, width), F32),
        ],
        in_specs=[vmem] * 3,
        out_specs=[vmem] * 2,
        scratch_shapes=[pltpu.VMEM((width // 2, slots), F32)] * 2,
        compiler_params=late,
        cost_estimate=cost(8_000_000),
        name="far",
    )(got, far_pairs, far_c)

    return pl.pallas_call(
        post_kernel,
        out_shape=jax.ShapeDtypeStruct((leaves, rhs, panels), F32),
        in_specs=[smem] + [vmem] * 13,
        out_specs=vmem,
        scratch_shapes=[
            pltpu.VMEM((width // 2, slots), F32),
            pltpu.VMEM((width // 2, slots), F32),
            pltpu.VMEM((pairs * rhs, rank), F32),
            pltpu.VMEM((pairs * rhs, rank), F32),
            pltpu.VMEM((leaves * rhs, rank), F32),
            pltpu.VMEM((parents * rhs, rank), F32),
            pltpu.VMEM((leaves * rhs, rank), F32),
        ],
        compiler_params=late,
        name="downward",
    )(
        far_pairs,
        half,
        back,
        mom2,
        got,
        bases,
        transfers,
        far_pairs,
        far_c,
        *prepared,
        near,
    )


def solution(mesh):
    split = ("grp", "sfc")
    cube, flat = P(split, None, None), P(split, None)
    placed = (cube, cube, cube, flat, cube, cube, P(split), flat, cube, flat, cube)
    return jax.shard_map(
        on_device, mesh=mesh, in_specs=placed, out_specs=cube, check_vma=False
    )
```

```python
import functools

import jax
import jax.numpy as jnp
from jax import lax
from jax.experimental import pallas as pl
from jax.experimental.pallas import tpu as pltpu
from jax.sharding import PartitionSpec as P

F32 = jnp.float32
BF16 = jnp.bfloat16
LANES = 128


def dot_nn(a, b):
    return lax.dot_general(a, b, (((1,), (0,)), ((), ())), preferred_element_type=F32)


def dot_nt(a, b):
    return lax.dot_general(a, b, (((1,), (1,)), ((), ())), preferred_element_type=F32)


def dot_tn(a, b):
    return lax.dot_general(a, b, (((0,), (0,)), ((), ())), preferred_element_type=F32)


def split2(x):
    high = x.astype(BF16)
    return high, (x - high.astype(F32)).astype(BF16)


def iota(shape, axis):
    return lax.broadcasted_iota(jnp.int32, shape, axis)


def one_hot(condition):
    return jnp.where(condition, 1.0, 0.0).astype(BF16)


def rows_to_lanes(ref, count, rhs):
    return jnp.concatenate([ref[pl.ds(r, count, stride=rhs), :] for r in range(rhs)], axis=1)


def lanes_to_rows(ref, value, rhs):
    count, width = value.shape
    rank = width // rhs
    for r in range(rhs):
        ref[pl.ds(r, count, stride=rhs), :] = value[:, r * rank : (r + 1) * rank]


def repeated(values, times):
    count = values.shape[1]
    spread = one_hot(iota((count, count * times), 1) // times == iota((count, count * times), 0))
    rows = jnp.broadcast_to(values.astype(F32), (8, count)).astype(BF16)
    return dot_nn(rows, spread)[0:1].astype(jnp.int32)


def by_rows(targets, parents, rhs):
    shape = (parents * rhs, targets.shape[1] * rhs)
    row, column = iota(shape, 0), iota(shape, 1)
    same = (repeated(targets % parents, rhs) == row // rhs) & (row % rhs == column % rhs)
    return jnp.where(same, 1.0, 0.0)


def row_sums(parts):
    row = iota(parts[0].shape, 0)
    for step in (4, 2, 1):
        upper = row % (2 * step) >= step
        merged = []
        for a, b in zip(parts[:step], parts[step:]):
            swapped = jnp.where(upper, a, b)
            if step == 4:
                moved = pltpu.roll(swapped, 4, axis=0)
            else:
                moved = jnp.where(
                    upper,
                    pltpu.roll(swapped, step, axis=0),
                    pltpu.roll(swapped, 8 - step, axis=0),
                )
            merged.append(jnp.where(upper, b, a) + moved)
        parts = merged
    return parts[0]


def fetch(pairs, sems):
    copies = [pltpu.make_async_copy(src, dst, sems.at[i]) for i, (src, dst) in enumerate(pairs)]
    for copy in copies:
        copy.start()
    return copies


def pre_kernel(
    charges_h,
    bases_h,
    transfers_h,
    parent_of_h,
    far_pairs_h,
    far_c_h,
    par_pairs_h,
    par_c_h,
    send,
    charges,
    bases,
    transfers,
    parent_of,
    far_pairs,
    far_c,
    par_pairs,
    par_c,
    par_smem,
    sems,
    mo,
    ch,
    pm3,
    pb,
    a_ref,
    ob,
):
    leaves, rhs, _ = charges.shape
    rank = bases.shape[1]
    width = rhs * rank
    slots = far_c.shape[2]
    pairs = par_c.shape[0]
    parents = leaves // 2
    rows = send.shape[0]
    copies = fetch(
        [
            (parent_of_h, parent_of),
            (charges_h, charges),
            (bases_h, bases),
            (transfers_h, transfers),
            (far_pairs_h, far_pairs),
            (par_pairs_h, par_pairs),
            (par_pairs_h, par_smem),
            (far_c_h, far_c),
            (par_c_h, par_c),
        ],
        sems,
    )
    copies[0].wait()
    to_parent = by_rows(parent_of[...], parents, rhs).astype(BF16)
    for copy in copies[1:4]:
        copy.wait()

    for l in range(leaves):
        m = dot_nt(charges[l], bases[l]).astype(BF16)
        mo[l * rhs : (l + 1) * rhs, :] = m.astype(F32)
        ch[l * rhs : (l + 1) * rhs, :] = dot_nt(m, transfers[l])
    for copy in copies[4:]:
        copy.wait()
    high, low = split2(ch[...])
    pm3[...] = (dot_nn(to_parent, high) + dot_nn(to_parent, low)).astype(BF16).astype(F32)
    m2 = rows_to_lanes(mo, leaves, rhs)
    pm = rows_to_lanes(pm3, parents, rhs)
    half = 3 * width // 2
    shared = [
        jnp.concatenate([x[:, c * width // 2 : (c + 1) * width // 2] for x in (m2[:parents], m2[parents:], pm)], axis=1)
        for c in range(2)
    ]
    shared = jnp.concatenate(shared, axis=0).astype(BF16)
    at = 2 * width + LANES
    for p in range(rows // (2 * parents)):
        send[p * 2 * parents : (p + 1) * 2 * parents, at : at + half] = shared

    owner_hot = one_hot(far_pairs[0:1, :] % leaves == iota((leaves, slots), 0))
    a_ref[...] = dot_tn(m2.astype(BF16), owner_hot)
    for s in range(pairs):
        q = par_smem[0, s] % parents
        x = pm3[pl.ds(pl.multiple_of(q * rhs, rhs), rhs), :].astype(BF16)
        pb[s * rhs : (s + 1) * rhs, :] = dot_nn(x, par_c[s])
    some = rank // 4
    for sb in range(slots // LANES):
        lanes = slice(sb * LANES, (sb + 1) * LANES)
        for first in range(0, rank, some):
            acc = [None] * rhs
            for k in range(rank):
                c = far_c[k, first : first + some, lanes].astype(F32)
                for r in range(rhs):
                    term = c * a_ref[r * rank + k : r * rank + k + 1, lanes]
                    acc[r] = term if k == 0 else acc[r] + term
            for r in range(rhs):
                at = r * rank + first
                ob[at : at + some, lanes] = acc[r].astype(BF16)
    partner = far_pairs[1:2, :]
    local = jnp.where(partner >= 0, partner % leaves, -1).astype(F32)
    ob[width : width + LANES, :] = jnp.broadcast_to(local, (LANES, slots)).astype(BF16)
    unit = one_hot(iota((LANES, LANES), 0) == iota((LANES, LANES), 1))
    for sb in range(slots // LANES):
        lanes = slice(sb * LANES, (sb + 1) * LANES)
        send[lanes, 0 : width + LANES] = dot_nt(unit, ob[:, lanes]).astype(BF16)

    high, low = split2(rows_to_lanes(pb, pairs, rhs))
    hot = one_hot(par_pairs[1:2, :] == iota((rows, pairs), 0))
    at = width + LANES
    send[:, at : at + width] = (dot_nn(hot, high) + dot_nn(hot, low)).astype(BF16)


def near_kernel(pairs, charges, following, self_blocks, near_blocks, own, away, ext, out):
    leaves = charges.shape[0]
    step = pl.program_id(0)
    selves, nears = self_blocks.shape[0], near_blocks.shape[0]

    @pl.when(step == 0)
    def _():
        ext[0:leaves] = charges[...]
        ext[leaves:] = following[...]
        out[...] = jnp.zeros_like(out)

    terms = [(step * selves + i, dot_nt(ext[step * selves + i], self_blocks[i])) for i in range(selves)]
    for i in range(nears):
        a, b = pairs[0, step * nears + i], pairs[1, step * nears + i]
        first = (a // leaves) * leaves
        a, b = a - first, b - first
        terms.append((a, dot_nt(ext[b], near_blocks[i])))
        terms.append((b, dot_nn(ext[a], near_blocks[i])))
    for at, term in terms:
        out[at] += term

    @pl.when(step == pl.num_programs(0) - 1)
    def _():
        own[...] = out[0:leaves]
        away[...] = out[leaves:].astype(BF16)


def far_half(mom, far_pairs, far_c, b_ref, fw, leaves, parents):
    rows, slots = mom.shape[0], far_c.shape[2]
    rank = far_c.shape[0]
    wide = mom.shape[1] // 3
    some = wide // rank
    row_id = iota((rows, slots), 0)
    base_leaf = row_id // parents * leaves + row_id % parents
    partner = far_pairs[1:2, :]
    total = None
    for h in range(2):
        hot = one_hot(partner == base_leaf + h * parents)
        part = dot_tn(mom[:, h * wide : (h + 1) * wide], hot)
        total = part if total is None else total + part
    b_ref[...] = total

    for sb in range(slots // LANES):
        lanes = slice(sb * LANES, (sb + 1) * LANES)

        def body(k8, carry):
            parts = [[] for _ in range(some)]
            for i in range(8):
                c = far_c[k8 * 8 + i, :, lanes].astype(F32)
                for r in range(some):
                    prod = c * b_ref[r * rank : (r + 1) * rank, lanes]
                    parts[r].append(sum(prod[j * 8 : (j + 1) * 8] for j in range(rank // 8)))
            for r in range(some):
                fw[pl.ds(pl.multiple_of(r * rank + k8 * 8, 8), 8), lanes] = row_sums(parts[r])
            return carry

        lax.fori_loop(0, rank // 8, body, 0, unroll=8)

    hot = one_hot(far_pairs[0:1, :] % leaves == iota((leaves, slots), 0))
    high, low = split2(fw[...])
    return dot_nt(hot, high) + dot_nt(hot, low)


def far_kernel(
    got,
    far_pairs,
    far_c,
    par_pairs,
    parent_of,
    par_c,
    half,
    back,
    par_t,
    pick,
    to_owner,
    to_leaf,
    b_ref,
    fw,
):
    leaves, width = back.shape
    parents = leaves // 2
    rows = got.shape[0]
    index = got[:, width : width + LANES].astype(F32)[:, :leaves].astype(jnp.int32)
    hot = one_hot(index == iota((rows, leaves), 1))
    back[...] = dot_tn(hot, got[:, 0:width])
    mom = got[:, 2 * width + LANES :]
    half[...] = far_half(mom, far_pairs, far_c, b_ref, fw, leaves, parents)

    pairs = par_c.shape[0]
    rhs = to_owner.shape[0] // parents
    for s in range(pairs):
        par_t[s] = par_c[s].astype(F32).T.astype(BF16)
    hot = jnp.where(par_pairs[1:2, :] == iota((rows, pairs), 0), 1.0, 0.0)
    pick[...] = hot.T.astype(BF16)
    to_owner[...] = by_rows(par_pairs[0:1, :], parents, rhs).astype(BF16)
    to_leaf[...] = by_rows(parent_of[...], parents, rhs).T.astype(BF16)


def post_kernel(
    core_smem,
    half,
    back,
    mom2,
    got,
    bases,
    transfers,
    far_pairs,
    far_c,
    par_t,
    pick,
    to_owner,
    to_leaf,
    near_own,
    near_back,
    out,
    b_ref,
    fw,
    g_ref,
    pf,
    lf,
    pb,
    dn,
):
    leaves, rank, _ = bases.shape
    width = back.shape[1]
    rhs = width // rank
    pairs = par_t.shape[0]
    parents = leaves // 2
    rows = got.shape[0]
    core = core_smem[0, 0] // leaves % 2

    def in_order(mine, other):
        return jnp.concatenate(
            [jnp.where(core == 0, mine, other), jnp.where(core == 0, other, mine)], axis=1
        )

    wide = mom2.shape[1] // 3
    shared = in_order(got[:, got.shape[1] - wide :], mom2[:, 2 * wide :])
    fold = one_hot(iota((parents, rows), 1) % parents == iota((parents, rows), 0))
    at = width + LANES
    lanes_to_rows(pb, dot_nn(fold, got[:, at : at + width]), rhs)
    lanes_to_rows(g_ref, dot_nn(pick[...], shared), rhs)
    for s in range(pairs):
        at = slice(s * rhs, (s + 1) * rhs)
        pf[at, :] = dot_nn(g_ref[at, :].astype(BF16), par_t[s])
    high, low = split2(pf[...])
    locals_p = dot_nn(to_owner[...], high) + dot_nn(to_owner[...], low) + pb[...]
    picked = dot_nn(to_leaf[...], locals_p.astype(BF16)).astype(BF16)
    for l in range(leaves):
        at = slice(l * rhs, (l + 1) * rhs)
        dn[at, :] = dot_nn(picked[at, :], transfers[l])

    other = far_half(mom2[...], far_pairs, far_c, b_ref, fw, leaves, parents)
    lanes_to_rows(lf, back[...] + in_order(half[...], other), rhs)
    for l in range(leaves):
        at = slice(l * rhs, (l + 1) * rhs)
        mine = (lf[at, :] + dn[at, :]).astype(BF16)
        near = near_own[l] + near_back[l].astype(F32)
        out[l] = dot_nn(mine, bases[l]) + near


def after(value, earlier, vmem_limit):
    anywhere = pl.BlockSpec(memory_space=pl.ANY)
    return pl.pallas_call(
        lambda *refs: None,
        out_shape=jax.ShapeDtypeStruct(value.shape, value.dtype),
        in_specs=[anywhere] * (1 + len(earlier)),
        out_specs=anywhere,
        input_output_aliases={0: 0},
        compiler_params=pltpu.CompilerParams(vmem_limit_bytes=vmem_limit),
        name="after",
    )(value, *earlier)


def passed_along(value, axis, steps):
    count = lax.axis_size(axis)
    leading, last = (max(0, -steps), min(count, count - steps))
    return lax.ppermute(value, axis, [(source, source + steps) for source in range(leading, last)])


def on_device(
    charges,
    self_blocks,
    near_blocks,
    near_pairs,
    bases,
    transfers,
    parent_of,
    far_pairs,
    far_coupling,
    par_pairs,
    par_coupling,
):
    leaves, rhs, panels = charges.shape
    rank = bases.shape[1]
    width = rhs * rank
    slots = far_coupling.shape[0]
    pairs = par_coupling.shape[0]
    parents = leaves // 2
    devices = lax.axis_size("sfc")
    rows = devices * parents
    columns = 2 * width + LANES + 3 * width // 2
    vmem = pl.BlockSpec(memory_space=pltpu.VMEM)
    smem = pl.BlockSpec(memory_space=pltpu.SMEM)
    hbm = pl.BlockSpec(memory_space=pltpu.HBM)
    params = pltpu.CompilerParams(vmem_limit_bytes=60 * 1024 * 1024)
    late = pltpu.CompilerParams(vmem_limit_bytes=48 * 1024 * 1024)

    def cost(moved):
        return pl.CostEstimate(flops=4 * moved, bytes_accessed=moved, transcendentals=0)

    following = passed_along(charges, "sfc", -1)
    far_pairs = far_pairs.T
    par_pairs = par_pairs.T
    near_pairs = near_pairs.T
    far_c = jnp.transpose(far_coupling, (1, 2, 0))
    parent_of = parent_of.reshape(1, leaves)

    def like(value, memory=pltpu.VMEM):
        return memory(value.shape, value.dtype)

    send = pl.pallas_call(
        pre_kernel,
        out_shape=jax.ShapeDtypeStruct((rows, columns), BF16),
        in_specs=[hbm] * 8,
        out_specs=vmem,
        scratch_shapes=[
            like(charges),
            like(bases),
            like(transfers),
            like(parent_of),
            like(far_pairs),
            like(far_c),
            like(par_pairs),
            like(par_coupling),
            like(par_pairs, pltpu.SMEM),
            pltpu.SemaphoreType.DMA((9,)),
            pltpu.VMEM((leaves * rhs, rank), F32),
            pltpu.VMEM((leaves * rhs, rank), F32),
            pltpu.VMEM((parents * rhs, rank), F32),
            pltpu.VMEM((pairs * rhs, rank), F32),
            pltpu.VMEM((width, slots), F32),
            pltpu.VMEM((width + LANES, slots), BF16),
        ],
        compiler_params=params,
        cost_estimate=cost(10_000_000),
        name="upward",
    )(charges, bases, transfers, parent_of, far_pairs, far_c, par_pairs, par_coupling)
    send = after(send, [following], 107 << 19)
    got = lax.all_to_all(send, "sfc", split_axis=0, concat_axis=0, tiled=True)
    steps = 4
    selves, nears = leaves // steps, near_blocks.shape[0] // steps
    whole = lambda *shape: pl.BlockSpec(shape, lambda i: (0,) * len(shape))
    near_own, near_away = pl.pallas_call(
        near_kernel,
        grid=(steps,),
        out_shape=[
            jax.ShapeDtypeStruct((leaves, rhs, panels), F32),
            jax.ShapeDtypeStruct((leaves, rhs, panels), BF16),
        ],
        in_specs=[
            smem,
            whole(leaves, rhs, panels),
            whole(leaves, rhs, panels),
            pl.BlockSpec((selves, panels, panels), lambda i: (i, 0, 0)),
            pl.BlockSpec((nears, panels, panels), lambda i: (i, 0, 0)),
        ],
        out_specs=[whole(leaves, rhs, panels)] * 2,
        scratch_shapes=[
            pltpu.VMEM((2 * leaves, rhs, panels), BF16),
            pltpu.VMEM((2 * leaves, rhs, panels), F32),
        ],
        compiler_params=pltpu.CompilerParams(vmem_limit_bytes=52 * 1024 * 1024),
        cost_estimate=cost(20_000_000),
        name="near",
    )(near_pairs, charges, following, self_blocks, near_blocks)
    near_back = passed_along(near_away, "sfc", 1)

    got = after(got, [near_back], 1 << 20)
    mom2 = lax.ppermute(
        got[:, 2 * width + LANES :], "sfc", [(i, i ^ 1) for i in range(devices)]
    )

    half, back, *prepared = pl.pallas_call(
        far_kernel,
        out_shape=[
            jax.ShapeDtypeStruct((leaves, width // 2), F32),
            jax.ShapeDtypeStruct((leaves, width), F32),
            jax.ShapeDtypeStruct(par_coupling.shape, BF16),
            jax.ShapeDtypeStruct((pairs, rows), BF16),
            jax.ShapeDtypeStruct((parents * rhs, pairs * rhs), BF16),
            jax.ShapeDtypeStruct((leaves * rhs, parents * rhs), BF16),
        ],
        in_specs=[vmem] * 6,
        out_specs=[vmem] * 6,
        scratch_shapes=[pltpu.VMEM((width // 2, slots), F32)] * 2,
        compiler_params=late,
        cost_estimate=cost(8_000_000),
        name="far",
    )(got, far_pairs, far_c, par_pairs, parent_of, par_coupling)

    return pl.pallas_call(
        post_kernel,
        out_shape=jax.ShapeDtypeStruct((leaves, rhs, panels), F32),
        in_specs=[smem] + [vmem] * 14,
        out_specs=vmem,
        scratch_shapes=[
            pltpu.VMEM((width // 2, slots), F32),
            pltpu.VMEM((width // 2, slots), F32),
            pltpu.VMEM((pairs * rhs, rank), F32),
            pltpu.VMEM((pairs * rhs, rank), F32),
            pltpu.VMEM((leaves * rhs, rank), F32),
            pltpu.VMEM((parents * rhs, rank), F32),
            pltpu.VMEM((leaves * rhs, rank), F32),
        ],
        compiler_params=late,
        name="downward",
    )(
        far_pairs,
        half,
        back,
        mom2,
        got,
        bases,
        transfers,
        far_pairs,
        far_c,
        *prepared,
        near_own,
        near_back,
    )


def solution(mesh):
    split = ("grp", "sfc")
    cube, flat = P(split, None, None), P(split, None)
    placed = (cube, cube, cube, flat, cube, cube, P(split), flat, cube, flat, cube)
    return jax.shard_map(
        on_device, mesh=mesh, in_specs=placed, out_specs=cube, check_vma=False
    )
```

```python
import functools

import jax
import jax.numpy as jnp
from jax import lax
from jax.experimental import pallas as pl
from jax.experimental.pallas import tpu as pltpu
from jax.sharding import PartitionSpec as P

F32 = jnp.float32
BF16 = jnp.bfloat16
LANES = 128


def dot_nn(a, b):
    return lax.dot_general(a, b, (((1,), (0,)), ((), ())), preferred_element_type=F32)


def dot_nt(a, b):
    return lax.dot_general(a, b, (((1,), (1,)), ((), ())), preferred_element_type=F32)


def dot_tn(a, b):
    return lax.dot_general(a, b, (((0,), (0,)), ((), ())), preferred_element_type=F32)


def split2(x):
    high = x.astype(BF16)
    return high, (x - high.astype(F32)).astype(BF16)


def iota(shape, axis):
    return lax.broadcasted_iota(jnp.int32, shape, axis)


def one_hot(condition):
    return jnp.where(condition, 1.0, 0.0).astype(BF16)


def rows_to_lanes(ref, count, rhs):
    return jnp.concatenate([ref[pl.ds(r, count, stride=rhs), :] for r in range(rhs)], axis=1)


def lanes_to_rows(ref, value, rhs):
    count, width = value.shape
    rank = width // rhs
    for r in range(rhs):
        ref[pl.ds(r, count, stride=rhs), :] = value[:, r * rank : (r + 1) * rank]


def repeated(values, times):
    count = values.shape[1]
    spread = one_hot(iota((count, count * times), 1) // times == iota((count, count * times), 0))
    rows = jnp.broadcast_to(values.astype(F32), (8, count)).astype(BF16)
    return dot_nn(rows, spread)[0:1].astype(jnp.int32)


def by_rows(targets, parents, rhs):
    shape = (parents * rhs, targets.shape[1] * rhs)
    row, column = iota(shape, 0), iota(shape, 1)
    same = (repeated(targets % parents, rhs) == row // rhs) & (row % rhs == column % rhs)
    return jnp.where(same, 1.0, 0.0)


def row_sums(parts):
    row = iota(parts[0].shape, 0)
    for step in (4, 2, 1):
        upper = row % (2 * step) >= step
        merged = []
        for a, b in zip(parts[:step], parts[step:]):
            swapped = jnp.where(upper, a, b)
            if step == 4:
                moved = pltpu.roll(swapped, 4, axis=0)
            else:
                moved = jnp.where(
                    upper,
                    pltpu.roll(swapped, step, axis=0),
                    pltpu.roll(swapped, 8 - step, axis=0),
                )
            merged.append(jnp.where(upper, b, a) + moved)
        parts = merged
    return parts[0]


def fetch(pairs, sems):
    copies = [pltpu.make_async_copy(src, dst, sems.at[i]) for i, (src, dst) in enumerate(pairs)]
    for copy in copies:
        copy.start()
    return copies


def pre_kernel(
    charges_h,
    bases_h,
    transfers_h,
    parent_of_h,
    far_pairs_h,
    far_c_h,
    par_pairs_h,
    par_c_h,
    send,
    charges,
    bases,
    transfers,
    parent_of,
    far_pairs,
    far_c,
    par_pairs,
    par_c,
    par_smem,
    sems,
    mo,
    ch,
    pm3,
    pb,
    a_ref,
    ob,
):
    leaves, rhs, _ = charges.shape
    rank = bases.shape[1]
    width = rhs * rank
    slots = far_c.shape[2]
    pairs = par_c.shape[0]
    parents = leaves // 2
    rows = send.shape[0]
    copies = fetch(
        [
            (parent_of_h, parent_of),
            (charges_h, charges),
            (bases_h, bases),
            (transfers_h, transfers),
            (far_pairs_h, far_pairs),
            (par_pairs_h, par_pairs),
            (par_pairs_h, par_smem),
            (far_c_h, far_c),
            (par_c_h, par_c),
        ],
        sems,
    )
    copies[0].wait()
    to_parent = by_rows(parent_of[...], parents, rhs).astype(BF16)
    for copy in copies[1:4]:
        copy.wait()

    for l in range(leaves):
        m = dot_nt(charges[l], bases[l]).astype(BF16)
        mo[l * rhs : (l + 1) * rhs, :] = m.astype(F32)
        ch[l * rhs : (l + 1) * rhs, :] = dot_nt(m, transfers[l])
    for copy in copies[4:]:
        copy.wait()
    high, low = split2(ch[...])
    pm3[...] = (dot_nn(to_parent, high) + dot_nn(to_parent, low)).astype(BF16).astype(F32)
    m2 = rows_to_lanes(mo, leaves, rhs)
    pm = rows_to_lanes(pm3, parents, rhs)
    half = 3 * width // 2
    shared = [
        jnp.concatenate([x[:, c * width // 2 : (c + 1) * width // 2] for x in (m2[:parents], m2[parents:], pm)], axis=1)
        for c in range(2)
    ]
    shared = jnp.concatenate(shared, axis=0).astype(BF16)
    at = 2 * width + LANES
    for p in range(rows // (2 * parents)):
        send[p * 2 * parents : (p + 1) * 2 * parents, at : at + half] = shared

    owner_hot = one_hot(far_pairs[0:1, :] % leaves == iota((leaves, slots), 0))
    a_ref[...] = dot_tn(m2.astype(BF16), owner_hot)
    def parent_products(first, last):
        for s in range(first, last):
            q = par_smem[0, s] % parents
            x = pm3[pl.ds(pl.multiple_of(q * rhs, rhs), rhs), :].astype(BF16)
            pb[s * rhs : (s + 1) * rhs, :] = dot_nn(x, par_c[s])

    some = rank // 4
    parent_products(0, pairs // 4)
    for sb in range(slots // LANES):
        lanes = slice(sb * LANES, (sb + 1) * LANES)
        for part in range(4):
            first = part * some
            acc = [None] * rhs
            for k in range(rank):
                c = far_c[k, first : first + some, lanes].astype(F32)
                for r in range(rhs):
                    term = c * a_ref[r * rank + k : r * rank + k + 1, lanes]
                    acc[r] = term if k == 0 else acc[r] + term
            for r in range(rhs):
                at = r * rank + first
                ob[at : at + some, lanes] = acc[r].astype(BF16)
            if sb == 0 and part < 2:
                parent_products(pairs // 4 * (part + 1), pairs // 4 * (part + 2))
            if sb == 0 and part == 2:
                parent_products(pairs // 4 * 3, pairs)
                high, low = split2(rows_to_lanes(pb, pairs, rhs))
                hot = one_hot(par_pairs[1:2, :] == iota((rows, pairs), 0))
                at = width + LANES
                send[:, at : at + width] = (dot_nn(hot, high) + dot_nn(hot, low)).astype(BF16)
    partner = far_pairs[1:2, :]
    local = jnp.where(partner >= 0, partner % leaves, -1).astype(F32)
    ob[width : width + LANES, :] = jnp.broadcast_to(local, (LANES, slots)).astype(BF16)
    unit = one_hot(iota((LANES, LANES), 0) == iota((LANES, LANES), 1))
    for sb in range(slots // LANES):
        lanes = slice(sb * LANES, (sb + 1) * LANES)
        send[lanes, 0 : width + LANES] = dot_nt(unit, ob[:, lanes]).astype(BF16)


def near_kernel(pairs, charges, following, self_blocks, near_blocks, own, away, ext, out):
    leaves = charges.shape[0]
    step = pl.program_id(0)
    selves, nears = self_blocks.shape[0], near_blocks.shape[0]

    @pl.when(step == 0)
    def _():
        ext[0:leaves] = charges[...]
        ext[leaves:] = following[...]
        out[...] = jnp.zeros_like(out)

    terms = [(step * selves + i, dot_nt(ext[step * selves + i], self_blocks[i])) for i in range(selves)]
    for i in range(nears):
        a, b = pairs[0, step * nears + i], pairs[1, step * nears + i]
        first = (a // leaves) * leaves
        a, b = a - first, b - first
        terms.append((a, dot_nt(ext[b], near_blocks[i])))
        terms.append((b, dot_nn(ext[a], near_blocks[i])))
    for at, term in terms:
        out[at] += term

    @pl.when(step == pl.num_programs(0) - 1)
    def _():
        own[...] = out[0:leaves]
        away[...] = out[leaves:].astype(BF16)


def far_gather(mom, far_pairs, b_ref, leaves, parents):
    rows, slots = mom.shape[0], b_ref.shape[1]
    wide = mom.shape[1] // 3
    row_id = iota((rows, slots), 0)
    base_leaf = row_id // parents * leaves + row_id % parents
    partner = far_pairs[1:2, :]
    total = None
    for h in range(2):
        hot = one_hot(partner == base_leaf + h * parents)
        part = dot_tn(mom[:, h * wide : (h + 1) * wide], hot)
        total = part if total is None else total + part
    b_ref[...] = total


def far_chunks(far_c, b_ref, fw):
    rank, slots = far_c.shape[0], far_c.shape[2]
    some = b_ref.shape[0] // rank

    def chunk(sb, k8):
        lanes = slice(sb * LANES, (sb + 1) * LANES)
        parts = [[] for _ in range(some)]
        for i in range(8):
            c = far_c[k8 * 8 + i, :, lanes].astype(F32)
            for r in range(some):
                prod = c * b_ref[r * rank : (r + 1) * rank, lanes]
                parts[r].append(sum(prod[j * 8 : (j + 1) * 8] for j in range(rank // 8)))
        for r in range(some):
            first = r * rank + k8 * 8
            fw[first : first + 8, lanes] = row_sums(parts[r])

    return [
        functools.partial(chunk, sb, k8) for sb in range(slots // LANES) for k8 in range(rank // 8)
    ]


def far_scatter(far_pairs, fw, leaves):
    hot = one_hot(far_pairs[0:1, :] % leaves == iota((leaves, fw.shape[1]), 0))
    high, low = split2(fw[...])
    return dot_nt(hot, high) + dot_nt(hot, low)


def far_kernel(
    got,
    far_pairs,
    far_c,
    par_pairs,
    parent_of,
    par_c,
    half,
    back,
    par_t,
    pick,
    to_owner,
    to_leaf,
    b_ref,
    fw,
):
    leaves, width = back.shape
    parents = leaves // 2
    rows = got.shape[0]
    index = got[:, width : width + LANES].astype(F32)[:, :leaves].astype(jnp.int32)
    hot = one_hot(index == iota((rows, leaves), 1))
    back[...] = dot_tn(hot, got[:, 0:width])
    mom = got[:, 2 * width + LANES :]
    far_gather(mom, far_pairs, b_ref, leaves, parents)
    for chunk in far_chunks(far_c, b_ref, fw):
        chunk()
    half[...] = far_scatter(far_pairs, fw, leaves)

    pairs = par_c.shape[0]
    rhs = to_owner.shape[0] // parents
    for s in range(pairs):
        par_t[s] = par_c[s].astype(F32).T.astype(BF16)
    hot = jnp.where(par_pairs[1:2, :] == iota((rows, pairs), 0), 1.0, 0.0)
    pick[...] = hot.T.astype(BF16)
    to_owner[...] = by_rows(par_pairs[0:1, :], parents, rhs).astype(BF16)
    to_leaf[...] = by_rows(parent_of[...], parents, rhs).T.astype(BF16)


def post_kernel(
    core_smem,
    half,
    back,
    mom2,
    got,
    bases,
    transfers,
    far_pairs,
    far_c,
    par_t,
    pick,
    to_owner,
    to_leaf,
    near_own,
    near_back,
    out,
    b_ref,
    fw,
    g_ref,
    pf,
    lf,
    pb,
    dn,
):
    leaves, rank, _ = bases.shape
    width = back.shape[1]
    rhs = width // rank
    pairs = par_t.shape[0]
    parents = leaves // 2
    rows = got.shape[0]
    core = core_smem[0, 0] // leaves % 2

    def in_order(mine, other):
        return jnp.concatenate(
            [jnp.where(core == 0, mine, other), jnp.where(core == 0, other, mine)], axis=1
        )

    wide = mom2.shape[1] // 3
    shared = in_order(got[:, got.shape[1] - wide :], mom2[:, 2 * wide :])
    fold = one_hot(iota((parents, rows), 1) % parents == iota((parents, rows), 0))
    at = width + LANES
    lanes_to_rows(pb, dot_nn(fold, got[:, at : at + width]), rhs)
    lanes_to_rows(g_ref, dot_nn(pick[...], shared), rhs)
    far_gather(mom2[...], far_pairs, b_ref, leaves, parents)
    chunks = far_chunks(far_c, b_ref, fw)
    each = -(-len(chunks) // 8)
    for s in range(pairs):
        at = slice(s * rhs, (s + 1) * rhs)
        pf[at, :] = dot_nn(g_ref[at, :].astype(BF16), par_t[s])
        if s % 4 == 3:
            for chunk in chunks[s // 4 * each : (s // 4 + 1) * each]:
                chunk()
    for chunk in chunks[pairs // 4 * each :]:
        chunk()
    high, low = split2(pf[...])
    locals_p = dot_nn(to_owner[...], high) + dot_nn(to_owner[...], low) + pb[...]
    picked = dot_nn(to_leaf[...], locals_p.astype(BF16))
    for l in range(leaves):
        at = slice(l * rhs, (l + 1) * rhs)
        dn[at, :] = dot_nn(picked[at, :].astype(BF16), transfers[l])

    other = far_scatter(far_pairs, fw, leaves)
    lanes_to_rows(lf, back[...] + in_order(half[...], other), rhs)
    for l in range(leaves):
        at = slice(l * rhs, (l + 1) * rhs)
        mine = (lf[at, :] + dn[at, :]).astype(BF16)
        near = near_own[l] + near_back[l].astype(F32)
        out[l] = dot_nn(mine, bases[l]) + near


def after(value, earlier, vmem_limit):
    anywhere = pl.BlockSpec(memory_space=pl.ANY)
    return pl.pallas_call(
        lambda *refs: None,
        out_shape=jax.ShapeDtypeStruct(value.shape, value.dtype),
        in_specs=[anywhere] * (1 + len(earlier)),
        out_specs=anywhere,
        input_output_aliases={0: 0},
        compiler_params=pltpu.CompilerParams(vmem_limit_bytes=vmem_limit),
        name="after",
    )(value, *earlier)


def passed_along(value, axis, steps):
    count = lax.axis_size(axis)
    leading, last = (max(0, -steps), min(count, count - steps))
    return lax.ppermute(value, axis, [(source, source + steps) for source in range(leading, last)])


def on_device(
    charges,
    self_blocks,
    near_blocks,
    near_pairs,
    bases,
    transfers,
    parent_of,
    far_pairs,
    far_coupling,
    par_pairs,
    par_coupling,
):
    leaves, rhs, panels = charges.shape
    rank = bases.shape[1]
    width = rhs * rank
    slots = far_coupling.shape[0]
    pairs = par_coupling.shape[0]
    parents = leaves // 2
    devices = lax.axis_size("sfc")
    rows = devices * parents
    columns = 2 * width + LANES + 3 * width // 2
    vmem = pl.BlockSpec(memory_space=pltpu.VMEM)
    smem = pl.BlockSpec(memory_space=pltpu.SMEM)
    hbm = pl.BlockSpec(memory_space=pltpu.HBM)
    params = pltpu.CompilerParams(vmem_limit_bytes=60 * 1024 * 1024)
    late = pltpu.CompilerParams(vmem_limit_bytes=48 * 1024 * 1024)

    def cost(moved):
        return pl.CostEstimate(flops=4 * moved, bytes_accessed=moved, transcendentals=0)

    following = passed_along(charges, "sfc", -1)
    far_pairs = far_pairs.T
    par_pairs = par_pairs.T
    near_pairs = near_pairs.T
    far_c = jnp.transpose(far_coupling, (1, 2, 0))
    parent_of = parent_of.reshape(1, leaves)

    def like(value, memory=pltpu.VMEM):
        return memory(value.shape, value.dtype)

    send = pl.pallas_call(
        pre_kernel,
        out_shape=jax.ShapeDtypeStruct((rows, columns), BF16),
        in_specs=[hbm] * 8,
        out_specs=vmem,
        scratch_shapes=[
            like(charges),
            like(bases),
            like(transfers),
            like(parent_of),
            like(far_pairs),
            like(far_c),
            like(par_pairs),
            like(par_coupling),
            like(par_pairs, pltpu.SMEM),
            pltpu.SemaphoreType.DMA((9,)),
            pltpu.VMEM((leaves * rhs, rank), F32),
            pltpu.VMEM((leaves * rhs, rank), F32),
            pltpu.VMEM((parents * rhs, rank), F32),
            pltpu.VMEM((pairs * rhs, rank), F32),
            pltpu.VMEM((width, slots), F32),
            pltpu.VMEM((width + LANES, slots), BF16),
        ],
        compiler_params=params,
        cost_estimate=cost(10_000_000),
        name="upward",
    )(charges, bases, transfers, parent_of, far_pairs, far_c, par_pairs, par_coupling)
    send = after(send, [following], 107 << 19)
    got = lax.all_to_all(send, "sfc", split_axis=0, concat_axis=0, tiled=True)
    steps = 4
    selves, nears = leaves // steps, near_blocks.shape[0] // steps
    whole = lambda *shape: pl.BlockSpec(shape, lambda i: (0,) * len(shape))
    near_own, near_away = pl.pallas_call(
        near_kernel,
        grid=(steps,),
        out_shape=[
            jax.ShapeDtypeStruct((leaves, rhs, panels), F32),
            jax.ShapeDtypeStruct((leaves, rhs, panels), BF16),
        ],
        in_specs=[
            smem,
            whole(leaves, rhs, panels),
            whole(leaves, rhs, panels),
            pl.BlockSpec((selves, panels, panels), lambda i: (i, 0, 0)),
            pl.BlockSpec((nears, panels, panels), lambda i: (i, 0, 0)),
        ],
        out_specs=[whole(leaves, rhs, panels)] * 2,
        scratch_shapes=[
            pltpu.VMEM((2 * leaves, rhs, panels), BF16),
            pltpu.VMEM((2 * leaves, rhs, panels), F32),
        ],
        compiler_params=pltpu.CompilerParams(vmem_limit_bytes=52 * 1024 * 1024),
        cost_estimate=cost(20_000_000),
        name="near",
    )(near_pairs, charges, following, self_blocks, near_blocks)
    near_back = passed_along(near_away, "sfc", 1)

    got = after(got, [near_back], 1 << 20)
    mom2 = lax.ppermute(
        got[:, 2 * width + LANES :], "sfc", [(i, i ^ 1) for i in range(devices)]
    )

    half, back, *prepared = pl.pallas_call(
        far_kernel,
        out_shape=[
            jax.ShapeDtypeStruct((leaves, width // 2), F32),
            jax.ShapeDtypeStruct((leaves, width), F32),
            jax.ShapeDtypeStruct(par_coupling.shape, BF16),
            jax.ShapeDtypeStruct((pairs, rows), BF16),
            jax.ShapeDtypeStruct((parents * rhs, pairs * rhs), BF16),
            jax.ShapeDtypeStruct((leaves * rhs, parents * rhs), BF16),
        ],
        in_specs=[vmem] * 6,
        out_specs=[vmem] * 6,
        scratch_shapes=[pltpu.VMEM((width // 2, slots), F32)] * 2,
        compiler_params=late,
        cost_estimate=cost(8_000_000),
        name="far",
    )(got, far_pairs, far_c, par_pairs, parent_of, par_coupling)

    return pl.pallas_call(
        post_kernel,
        out_shape=jax.ShapeDtypeStruct((leaves, rhs, panels), F32),
        in_specs=[smem] + [vmem] * 14,
        out_specs=vmem,
        scratch_shapes=[
            pltpu.VMEM((width // 2, slots), F32),
            pltpu.VMEM((width // 2, slots), F32),
            pltpu.VMEM((pairs * rhs, rank), F32),
            pltpu.VMEM((pairs * rhs, rank), F32),
            pltpu.VMEM((leaves * rhs, rank), F32),
            pltpu.VMEM((parents * rhs, rank), F32),
            pltpu.VMEM((leaves * rhs, rank), F32),
        ],
        compiler_params=late,
        name="downward",
    )(
        far_pairs,
        half,
        back,
        mom2,
        got,
        bases,
        transfers,
        far_pairs,
        far_c,
        *prepared,
        near_own,
        near_back,
    )


def solution(mesh):
    split = ("grp", "sfc")
    cube, flat = P(split, None, None), P(split, None)
    placed = (cube, cube, cube, flat, cube, cube, P(split), flat, cube, flat, cube)
    return jax.shard_map(
        on_device, mesh=mesh, in_specs=placed, out_specs=cube, check_vma=False
    )
```

```python
import functools

import jax
import jax.numpy as jnp
from jax import lax
from jax.experimental import pallas as pl
from jax.experimental.pallas import tpu as pltpu
from jax.sharding import PartitionSpec as P

F32 = jnp.float32
BF16 = jnp.bfloat16
LANES = 128


def dot_nn(a, b):
    return lax.dot_general(a, b, (((1,), (0,)), ((), ())), preferred_element_type=F32)


def dot_nt(a, b):
    return lax.dot_general(a, b, (((1,), (1,)), ((), ())), preferred_element_type=F32)


def dot_tn(a, b):
    return lax.dot_general(a, b, (((0,), (0,)), ((), ())), preferred_element_type=F32)


def split2(x):
    high = x.astype(BF16)
    return high, (x - high.astype(F32)).astype(BF16)


def iota(shape, axis):
    return lax.broadcasted_iota(jnp.int32, shape, axis)


def one_hot(condition):
    return jnp.where(condition, 1.0, 0.0).astype(BF16)


def rows_to_lanes(ref, count, rhs):
    return jnp.concatenate([ref[pl.ds(r, count, stride=rhs), :] for r in range(rhs)], axis=1)


def lanes_to_rows(ref, value, rhs):
    count, width = value.shape
    rank = width // rhs
    for r in range(rhs):
        ref[pl.ds(r, count, stride=rhs), :] = value[:, r * rank : (r + 1) * rank]


def repeated(values, times):
    count = values.shape[1]
    spread = one_hot(iota((count, count * times), 1) // times == iota((count, count * times), 0))
    rows = jnp.broadcast_to(values.astype(F32), (8, count)).astype(BF16)
    return dot_nn(rows, spread)[0:1].astype(jnp.int32)


def by_rows(targets, parents, rhs):
    shape = (parents * rhs, targets.shape[1] * rhs)
    row, column = iota(shape, 0), iota(shape, 1)
    same = (repeated(targets % parents, rhs) == row // rhs) & (row % rhs == column % rhs)
    return jnp.where(same, 1.0, 0.0)


def row_sums(parts):
    row = iota(parts[0].shape, 0)
    for step in (4, 2, 1):
        upper = row % (2 * step) >= step
        merged = []
        for a, b in zip(parts[:step], parts[step:]):
            swapped = jnp.where(upper, a, b)
            if step == 4:
                moved = pltpu.roll(swapped, 4, axis=0)
            else:
                moved = jnp.where(
                    upper,
                    pltpu.roll(swapped, step, axis=0),
                    pltpu.roll(swapped, 8 - step, axis=0),
                )
            merged.append(jnp.where(upper, b, a) + moved)
        parts = merged
    return parts[0]


def fetch(pairs, sems):
    copies = [pltpu.make_async_copy(src, dst, sems.at[i]) for i, (src, dst) in enumerate(pairs)]
    for copy in copies:
        copy.start()
    return copies


def pre_kernel(
    charges_h,
    bases_h,
    transfers_h,
    parent_of_h,
    far_pairs_h,
    far_c_h,
    par_pairs_h,
    par_c_h,
    send,
    charges,
    bases,
    transfers,
    parent_of,
    far_pairs,
    far_c,
    par_pairs,
    par_c,
    par_smem,
    sems,
    mo,
    ch,
    pm3,
    pb,
    a_ref,
    ob,
):
    leaves, rhs, _ = charges.shape
    rank = bases.shape[1]
    width = rhs * rank
    slots = far_c.shape[2]
    pairs = par_c.shape[0]
    parents = leaves // 2
    rows = send.shape[0]
    copies = fetch(
        [
            (parent_of_h, parent_of),
            (far_pairs_h, far_pairs),
            (par_pairs_h, par_pairs),
            (charges_h, charges),
            (bases_h, bases),
            (transfers_h, transfers),
            (par_pairs_h, par_smem),
            (far_c_h, far_c),
            (par_c_h, par_c),
        ],
        sems,
    )
    for copy in copies[:3]:
        copy.wait()
    to_parent = by_rows(parent_of[...], parents, rhs).astype(BF16)
    owner_hot = one_hot(far_pairs[0:1, :] % leaves == iota((leaves, slots), 0))
    partner_hot = one_hot(par_pairs[1:2, :] == iota((rows, pairs), 0))
    partner = far_pairs[1:2, :]
    local = jnp.where(partner >= 0, partner % leaves, -1).astype(F32)
    ob[width : width + LANES, :] = jnp.broadcast_to(local, (LANES, slots)).astype(BF16)
    unit = one_hot(iota((LANES, LANES), 0) == iota((LANES, LANES), 1))

    for copy in copies[3:5]:
        copy.wait()
    ms = [dot_nt(charges[l], bases[l]).astype(BF16) for l in range(leaves)]
    for l in range(leaves):
        mo[l * rhs : (l + 1) * rhs, :] = ms[l].astype(F32)
    copies[5].wait()
    for l in range(leaves):
        ch[l * rhs : (l + 1) * rhs, :] = dot_nt(ms[l], transfers[l])
    m2 = rows_to_lanes(mo, leaves, rhs)
    a_ref[...] = dot_tn(m2.astype(BF16), owner_hot)
    high, low = split2(ch[...])
    pm3[...] = (dot_nn(to_parent, high) + dot_nn(to_parent, low)).astype(BF16).astype(F32)
    for copy in copies[6:]:
        copy.wait()
    pm = rows_to_lanes(pm3, parents, rhs)
    half = 3 * width // 2
    shared = [
        jnp.concatenate([x[:, c * width // 2 : (c + 1) * width // 2] for x in (m2[:parents], m2[parents:], pm)], axis=1)
        for c in range(2)
    ]
    shared = jnp.concatenate(shared, axis=0).astype(BF16)
    at = 2 * width + LANES
    for p in range(rows // (2 * parents)):
        send[p * 2 * parents : (p + 1) * 2 * parents, at : at + half] = shared

    def parent_products(first, last):
        for s in range(first, last):
            q = par_smem[0, s] % parents
            x = pm3[pl.ds(pl.multiple_of(q * rhs, rhs), rhs), :].astype(BF16)
            pb[s * rhs : (s + 1) * rhs, :] = dot_nn(x, par_c[s])

    some = rank // 4
    parent_products(0, pairs // 4)
    for sb in range(slots // LANES):
        lanes = slice(sb * LANES, (sb + 1) * LANES)
        for part in range(4):
            first = part * some
            acc = [None] * rhs
            for k in range(rank):
                c = far_c[k, first : first + some, lanes].astype(F32)
                for r in range(rhs):
                    term = c * a_ref[r * rank + k : r * rank + k + 1, lanes]
                    acc[r] = term if k == 0 else acc[r] + term
            for r in range(rhs):
                at = r * rank + first
                ob[at : at + some, lanes] = acc[r].astype(BF16)
            if sb == 0 and part < 2:
                parent_products(pairs // 4 * (part + 1), pairs // 4 * (part + 2))
            if sb == 0 and part == 2:
                parent_products(pairs // 4 * 3, pairs)
                high, low = split2(rows_to_lanes(pb, pairs, rhs))
                at = width + LANES
                sums = dot_nn(partner_hot, high) + dot_nn(partner_hot, low)
                send[:, at : at + width] = sums.astype(BF16)
    for sb in range(slots // LANES):
        lanes = slice(sb * LANES, (sb + 1) * LANES)
        send[lanes, 0 : width + LANES] = dot_nt(unit, ob[:, lanes]).astype(BF16)


def near_kernel(pairs, charges, following, self_blocks, near_blocks, own, away, ext, out):
    leaves = charges.shape[0]
    step = pl.program_id(0)
    selves, nears = self_blocks.shape[0], near_blocks.shape[0]

    @pl.when(step == 0)
    def _():
        ext[0:leaves] = charges[...]
        ext[leaves:] = following[...]
        out[...] = jnp.zeros_like(out)

    terms = [(step * selves + i, dot_nt(ext[step * selves + i], self_blocks[i])) for i in range(selves)]
    for i in range(nears):
        a, b = pairs[0, step * nears + i], pairs[1, step * nears + i]
        first = (a // leaves) * leaves
        a, b = a - first, b - first
        terms.append((a, dot_nt(ext[b], near_blocks[i])))
        terms.append((b, dot_nn(ext[a], near_blocks[i])))
    for at, term in terms:
        out[at] += term

    @pl.when(step == pl.num_programs(0) - 1)
    def _():
        own[...] = out[0:leaves]
        away[...] = out[leaves:].astype(BF16)


def far_gather(mom, far_pairs, b_ref, leaves, parents):
    rows, slots = mom.shape[0], b_ref.shape[1]
    wide = mom.shape[1] // 3
    row_id = iota((rows, slots), 0)
    base_leaf = row_id // parents * leaves + row_id % parents
    partner = far_pairs[1:2, :]
    total = None
    for h in range(2):
        hot = one_hot(partner == base_leaf + h * parents)
        part = dot_tn(mom[:, h * wide : (h + 1) * wide], hot)
        total = part if total is None else total + part
    b_ref[...] = total


def far_chunks(far_c, b_ref, fw):
    rank, slots = far_c.shape[0], far_c.shape[2]
    some = b_ref.shape[0] // rank

    def chunk(sb, k8):
        lanes = slice(sb * LANES, (sb + 1) * LANES)
        parts = [[] for _ in range(some)]
        for i in range(8):
            c = far_c[k8 * 8 + i, :, lanes].astype(F32)
            for r in range(some):
                prod = c * b_ref[r * rank : (r + 1) * rank, lanes]
                parts[r].append(sum(prod[j * 8 : (j + 1) * 8] for j in range(rank // 8)))
        for r in range(some):
            first = r * rank + k8 * 8
            fw[first : first + 8, lanes] = row_sums(parts[r])

    return [
        functools.partial(chunk, sb, k8) for sb in range(slots // LANES) for k8 in range(rank // 8)
    ]


def far_scatter(far_pairs, fw, leaves):
    hot = one_hot(far_pairs[0:1, :] % leaves == iota((leaves, fw.shape[1]), 0))
    high, low = split2(fw[...])
    return dot_nt(hot, high) + dot_nt(hot, low)


def far_kernel(
    got,
    far_pairs,
    far_c,
    par_pairs,
    parent_of,
    par_c,
    half,
    back,
    par_t,
    pick,
    to_owner,
    to_leaf,
    b_ref,
    fw,
):
    leaves, width = back.shape
    parents = leaves // 2
    rows = got.shape[0]
    index = got[:, width : width + LANES].astype(F32)[:, :leaves].astype(jnp.int32)
    hot = one_hot(index == iota((rows, leaves), 1))
    back[...] = dot_tn(hot, got[:, 0:width])
    mom = got[:, 2 * width + LANES :]
    far_gather(mom, far_pairs, b_ref, leaves, parents)
    for chunk in far_chunks(far_c, b_ref, fw):
        chunk()
    half[...] = far_scatter(far_pairs, fw, leaves)

    pairs = par_c.shape[0]
    rhs = to_owner.shape[0] // parents
    for s in range(pairs):
        par_t[s] = par_c[s].astype(F32).T.astype(BF16)
    hot = jnp.where(par_pairs[1:2, :] == iota((rows, pairs), 0), 1.0, 0.0)
    pick[...] = hot.T.astype(BF16)
    to_owner[...] = by_rows(par_pairs[0:1, :], parents, rhs).astype(BF16)
    to_leaf[...] = by_rows(parent_of[...], parents, rhs).T.astype(BF16)


def post_kernel(
    core_smem,
    half,
    back,
    mom2,
    got,
    bases,
    transfers,
    far_pairs,
    far_c,
    par_t,
    pick,
    to_owner,
    to_leaf,
    near_own,
    near_back,
    out,
    b_ref,
    fw,
    g_ref,
    pf,
    lf,
    pb,
    dn,
):
    leaves, rank, _ = bases.shape
    width = back.shape[1]
    rhs = width // rank
    pairs = par_t.shape[0]
    parents = leaves // 2
    rows = got.shape[0]
    core = core_smem[0, 0] // leaves % 2

    def in_order(mine, other):
        return jnp.concatenate(
            [jnp.where(core == 0, mine, other), jnp.where(core == 0, other, mine)], axis=1
        )

    wide = mom2.shape[1] // 3
    shared = in_order(got[:, got.shape[1] - wide :], mom2[:, 2 * wide :])
    fold = one_hot(iota((parents, rows), 1) % parents == iota((parents, rows), 0))
    at = width + LANES
    lanes_to_rows(pb, dot_nn(fold, got[:, at : at + width]), rhs)
    far_gather(mom2[...], far_pairs, b_ref, leaves, parents)
    chunks = far_chunks(far_c, b_ref, fw)
    each = len(chunks) // 8

    def some_chunks(group):
        for chunk in chunks[group * each : (group + 1) * each]:
            chunk()

    picked = dot_nn(pick[...], shared)
    some_chunks(0)
    lanes_to_rows(g_ref, picked, rhs)
    for s in range(pairs):
        at = slice(s * rhs, (s + 1) * rhs)
        pf[at, :] = dot_nn(g_ref[at, :].astype(BF16), par_t[s])
        if s % (pairs // 4) == pairs // 4 - 1:
            some_chunks(1 + s // (pairs // 4))
    high, low = split2(pf[...])
    locals_p = dot_nn(to_owner[...], high) + dot_nn(to_owner[...], low) + pb[...]
    some_chunks(5)
    picked = dot_nn(to_leaf[...], locals_p.astype(BF16))
    some_chunks(6)
    some_chunks(7)
    for l in range(leaves):
        at = slice(l * rhs, (l + 1) * rhs)
        dn[at, :] = dot_nn(picked[at, :].astype(BF16), transfers[l])

    other = far_scatter(far_pairs, fw, leaves)
    lanes_to_rows(lf, back[...] + in_order(half[...], other), rhs)
    for l in range(leaves):
        at = slice(l * rhs, (l + 1) * rhs)
        mine = (lf[at, :] + dn[at, :]).astype(BF16)
        near = near_own[l] + near_back[l].astype(F32)
        out[l] = dot_nn(mine, bases[l]) + near


def after(value, earlier, vmem_limit):
    anywhere = pl.BlockSpec(memory_space=pl.ANY)
    return pl.pallas_call(
        lambda *refs: None,
        out_shape=jax.ShapeDtypeStruct(value.shape, value.dtype),
        in_specs=[anywhere] * (1 + len(earlier)),
        out_specs=anywhere,
        input_output_aliases={0: 0},
        compiler_params=pltpu.CompilerParams(vmem_limit_bytes=vmem_limit),
        name="after",
    )(value, *earlier)


def passed_along(value, axis, steps):
    count = lax.axis_size(axis)
    leading, last = (max(0, -steps), min(count, count - steps))
    return lax.ppermute(value, axis, [(source, source + steps) for source in range(leading, last)])


def on_device(
    charges,
    self_blocks,
    near_blocks,
    near_pairs,
    bases,
    transfers,
    parent_of,
    far_pairs,
    far_coupling,
    par_pairs,
    par_coupling,
):
    leaves, rhs, panels = charges.shape
    rank = bases.shape[1]
    width = rhs * rank
    slots = far_coupling.shape[0]
    pairs = par_coupling.shape[0]
    parents = leaves // 2
    devices = lax.axis_size("sfc")
    rows = devices * parents
    columns = 2 * width + LANES + 3 * width // 2
    vmem = pl.BlockSpec(memory_space=pltpu.VMEM)
    smem = pl.BlockSpec(memory_space=pltpu.SMEM)
    hbm = pl.BlockSpec(memory_space=pltpu.HBM)
    params = pltpu.CompilerParams(vmem_limit_bytes=60 * 1024 * 1024)
    late = pltpu.CompilerParams(vmem_limit_bytes=48 * 1024 * 1024)

    def cost(moved):
        return pl.CostEstimate(flops=4 * moved, bytes_accessed=moved, transcendentals=0)

    following = passed_along(charges, "sfc", -1)
    far_pairs = far_pairs.T
    par_pairs = par_pairs.T
    near_pairs = near_pairs.T
    far_c = jnp.transpose(far_coupling, (1, 2, 0))
    parent_of = parent_of.reshape(1, leaves)

    def like(value, memory=pltpu.VMEM):
        return memory(value.shape, value.dtype)

    send = pl.pallas_call(
        pre_kernel,
        out_shape=jax.ShapeDtypeStruct((rows, columns), BF16),
        in_specs=[hbm] * 8,
        out_specs=vmem,
        scratch_shapes=[
            like(charges),
            like(bases),
            like(transfers),
            like(parent_of),
            like(far_pairs),
            like(far_c),
            like(par_pairs),
            like(par_coupling),
            like(par_pairs, pltpu.SMEM),
            pltpu.SemaphoreType.DMA((9,)),
            pltpu.VMEM((leaves * rhs, rank), F32),
            pltpu.VMEM((leaves * rhs, rank), F32),
            pltpu.VMEM((parents * rhs, rank), F32),
            pltpu.VMEM((pairs * rhs, rank), F32),
            pltpu.VMEM((width, slots), F32),
            pltpu.VMEM((width + LANES, slots), BF16),
        ],
        compiler_params=params,
        cost_estimate=cost(10_000_000),
        name="upward",
    )(charges, bases, transfers, parent_of, far_pairs, far_c, par_pairs, par_coupling)
    send = after(send, [following], 107 << 19)
    got = lax.all_to_all(send, "sfc", split_axis=0, concat_axis=0, tiled=True)
    steps = 4
    selves, nears = leaves // steps, near_blocks.shape[0] // steps
    whole = lambda *shape: pl.BlockSpec(shape, lambda i: (0,) * len(shape))
    near_own, near_away = pl.pallas_call(
        near_kernel,
        grid=(steps,),
        out_shape=[
            jax.ShapeDtypeStruct((leaves, rhs, panels), F32),
            jax.ShapeDtypeStruct((leaves, rhs, panels), BF16),
        ],
        in_specs=[
            smem,
            whole(leaves, rhs, panels),
            whole(leaves, rhs, panels),
            pl.BlockSpec((selves, panels, panels), lambda i: (i, 0, 0)),
            pl.BlockSpec((nears, panels, panels), lambda i: (i, 0, 0)),
        ],
        out_specs=[whole(leaves, rhs, panels)] * 2,
        scratch_shapes=[
            pltpu.VMEM((2 * leaves, rhs, panels), BF16),
            pltpu.VMEM((2 * leaves, rhs, panels), F32),
        ],
        compiler_params=pltpu.CompilerParams(vmem_limit_bytes=52 * 1024 * 1024),
        cost_estimate=cost(20_000_000),
        name="near",
    )(near_pairs, charges, following, self_blocks, near_blocks)
    near_back = passed_along(near_away, "sfc", 1)

    got = after(got, [near_back], 1 << 20)
    mom2 = lax.ppermute(
        got[:, 2 * width + LANES :], "sfc", [(i, i ^ 1) for i in range(devices)]
    )

    half, back, *prepared = pl.pallas_call(
        far_kernel,
        out_shape=[
            jax.ShapeDtypeStruct((leaves, width // 2), F32),
            jax.ShapeDtypeStruct((leaves, width), F32),
            jax.ShapeDtypeStruct(par_coupling.shape, BF16),
            jax.ShapeDtypeStruct((pairs, rows), BF16),
            jax.ShapeDtypeStruct((parents * rhs, pairs * rhs), BF16),
            jax.ShapeDtypeStruct((leaves * rhs, parents * rhs), BF16),
        ],
        in_specs=[vmem] * 6,
        out_specs=[vmem] * 6,
        scratch_shapes=[pltpu.VMEM((width // 2, slots), F32)] * 2,
        compiler_params=late,
        cost_estimate=cost(8_000_000),
        name="far",
    )(got, far_pairs, far_c, par_pairs, parent_of, par_coupling)

    return pl.pallas_call(
        post_kernel,
        out_shape=jax.ShapeDtypeStruct((leaves, rhs, panels), F32),
        in_specs=[smem] + [vmem] * 14,
        out_specs=vmem,
        scratch_shapes=[
            pltpu.VMEM((width // 2, slots), F32),
            pltpu.VMEM((width // 2, slots), F32),
            pltpu.VMEM((pairs * rhs, rank), F32),
            pltpu.VMEM((pairs * rhs, rank), F32),
            pltpu.VMEM((leaves * rhs, rank), F32),
            pltpu.VMEM((parents * rhs, rank), F32),
            pltpu.VMEM((leaves * rhs, rank), F32),
        ],
        compiler_params=late,
        name="downward",
    )(
        far_pairs,
        half,
        back,
        mom2,
        got,
        bases,
        transfers,
        far_pairs,
        far_c,
        *prepared,
        near_own,
        near_back,
    )


def solution(mesh):
    split = ("grp", "sfc")
    cube, flat = P(split, None, None), P(split, None)
    placed = (cube, cube, cube, flat, cube, cube, P(split), flat, cube, flat, cube)
    return jax.shard_map(
        on_device, mesh=mesh, in_specs=placed, out_specs=cube, check_vma=False
    )
```

```python
import functools

import jax
import jax.numpy as jnp
from jax import lax
from jax.experimental import pallas as pl
from jax.experimental.pallas import tpu as pltpu
from jax.sharding import PartitionSpec as P

F32 = jnp.float32
BF16 = jnp.bfloat16
LANES = 128


def dot_nn(a, b):
    return lax.dot_general(a, b, (((1,), (0,)), ((), ())), preferred_element_type=F32)


def dot_nt(a, b):
    return lax.dot_general(a, b, (((1,), (1,)), ((), ())), preferred_element_type=F32)


def dot_tn(a, b):
    return lax.dot_general(a, b, (((0,), (0,)), ((), ())), preferred_element_type=F32)


def split2(x):
    high = x.astype(BF16)
    return high, (x - high.astype(F32)).astype(BF16)


def iota(shape, axis):
    return lax.broadcasted_iota(jnp.int32, shape, axis)


def one_hot(condition):
    return jnp.where(condition, 1.0, 0.0).astype(BF16)


def rows_to_lanes(ref, count, rhs):
    return jnp.concatenate([ref[pl.ds(r, count, stride=rhs), :] for r in range(rhs)], axis=1)


def lanes_to_rows(ref, value, rhs):
    count, width = value.shape
    rank = width // rhs
    for r in range(rhs):
        ref[pl.ds(r, count, stride=rhs), :] = value[:, r * rank : (r + 1) * rank]


def repeated(values, times):
    count = values.shape[1]
    spread = one_hot(iota((count, count * times), 1) // times == iota((count, count * times), 0))
    rows = jnp.broadcast_to(values.astype(F32), (8, count)).astype(BF16)
    return dot_nn(rows, spread)[0:1].astype(jnp.int32)


def by_rows(targets, parents, rhs):
    shape = (parents * rhs, targets.shape[1] * rhs)
    row, column = iota(shape, 0), iota(shape, 1)
    same = (repeated(targets % parents, rhs) == row // rhs) & (row % rhs == column % rhs)
    return jnp.where(same, 1.0, 0.0)


def row_sums(parts):
    row = iota(parts[0].shape, 0)
    for step in (4, 2, 1):
        upper = row % (2 * step) >= step
        merged = []
        for a, b in zip(parts[:step], parts[step:]):
            swapped = jnp.where(upper, a, b)
            if step == 4:
                moved = pltpu.roll(swapped, 4, axis=0)
            else:
                moved = jnp.where(
                    upper,
                    pltpu.roll(swapped, step, axis=0),
                    pltpu.roll(swapped, 8 - step, axis=0),
                )
            merged.append(jnp.where(upper, b, a) + moved)
        parts = merged
    return parts[0]


def fetch(pairs, sems):
    copies = [pltpu.make_async_copy(src, dst, sems.at[i]) for i, (src, dst) in enumerate(pairs)]
    for copy in copies:
        copy.start()
    return copies


def pre_kernel(
    charges_h,
    bases_h,
    transfers_h,
    parent_of_h,
    far_pairs_h,
    far_c_h,
    par_pairs_h,
    par_c_h,
    send,
    charges,
    bases,
    transfers,
    parent_of,
    far_pairs,
    far_c,
    par_pairs,
    par_c,
    par_smem,
    sems,
    mo,
    ch,
    pm3,
    pb,
    a_ref,
    ob,
):
    leaves, rhs, _ = charges.shape
    rank = bases.shape[1]
    width = rhs * rank
    slots = far_c.shape[2]
    pairs = par_c.shape[0]
    parents = leaves // 2
    rows = send.shape[0]
    copies = fetch(
        [
            (parent_of_h, parent_of),
            (far_pairs_h, far_pairs),
            (par_pairs_h, par_pairs),
            (charges_h, charges),
            (bases_h, bases),
            (transfers_h, transfers),
            (par_pairs_h, par_smem),
            (far_c_h, far_c),
            (par_c_h, par_c),
        ],
        sems,
    )
    for copy in copies[:3]:
        copy.wait()
    to_parent = by_rows(parent_of[...], parents, rhs).astype(BF16)
    owner_hot = one_hot(far_pairs[0:1, :] % leaves == iota((leaves, slots), 0))
    partner_hot = one_hot(par_pairs[1:2, :] == iota((rows, pairs), 0))
    partner = far_pairs[1:2, :]
    local = jnp.where(partner >= 0, partner % leaves, -1).astype(F32)
    ob[width : width + LANES, :] = jnp.broadcast_to(local, (LANES, slots)).astype(BF16)
    unit = one_hot(iota((LANES, LANES), 0) == iota((LANES, LANES), 1))

    for copy in copies[3:5]:
        copy.wait()
    ms = [dot_nt(charges[l], bases[l]).astype(BF16) for l in range(leaves)]
    for l in range(leaves):
        mo[l * rhs : (l + 1) * rhs, :] = ms[l].astype(F32)
    copies[5].wait()
    for l in range(leaves):
        ch[l * rhs : (l + 1) * rhs, :] = dot_nt(ms[l], transfers[l])
    m2 = rows_to_lanes(mo, leaves, rhs)
    a_ref[...] = dot_tn(m2.astype(BF16), owner_hot)
    high, low = split2(ch[...])
    pm3[...] = (dot_nn(to_parent, high) + dot_nn(to_parent, low)).astype(BF16).astype(F32)
    for copy in copies[6:]:
        copy.wait()
    pm = rows_to_lanes(pm3, parents, rhs)
    half = 3 * width // 2
    shared = [
        jnp.concatenate([x[:, c * width // 2 : (c + 1) * width // 2] for x in (m2[:parents], m2[parents:], pm)], axis=1)
        for c in range(2)
    ]
    shared = jnp.concatenate(shared, axis=0).astype(BF16)
    at = 2 * width + LANES
    for p in range(rows // (2 * parents)):
        send[p * 2 * parents : (p + 1) * 2 * parents, at : at + half] = shared

    def parent_products(first, last):
        for s in range(first, last):
            q = par_smem[0, s] % parents
            x = pm3[pl.ds(pl.multiple_of(q * rhs, rhs), rhs), :].astype(BF16)
            pb[s * rhs : (s + 1) * rhs, :] = dot_nn(x, par_c[s])

    some = rank // 4
    parent_products(0, pairs // 4)
    for sb in range(slots // LANES):
        lanes = slice(sb * LANES, (sb + 1) * LANES)
        for part in range(4):
            first = part * some
            acc = [None] * rhs
            for k in range(rank):
                c = far_c[k, first : first + some, lanes].astype(F32)
                for r in range(rhs):
                    term = c * a_ref[r * rank + k : r * rank + k + 1, lanes]
                    acc[r] = term if k == 0 else acc[r] + term
            for r in range(rhs):
                at = r * rank + first
                ob[at : at + some, lanes] = acc[r].astype(BF16)
            if sb == 0 and part < 2:
                parent_products(pairs // 4 * (part + 1), pairs // 4 * (part + 2))
            if sb == 0 and part == 2:
                parent_products(pairs // 4 * 3, pairs)
                high, low = split2(rows_to_lanes(pb, pairs, rhs))
                at = width + LANES
                sums = dot_nn(partner_hot, high) + dot_nn(partner_hot, low)
                send[:, at : at + width] = sums.astype(BF16)
    for sb in range(slots // LANES):
        lanes = slice(sb * LANES, (sb + 1) * LANES)
        send[lanes, 0 : width + LANES] = dot_nt(unit, ob[:, lanes]).astype(BF16)


def near_kernel(pairs, earlier, charges, self_blocks, near_blocks, own, away, out):
    leaves = charges.shape[0]
    step = pl.program_id(0)
    selves, nears = self_blocks.shape[0], near_blocks.shape[0]

    @pl.when(step == 0)
    def _():
        out[...] = jnp.zeros_like(out)

    terms = []
    for i in range(selves):
        l = step * selves + i
        terms.append((l, dot_nt(charges[l], self_blocks[i])))
    for i in range(nears):
        a, b = pairs[0, step * nears + i], pairs[1, step * nears + i]
        first = (a // leaves) * leaves
        a, b = a - first, b - first
        x = charges[b % leaves]
        x = jnp.where(b < leaves, x, jnp.zeros_like(x))
        terms.append((a, dot_nt(x, near_blocks[i])))
        terms.append((b, dot_nn(charges[a], near_blocks[i])))
    for at, term in terms:
        out[at] += term

    @pl.when(step == pl.num_programs(0) - 1)
    def _():
        own[...] = out[0:leaves]
        away[...] = out[leaves:].astype(BF16)


def cross_kernel(pairs, near_own, following, near_blocks, total):
    leaves = following.shape[0]
    step = pl.program_id(0)
    nears = near_blocks.shape[0]

    @pl.when(step == 0)
    def _():
        total[...] = near_own[...]

    for i in range(nears):
        a, b = pairs[0, step * nears + i], pairs[1, step * nears + i]
        first = (a // leaves) * leaves
        a, b = a - first, b - first

        @pl.when(b >= leaves)
        def _():
            total[a] += dot_nt(following[b % leaves], near_blocks[i])


def far_gather(mom, far_pairs, b_ref, leaves, parents):
    rows, slots = mom.shape[0], b_ref.shape[1]
    wide = mom.shape[1] // 3
    row_id = iota((rows, slots), 0)
    base_leaf = row_id // parents * leaves + row_id % parents
    partner = far_pairs[1:2, :]
    total = None
    for h in range(2):
        hot = one_hot(partner == base_leaf + h * parents)
        part = dot_tn(mom[:, h * wide : (h + 1) * wide], hot)
        total = part if total is None else total + part
    b_ref[...] = total


def far_chunks(far_c, b_ref, fw):
    rank, slots = far_c.shape[0], far_c.shape[2]
    some = b_ref.shape[0] // rank

    def chunk(sb, k8):
        lanes = slice(sb * LANES, (sb + 1) * LANES)
        parts = [[] for _ in range(some)]
        for i in range(8):
            c = far_c[k8 * 8 + i, :, lanes].astype(F32)
            for r in range(some):
                prod = c * b_ref[r * rank : (r + 1) * rank, lanes]
                parts[r].append(sum(prod[j * 8 : (j + 1) * 8] for j in range(rank // 8)))
        for r in range(some):
            first = r * rank + k8 * 8
            fw[first : first + 8, lanes] = row_sums(parts[r])

    return [
        functools.partial(chunk, sb, k8) for sb in range(slots // LANES) for k8 in range(rank // 8)
    ]


def far_scatter(far_pairs, fw, leaves):
    hot = one_hot(far_pairs[0:1, :] % leaves == iota((leaves, fw.shape[1]), 0))
    high, low = split2(fw[...])
    return dot_nt(hot, high) + dot_nt(hot, low)


def far_kernel(
    got,
    far_pairs,
    far_c,
    par_pairs,
    parent_of,
    par_c,
    half,
    back,
    par_t,
    pick,
    to_owner,
    to_leaf,
    b_ref,
    fw,
):
    leaves, width = back.shape
    parents = leaves // 2
    rows = got.shape[0]
    index = got[:, width : width + LANES].astype(F32)[:, :leaves].astype(jnp.int32)
    hot = one_hot(index == iota((rows, leaves), 1))
    back[...] = dot_tn(hot, got[:, 0:width])
    mom = got[:, 2 * width + LANES :]
    far_gather(mom, far_pairs, b_ref, leaves, parents)
    for chunk in far_chunks(far_c, b_ref, fw):
        chunk()
    half[...] = far_scatter(far_pairs, fw, leaves)

    pairs = par_c.shape[0]
    rhs = to_owner.shape[0] // parents
    for s in range(pairs):
        par_t[s] = par_c[s].astype(F32).T.astype(BF16)
    hot = jnp.where(par_pairs[1:2, :] == iota((rows, pairs), 0), 1.0, 0.0)
    pick[...] = hot.T.astype(BF16)
    to_owner[...] = by_rows(par_pairs[0:1, :], parents, rhs).astype(BF16)
    to_leaf[...] = by_rows(parent_of[...], parents, rhs).T.astype(BF16)


def post_kernel(
    core_smem,
    half,
    back,
    mom2,
    got,
    bases,
    transfers,
    far_pairs,
    far_c,
    par_t,
    pick,
    to_owner,
    to_leaf,
    near_own,
    near_back,
    out,
    b_ref,
    fw,
    g_ref,
    pf,
    lf,
    pb,
    dn,
):
    leaves, rank, _ = bases.shape
    width = back.shape[1]
    rhs = width // rank
    pairs = par_t.shape[0]
    parents = leaves // 2
    rows = got.shape[0]
    core = core_smem[0, 0] // leaves % 2

    def in_order(mine, other):
        return jnp.concatenate(
            [jnp.where(core == 0, mine, other), jnp.where(core == 0, other, mine)], axis=1
        )

    wide = mom2.shape[1] // 3
    shared = in_order(got[:, got.shape[1] - wide :], mom2[:, 2 * wide :])
    fold = one_hot(iota((parents, rows), 1) % parents == iota((parents, rows), 0))
    at = width + LANES
    lanes_to_rows(pb, dot_nn(fold, got[:, at : at + width]), rhs)
    far_gather(mom2[...], far_pairs, b_ref, leaves, parents)
    chunks = far_chunks(far_c, b_ref, fw)
    each = len(chunks) // 8

    def some_chunks(group):
        for chunk in chunks[group * each : (group + 1) * each]:
            chunk()

    picked = dot_nn(pick[...], shared)
    some_chunks(0)
    lanes_to_rows(g_ref, picked, rhs)
    for s in range(pairs):
        at = slice(s * rhs, (s + 1) * rhs)
        pf[at, :] = dot_nn(g_ref[at, :].astype(BF16), par_t[s])
        if s % (pairs // 4) == pairs // 4 - 1:
            some_chunks(1 + s // (pairs // 4))
    high, low = split2(pf[...])
    locals_p = dot_nn(to_owner[...], high) + dot_nn(to_owner[...], low) + pb[...]
    some_chunks(5)
    picked = dot_nn(to_leaf[...], locals_p.astype(BF16))
    some_chunks(6)
    some_chunks(7)
    for l in range(leaves):
        at = slice(l * rhs, (l + 1) * rhs)
        dn[at, :] = dot_nn(picked[at, :].astype(BF16), transfers[l])

    other = far_scatter(far_pairs, fw, leaves)
    lanes_to_rows(lf, back[...] + in_order(half[...], other), rhs)
    for l in range(leaves):
        at = slice(l * rhs, (l + 1) * rhs)
        mine = (lf[at, :] + dn[at, :]).astype(BF16)
        near = near_own[l] + near_back[l].astype(F32)
        out[l] = dot_nn(mine, bases[l]) + near


def after(value, earlier, vmem_limit):
    anywhere = pl.BlockSpec(memory_space=pl.ANY)
    return pl.pallas_call(
        lambda *refs: None,
        out_shape=jax.ShapeDtypeStruct(value.shape, value.dtype),
        in_specs=[anywhere] * (1 + len(earlier)),
        out_specs=anywhere,
        input_output_aliases={0: 0},
        compiler_params=pltpu.CompilerParams(vmem_limit_bytes=vmem_limit),
        name="after",
    )(value, *earlier)


def passed_along(value, axis, steps):
    count = lax.axis_size(axis)
    leading, last = (max(0, -steps), min(count, count - steps))
    return lax.ppermute(value, axis, [(source, source + steps) for source in range(leading, last)])


def on_device(
    charges,
    self_blocks,
    near_blocks,
    near_pairs,
    bases,
    transfers,
    parent_of,
    far_pairs,
    far_coupling,
    par_pairs,
    par_coupling,
):
    leaves, rhs, panels = charges.shape
    rank = bases.shape[1]
    width = rhs * rank
    slots = far_coupling.shape[0]
    pairs = par_coupling.shape[0]
    parents = leaves // 2
    devices = lax.axis_size("sfc")
    rows = devices * parents
    columns = 2 * width + LANES + 3 * width // 2
    vmem = pl.BlockSpec(memory_space=pltpu.VMEM)
    smem = pl.BlockSpec(memory_space=pltpu.SMEM)
    hbm = pl.BlockSpec(memory_space=pltpu.HBM)
    params = pltpu.CompilerParams(vmem_limit_bytes=60 * 1024 * 1024)
    late = pltpu.CompilerParams(vmem_limit_bytes=48 * 1024 * 1024)

    def cost(moved):
        return pl.CostEstimate(flops=4 * moved, bytes_accessed=moved, transcendentals=0)

    following = passed_along(charges, "sfc", -1)
    far_pairs = far_pairs.T
    par_pairs = par_pairs.T
    near_pairs = near_pairs.T
    far_c = jnp.transpose(far_coupling, (1, 2, 0))
    parent_of = parent_of.reshape(1, leaves)

    def like(value, memory=pltpu.VMEM):
        return memory(value.shape, value.dtype)

    send = pl.pallas_call(
        pre_kernel,
        out_shape=jax.ShapeDtypeStruct((rows, columns), BF16),
        in_specs=[hbm] * 8,
        out_specs=vmem,
        scratch_shapes=[
            like(charges),
            like(bases),
            like(transfers),
            like(parent_of),
            like(far_pairs),
            like(far_c),
            like(par_pairs),
            like(par_coupling),
            like(par_pairs, pltpu.SMEM),
            pltpu.SemaphoreType.DMA((9,)),
            pltpu.VMEM((leaves * rhs, rank), F32),
            pltpu.VMEM((leaves * rhs, rank), F32),
            pltpu.VMEM((parents * rhs, rank), F32),
            pltpu.VMEM((pairs * rhs, rank), F32),
            pltpu.VMEM((width, slots), F32),
            pltpu.VMEM((width + LANES, slots), BF16),
        ],
        compiler_params=params,
        cost_estimate=cost(10_000_000),
        name="upward",
    )(charges, bases, transfers, parent_of, far_pairs, far_c, par_pairs, par_coupling)
    got = lax.all_to_all(send, "sfc", split_axis=0, concat_axis=0, tiled=True)
    steps = 4
    selves, nears = leaves // steps, near_blocks.shape[0] // steps
    whole = lambda *shape: pl.BlockSpec(shape, lambda i: (0,) * len(shape))
    near_params = pltpu.CompilerParams(vmem_limit_bytes=52 * 1024 * 1024)
    near_own, near_away = pl.pallas_call(
        near_kernel,
        grid=(steps,),
        out_shape=[
            jax.ShapeDtypeStruct((leaves, rhs, panels), F32),
            jax.ShapeDtypeStruct((leaves, rhs, panels), BF16),
        ],
        in_specs=[
            smem,
            pl.BlockSpec(memory_space=pl.ANY),
            whole(leaves, rhs, panels),
            pl.BlockSpec((selves, panels, panels), lambda i: (i, 0, 0)),
            pl.BlockSpec((nears, panels, panels), lambda i: (i, 0, 0)),
        ],
        out_specs=[whole(leaves, rhs, panels)] * 2,
        scratch_shapes=[pltpu.VMEM((2 * leaves, rhs, panels), F32)],
        compiler_params=near_params,
        cost_estimate=cost(20_000_000),
        name="near",
    )(near_pairs, send, charges, self_blocks, near_blocks)
    near_own = pl.pallas_call(
        cross_kernel,
        grid=(steps,),
        out_shape=jax.ShapeDtypeStruct((leaves, rhs, panels), F32),
        in_specs=[
            smem,
            whole(leaves, rhs, panels),
            whole(leaves, rhs, panels),
            pl.BlockSpec((nears, panels, panels), lambda i: (i, 0, 0)),
        ],
        out_specs=whole(leaves, rhs, panels),
        compiler_params=near_params,
        cost_estimate=cost(8_000_000),
        name="cross",
    )(near_pairs, near_own, following, near_blocks)
    near_back = passed_along(near_away, "sfc", 1)

    got = after(got, [near_back, near_own], 1 << 20)
    mom2 = lax.ppermute(
        got[:, 2 * width + LANES :], "sfc", [(i, i ^ 1) for i in range(devices)]
    )

    half, back, *prepared = pl.pallas_call(
        far_kernel,
        out_shape=[
            jax.ShapeDtypeStruct((leaves, width // 2), F32),
            jax.ShapeDtypeStruct((leaves, width), F32),
            jax.ShapeDtypeStruct(par_coupling.shape, BF16),
            jax.ShapeDtypeStruct((pairs, rows), BF16),
            jax.ShapeDtypeStruct((parents * rhs, pairs * rhs), BF16),
            jax.ShapeDtypeStruct((leaves * rhs, parents * rhs), BF16),
        ],
        in_specs=[vmem] * 6,
        out_specs=[vmem] * 6,
        scratch_shapes=[pltpu.VMEM((width // 2, slots), F32)] * 2,
        compiler_params=late,
        cost_estimate=cost(8_000_000),
        name="far",
    )(got, far_pairs, far_c, par_pairs, parent_of, par_coupling)

    return pl.pallas_call(
        post_kernel,
        out_shape=jax.ShapeDtypeStruct((leaves, rhs, panels), F32),
        in_specs=[smem] + [vmem] * 14,
        out_specs=vmem,
        scratch_shapes=[
            pltpu.VMEM((width // 2, slots), F32),
            pltpu.VMEM((width // 2, slots), F32),
            pltpu.VMEM((pairs * rhs, rank), F32),
            pltpu.VMEM((pairs * rhs, rank), F32),
            pltpu.VMEM((leaves * rhs, rank), F32),
            pltpu.VMEM((parents * rhs, rank), F32),
            pltpu.VMEM((leaves * rhs, rank), F32),
        ],
        compiler_params=late,
        name="downward",
    )(
        far_pairs,
        half,
        back,
        mom2,
        got,
        bases,
        transfers,
        far_pairs,
        far_c,
        *prepared,
        near_own,
        near_back,
    )


def solution(mesh):
    split = ("grp", "sfc")
    cube, flat = P(split, None, None), P(split, None)
    placed = (cube, cube, cube, flat, cube, cube, P(split), flat, cube, flat, cube)
    return jax.shard_map(
        on_device, mesh=mesh, in_specs=placed, out_specs=cube, check_vma=False
    )
```

```python
import functools

import jax
import jax.numpy as jnp
from jax import lax
from jax.experimental import pallas as pl
from jax.experimental.pallas import tpu as pltpu
from jax.sharding import PartitionSpec as P

F32 = jnp.float32
BF16 = jnp.bfloat16
LANES = 128


def dot_nn(a, b):
    return lax.dot_general(a, b, (((1,), (0,)), ((), ())), preferred_element_type=F32)


def dot_nt(a, b):
    return lax.dot_general(a, b, (((1,), (1,)), ((), ())), preferred_element_type=F32)


def dot_tn(a, b):
    return lax.dot_general(a, b, (((0,), (0,)), ((), ())), preferred_element_type=F32)


def split2(x):
    high = x.astype(BF16)
    return high, (x - high.astype(F32)).astype(BF16)


def iota(shape, axis):
    return lax.broadcasted_iota(jnp.int32, shape, axis)


def one_hot(condition):
    return jnp.where(condition, 1.0, 0.0).astype(BF16)


def rows_to_lanes(ref, count, rhs):
    return jnp.concatenate([ref[pl.ds(r, count, stride=rhs), :] for r in range(rhs)], axis=1)


def lanes_to_rows(ref, value, rhs):
    count, width = value.shape
    rank = width // rhs
    for r in range(rhs):
        ref[pl.ds(r, count, stride=rhs), :] = value[:, r * rank : (r + 1) * rank]


def repeated(values, times):
    count = values.shape[1]
    spread = one_hot(iota((count, count * times), 1) // times == iota((count, count * times), 0))
    rows = jnp.broadcast_to(values.astype(F32), (8, count)).astype(BF16)
    return dot_nn(rows, spread)[0:1].astype(jnp.int32)


def by_rows(targets, parents, rhs):
    shape = (parents * rhs, targets.shape[1] * rhs)
    row, column = iota(shape, 0), iota(shape, 1)
    same = (repeated(targets % parents, rhs) == row // rhs) & (row % rhs == column % rhs)
    return jnp.where(same, 1.0, 0.0)


def row_sums(parts):
    row = iota(parts[0].shape, 0)
    for step in (4, 2, 1):
        upper = row % (2 * step) >= step
        merged = []
        for a, b in zip(parts[:step], parts[step:]):
            swapped = jnp.where(upper, a, b)
            if step == 4:
                moved = pltpu.roll(swapped, 4, axis=0)
            else:
                moved = jnp.where(
                    upper,
                    pltpu.roll(swapped, step, axis=0),
                    pltpu.roll(swapped, 8 - step, axis=0),
                )
            merged.append(jnp.where(upper, b, a) + moved)
        parts = merged
    return parts[0]


def fetch(pairs, sems):
    copies = [pltpu.make_async_copy(src, dst, sems.at[i]) for i, (src, dst) in enumerate(pairs)]
    for copy in copies:
        copy.start()
    return copies


def pre_kernel(
    charges_h,
    bases_h,
    transfers_h,
    parent_of_h,
    far_pairs_h,
    far_c_h,
    par_pairs_h,
    par_c_h,
    send,
    token,
    charges,
    bases,
    transfers,
    parent_of,
    far_pairs,
    far_c,
    par_pairs,
    par_c,
    par_smem,
    sems,
    mo,
    ch,
    pm3,
    pb,
    a_ref,
    ob,
):
    token[...] = jnp.zeros_like(token)
    leaves, rhs, _ = charges.shape
    rank = bases.shape[1]
    width = rhs * rank
    slots = far_c.shape[2]
    pairs = par_c.shape[0]
    parents = leaves // 2
    rows = send.shape[0]
    copies = fetch(
        [
            (parent_of_h, parent_of),
            (far_pairs_h, far_pairs),
            (par_pairs_h, par_pairs),
            (charges_h, charges),
            (bases_h, bases),
            (transfers_h, transfers),
            (par_pairs_h, par_smem),
            (far_c_h, far_c),
            (par_c_h, par_c),
        ],
        sems,
    )
    for copy in copies[:3]:
        copy.wait()
    to_parent = by_rows(parent_of[...], parents, rhs).astype(BF16)
    owner_hot = one_hot(far_pairs[0:1, :] % leaves == iota((leaves, slots), 0))
    partner_hot = one_hot(par_pairs[1:2, :] == iota((rows, pairs), 0))
    partner = far_pairs[1:2, :]
    local = jnp.where(partner >= 0, partner % leaves, -1).astype(F32)
    ob[width : width + LANES, :] = jnp.broadcast_to(local, (LANES, slots)).astype(BF16)
    unit = one_hot(iota((LANES, LANES), 0) == iota((LANES, LANES), 1))

    for copy in copies[3:5]:
        copy.wait()
    ms = [dot_nt(charges[l], bases[l]).astype(BF16) for l in range(leaves)]
    for l in range(leaves):
        mo[l * rhs : (l + 1) * rhs, :] = ms[l].astype(F32)
    copies[5].wait()
    for l in range(leaves):
        ch[l * rhs : (l + 1) * rhs, :] = dot_nt(ms[l], transfers[l])
    m2 = rows_to_lanes(mo, leaves, rhs)
    a_ref[...] = dot_tn(m2.astype(BF16), owner_hot)
    high, low = split2(ch[...])
    pm3[...] = (dot_nn(to_parent, high) + dot_nn(to_parent, low)).astype(BF16).astype(F32)
    for copy in copies[6:]:
        copy.wait()
    pm = rows_to_lanes(pm3, parents, rhs)
    half = 3 * width // 2
    shared = [
        jnp.concatenate([x[:, c * width // 2 : (c + 1) * width // 2] for x in (m2[:parents], m2[parents:], pm)], axis=1)
        for c in range(2)
    ]
    shared = jnp.concatenate(shared, axis=0).astype(BF16)
    at = 2 * width + LANES
    for p in range(rows // (2 * parents)):
        send[p * 2 * parents : (p + 1) * 2 * parents, at : at + half] = shared

    def parent_products(first, last):
        for s in range(first, last):
            q = par_smem[0, s] % parents
            x = pm3[pl.ds(pl.multiple_of(q * rhs, rhs), rhs), :].astype(BF16)
            pb[s * rhs : (s + 1) * rhs, :] = dot_nn(x, par_c[s])

    some = rank // 4
    parent_products(0, pairs // 4)
    for sb in range(slots // LANES):
        lanes = slice(sb * LANES, (sb + 1) * LANES)
        for part in range(4):
            first = part * some
            acc = [None] * rhs
            for k in range(rank):
                c = far_c[k, first : first + some, lanes].astype(F32)
                for r in range(rhs):
                    term = c * a_ref[r * rank + k : r * rank + k + 1, lanes]
                    acc[r] = term if k == 0 else acc[r] + term
            for r in range(rhs):
                at = r * rank + first
                ob[at : at + some, lanes] = acc[r].astype(BF16)
            if sb == 0 and part < 2:
                parent_products(pairs // 4 * (part + 1), pairs // 4 * (part + 2))
            if sb == 0 and part == 2:
                parent_products(pairs // 4 * 3, pairs)
                high, low = split2(rows_to_lanes(pb, pairs, rhs))
                at = width + LANES
                sums = dot_nn(partner_hot, high) + dot_nn(partner_hot, low)
                send[:, at : at + width] = sums.astype(BF16)
    for sb in range(slots // LANES):
        lanes = slice(sb * LANES, (sb + 1) * LANES)
        send[lanes, 0 : width + LANES] = dot_nt(unit, ob[:, lanes]).astype(BF16)


def near_kernel(pairs, earlier, charges, self_blocks, near_blocks, own, away, out):
    leaves = charges.shape[0]
    step = pl.program_id(0)
    selves, nears = self_blocks.shape[0], near_blocks.shape[0]

    @pl.when(step == 0)
    def _():
        out[...] = jnp.zeros_like(out)

    terms = []
    for i in range(selves):
        l = step * selves + i
        terms.append((l, dot_nt(charges[l], self_blocks[i])))
    for i in range(nears):
        a, b = pairs[0, step * nears + i], pairs[1, step * nears + i]
        first = (a // leaves) * leaves
        a, b = a - first, b - first
        x = charges[b % leaves]
        x = jnp.where(b < leaves, x, jnp.zeros_like(x))
        terms.append((a, dot_nt(x, near_blocks[i])))
        terms.append((b, dot_nn(charges[a], near_blocks[i])))
    for at, term in terms:
        out[at] += term

    @pl.when(step == pl.num_programs(0) - 1)
    def _():
        own[...] = out[0:leaves]
        away[...] = out[leaves:].astype(BF16)


def cross_kernel(pairs, near_own, following, near_blocks, total):
    leaves = following.shape[0]
    step = pl.program_id(0)
    nears = near_blocks.shape[0]

    @pl.when(step == 0)
    def _():
        total[...] = near_own[...]

    terms = []
    for i in range(nears):
        a, b = pairs[0, step * nears + i], pairs[1, step * nears + i]
        first = (a // leaves) * leaves
        a, b = a - first, b - first

        x = following[b % leaves]
        x = jnp.where(b >= leaves, x, jnp.zeros_like(x))
        terms.append((a, dot_nt(x, near_blocks[i])))
    for at, term in terms:
        total[at] += term


def far_gather(mom, far_pairs, b_ref, leaves, parents):
    rows, slots = mom.shape[0], b_ref.shape[1]
    wide = mom.shape[1] // 3
    row_id = iota((rows, slots), 0)
    base_leaf = row_id // parents * leaves + row_id % parents
    partner = far_pairs[1:2, :]
    total = None
    for h in range(2):
        hot = one_hot(partner == base_leaf + h * parents)
        part = dot_tn(mom[:, h * wide : (h + 1) * wide], hot)
        total = part if total is None else total + part
    b_ref[...] = total


def far_chunks(far_c, b_ref, fw):
    rank, slots = far_c.shape[0], far_c.shape[2]
    some = b_ref.shape[0] // rank

    def chunk(sb, k8):
        lanes = slice(sb * LANES, (sb + 1) * LANES)
        parts = [[] for _ in range(some)]
        for i in range(8):
            c = far_c[k8 * 8 + i, :, lanes].astype(F32)
            for r in range(some):
                prod = c * b_ref[r * rank : (r + 1) * rank, lanes]
                parts[r].append(sum(prod[j * 8 : (j + 1) * 8] for j in range(rank // 8)))
        for r in range(some):
            first = r * rank + k8 * 8
            fw[first : first + 8, lanes] = row_sums(parts[r])

    return [
        functools.partial(chunk, sb, k8) for sb in range(slots // LANES) for k8 in range(rank // 8)
    ]


def far_scatter(far_pairs, fw, leaves):
    hot = one_hot(far_pairs[0:1, :] % leaves == iota((leaves, fw.shape[1]), 0))
    high, low = split2(fw[...])
    return dot_nt(hot, high) + dot_nt(hot, low)


def far_kernel(
    got,
    far_pairs,
    far_c,
    par_pairs,
    parent_of,
    par_c,
    half,
    back,
    par_t,
    pick,
    to_owner,
    to_leaf,
    b_ref,
    fw,
):
    leaves, width = back.shape
    parents = leaves // 2
    rows = got.shape[0]
    index = got[:, width : width + LANES].astype(F32)[:, :leaves].astype(jnp.int32)
    hot = one_hot(index == iota((rows, leaves), 1))
    back[...] = dot_tn(hot, got[:, 0:width])
    mom = got[:, 2 * width + LANES :]
    far_gather(mom, far_pairs, b_ref, leaves, parents)
    for chunk in far_chunks(far_c, b_ref, fw):
        chunk()
    half[...] = far_scatter(far_pairs, fw, leaves)

    pairs = par_c.shape[0]
    rhs = to_owner.shape[0] // parents
    for s in range(pairs):
        par_t[s] = par_c[s].astype(F32).T.astype(BF16)
    hot = jnp.where(par_pairs[1:2, :] == iota((rows, pairs), 0), 1.0, 0.0)
    pick[...] = hot.T.astype(BF16)
    to_owner[...] = by_rows(par_pairs[0:1, :], parents, rhs).astype(BF16)
    to_leaf[...] = by_rows(parent_of[...], parents, rhs).T.astype(BF16)


def post_kernel(
    core_smem,
    half,
    back,
    mom2,
    got,
    bases,
    transfers,
    far_pairs,
    far_c,
    par_t,
    pick,
    to_owner,
    to_leaf,
    near_own,
    near_back,
    out,
    b_ref,
    fw,
    g_ref,
    pf,
    lf,
    pb,
    dn,
):
    leaves, rank, _ = bases.shape
    width = back.shape[1]
    rhs = width // rank
    pairs = par_t.shape[0]
    parents = leaves // 2
    rows = got.shape[0]
    core = core_smem[0, 0] // leaves % 2

    def in_order(mine, other):
        return jnp.concatenate(
            [jnp.where(core == 0, mine, other), jnp.where(core == 0, other, mine)], axis=1
        )

    wide = mom2.shape[1] // 3
    shared = in_order(got[:, got.shape[1] - wide :], mom2[:, 2 * wide :])
    fold = one_hot(iota((parents, rows), 1) % parents == iota((parents, rows), 0))
    at = width + LANES
    lanes_to_rows(pb, dot_nn(fold, got[:, at : at + width]), rhs)
    far_gather(mom2[...], far_pairs, b_ref, leaves, parents)
    chunks = far_chunks(far_c, b_ref, fw)
    each = len(chunks) // 8

    def some_chunks(group):
        for chunk in chunks[group * each : (group + 1) * each]:
            chunk()

    picked = dot_nn(pick[...], shared)
    some_chunks(0)
    lanes_to_rows(g_ref, picked, rhs)
    for s in range(pairs):
        at = slice(s * rhs, (s + 1) * rhs)
        pf[at, :] = dot_nn(g_ref[at, :].astype(BF16), par_t[s])
        if s % (pairs // 4) == pairs // 4 - 1:
            some_chunks(1 + s // (pairs // 4))
    high, low = split2(pf[...])
    locals_p = dot_nn(to_owner[...], high) + dot_nn(to_owner[...], low) + pb[...]
    some_chunks(5)
    picked = dot_nn(to_leaf[...], locals_p.astype(BF16))
    some_chunks(6)
    some_chunks(7)
    for l in range(leaves):
        at = slice(l * rhs, (l + 1) * rhs)
        dn[at, :] = dot_nn(picked[at, :].astype(BF16), transfers[l])

    other = far_scatter(far_pairs, fw, leaves)
    lanes_to_rows(lf, back[...] + in_order(half[...], other), rhs)
    for l in range(leaves):
        at = slice(l * rhs, (l + 1) * rhs)
        mine = (lf[at, :] + dn[at, :]).astype(BF16)
        near = near_own[l] + near_back[l].astype(F32)
        out[l] = dot_nn(mine, bases[l]) + near


def after(value, earlier, vmem_limit):
    anywhere = pl.BlockSpec(memory_space=pl.ANY)
    return pl.pallas_call(
        lambda *refs: None,
        out_shape=jax.ShapeDtypeStruct(value.shape, value.dtype),
        in_specs=[anywhere] * (1 + len(earlier)),
        out_specs=anywhere,
        input_output_aliases={0: 0},
        compiler_params=pltpu.CompilerParams(vmem_limit_bytes=vmem_limit),
        name="after",
    )(value, *earlier)


def passed_along(value, axis, steps):
    count = lax.axis_size(axis)
    leading, last = (max(0, -steps), min(count, count - steps))
    return lax.ppermute(value, axis, [(source, source + steps) for source in range(leading, last)])


def on_device(
    charges,
    self_blocks,
    near_blocks,
    near_pairs,
    bases,
    transfers,
    parent_of,
    far_pairs,
    far_coupling,
    par_pairs,
    par_coupling,
):
    leaves, rhs, panels = charges.shape
    rank = bases.shape[1]
    width = rhs * rank
    slots = far_coupling.shape[0]
    pairs = par_coupling.shape[0]
    parents = leaves // 2
    devices = lax.axis_size("sfc")
    rows = devices * parents
    columns = 2 * width + LANES + 3 * width // 2
    vmem = pl.BlockSpec(memory_space=pltpu.VMEM)
    smem = pl.BlockSpec(memory_space=pltpu.SMEM)
    hbm = pl.BlockSpec(memory_space=pltpu.HBM)
    params = pltpu.CompilerParams(vmem_limit_bytes=60 * 1024 * 1024)
    late = pltpu.CompilerParams(vmem_limit_bytes=48 * 1024 * 1024)

    def cost(moved):
        return pl.CostEstimate(flops=4 * moved, bytes_accessed=moved, transcendentals=0)

    following = passed_along(charges, "sfc", -1)
    far_pairs = far_pairs.T
    par_pairs = par_pairs.T
    near_pairs = near_pairs.T
    far_c = jnp.transpose(far_coupling, (1, 2, 0))
    parent_of = parent_of.reshape(1, leaves)

    def like(value, memory=pltpu.VMEM):
        return memory(value.shape, value.dtype)

    send, token = pl.pallas_call(
        pre_kernel,
        out_shape=[
            jax.ShapeDtypeStruct((rows, columns), BF16),
            jax.ShapeDtypeStruct((8, LANES), F32),
        ],
        in_specs=[hbm] * 8,
        out_specs=[vmem] * 2,
        scratch_shapes=[
            like(charges),
            like(bases),
            like(transfers),
            like(parent_of),
            like(far_pairs),
            like(far_c),
            like(par_pairs),
            like(par_coupling),
            like(par_pairs, pltpu.SMEM),
            pltpu.SemaphoreType.DMA((9,)),
            pltpu.VMEM((leaves * rhs, rank), F32),
            pltpu.VMEM((leaves * rhs, rank), F32),
            pltpu.VMEM((parents * rhs, rank), F32),
            pltpu.VMEM((pairs * rhs, rank), F32),
            pltpu.VMEM((width, slots), F32),
            pltpu.VMEM((width + LANES, slots), BF16),
        ],
        compiler_params=params,
        cost_estimate=cost(10_000_000),
        name="upward",
    )(charges, bases, transfers, parent_of, far_pairs, far_c, par_pairs, par_coupling)
    got = lax.all_to_all(send, "sfc", split_axis=0, concat_axis=0, tiled=True)
    steps = 4
    selves, nears = leaves // steps, near_blocks.shape[0] // steps
    whole = lambda *shape: pl.BlockSpec(shape, lambda i: (0,) * len(shape))
    near_params = pltpu.CompilerParams(vmem_limit_bytes=52 * 1024 * 1024)
    near_own, near_away = pl.pallas_call(
        near_kernel,
        grid=(steps,),
        out_shape=[
            jax.ShapeDtypeStruct((leaves, rhs, panels), F32),
            jax.ShapeDtypeStruct((leaves, rhs, panels), BF16),
        ],
        in_specs=[
            smem,
            pl.BlockSpec(memory_space=pl.ANY),
            whole(leaves, rhs, panels),
            pl.BlockSpec((selves, panels, panels), lambda i: (i, 0, 0)),
            pl.BlockSpec((nears, panels, panels), lambda i: (i, 0, 0)),
        ],
        out_specs=[whole(leaves, rhs, panels)] * 2,
        scratch_shapes=[pltpu.VMEM((2 * leaves, rhs, panels), F32)],
        compiler_params=near_params,
        cost_estimate=cost(20_000_000),
        name="near",
    )(near_pairs, token, charges, self_blocks, near_blocks)
    near_own = pl.pallas_call(
        cross_kernel,
        grid=(steps,),
        out_shape=jax.ShapeDtypeStruct((leaves, rhs, panels), F32),
        in_specs=[
            smem,
            whole(leaves, rhs, panels),
            whole(leaves, rhs, panels),
            pl.BlockSpec((nears, panels, panels), lambda i: (i, 0, 0)),
        ],
        out_specs=whole(leaves, rhs, panels),
        compiler_params=near_params,
        cost_estimate=cost(8_000_000),
        name="cross",
    )(near_pairs, near_own, following, near_blocks)
    near_back = passed_along(near_away, "sfc", 1)

    got = after(got, [near_back, near_own], 1 << 20)
    mom2 = lax.ppermute(
        got[:, 2 * width + LANES :], "sfc", [(i, i ^ 1) for i in range(devices)]
    )

    half, back, *prepared = pl.pallas_call(
        far_kernel,
        out_shape=[
            jax.ShapeDtypeStruct((leaves, width // 2), F32),
            jax.ShapeDtypeStruct((leaves, width), F32),
            jax.ShapeDtypeStruct(par_coupling.shape, BF16),
            jax.ShapeDtypeStruct((pairs, rows), BF16),
            jax.ShapeDtypeStruct((parents * rhs, pairs * rhs), BF16),
            jax.ShapeDtypeStruct((leaves * rhs, parents * rhs), BF16),
        ],
        in_specs=[vmem] * 6,
        out_specs=[vmem] * 6,
        scratch_shapes=[pltpu.VMEM((width // 2, slots), F32)] * 2,
        compiler_params=late,
        cost_estimate=cost(8_000_000),
        name="far",
    )(got, far_pairs, far_c, par_pairs, parent_of, par_coupling)

    return pl.pallas_call(
        post_kernel,
        out_shape=jax.ShapeDtypeStruct((leaves, rhs, panels), F32),
        in_specs=[smem] + [vmem] * 14,
        out_specs=vmem,
        scratch_shapes=[
            pltpu.VMEM((width // 2, slots), F32),
            pltpu.VMEM((width // 2, slots), F32),
            pltpu.VMEM((pairs * rhs, rank), F32),
            pltpu.VMEM((pairs * rhs, rank), F32),
            pltpu.VMEM((leaves * rhs, rank), F32),
            pltpu.VMEM((parents * rhs, rank), F32),
            pltpu.VMEM((leaves * rhs, rank), F32),
        ],
        compiler_params=late,
        name="downward",
    )(
        far_pairs,
        half,
        back,
        mom2,
        got,
        bases,
        transfers,
        far_pairs,
        far_c,
        *prepared,
        near_own,
        near_back,
    )


def solution(mesh):
    split = ("grp", "sfc")
    cube, flat = P(split, None, None), P(split, None)
    placed = (cube, cube, cube, flat, cube, cube, P(split), flat, cube, flat, cube)
    return jax.shard_map(
        on_device, mesh=mesh, in_specs=placed, out_specs=cube, check_vma=False
    )
```

```python
import functools

import jax
import jax.numpy as jnp
from jax import lax
from jax.experimental import pallas as pl
from jax.experimental.pallas import tpu as pltpu
from jax.sharding import PartitionSpec as P

F32 = jnp.float32
BF16 = jnp.bfloat16
LANES = 128


def dot_nn(a, b):
    return lax.dot_general(a, b, (((1,), (0,)), ((), ())), preferred_element_type=F32)


def dot_nt(a, b):
    return lax.dot_general(a, b, (((1,), (1,)), ((), ())), preferred_element_type=F32)


def dot_tn(a, b):
    return lax.dot_general(a, b, (((0,), (0,)), ((), ())), preferred_element_type=F32)


def split2(x):
    high = x.astype(BF16)
    return high, (x - high.astype(F32)).astype(BF16)


def iota(shape, axis):
    return lax.broadcasted_iota(jnp.int32, shape, axis)


def one_hot(condition):
    return jnp.where(condition, 1.0, 0.0).astype(BF16)


def rows_to_lanes(ref, count, rhs):
    return jnp.concatenate([ref[pl.ds(r, count, stride=rhs), :] for r in range(rhs)], axis=1)


def lanes_to_rows(ref, value, rhs):
    count, width = value.shape
    rank = width // rhs
    for r in range(rhs):
        ref[pl.ds(r, count, stride=rhs), :] = value[:, r * rank : (r + 1) * rank]


def repeated(values, times):
    count = values.shape[1]
    spread = one_hot(iota((count, count * times), 1) // times == iota((count, count * times), 0))
    rows = jnp.broadcast_to(values.astype(F32), (8, count)).astype(BF16)
    return dot_nn(rows, spread)[0:1].astype(jnp.int32)


def by_rows(targets, parents, rhs):
    shape = (parents * rhs, targets.shape[1] * rhs)
    row, column = iota(shape, 0), iota(shape, 1)
    same = (repeated(targets % parents, rhs) == row // rhs) & (row % rhs == column % rhs)
    return jnp.where(same, 1.0, 0.0)


def row_sums(parts):
    row = iota(parts[0].shape, 0)
    for step in (4, 2, 1):
        upper = row % (2 * step) >= step
        merged = []
        for a, b in zip(parts[:step], parts[step:]):
            swapped = jnp.where(upper, a, b)
            if step == 4:
                moved = pltpu.roll(swapped, 4, axis=0)
            else:
                moved = jnp.where(
                    upper,
                    pltpu.roll(swapped, step, axis=0),
                    pltpu.roll(swapped, 8 - step, axis=0),
                )
            merged.append(jnp.where(upper, b, a) + moved)
        parts = merged
    return parts[0]


def fetch(pairs, sems):
    copies = [pltpu.make_async_copy(src, dst, sems.at[i]) for i, (src, dst) in enumerate(pairs)]
    for copy in copies:
        copy.start()
    return copies


def pre_kernel(
    charges_h,
    bases_h,
    transfers_h,
    parent_of_h,
    far_pairs_h,
    far_c_h,
    par_pairs_h,
    par_c_h,
    send,
    token,
    charges,
    bases,
    transfers,
    parent_of,
    far_pairs,
    far_c,
    par_pairs,
    par_c,
    par_smem,
    sems,
    mo,
    ch,
    pm3,
    pb,
    a_ref,
    ob,
):
    token[...] = jnp.zeros_like(token)
    leaves, rhs, _ = charges.shape
    rank = bases.shape[1]
    width = rhs * rank
    slots = far_c.shape[2]
    pairs = par_c.shape[0]
    parents = leaves // 2
    rows = send.shape[0]
    copies = fetch(
        [
            (parent_of_h, parent_of),
            (far_pairs_h, far_pairs),
            (par_pairs_h, par_pairs),
            (charges_h, charges),
            (bases_h, bases),
            (transfers_h, transfers),
            (par_pairs_h, par_smem),
            (far_c_h, far_c),
            (par_c_h, par_c),
        ],
        sems,
    )
    for copy in copies[:3]:
        copy.wait()
    to_parent = by_rows(parent_of[...], parents, rhs).astype(BF16)
    owner_hot = one_hot(far_pairs[0:1, :] % leaves == iota((leaves, slots), 0))
    partner_hot = one_hot(par_pairs[1:2, :] == iota((rows, pairs), 0))
    partner = far_pairs[1:2, :]
    local = jnp.where(partner >= 0, partner % leaves, -1).astype(F32)
    ob[width : width + LANES, :] = jnp.broadcast_to(local, (LANES, slots)).astype(BF16)
    unit = one_hot(iota((LANES, LANES), 0) == iota((LANES, LANES), 1))

    for copy in copies[3:5]:
        copy.wait()
    ms = [dot_nt(charges[l], bases[l]).astype(BF16) for l in range(leaves)]
    for l in range(leaves):
        mo[l * rhs : (l + 1) * rhs, :] = ms[l].astype(F32)
    copies[5].wait()
    for l in range(leaves):
        ch[l * rhs : (l + 1) * rhs, :] = dot_nt(ms[l], transfers[l])
    m2 = rows_to_lanes(mo, leaves, rhs)
    a_ref[...] = dot_tn(m2.astype(BF16), owner_hot)
    high, low = split2(ch[...])
    pm3[...] = (dot_nn(to_parent, high) + dot_nn(to_parent, low)).astype(BF16).astype(F32)
    for copy in copies[6:]:
        copy.wait()
    pm = rows_to_lanes(pm3, parents, rhs)
    half = 3 * width // 2
    shared = [
        jnp.concatenate([x[:, c * width // 2 : (c + 1) * width // 2] for x in (m2[:parents], m2[parents:], pm)], axis=1)
        for c in range(2)
    ]
    shared = jnp.concatenate(shared, axis=0).astype(BF16)
    at = 2 * width + LANES
    for p in range(rows // (2 * parents)):
        send[p * 2 * parents : (p + 1) * 2 * parents, at : at + half] = shared

    def parent_products(first, last):
        for s in range(first, last):
            q = par_smem[0, s] % parents
            x = pm3[pl.ds(pl.multiple_of(q * rhs, rhs), rhs), :].astype(BF16)
            pb[s * rhs : (s + 1) * rhs, :] = dot_nn(x, par_c[s])

    some = rank // 4
    parent_products(0, pairs // 4)
    for sb in range(slots // LANES):
        lanes = slice(sb * LANES, (sb + 1) * LANES)
        for part in range(4):
            first = part * some
            acc = [None] * rhs
            for k in range(rank):
                c = far_c[k, first : first + some, lanes].astype(F32)
                for r in range(rhs):
                    term = c * a_ref[r * rank + k : r * rank + k + 1, lanes]
                    acc[r] = term if k == 0 else acc[r] + term
            for r in range(rhs):
                at = r * rank + first
                ob[at : at + some, lanes] = acc[r].astype(BF16)
            if sb == 0 and part < 2:
                parent_products(pairs // 4 * (part + 1), pairs // 4 * (part + 2))
            if sb == 0 and part == 2:
                parent_products(pairs // 4 * 3, pairs)
                high, low = split2(rows_to_lanes(pb, pairs, rhs))
                at = width + LANES
                sums = dot_nn(partner_hot, high) + dot_nn(partner_hot, low)
                send[:, at : at + width] = sums.astype(BF16)
    for sb in range(slots // LANES):
        lanes = slice(sb * LANES, (sb + 1) * LANES)
        send[lanes, 0 : width + LANES] = dot_nt(unit, ob[:, lanes]).astype(BF16)


def near_kernel(pairs, earlier, charges, self_blocks, near_blocks, own, away, out):
    leaves = charges.shape[0]
    step = pl.program_id(0)
    selves, nears = self_blocks.shape[0], near_blocks.shape[0]

    @pl.when(step == 0)
    def _():
        out[...] = jnp.zeros_like(out)

    terms = []
    for i in range(selves):
        l = step * selves + i
        terms.append((l, dot_nt(charges[l], self_blocks[i])))
    for i in range(nears):
        a, b = pairs[0, step * nears + i], pairs[1, step * nears + i]
        first = (a // leaves) * leaves
        a, b = a - first, b - first
        x = charges[b % leaves]
        x = jnp.where(b < leaves, x, jnp.zeros_like(x))
        terms.append((a, dot_nt(x, near_blocks[i])))
        terms.append((b, dot_nn(charges[a], near_blocks[i])))
    for at, term in terms:
        out[at] += term

    @pl.when(step == pl.num_programs(0) - 1)
    def _():
        own[...] = out[0:leaves]
        away[...] = out[leaves:].astype(BF16)


def cross_kernel(pairs, near_own, following, near_blocks, total):
    leaves = following.shape[0]
    step = pl.program_id(0)
    nears = near_blocks.shape[0]

    @pl.when(step == 0)
    def _():
        total[...] = near_own[...]

    terms = []
    for i in range(nears):
        a, b = pairs[0, step * nears + i], pairs[1, step * nears + i]
        first = (a // leaves) * leaves
        a, b = a - first, b - first

        x = following[b % leaves]
        x = jnp.where(b >= leaves, x, jnp.zeros_like(x))
        terms.append((a, dot_nt(x, near_blocks[i])))
    for at, term in terms:
        total[at] += term


def far_gather(mom, far_pairs, b_ref, leaves, parents):
    rows, slots = mom.shape[0], b_ref.shape[1]
    wide = mom.shape[1] // 3
    row_id = iota((rows, slots), 0)
    base_leaf = row_id // parents * leaves + row_id % parents
    partner = far_pairs[1:2, :]
    total = None
    for h in range(2):
        hot = one_hot(partner == base_leaf + h * parents)
        part = dot_tn(mom[:, h * wide : (h + 1) * wide], hot)
        total = part if total is None else total + part
    b_ref[...] = total


def far_chunks(far_c, b_ref, fw):
    rank, slots = far_c.shape[0], far_c.shape[2]
    some = b_ref.shape[0] // rank

    def chunk(sb, k8):
        lanes = slice(sb * LANES, (sb + 1) * LANES)
        parts = [[] for _ in range(some)]
        for i in range(8):
            c = far_c[k8 * 8 + i, :, lanes].astype(F32)
            for r in range(some):
                prod = c * b_ref[r * rank : (r + 1) * rank, lanes]
                parts[r].append(sum(prod[j * 8 : (j + 1) * 8] for j in range(rank // 8)))
        for r in range(some):
            first = r * rank + k8 * 8
            fw[first : first + 8, lanes] = row_sums(parts[r])

    return [
        functools.partial(chunk, sb, k8) for sb in range(slots // LANES) for k8 in range(rank // 8)
    ]


def far_scatter(far_pairs, fw, leaves):
    hot = one_hot(far_pairs[0:1, :] % leaves == iota((leaves, fw.shape[1]), 0))
    high, low = split2(fw[...])
    return dot_nt(hot, high) + dot_nt(hot, low)


def far_kernel(
    got,
    far_pairs,
    far_c,
    par_pairs,
    parent_of,
    par_c,
    half,
    back,
    par_t,
    pick,
    to_owner,
    to_leaf,
    b_ref,
    fw,
):
    leaves, width = back.shape
    parents = leaves // 2
    rows = got.shape[0]
    index = got[:, width : width + LANES].astype(F32)[:, :leaves].astype(jnp.int32)
    hot = one_hot(index == iota((rows, leaves), 1))
    back[...] = dot_tn(hot, got[:, 0:width])
    mom = got[:, 2 * width + LANES :]
    far_gather(mom, far_pairs, b_ref, leaves, parents)
    for chunk in far_chunks(far_c, b_ref, fw):
        chunk()
    half[...] = far_scatter(far_pairs, fw, leaves)

    pairs = par_c.shape[0]
    rhs = to_owner.shape[0] // parents
    for s in range(pairs):
        par_t[s] = par_c[s].astype(F32).T.astype(BF16)
    hot = jnp.where(par_pairs[1:2, :] == iota((rows, pairs), 0), 1.0, 0.0)
    pick[...] = hot.T.astype(BF16)
    to_owner[...] = by_rows(par_pairs[0:1, :], parents, rhs).astype(BF16)
    to_leaf[...] = by_rows(parent_of[...], parents, rhs).T.astype(BF16)


def post_kernel(
    core_smem,
    half,
    back,
    mom2,
    got,
    bases,
    transfers,
    far_pairs,
    far_c,
    par_t,
    pick,
    to_owner,
    to_leaf,
    near_own,
    near_back,
    out,
    b_ref,
    fw,
    g_ref,
    pf,
    lf,
    pb,
    dn,
):
    leaves, rank, _ = bases.shape
    width = back.shape[1]
    rhs = width // rank
    pairs = par_t.shape[0]
    parents = leaves // 2
    rows = got.shape[0]
    core = core_smem[0, 0] // leaves % 2

    def in_order(mine, other):
        return jnp.concatenate(
            [jnp.where(core == 0, mine, other), jnp.where(core == 0, other, mine)], axis=1
        )

    wide = mom2.shape[1] // 3
    shared = in_order(got[:, got.shape[1] - wide :], mom2[:, 2 * wide :])
    fold = one_hot(iota((parents, rows), 1) % parents == iota((parents, rows), 0))
    at = width + LANES
    lanes_to_rows(pb, dot_nn(fold, got[:, at : at + width]), rhs)
    far_gather(mom2[...], far_pairs, b_ref, leaves, parents)
    chunks = far_chunks(far_c, b_ref, fw)
    each = len(chunks) // 8

    def some_chunks(group):
        for chunk in chunks[group * each : (group + 1) * each]:
            chunk()

    picked = dot_nn(pick[...], shared)
    some_chunks(0)
    lanes_to_rows(g_ref, picked, rhs)
    for s in range(pairs):
        at = slice(s * rhs, (s + 1) * rhs)
        pf[at, :] = dot_nn(g_ref[at, :].astype(BF16), par_t[s])
        if s % (pairs // 4) == pairs // 4 - 1:
            some_chunks(1 + s // (pairs // 4))
    high, low = split2(pf[...])
    locals_p = dot_nn(to_owner[...], high) + dot_nn(to_owner[...], low) + pb[...]
    some_chunks(5)
    picked = dot_nn(to_leaf[...], locals_p.astype(BF16))
    some_chunks(6)
    some_chunks(7)
    for l in range(leaves):
        at = slice(l * rhs, (l + 1) * rhs)
        dn[at, :] = dot_nn(picked[at, :].astype(BF16), transfers[l])

    other = far_scatter(far_pairs, fw, leaves)
    lanes_to_rows(lf, back[...] + in_order(half[...], other), rhs)
    for l in range(leaves):
        at = slice(l * rhs, (l + 1) * rhs)
        mine = (lf[at, :] + dn[at, :]).astype(BF16)
        near = near_own[l] + near_back[l].astype(F32)
        out[l] = dot_nn(mine, bases[l]) + near


def after(value, earlier, vmem_limit):
    anywhere = pl.BlockSpec(memory_space=pl.ANY)
    return pl.pallas_call(
        lambda *refs: None,
        out_shape=jax.ShapeDtypeStruct(value.shape, value.dtype),
        in_specs=[anywhere] * (1 + len(earlier)),
        out_specs=anywhere,
        input_output_aliases={0: 0},
        compiler_params=pltpu.CompilerParams(vmem_limit_bytes=vmem_limit),
        name="after",
    )(value, *earlier)


def passed_along(value, axis, steps):
    count = lax.axis_size(axis)
    leading, last = (max(0, -steps), min(count, count - steps))
    return lax.ppermute(value, axis, [(source, source + steps) for source in range(leading, last)])


def on_device(
    charges,
    self_blocks,
    near_blocks,
    near_pairs,
    bases,
    transfers,
    parent_of,
    far_pairs,
    far_coupling,
    par_pairs,
    par_coupling,
):
    leaves, rhs, panels = charges.shape
    rank = bases.shape[1]
    width = rhs * rank
    slots = far_coupling.shape[0]
    pairs = par_coupling.shape[0]
    parents = leaves // 2
    devices = lax.axis_size("sfc")
    rows = devices * parents
    columns = 2 * width + LANES + 3 * width // 2
    vmem = pl.BlockSpec(memory_space=pltpu.VMEM)
    smem = pl.BlockSpec(memory_space=pltpu.SMEM)
    hbm = pl.BlockSpec(memory_space=pltpu.HBM)
    params = pltpu.CompilerParams(vmem_limit_bytes=60 * 1024 * 1024)
    late = pltpu.CompilerParams(vmem_limit_bytes=48 * 1024 * 1024)

    def cost(moved):
        return pl.CostEstimate(flops=4 * moved, bytes_accessed=moved, transcendentals=0)

    following = passed_along(charges, "sfc", -1)
    far_pairs = far_pairs.T
    par_pairs = par_pairs.T
    near_pairs = near_pairs.T
    far_c = jnp.transpose(far_coupling, (1, 2, 0))
    parent_of = parent_of.reshape(1, leaves)

    def like(value, memory=pltpu.VMEM):
        return memory(value.shape, value.dtype)

    send, token = pl.pallas_call(
        pre_kernel,
        out_shape=[
            jax.ShapeDtypeStruct((rows, columns), BF16),
            jax.ShapeDtypeStruct((8, LANES), F32),
        ],
        in_specs=[hbm] * 8,
        out_specs=[vmem] * 2,
        scratch_shapes=[
            like(charges),
            like(bases),
            like(transfers),
            like(parent_of),
            like(far_pairs),
            like(far_c),
            like(par_pairs),
            like(par_coupling),
            like(par_pairs, pltpu.SMEM),
            pltpu.SemaphoreType.DMA((9,)),
            pltpu.VMEM((leaves * rhs, rank), F32),
            pltpu.VMEM((leaves * rhs, rank), F32),
            pltpu.VMEM((parents * rhs, rank), F32),
            pltpu.VMEM((pairs * rhs, rank), F32),
            pltpu.VMEM((width, slots), F32),
            pltpu.VMEM((width + LANES, slots), BF16),
        ],
        compiler_params=params,
        cost_estimate=cost(10_000_000),
        name="upward",
    )(charges, bases, transfers, parent_of, far_pairs, far_c, par_pairs, par_coupling)
    got = lax.all_to_all(send, "sfc", split_axis=0, concat_axis=0, tiled=True)
    steps = 4
    selves, nears = leaves // steps, near_blocks.shape[0] // steps
    whole = lambda *shape: pl.BlockSpec(shape, lambda i: (0,) * len(shape))
    near_params = pltpu.CompilerParams(vmem_limit_bytes=52 * 1024 * 1024)
    near_own, near_away = pl.pallas_call(
        near_kernel,
        grid=(steps,),
        out_shape=[
            jax.ShapeDtypeStruct((leaves, rhs, panels), F32),
            jax.ShapeDtypeStruct((leaves, rhs, panels), BF16),
        ],
        in_specs=[
            smem,
            pl.BlockSpec(memory_space=pl.ANY),
            whole(leaves, rhs, panels),
            pl.BlockSpec((selves, panels, panels), lambda i: (i, 0, 0)),
            pl.BlockSpec((nears, panels, panels), lambda i: (i, 0, 0)),
        ],
        out_specs=[whole(leaves, rhs, panels)] * 2,
        scratch_shapes=[pltpu.VMEM((2 * leaves, rhs, panels), F32)],
        compiler_params=params,
        cost_estimate=cost(20_000_000),
        name="near",
    )(near_pairs, token, charges, self_blocks, near_blocks)
    near_own = pl.pallas_call(
        cross_kernel,
        grid=(steps,),
        out_shape=jax.ShapeDtypeStruct((leaves, rhs, panels), F32),
        in_specs=[
            smem,
            whole(leaves, rhs, panels),
            whole(leaves, rhs, panels),
            pl.BlockSpec((nears, panels, panels), lambda i: (i, 0, 0)),
        ],
        out_specs=whole(leaves, rhs, panels),
        compiler_params=near_params,
        cost_estimate=cost(8_000_000),
        name="cross",
    )(near_pairs, near_own, following, near_blocks)
    near_back = passed_along(near_away, "sfc", 1)

    got = after(got, [near_back, near_own], 1 << 20)
    mom2 = lax.ppermute(
        got[:, 2 * width + LANES :], "sfc", [(i, i ^ 1) for i in range(devices)]
    )

    half, back, *prepared = pl.pallas_call(
        far_kernel,
        out_shape=[
            jax.ShapeDtypeStruct((leaves, width // 2), F32),
            jax.ShapeDtypeStruct((leaves, width), F32),
            jax.ShapeDtypeStruct(par_coupling.shape, BF16),
            jax.ShapeDtypeStruct((pairs, rows), BF16),
            jax.ShapeDtypeStruct((parents * rhs, pairs * rhs), BF16),
            jax.ShapeDtypeStruct((leaves * rhs, parents * rhs), BF16),
        ],
        in_specs=[vmem] * 6,
        out_specs=[vmem] * 6,
        scratch_shapes=[pltpu.VMEM((width // 2, slots), F32)] * 2,
        compiler_params=late,
        cost_estimate=cost(8_000_000),
        name="far",
    )(got, far_pairs, far_c, par_pairs, parent_of, par_coupling)

    return pl.pallas_call(
        post_kernel,
        out_shape=jax.ShapeDtypeStruct((leaves, rhs, panels), F32),
        in_specs=[smem] + [vmem] * 14,
        out_specs=vmem,
        scratch_shapes=[
            pltpu.VMEM((width // 2, slots), F32),
            pltpu.VMEM((width // 2, slots), F32),
            pltpu.VMEM((pairs * rhs, rank), F32),
            pltpu.VMEM((pairs * rhs, rank), F32),
            pltpu.VMEM((leaves * rhs, rank), F32),
            pltpu.VMEM((parents * rhs, rank), F32),
            pltpu.VMEM((leaves * rhs, rank), F32),
        ],
        compiler_params=late,
        name="downward",
    )(
        far_pairs,
        half,
        back,
        mom2,
        got,
        bases,
        transfers,
        far_pairs,
        far_c,
        *prepared,
        near_own,
        near_back,
    )


def solution(mesh):
    split = ("grp", "sfc")
    cube, flat = P(split, None, None), P(split, None)
    placed = (cube, cube, cube, flat, cube, cube, P(split), flat, cube, flat, cube)
    return jax.shard_map(
        on_device, mesh=mesh, in_specs=placed, out_specs=cube, check_vma=False
    )
```
